32 devices in a mesh: task: 4 (over y, x), batch: 8 (over z, core).
Axes of the slice: x: 2, y: 2, z: 4, core: 2. Of those that a mesh axis runs over, the one named last changes fastest.
Arguments:
- tokens: bfloat16 [32768, 1024], P(('task', 'batch')), may hold values from -6 to 6
- lengths: int32 [32, 4], P(('task', 'batch')), may hold values from 0 to 1024, as said below
- task_ids: int32 [32, 4], replicated, may hold values from 0 to 63, as said below
- prefix_embed: bfloat16 [64, 10, 1024], P('task', None, 'batch'), may hold values from -6 to 6
- reparam_inner: bfloat16 [64, 1024, 512], P('task', 'batch'), may hold values from -0.1875 to 0.1875
- reparam_inner_bias: bfloat16 [64, 512], P('task'), may hold values from -3 to 3
- reparam_outer: bfloat16 [64, 512, 2048], P('task', None, 'batch'), may hold values from -0.4375 to 0.4375
- reparam_outer_bias: bfloat16 [64, 2048], P('task', 'batch'), may hold values from -3 to 3
- first_gain: bfloat16 [1024], replicated, may hold values from 0.5 to 1.5
- first_bias: bfloat16 [1024], replicated, may hold values from -3 to 3
- input_weight: bfloat16 [1024, 3072], replicated, may hold values from -0.1875 to 0.1875
- output_weight: bfloat16 [1024, 1024], replicated, may hold values from -1.5 to 1.5
- second_gain: bfloat16 [1024], replicated, may hold values from 0.5 to 1.5
- second_bias: bfloat16 [1024], replicated, may hold values from -3 to 3
- expand_weight: bfloat16 [1024, 4096], replicated, may hold values from -0.1875 to 0.1875
- contract_weight: bfloat16 [4096, 1024], replicated, may hold values from -0.09375 to 0.09375
- output_cotangent: bfloat16 [32768, 1024], P(('task', 'batch')), may hold values from -6 to 6
Outputs:
- output: bfloat16 [32768, 1024], P(('task', 'batch'))
- input_grad: bfloat16 [32768, 1024], P(('task', 'batch'))
- grad_embed: float32 [64, 10, 1024], P('task', None, 'batch')
- grad_inner: float32 [64, 1024, 512], P('task', 'batch')
- grad_inner_bias: float32 [64, 512], P('task')
- grad_outer: float32 [64, 512, 2048], P('task', None, 'batch')
- grad_outer_bias: float32 [64, 2048], P('task', 'batch')
The draws below stay inside these ranges and needn't reach their ends.
Inputs may be any that keep to these rules, and one draw needn't show every extreme that they name: `task_ids`: the 4 examples of one device have tasks t with 4 different values of t // 16. Each device's row is either 1024 followed by zeros (one sequence) or 4 lengths of 256; both kinds occur in every draw.
All inputs are finite; a program needn't handle non-finite values.
Results may differ from the reference program's by a relative error of at most 0.013.
Values may be sent and summed in bfloat16 or wider, within the bound.
A program may use at most 256 MiB of HBM per device.

```python
import jax
import jax.numpy as jnp
from jax import lax

D = 1024
HEADS = 16
FF = 4096
PREFIX = 10
REPARAM = 512
TASK_DEV = 16
TOK_DEV = 1024
SLOTS = 4
TASKS = 64
TOKENS = 32768
N_TASK = 4
N_BATCH = 8


def draw_lengths(key, part):
    key = jax.random.fold_in(key, 7)
    coin_key, pick_key = jax.random.split(key)
    device_count = N_TASK * N_BATCH
    longer = jax.random.randint(coin_key, (device_count,), 0, 4) > 0
    chosen = jax.random.permutation(pick_key, device_count)
    longer = longer.at[chosen[0]].set(True).at[chosen[1]].set(False)
    short_row = jnp.full((SLOTS,), TOK_DEV // SLOTS, dtype=jnp.int32)
    long_row = jnp.zeros((SLOTS,), dtype=jnp.int32).at[0].set(TOK_DEV)
    return jnp.where(longer[:, None], long_row[None, :], short_row[None, :]).astype(jnp.int32)


def draw_task_ids(key, part):
    key = jax.random.fold_in(key, 11)
    order_key, inside_key = jax.random.split(key)
    device_count = N_TASK * N_BATCH
    ranking = jax.random.randint(order_key, (device_count, SLOTS), 0, 1 << 20) * SLOTS + jnp.arange(SLOTS, dtype=jnp.int32)[None, :]
    owner_rows = jnp.argsort(ranking, axis=1).astype(jnp.int32)
    inside = jax.random.randint(inside_key, (device_count, SLOTS), 0, TASK_DEV)
    return (owner_rows * TASK_DEV + inside).astype(jnp.int32)


def shard_levels(key, extent, shards, least, high):
    loudness = 1.0
    for position, shards_of in shards:
        heights = jax.random.uniform(jax.random.fold_in(jax.random.fold_in(key, 6), position), (shards_of,), jnp.float32, least / len(shards), high / len(shards))
        loudness = loudness * jnp.repeat(jnp.exp(heights), extent[position] // shards_of).reshape((-1,) + (1,) * (len(extent) - 1 - position))
    return loudness


def bell_draw(key, dims, deviation, reach, shards=(), kind=jnp.bfloat16):
    values = deviation * jax.random.normal(key, dims, jnp.float32)
    if shards:
        values = values * shard_levels(key, dims, shards, -0.22, 0.18)
    return jnp.clip(values, -reach, reach).astype(kind)


def setup_inputs(seed: int = 0) -> dict:
    keys = jax.random.split(jax.random.key(seed), 18)
    return {
        "tokens": bell_draw(keys[0], (TOKENS, D), 1.0, 6.0, ((0, 32),)),
        "lengths": draw_lengths(jax.random.fold_in(keys[17], 71), 0),
        "task_ids": draw_task_ids(jax.random.fold_in(keys[17], 71), 0),
        "prefix_embed": bell_draw(keys[3], (TASKS, PREFIX, D), 1.0, 6.0, ((0, 4), (2, 8))),
        "reparam_inner": bell_draw(keys[4], (TASKS, D, REPARAM), D ** -0.5, 0.1875, ((0, 4), (1, 8))),
        "reparam_inner_bias": bell_draw(keys[5], (TASKS, REPARAM), 0.5, 3.0, ((0, 4),)),
        "reparam_outer": bell_draw(keys[6], (TASKS, REPARAM, 2 * D), (REPARAM // 3) ** -0.5, 0.4375, ((0, 4), (2, 8))),
        "reparam_outer_bias": bell_draw(keys[7], (TASKS, 2 * D), 0.5, 3.0, ((0, 4), (1, 8))),
        "first_gain": jnp.clip(1.0 + 0.1 * jax.random.normal(keys[8], (D,), jnp.float32), 0.5, 1.5).astype(jnp.bfloat16),
        "first_bias": bell_draw(keys[9], (D,), 0.3, 3.0),
        "input_weight": bell_draw(keys[10], (D, 3 * D), D ** -0.5, 0.1875),
        "output_weight": bell_draw(keys[11], (D, D), (D // 64) ** -0.5, 1.5),
        "second_gain": jnp.clip(1.0 + 0.1 * jax.random.normal(keys[12], (D,), jnp.float32), 0.5, 1.5).astype(jnp.bfloat16),
        "second_bias": bell_draw(keys[13], (D,), 0.3, 3.0),
        "expand_weight": bell_draw(keys[14], (D, FF), D ** -0.5, 0.1875),
        "contract_weight": bell_draw(keys[15], (FF, D), FF ** -0.5, 0.09375),
        "output_cotangent": bell_draw(keys[16], (TOKENS, D), 1.0, 6.0, ((0, 32),)),
    }


@jax.custom_vjp
def low(v):
    return lax.optimization_barrier(v.astype(jnp.bfloat16)).astype(jnp.float32)

@jax.custom_vjp
def low_back(v):
    return v

def low_keep(v):
    return (low(v), None)

def low_pass(kept, grad):
    return (grad,)

def back_keep(v):
    return (v, None)

def back_low(kept, grad):
    return (low(grad),)
low.defvjp(low_keep, low_pass)
low_back.defvjp(back_keep, back_low)
highest = lax.Precision.HIGHEST

def layer_norm(values, norm_gain, norm_bias):
    average = lax.optimization_barrier(jnp.mean(values, axis=-1, keepdims=True))
    centered = values - average
    variance = lax.optimization_barrier(jnp.mean(centered * centered, axis=-1, keepdims=True))
    return centered * lax.rsqrt(variance + 1e-05) * norm_gain + norm_bias

def gelu_tanh(values):
    return 0.5 * values * (1.0 + jnp.tanh(0.7978845608028654 * (values + 0.044715 * values * values * values)))

def build_visible(lengths_row, row_count, prefix_len):
    slot_ends = jnp.cumsum(lengths_row)
    positions = jnp.arange(row_count, dtype=jnp.int32)
    segment = lax.optimization_barrier(jnp.sum((positions[:, None] >= slot_ends[None, :]).astype(jnp.int32), axis=1))
    prefix_slot = jnp.arange(lengths_row.shape[0] * prefix_len, dtype=jnp.int32) // prefix_len
    prefix_seen = segment[:, None] == prefix_slot[None, :]
    token_seen = (segment[:, None] == segment[None, :]) & (positions[None, :] <= positions[:, None])
    return jnp.concatenate([prefix_seen, token_seen], axis=1)

def layer_rows(residual_in, prefix_kv, lengths_row, weights):
    first_gain, first_bias, input_weight, output_weight, second_gain, second_bias, expand_weight, contract_weight = weights
    row_count = residual_in.shape[0]
    head_dim = D // HEADS
    normed = low(layer_norm(residual_in, first_gain, first_bias))
    projected = low_back(low(jnp.dot(normed, input_weight, precision=highest)))
    queries = projected[:, :D].reshape(row_count, HEADS, head_dim)
    prefix_keys = prefix_kv[:, :, :D].reshape(SLOTS * PREFIX, D)
    prefix_values = prefix_kv[:, :, D:].reshape(SLOTS * PREFIX, D)
    keys_all = jnp.concatenate([prefix_keys, projected[:, D:2 * D]], axis=0).reshape(-1, HEADS, head_dim)
    values_all = jnp.concatenate([prefix_values, projected[:, 2 * D:]], axis=0).reshape(-1, HEADS, head_dim)
    visible = build_visible(lengths_row, row_count, PREFIX)
    scores = low_back(jnp.einsum('qhd,khd->hqk', queries, keys_all, precision=highest) * head_dim ** (-0.5))
    probs = jax.nn.softmax(jnp.where(visible[None], scores, -1e+30), axis=-1)
    mixed = jnp.einsum('hqk,khd->qhd', low(probs), values_all, precision=highest)
    attended = low_back(low(mixed.reshape(row_count, D)))
    mid = residual_in + low_back(jnp.dot(attended, output_weight, precision=highest))
    normed_two = low(layer_norm(mid, second_gain, second_bias))
    hidden_pre = low_back(jnp.dot(normed_two, expand_weight, precision=highest))
    activated = low(gelu_tanh(hidden_pre))
    return mid + jnp.dot(activated, contract_weight, precision=highest)

def reference(tokens, lengths, task_ids, prefix_embed, reparam_inner, reparam_inner_bias, reparam_outer, reparam_outer_bias, first_gain, first_bias, input_weight, output_weight, second_gain, second_bias, expand_weight, contract_weight, output_cotangent):
    weights = tuple((weight.astype(jnp.float32) for weight in (first_gain, first_bias, input_weight, output_weight, second_gain, second_bias, expand_weight, contract_weight)))
    device_count = N_TASK * N_BATCH

    def forward(residual_all, embed, inner, inner_bias, outer, outer_bias):
        pre = low_back(jnp.einsum('tpd,tdh->tph', embed, inner, precision=highest) + inner_bias[:, None, :])
        hidden = jnp.tanh(pre)
        table = low_back(low(jnp.einsum('tph,thc->tpc', low(hidden), outer, precision=highest) + outer_bias[:, None, :]))
        prefix_all = jnp.take(table, task_ids, axis=0)
        blocks = residual_all.reshape(device_count, TOK_DEV, D)
        run_block = jax.checkpoint(lambda block_parts: layer_rows(block_parts[0], block_parts[1], block_parts[2], weights))
        return lax.map(run_block, (blocks, prefix_all, lengths)).reshape(device_count * TOK_DEV, D)
    primal = tuple((array.astype(jnp.float32) for array in (tokens, prefix_embed, reparam_inner, reparam_inner_bias, reparam_outer, reparam_outer_bias)))
    result, pullback = jax.vjp(forward, *primal)
    grads = pullback(output_cotangent.astype(jnp.float32))
    return (result.astype(jnp.bfloat16), grads[0].astype(jnp.bfloat16), grads[1], grads[2], grads[3], grads[4], grads[5])
```

```python
import functools

import jax
import jax.numpy as jnp
from jax import lax
from jax.experimental import pallas as pl
from jax.experimental.pallas import tpu as pltpu
from jax.sharding import PartitionSpec as P


BF = jnp.bfloat16
F = jnp.float32
PAD = 16
NEG = -1e30


def dg(a, b, ca, cb):
    return lax.dot_general(a, b, (((ca,), (cb,)), ((), ())), preferred_element_type=F)


def attn_fwd_kernel(slots, plen, len_ref, q_ref, k_ref, v_ref, pk_ref, pv_ref, o_ref, lse_ref, km):
    rows, pair = q_ref.shape
    blk = rows // slots
    hd = pair // 2
    scale = hd ** -0.5
    single = len_ref[0, 0] > blk
    first = lax.broadcasted_iota(jnp.int32, (1, pair), 1) < hd
    zero = jnp.zeros((), BF)
    k = k_ref[...]
    km[0] = jnp.where(first, k, zero)
    km[1] = jnp.where(first, zero, k)
    vt = v_ref[...].T
    tri = lax.broadcasted_iota(jnp.int32, (blk, blk), 0) <= lax.broadcasted_iota(jnp.int32, (blk, blk), 1)
    live = lax.broadcasted_iota(jnp.int32, (PAD, blk), 0) < plen
    for i in range(slots):
        lo, hi = i * blk, (i + 1) * blk
        q = q_ref[lo:hi, :] * jnp.asarray(scale, BF)
        kp = jnp.where(single, pk_ref[0:PAD, :], pk_ref[i * PAD:(i + 1) * PAD, :])
        vp = jnp.where(single, pv_ref[0:PAD, :], pv_ref[i * PAD:(i + 1) * PAD, :])
        vpt = jnp.concatenate([jnp.where(first, vp, zero), jnp.where(first, zero, vp)], axis=0).T
        sp = dg(jnp.concatenate([jnp.where(first, kp, zero), jnp.where(first, zero, kp)], axis=0), q, 1, 1)
        outs, tops, sums, pps = [], [], [], []
        for h in range(2):
            s_pre = jnp.where(live, sp[h * PAD:(h + 1) * PAD], NEG)
            s_dia = jnp.where(tri, dg(km[h, lo:hi, :], q, 1, 1), NEG)
            top = jnp.maximum(jnp.max(s_dia, axis=0, keepdims=True), jnp.max(s_pre, axis=0, keepdims=True))
            if i:
                s_off = dg(km[h, 0:lo, :], q, 1, 1)
                top = jnp.maximum(top, jnp.where(single, jnp.max(s_off, axis=0, keepdims=True), NEG))
            p_pre = jnp.exp(s_pre - top)
            p_dia = jnp.exp(s_dia - top)
            total = jnp.sum(p_dia, axis=0, keepdims=True) + jnp.sum(p_pre, axis=0, keepdims=True)
            ot = dg(vt[h * hd:(h + 1) * hd, lo:hi], p_dia.astype(BF), 1, 0)
            if i:
                p_off = jnp.exp(s_off - jnp.where(single, top, -NEG))
                total = total + jnp.sum(p_off, axis=0, keepdims=True)
                ot = ot + dg(vt[h * hd:(h + 1) * hd, 0:lo], p_off.astype(BF), 1, 0)
            outs.append(ot)
            tops.append(top)
            sums.append(total)
            pps.append(p_pre.astype(BF))
        pre = dg(vpt, jnp.concatenate(pps, axis=0), 1, 0)
        for h in range(2):
            outs[h] = (outs[h] + pre[h * hd:(h + 1) * hd]) / sums[h]
            lse_ref[0, h:h + 1, lo:hi] = tops[h] + jnp.log(sums[h])
        o_ref[lo:hi, :] = jnp.concatenate(outs, axis=0).T.astype(BF)


def attn_fwd(lengths, qkv, pkv, plen):
    rows = qkv.shape[0]
    width = qkv.shape[1] // 3
    slots = lengths.shape[1]
    pairs = width // 128
    col = lambda off: pl.BlockSpec((rows, 128), lambda h: (0, h + off))
    pcol = lambda off: pl.BlockSpec((slots * PAD, 128), lambda h: (0, h + off))
    return pl.pallas_call(
        functools.partial(attn_fwd_kernel, slots, plen),
        grid=(pairs,),
        in_specs=[pl.BlockSpec(memory_space=pltpu.SMEM), col(0), col(pairs), col(2 * pairs), pcol(0), pcol(pairs)],
        out_specs=[col(0), pl.BlockSpec((1, 2, rows), lambda h: (h, 0, 0))],
        out_shape=[jax.ShapeDtypeStruct((rows, width), BF), jax.ShapeDtypeStruct((pairs, 2, rows), F)],
        scratch_shapes=[pltpu.VMEM((2, rows, 128), BF)],
        compiler_params=pltpu.CompilerParams(vmem_limit_bytes=48 * 2**20),
        name="attend",
    )(lengths, qkv, qkv, qkv, pkv, pkv)


def attn_bwd_kernel(slots, plen, len_ref, q_ref, k_ref, v_ref, pk_ref, pv_ref, o_ref, do_ref, lse_ref,
                    dq_ref, dk_ref, dv_ref, dpk_ref, dpv_ref, km, vm, dka, dva):
    rows, pair = q_ref.shape
    blk = rows // slots
    hd = pair // 2
    scale = hd ** -0.5
    single = len_ref[0, 0] > blk
    first = lax.broadcasted_iota(jnp.int32, (1, pair), 1) < hd
    zero = jnp.zeros((), BF)
    split = lambda a: (jnp.where(first, a, zero), jnp.where(first, zero, a))
    stack = lambda a: jnp.concatenate(split(a), axis=0)
    k = k_ref[...]
    km[0], km[1] = split(k)
    vm[0], vm[1] = split(v_ref[...])
    kt = k.T
    tri = lax.broadcasted_iota(jnp.int32, (blk, blk), 0) <= lax.broadcasted_iota(jnp.int32, (blk, blk), 1)
    live = lax.broadcasted_iota(jnp.int32, (PAD, blk), 0) < plen
    pk_sum = pv_sum = None
    pk_parts, pv_parts = [], []
    for i in range(slots):
        lo, hi = i * blk, (i + 1) * blk
        q = q_ref[lo:hi, :] * jnp.asarray(scale, BF)
        do = do_ref[lo:hi, :]
        kp = stack(jnp.where(single, pk_ref[0:PAD, :], pk_ref[i * PAD:(i + 1) * PAD, :]))
        vp = stack(jnp.where(single, pv_ref[0:PAD, :], pv_ref[i * PAD:(i + 1) * PAD, :]))
        sp = dg(kp, q, 1, 1)
        dpp = dg(vp, do, 1, 1)
        prod = (do.astype(F) * o_ref[lo:hi, :].astype(F)).T
        qs = split(q)
        dos = split(do)
        dqs, dsps = [], []
        dk_new = dv_new = None
        add = lambda a, b: b if a is None else a + b
        pkp = pvp = None
        offk = offv = diak = diav = None
        for h in range(2):
            lse = lse_ref[0, h:h + 1, lo:hi]
            delta = jnp.sum(prod[h * hd:(h + 1) * hd], axis=0, keepdims=True)
            p_pre = jnp.where(live, jnp.exp(sp[h * PAD:(h + 1) * PAD] - lse), 0.0)
            ds_pre = (p_pre * (dpp[h * PAD:(h + 1) * PAD] - delta)).astype(BF)
            p_dia = jnp.where(tri, jnp.exp(dg(km[h, lo:hi, :], q, 1, 1) - lse), 0.0)
            ds_dia = (p_dia * (dg(vm[h, lo:hi, :], do, 1, 1) - delta)).astype(BF)
            diav = add(diav, dg(p_dia.astype(BF), dos[h], 1, 0))
            diak = add(diak, dg(ds_dia, qs[h], 1, 0))
            pvp = add(pvp, dg(p_pre.astype(BF), dos[h], 1, 0))
            pkp = add(pkp, dg(ds_pre, qs[h], 1, 0))
            dqt = dg(kt[h * hd:(h + 1) * hd, lo:hi], ds_dia, 1, 0)
            if i:
                p_off = jnp.exp(dg(km[h, 0:lo, :], q, 1, 1) - jnp.where(single, lse, -NEG))
                ds_off = (p_off * (dg(vm[h, 0:lo, :], do, 1, 1) - delta)).astype(BF)
                offv = add(offv, dg(p_off.astype(BF), dos[h], 1, 0))
                offk = add(offk, dg(ds_off, qs[h], 1, 0))
                dqt = dqt + dg(kt[h * hd:(h + 1) * hd, 0:lo], ds_off, 1, 0)
            dqs.append(dqt)
            dsps.append(ds_pre)
        dqt = jnp.concatenate(dqs, axis=0) + dg(kp.T, jnp.concatenate(dsps, axis=0), 1, 0)
        dq_ref[lo:hi, :] = (dqt.T * scale).astype(BF)
        dka[lo:hi, :] = diak
        dva[lo:hi, :] = diav
        if i:
            dka[0:lo, :] += offk
            dva[0:lo, :] += offv
        pk_parts.append(pkp)
        pv_parts.append(pvp)
    dk_ref[...] = dka[...].astype(BF)
    dv_ref[...] = dva[...].astype(BF)
    for i in range(slots):
        for ref, parts in ((dpk_ref, pk_parts), (dpv_ref, pv_parts)):
            whole = sum(parts) if i == 0 else jnp.zeros_like(parts[0])
            ref[i * PAD:(i + 1) * PAD, :] = jnp.where(single, whole, parts[i])


def attn_bwd(lengths, qkv, pkv, attended, grad_att, lse, plen):
    rows = qkv.shape[0]
    width = qkv.shape[1] // 3
    slots = lengths.shape[1]
    pairs = width // 128
    col = lambda off: pl.BlockSpec((rows, 128), lambda h: (0, h + off))
    pcol = lambda off: pl.BlockSpec((slots * PAD, 128), lambda h: (0, h + off))
    sds = jax.ShapeDtypeStruct
    return pl.pallas_call(
        functools.partial(attn_bwd_kernel, slots, plen),
        grid=(pairs,),
        in_specs=[pl.BlockSpec(memory_space=pltpu.SMEM), col(0), col(pairs), col(2 * pairs), pcol(0), pcol(pairs),
                  col(0), col(0), pl.BlockSpec((1, 2, rows), lambda h: (h, 0, 0))],
        out_specs=[col(0), col(0), col(0), pcol(0), pcol(0)],
        out_shape=[sds((rows, width), BF)] * 3 + [sds((slots * PAD, width), F)] * 2,
        scratch_shapes=[pltpu.VMEM((2, rows, 128), BF)] * 2 + [pltpu.VMEM((rows, 128), F)] * 2,
        compiler_params=pltpu.CompilerParams(vmem_limit_bytes=48 * 2**20),
        name="attend_back",
    )(lengths, qkv, qkv, qkv, pkv, pkv, attended, grad_att, lse)


def layer_norm(values, norm_gain, norm_bias):
    average = jnp.mean(values, axis=-1, keepdims=True)
    centered = values - average
    variance = jnp.mean(centered * centered, axis=-1, keepdims=True)
    return centered * lax.rsqrt(variance + 1e-05) * norm_gain + norm_bias


def gelu_tanh(values):
    return (
        0.5
        * values
        * (1.0 + jnp.tanh(0.7978845608028654 * (values + 0.044715 * values * values * values)))
    )


def pick_sum(selector, values):
    return jnp.sum(jnp.where(selector[:, :, None], values[:, None, :], 0.0), axis=0)


def local(
    tokens,
    lengths,
    task_ids,
    prefix_embed,
    reparam_inner,
    reparam_inner_bias,
    reparam_outer,
    reparam_outer_bias,
    first_gain,
    first_bias,
    input_weight,
    output_weight,
    second_gain,
    second_bias,
    expand_weight,
    contract_weight,
    output_cotangent,
):
    width = tokens.shape[1]
    task_dev = prefix_embed.shape[0]
    prefix_len = prefix_embed.shape[1]
    slot_count = lengths.shape[1]
    task_count = lax.axis_size("task")
    batch_count = lax.axis_size("batch")
    device_count = task_count * batch_count
    pair_cols = reparam_outer.shape[2]
    task_row = lax.axis_index("task")
    device_pos = lax.axis_index(("task", "batch"))
    owner_rows = task_ids // task_dev
    row_match = owner_rows[:, :, None] == jnp.arange(task_count, dtype=jnp.int32)[None, None, :]
    row_task = jnp.sum(jnp.where(row_match, task_ids[:, :, None], 0), axis=1)
    own_tasks = task_row * task_dev + jnp.arange(task_dev, dtype=jnp.int32)
    partner_tasks = jnp.take(row_task, task_row, axis=1)
    partner_pick = partner_tasks[:, None] == own_tasks[None, :]
    pre_part = jnp.einsum(
        "tpd,tdh->tph", prefix_embed, reparam_inner, preferred_element_type=jnp.float32
    )
    pre_sum = lax.psum(pre_part, "batch")
    hidden_full = jnp.tanh(pre_sum + reparam_inner_bias.astype(jnp.float32)[:, None, :])
    hidden_low = hidden_full.astype(jnp.bfloat16)
    kv_cols = (
        jnp.einsum("tph,thc->tpc", hidden_low, reparam_outer, preferred_element_type=jnp.float32)
        + reparam_outer_bias.astype(jnp.float32)[:, None, :]
    ).astype(jnp.bfloat16)
    outgoing = jnp.einsum(
        "et,tpc->epc",
        partner_pick.astype(jnp.bfloat16),
        kv_cols,
        preferred_element_type=jnp.float32,
    ).astype(jnp.bfloat16)
    incoming = lax.all_to_all(
        outgoing.reshape(device_count, prefix_len * pair_cols),
        ("task", "batch"),
        split_axis=0,
        concat_axis=0,
        tiled=True,
    )
    by_row = (
        incoming.reshape(task_count, batch_count, prefix_len, pair_cols)
        .transpose(0, 2, 1, 3)
        .reshape(task_count, prefix_len * 2 * width)
    )
    own_owner = jnp.take(owner_rows, device_pos, axis=0)
    slot_match = own_owner[:, None] == jnp.arange(task_count, dtype=jnp.int32)[None, :]
    slot_pick = slot_match.astype(jnp.bfloat16)
    prefix_kv = (
        jnp.dot(slot_pick, by_row, preferred_element_type=jnp.float32)
        .astype(jnp.bfloat16)
        .reshape(slot_count, prefix_len, 2 * width)
    )
    gain_one = first_gain.astype(jnp.float32)
    bias_one = first_bias.astype(jnp.float32)
    gain_two = second_gain.astype(jnp.float32)
    bias_two = second_bias.astype(jnp.float32)
    residual_in = tokens.astype(jnp.float32)
    normed = layer_norm(residual_in, gain_one, bias_one).astype(jnp.bfloat16)
    projected = jnp.dot(normed, input_weight, preferred_element_type=jnp.float32).astype(
        jnp.bfloat16
    )
    prefix_kv = jnp.pad(prefix_kv, ((0, 0), (0, PAD - prefix_len), (0, 0))).reshape(slot_count * PAD, 2 * width)
    attended, log_totals = attn_fwd(lengths, projected, prefix_kv, prefix_len)
    mid = residual_in + jnp.dot(attended, output_weight, preferred_element_type=jnp.float32)
    normed_two = layer_norm(mid, gain_two, bias_two).astype(jnp.bfloat16)
    hidden_pre = jnp.dot(normed_two, expand_weight, preferred_element_type=jnp.float32)
    activated = gelu_tanh(hidden_pre).astype(jnp.bfloat16)
    output = (mid + jnp.dot(activated, contract_weight, preferred_element_type=jnp.float32)).astype(
        jnp.bfloat16
    )
    grad_act = jnp.einsum(
        "rc,fc->rf", output_cotangent, contract_weight, preferred_element_type=jnp.float32
    )
    unused_gelu, gelu_pull = jax.vjp(gelu_tanh, hidden_pre)
    grad_hidden = gelu_pull(grad_act)[0].astype(jnp.bfloat16)
    grad_normed_two = jnp.einsum(
        "rf,cf->rc", grad_hidden, expand_weight, preferred_element_type=jnp.float32
    )
    unused_norm_two, norm_two_pull = jax.vjp(
        lambda values: layer_norm(values, gain_two, bias_two), mid
    )
    grad_mid = output_cotangent.astype(jnp.float32) + norm_two_pull(grad_normed_two)[0]
    grad_mid_low = grad_mid.astype(jnp.bfloat16)
    grad_attended = jnp.einsum(
        "rc,dc->rd", grad_mid_low, output_weight, preferred_element_type=jnp.float32
    ).astype(jnp.bfloat16)
    grad_q, grad_k, grad_v, grad_pk, grad_pv = attn_bwd(
        lengths, projected, prefix_kv, attended, grad_attended, log_totals, prefix_len
    )
    grad_qkv = jnp.concatenate([grad_q, grad_k, grad_v], axis=1)
    grad_normed = jnp.einsum(
        "rk,dk->rd", grad_qkv, input_weight, preferred_element_type=jnp.float32
    )
    unused_norm_one, norm_one_pull = jax.vjp(
        lambda values: layer_norm(values, gain_one, bias_one), residual_in
    )
    input_grad = (grad_mid + norm_one_pull(grad_normed)[0]).astype(jnp.bfloat16)
    grad_prefix = (
        jnp.concatenate([grad_pk, grad_pv], axis=1)
        .reshape(slot_count, PAD, 2 * width)[:, :prefix_len]
        .reshape(slot_count, prefix_len * 2 * width)
    )
    by_owner = pick_sum(slot_match, grad_prefix)
    outgoing_grad = (
        by_owner.reshape(task_count, prefix_len, batch_count, pair_cols)
        .transpose(0, 2, 1, 3)
        .reshape(device_count, prefix_len * pair_cols)
    )
    incoming_grad = lax.all_to_all(
        outgoing_grad, ("task", "batch"), split_axis=0, concat_axis=0, tiled=True
    )
    grad_cols = pick_sum(partner_pick, incoming_grad).reshape(task_dev, prefix_len, pair_cols)
    grad_table_low = grad_cols.astype(jnp.bfloat16)
    grad_outer_bias = jnp.sum(grad_table_low.astype(jnp.float32), axis=1)
    grad_outer = jnp.einsum(
        "tph,tpc->thc", hidden_low, grad_table_low, preferred_element_type=jnp.float32
    )
    grad_hidden_part = jnp.einsum(
        "tpc,thc->tph", grad_table_low, reparam_outer, preferred_element_type=jnp.float32
    )
    grad_hidden_table = lax.psum(grad_hidden_part, "batch")
    grad_pre = (grad_hidden_table * (1.0 - hidden_full * hidden_full)).astype(jnp.bfloat16)
    grad_inner_bias = jnp.sum(grad_pre.astype(jnp.float32), axis=1)
    grad_inner = jnp.einsum(
        "tpd,tph->tdh", prefix_embed, grad_pre, preferred_element_type=jnp.float32
    )
    grad_embed = jnp.einsum(
        "tph,tdh->tpd", grad_pre, reparam_inner, preferred_element_type=jnp.float32
    )
    return (
        output,
        input_grad,
        grad_embed,
        grad_inner,
        grad_inner_bias,
        grad_outer,
        grad_outer_bias,
    )


def solution(mesh):
    placed = (
        P(("task", "batch"), None),
        P(("task", "batch"), None),
        P(),
        P("task", None, "batch"),
        P("task", "batch", None),
        P("task", None),
        P("task", None, "batch"),
        P("task", "batch"),
        P(),
        P(),
        P(),
        P(),
        P(),
        P(),
        P(),
        P(),
        P(("task", "batch"), None),
    )
    return jax.shard_map(
        local,
        mesh=mesh,
        in_specs=placed,
        out_specs=(
            P(("task", "batch"), None),
            P(("task", "batch"), None),
            P("task", None, "batch"),
            P("task", "batch", None),
            P("task", None),
            P("task", None, "batch"),
            P("task", "batch"),
        ),
        check_vma=False,
    )
```

```python
import functools

import jax
import jax.numpy as jnp
from jax import lax
from jax.experimental import pallas as pl
from jax.experimental.pallas import tpu as pltpu
from jax.sharding import PartitionSpec as P


BF = jnp.bfloat16
F = jnp.float32
PAD = 16
NEG = -1e30
MESH = pl.DeviceIdType.MESH


def dg(a, b, ca, cb):
    return lax.dot_general(a, b, (((ca,), (cb,)), ((), ())), preferred_element_type=F)


def attn_fwd_kernel(slots, plen, len_ref, q_ref, k_ref, v_ref, pk_ref, pv_ref, o_ref, lse_ref, km):
    rows, pair = q_ref.shape
    blk = rows // slots
    hd = pair // 2
    scale = hd ** -0.5
    single = len_ref[0, 0] > blk
    first = lax.broadcasted_iota(jnp.int32, (1, pair), 1) < hd
    zero = jnp.zeros((), BF)
    k = k_ref[...]
    km[0] = jnp.where(first, k, zero)
    km[1] = jnp.where(first, zero, k)
    vt = v_ref[...].T
    tri = lax.broadcasted_iota(jnp.int32, (blk, blk), 0) <= lax.broadcasted_iota(jnp.int32, (blk, blk), 1)
    live = lax.broadcasted_iota(jnp.int32, (PAD, blk), 0) < plen
    for i in range(slots):
        lo, hi = i * blk, (i + 1) * blk
        q = q_ref[lo:hi, :] * jnp.asarray(scale, BF)
        kp = jnp.where(single, pk_ref[0:PAD, :], pk_ref[i * PAD:(i + 1) * PAD, :])
        vp = jnp.where(single, pv_ref[0:PAD, :], pv_ref[i * PAD:(i + 1) * PAD, :])
        vpt = jnp.concatenate([jnp.where(first, vp, zero), jnp.where(first, zero, vp)], axis=0).T
        sp = dg(jnp.concatenate([jnp.where(first, kp, zero), jnp.where(first, zero, kp)], axis=0), q, 1, 1)
        outs, tops, sums, pps = [], [], [], []
        for h in range(2):
            s_pre = jnp.where(live, sp[h * PAD:(h + 1) * PAD], NEG)
            s_dia = jnp.where(tri, dg(km[h, lo:hi, :], q, 1, 1), NEG)
            top = jnp.maximum(jnp.max(s_dia, axis=0, keepdims=True), jnp.max(s_pre, axis=0, keepdims=True))
            if i:
                s_off = dg(km[h, 0:lo, :], q, 1, 1)
                top = jnp.maximum(top, jnp.where(single, jnp.max(s_off, axis=0, keepdims=True), NEG))
            p_pre = jnp.exp(s_pre - top)
            p_dia = jnp.exp(s_dia - top)
            total = jnp.sum(p_dia, axis=0, keepdims=True) + jnp.sum(p_pre, axis=0, keepdims=True)
            ot = dg(vt[h * hd:(h + 1) * hd, lo:hi], p_dia.astype(BF), 1, 0)
            if i:
                p_off = jnp.exp(s_off - jnp.where(single, top, -NEG))
                total = total + jnp.sum(p_off, axis=0, keepdims=True)
                ot = ot + dg(vt[h * hd:(h + 1) * hd, 0:lo], p_off.astype(BF), 1, 0)
            outs.append(ot)
            tops.append(top)
            sums.append(total)
            pps.append(p_pre.astype(BF))
        pre = dg(vpt, jnp.concatenate(pps, axis=0), 1, 0)
        for h in range(2):
            outs[h] = (outs[h] + pre[h * hd:(h + 1) * hd]) / sums[h]
            lse_ref[0, h:h + 1, lo:hi] = tops[h] + jnp.log(sums[h])
        o_ref[lo:hi, :] = jnp.concatenate(outs, axis=0).T.astype(BF)


def attn_fwd(lengths, qkv, pkv, plen):
    rows = qkv.shape[0]
    width = qkv.shape[1] // 3
    slots = lengths.shape[1]
    pairs = width // 128
    col = lambda off: pl.BlockSpec((rows, 128), lambda h: (0, h + off))
    pcol = lambda off: pl.BlockSpec((slots * PAD, 128), lambda h: (0, h + off))
    return pl.pallas_call(
        functools.partial(attn_fwd_kernel, slots, plen),
        grid=(pairs,),
        in_specs=[pl.BlockSpec(memory_space=pltpu.SMEM), col(0), col(pairs), col(2 * pairs), pcol(0), pcol(pairs)],
        out_specs=[col(0), pl.BlockSpec((1, 2, rows), lambda h: (h, 0, 0))],
        out_shape=[jax.ShapeDtypeStruct((rows, width), BF), jax.ShapeDtypeStruct((pairs, 2, rows), F)],
        scratch_shapes=[pltpu.VMEM((2, rows, 128), BF)],
        compiler_params=pltpu.CompilerParams(vmem_limit_bytes=48 * 2**20),
        name="attend",
    )(lengths, qkv, qkv, qkv, pkv, pkv)


def attn_bwd_kernel(slots, plen, len_ref, q_ref, k_ref, v_ref, pk_ref, pv_ref, o_ref, do_ref, lse_ref,
                    dq_ref, dk_ref, dv_ref, dpk_ref, dpv_ref, km, vm, dka, dva):
    rows, pair = q_ref.shape
    blk = rows // slots
    hd = pair // 2
    scale = hd ** -0.5
    single = len_ref[0, 0] > blk
    first = lax.broadcasted_iota(jnp.int32, (1, pair), 1) < hd
    zero = jnp.zeros((), BF)
    split = lambda a: (jnp.where(first, a, zero), jnp.where(first, zero, a))
    stack = lambda a: jnp.concatenate(split(a), axis=0)
    k = k_ref[...]
    km[0], km[1] = split(k)
    vm[0], vm[1] = split(v_ref[...])
    kt = k.T
    tri = lax.broadcasted_iota(jnp.int32, (blk, blk), 0) <= lax.broadcasted_iota(jnp.int32, (blk, blk), 1)
    live = lax.broadcasted_iota(jnp.int32, (PAD, blk), 0) < plen
    pk_sum = pv_sum = None
    pk_parts, pv_parts = [], []
    for i in range(slots):
        lo, hi = i * blk, (i + 1) * blk
        q = q_ref[lo:hi, :] * jnp.asarray(scale, BF)
        do = do_ref[lo:hi, :]
        kp = stack(jnp.where(single, pk_ref[0:PAD, :], pk_ref[i * PAD:(i + 1) * PAD, :]))
        vp = stack(jnp.where(single, pv_ref[0:PAD, :], pv_ref[i * PAD:(i + 1) * PAD, :]))
        sp = dg(kp, q, 1, 1)
        dpp = dg(vp, do, 1, 1)
        prod = (do.astype(F) * o_ref[lo:hi, :].astype(F)).T
        qs = split(q)
        dos = split(do)
        dqs, dsps = [], []
        dk_new = dv_new = None
        add = lambda a, b: b if a is None else a + b
        pkp = pvp = None
        offk = offv = diak = diav = None
        for h in range(2):
            lse = lse_ref[0, h:h + 1, lo:hi]
            delta = jnp.sum(prod[h * hd:(h + 1) * hd], axis=0, keepdims=True)
            p_pre = jnp.where(live, jnp.exp(sp[h * PAD:(h + 1) * PAD] - lse), 0.0)
            ds_pre = (p_pre * (dpp[h * PAD:(h + 1) * PAD] - delta)).astype(BF)
            p_dia = jnp.where(tri, jnp.exp(dg(km[h, lo:hi, :], q, 1, 1) - lse), 0.0)
            ds_dia = (p_dia * (dg(vm[h, lo:hi, :], do, 1, 1) - delta)).astype(BF)
            diav = add(diav, dg(p_dia.astype(BF), dos[h], 1, 0))
            diak = add(diak, dg(ds_dia, qs[h], 1, 0))
            pvp = add(pvp, dg(p_pre.astype(BF), dos[h], 1, 0))
            pkp = add(pkp, dg(ds_pre, qs[h], 1, 0))
            dqt = dg(kt[h * hd:(h + 1) * hd, lo:hi], ds_dia, 1, 0)
            if i:
                p_off = jnp.exp(dg(km[h, 0:lo, :], q, 1, 1) - jnp.where(single, lse, -NEG))
                ds_off = (p_off * (dg(vm[h, 0:lo, :], do, 1, 1) - delta)).astype(BF)
                offv = add(offv, dg(p_off.astype(BF), dos[h], 1, 0))
                offk = add(offk, dg(ds_off, qs[h], 1, 0))
                dqt = dqt + dg(kt[h * hd:(h + 1) * hd, 0:lo], ds_off, 1, 0)
            dqs.append(dqt)
            dsps.append(ds_pre)
        dqt = jnp.concatenate(dqs, axis=0) + dg(kp.T, jnp.concatenate(dsps, axis=0), 1, 0)
        dq_ref[lo:hi, :] = (dqt.T * scale).astype(BF)
        dka[lo:hi, :] = diak
        dva[lo:hi, :] = diav
        if i:
            dka[0:lo, :] += offk
            dva[0:lo, :] += offv
        pk_parts.append(pkp)
        pv_parts.append(pvp)
    dk_ref[...] = dka[...].astype(BF)
    dv_ref[...] = dva[...].astype(BF)
    for i in range(slots):
        for ref, parts in ((dpk_ref, pk_parts), (dpv_ref, pv_parts)):
            whole = sum(parts) if i == 0 else jnp.zeros_like(parts[0])
            ref[i * PAD:(i + 1) * PAD, :] = jnp.where(single, whole, parts[i])


def attn_bwd(lengths, qkv, pkv, attended, grad_att, lse, plen):
    rows = qkv.shape[0]
    width = qkv.shape[1] // 3
    slots = lengths.shape[1]
    pairs = width // 128
    col = lambda off: pl.BlockSpec((rows, 128), lambda h: (0, h + off))
    pcol = lambda off: pl.BlockSpec((slots * PAD, 128), lambda h: (0, h + off))
    sds = jax.ShapeDtypeStruct
    return pl.pallas_call(
        functools.partial(attn_bwd_kernel, slots, plen),
        grid=(pairs,),
        in_specs=[pl.BlockSpec(memory_space=pltpu.SMEM), col(0), col(pairs), col(2 * pairs), pcol(0), pcol(pairs),
                  col(0), col(0), pl.BlockSpec((1, 2, rows), lambda h: (h, 0, 0))],
        out_specs=[col(0), col(0), col(0), pcol(0), pcol(0)],
        out_shape=[sds((rows, width), BF)] * 3 + [sds((slots * PAD, width), F)] * 2,
        scratch_shapes=[pltpu.VMEM((2, rows, 128), BF)] * 2 + [pltpu.VMEM((rows, 128), F)] * 2,
        compiler_params=pltpu.CompilerParams(vmem_limit_bytes=48 * 2**20),
        name="attend_back",
    )(lengths, qkv, qkv, qkv, pkv, pkv, attended, grad_att, lse)


def peer_id(flat, nb):
    return {"task": flat // nb, "batch": flat % nb}


def layer_norm_rows(x, gain, bias):
    inv = 1.0 / x.shape[1]
    mean = jnp.sum(x, axis=1, keepdims=True) * inv
    cen = x - mean
    var = jnp.sum(cen * cen, axis=1, keepdims=True) * inv
    return cen * lax.rsqrt(var + 1e-5) * gain + bias


def greet_all(nt, nb):
    me = lax.axis_index("task") * nb + lax.axis_index("batch")
    total = nt * nb
    barrier = pltpu.get_barrier_semaphore()

    def greet(d, c):
        pl.semaphore_signal(barrier, inc=1, device_id=peer_id(lax.rem(me + d, total), nb), device_id_type=MESH)
        return c

    lax.fori_loop(1, total, greet, 0)
    return barrier, me, total


def front_kernel(nt, nb, td, plen, chunk, cuts,
                 ids_ref, emb_ref, ib_ref, ob_ref, g_ref, b_ref, tok_hbm, w_hbm, inner_hbm, outer_hbm,
                 qkv_hbm, pkv_ref, hid_ref, low_ref,
                 tok, w, inner, outer, normed, qkv, pre, ibf, tbl, rs_out, rs_in, ag_out, ag_in, aa_out, aa_in,
                 ld_sem, st_sem, rs_ss, rs_rs, ag_ss, ag_rs, aa_ss, aa_rs):
    rows, width = tok.shape
    slots = ids_ref.shape[1]
    rc = td * PAD // nb
    pc = outer.shape[2]
    mt = lax.axis_index("task")
    mb = lax.axis_index("batch")
    loads = [pltpu.make_async_copy(s, d, ld_sem.at[i])
             for i, (s, d) in enumerate(((inner_hbm, inner), (tok_hbm, tok), (w_hbm, w), (outer_hbm, outer)))]
    for c in loads:
        c.start()
    barrier, me, total = greet_all(nt, nb)
    pre[...] = jnp.zeros_like(pre)
    loads[0].wait()
    for t in range(td):
        pre[t * PAD:t * PAD + plen, :] = dg(emb_ref[t], inner[t], 1, 0)
    for c in range(nb):
        rs_out[c, 0:rc, :] = pre[c * rc:(c + 1) * rc, :].astype(BF)
    ib = ib_ref[...].astype(F)
    for t in range(td):
        ibf[t * PAD:(t + 1) * PAD, :] = jnp.broadcast_to(ib[t:t + 1], (PAD, ib.shape[1]))
    pl.semaphore_wait(barrier, total - 1)

    def batch_copy(d, src, dst, ss, rs):
        to = lax.rem(mb + d, nb)
        return pltpu.make_async_remote_copy(src_ref=src(to), dst_ref=dst, send_sem=ss.at[d], recv_sem=rs.at[d],
                                            device_id={"task": mt, "batch": to}, device_id_type=MESH)

    rs_copy = [batch_copy(d, lambda to: rs_out.at[to], rs_in.at[d], rs_ss, rs_rs) for d in range(1, nb)]
    for c in rs_copy:
        c.start()
    loads[1].wait()
    gain = g_ref[...].astype(F)
    bias = b_ref[...].astype(F)

    def norm_step(i, c):
        r = pl.ds(pl.multiple_of(i * 128, 128), 128)
        normed[r, :] = layer_norm_rows(tok[r, :].astype(F), gain, bias).astype(BF)
        return c

    lax.fori_loop(0, rows // 128, norm_step, 0)
    loads[2].wait()

    def store(j):
        cols = pl.ds(pl.multiple_of(j * chunk, chunk), chunk)
        return pltpu.make_async_copy(qkv.at[:, cols], qkv_hbm.at[:, cols], st_sem.at[j])

    def mm_step(j, c):
        cols = pl.ds(pl.multiple_of(j * chunk, chunk), chunk)
        qkv[:, cols] = dg(normed[...], w[:, cols], 1, 0).astype(BF)
        store(j).start()
        return c

    steps = w.shape[1] // chunk
    c1, c2 = cuts
    lax.fori_loop(0, c1, mm_step, 0)
    mine = pl.ds(pl.multiple_of(mb * rc, rc), rc)
    own = pre[mine, :] + ibf[mine, :]
    for c in rs_copy:
        c.wait_recv()
    for d in range(1, nb):
        own = own + rs_in[d, 0:rc, :].astype(F)
    hid = jnp.tanh(own)
    hid_ref[...] = hid
    ag_out[0:rc, :] = hid.astype(BF)
    ag_copy = [batch_copy(d, lambda to: ag_out, ag_in.at[d], ag_ss, ag_rs) for d in range(1, nb)]
    for c in ag_copy:
        c.start()
    lax.fori_loop(c1, c2, mm_step, 0)

    def put_low(frm, block):
        low_ref[pl.ds(pl.multiple_of(frm * rc, rc), rc), :] = block

    put_low(mb, ag_out[0:rc, :])
    for c in ag_copy:
        c.wait_recv()
    for d in range(1, nb):
        put_low(lax.rem(mb + nb - d, nb), ag_in[d, 0:rc, :])
    loads[3].wait()
    ob = ob_ref[...].astype(F)
    for t in range(td):
        tbl[t] = (dg(low_ref[t * PAD:(t + 1) * PAD, :], outer[t], 1, 0) + ob[t:t + 1]).astype(BF)

    def aa_copy(d):
        to = lax.rem(me + d, total)
        return pltpu.make_async_remote_copy(src_ref=aa_out.at[to], dst_ref=aa_in.at[me], send_sem=aa_ss.at[d],
                                            recv_sem=aa_rs.at[me], device_id=peer_id(to, nb), device_id_type=MESH)

    def pick(e):
        idx = jnp.int32(0)
        for s in range(slots):
            tid = ids_ref[e, s]
            idx = idx + jnp.where(tid // td == mt, lax.rem(tid, td), 0)
        return tbl[idx]

    def aa_step(d, c):
        to = lax.rem(me + d, total)
        aa_out[to] = pick(to)
        aa_copy(d).start()
        return c

    lax.fori_loop(1, total, aa_step, 0)
    aa_in[me] = pick(me)
    lax.fori_loop(c2, steps, mm_step, 0)

    def aa_wait(d, c):
        frm = lax.rem(me + d, total)
        pltpu.make_async_remote_copy(src_ref=aa_out.at[frm], dst_ref=aa_in.at[frm], send_sem=aa_ss.at[d],
                                     recv_sem=aa_rs.at[frm], device_id=peer_id(frm, nb), device_id_type=MESH).wait()
        return c

    lax.fori_loop(1, total, aa_wait, 0)
    for s in range(slots):
        owner = ids_ref[me, s] // td
        for b in range(nb):
            pkv_ref[s * PAD:(s + 1) * PAD, b * pc:(b + 1) * pc] = aa_in[owner * nb + b]
    for c in rs_copy + ag_copy:
        c.wait_send()

    def st_wait(j, c):
        store(j).wait()
        return c

    lax.fori_loop(0, steps, st_wait, 0)


def front(nt, nb, task_ids, prefix_embed, inner, inner_bias, outer, outer_bias, gain, bias, tokens, weight):
    td, plen, depth = prefix_embed.shape
    rep = inner.shape[2]
    pc = outer.shape[2]
    rows, width = tokens.shape
    slots = task_ids.shape[1]
    total = nt * nb
    rc = td * PAD // nb
    rb = max(rc, PAD)
    chunk = 256
    steps = weight.shape[1] // chunk
    cuts = (steps // 3, 2 * steps // 3)
    sds = jax.ShapeDtypeStruct
    vm = pl.BlockSpec(memory_space=pltpu.VMEM)
    hb = pl.BlockSpec(memory_space=pl.ANY)
    dma = pltpu.SemaphoreType.DMA
    return pl.pallas_call(
        functools.partial(front_kernel, nt, nb, td, plen, chunk, cuts),
        in_specs=[pl.BlockSpec(memory_space=pltpu.SMEM), vm, vm, vm, vm, vm, hb, hb, hb, hb],
        out_specs=[hb, vm, vm, vm],
        out_shape=[sds((rows, weight.shape[1]), BF), sds((slots * PAD, nb * pc), BF), sds((rc, rep), F),
                   sds((td * PAD, rep), BF)],
        scratch_shapes=[
            pltpu.VMEM((rows, width), BF), pltpu.VMEM(weight.shape, BF), pltpu.VMEM(inner.shape, BF),
            pltpu.VMEM(outer.shape, BF), pltpu.VMEM((rows, width), BF), pltpu.VMEM((rows, weight.shape[1]), BF),
            pltpu.VMEM((td * PAD, rep), F), pltpu.VMEM((td * PAD, rep), F), pltpu.VMEM((td, PAD, pc), BF),
            pltpu.VMEM((nb, rb, rep), BF), pltpu.VMEM((nb, rb, rep), BF),
            pltpu.VMEM((rb, rep), BF), pltpu.VMEM((nb, rb, rep), BF),
            pltpu.VMEM((total, PAD, pc), BF), pltpu.VMEM((total, PAD, pc), BF),
            dma((4,)), dma((steps,)), dma((nb,)), dma((nb,)), dma((nb,)), dma((nb,)), dma((total,)), dma((total,)),
        ],
        compiler_params=pltpu.CompilerParams(vmem_limit_bytes=48 * 2**20, collective_id=0, has_side_effects=True),
        name="front",
    )(task_ids, prefix_embed, inner_bias, outer_bias, gain.reshape(1, width), bias.reshape(1, width),
      tokens, weight, inner, outer)


def layer_norm(values, norm_gain, norm_bias):
    average = jnp.mean(values, axis=-1, keepdims=True)
    centered = values - average
    variance = jnp.mean(centered * centered, axis=-1, keepdims=True)
    return centered * lax.rsqrt(variance + 1e-05) * norm_gain + norm_bias


def gelu_tanh(values):
    return (
        0.5
        * values
        * (1.0 + jnp.tanh(0.7978845608028654 * (values + 0.044715 * values * values * values)))
    )


def pick_sum(selector, values):
    return jnp.sum(jnp.where(selector[:, :, None], values[:, None, :], 0.0), axis=0)


def local(
    tokens,
    lengths,
    task_ids,
    prefix_embed,
    reparam_inner,
    reparam_inner_bias,
    reparam_outer,
    reparam_outer_bias,
    first_gain,
    first_bias,
    input_weight,
    output_weight,
    second_gain,
    second_bias,
    expand_weight,
    contract_weight,
    output_cotangent,
):
    width = tokens.shape[1]
    task_dev = prefix_embed.shape[0]
    prefix_len = prefix_embed.shape[1]
    slot_count = lengths.shape[1]
    task_count = lax.axis_size("task")
    batch_count = lax.axis_size("batch")
    device_count = task_count * batch_count
    pair_cols = reparam_outer.shape[2]
    task_row = lax.axis_index("task")
    device_pos = lax.axis_index(("task", "batch"))
    owner_rows = task_ids // task_dev
    row_match = owner_rows[:, :, None] == jnp.arange(task_count, dtype=jnp.int32)[None, None, :]
    row_task = jnp.sum(jnp.where(row_match, task_ids[:, :, None], 0), axis=1)
    own_tasks = task_row * task_dev + jnp.arange(task_dev, dtype=jnp.int32)
    partner_tasks = jnp.take(row_task, task_row, axis=1)
    partner_pick = partner_tasks[:, None] == own_tasks[None, :]
    projected, prefix_kv, hidden_chunk, hidden_low = front(
        task_count, batch_count, task_ids, prefix_embed, reparam_inner, reparam_inner_bias, reparam_outer,
        reparam_outer_bias, first_gain, first_bias, tokens, input_weight,
    )
    hidden_low = hidden_low.reshape(task_dev, PAD, -1)[:, :prefix_len]
    hidden_full = lax.all_gather(hidden_chunk, "batch", axis=0, tiled=True).reshape(task_dev, PAD, -1)[:, :prefix_len]
    own_owner = jnp.take(owner_rows, device_pos, axis=0)
    slot_match = own_owner[:, None] == jnp.arange(task_count, dtype=jnp.int32)[None, :]
    gain_one = first_gain.astype(jnp.float32)
    bias_one = first_bias.astype(jnp.float32)
    gain_two = second_gain.astype(jnp.float32)
    bias_two = second_bias.astype(jnp.float32)
    residual_in = tokens.astype(jnp.float32)
    attended, log_totals = attn_fwd(lengths, projected, prefix_kv, prefix_len)
    mid = residual_in + jnp.dot(attended, output_weight, preferred_element_type=jnp.float32)
    normed_two = layer_norm(mid, gain_two, bias_two).astype(jnp.bfloat16)
    hidden_pre = jnp.dot(normed_two, expand_weight, preferred_element_type=jnp.float32)
    activated = gelu_tanh(hidden_pre).astype(jnp.bfloat16)
    output = (mid + jnp.dot(activated, contract_weight, preferred_element_type=jnp.float32)).astype(
        jnp.bfloat16
    )
    grad_act = jnp.einsum(
        "rc,fc->rf", output_cotangent, contract_weight, preferred_element_type=jnp.float32
    )
    unused_gelu, gelu_pull = jax.vjp(gelu_tanh, hidden_pre)
    grad_hidden = gelu_pull(grad_act)[0].astype(jnp.bfloat16)
    grad_normed_two = jnp.einsum(
        "rf,cf->rc", grad_hidden, expand_weight, preferred_element_type=jnp.float32
    )
    unused_norm_two, norm_two_pull = jax.vjp(
        lambda values: layer_norm(values, gain_two, bias_two), mid
    )
    grad_mid = output_cotangent.astype(jnp.float32) + norm_two_pull(grad_normed_two)[0]
    grad_mid_low = grad_mid.astype(jnp.bfloat16)
    grad_attended = jnp.einsum(
        "rc,dc->rd", grad_mid_low, output_weight, preferred_element_type=jnp.float32
    ).astype(jnp.bfloat16)
    grad_q, grad_k, grad_v, grad_pk, grad_pv = attn_bwd(
        lengths, projected, prefix_kv, attended, grad_attended, log_totals, prefix_len
    )
    grad_qkv = jnp.concatenate([grad_q, grad_k, grad_v], axis=1)
    grad_normed = jnp.einsum(
        "rk,dk->rd", grad_qkv, input_weight, preferred_element_type=jnp.float32
    )
    unused_norm_one, norm_one_pull = jax.vjp(
        lambda values: layer_norm(values, gain_one, bias_one), residual_in
    )
    input_grad = (grad_mid + norm_one_pull(grad_normed)[0]).astype(jnp.bfloat16)
    grad_prefix = (
        jnp.concatenate([grad_pk, grad_pv], axis=1)
        .reshape(slot_count, PAD, 2 * width)[:, :prefix_len]
        .reshape(slot_count, prefix_len * 2 * width)
    )
    by_owner = pick_sum(slot_match, grad_prefix)
    outgoing_grad = (
        by_owner.reshape(task_count, prefix_len, batch_count, pair_cols)
        .transpose(0, 2, 1, 3)
        .reshape(device_count, prefix_len * pair_cols)
    )
    incoming_grad = lax.all_to_all(
        outgoing_grad, ("task", "batch"), split_axis=0, concat_axis=0, tiled=True
    )
    grad_cols = pick_sum(partner_pick, incoming_grad).reshape(task_dev, prefix_len, pair_cols)
    grad_table_low = grad_cols.astype(jnp.bfloat16)
    grad_outer_bias = jnp.sum(grad_table_low.astype(jnp.float32), axis=1)
    grad_outer = jnp.einsum(
        "tph,tpc->thc", hidden_low, grad_table_low, preferred_element_type=jnp.float32
    )
    grad_hidden_part = jnp.einsum(
        "tpc,thc->tph", grad_table_low, reparam_outer, preferred_element_type=jnp.float32
    )
    grad_hidden_table = lax.psum(grad_hidden_part, "batch")
    grad_pre = (grad_hidden_table * (1.0 - hidden_full * hidden_full)).astype(jnp.bfloat16)
    grad_inner_bias = jnp.sum(grad_pre.astype(jnp.float32), axis=1)
    grad_inner = jnp.einsum(
        "tpd,tph->tdh", prefix_embed, grad_pre, preferred_element_type=jnp.float32
    )
    grad_embed = jnp.einsum(
        "tph,tdh->tpd", grad_pre, reparam_inner, preferred_element_type=jnp.float32
    )
    return (
        output,
        input_grad,
        grad_embed,
        grad_inner,
        grad_inner_bias,
        grad_outer,
        grad_outer_bias,
    )


def solution(mesh):
    placed = (
        P(("task", "batch"), None),
        P(("task", "batch"), None),
        P(),
        P("task", None, "batch"),
        P("task", "batch", None),
        P("task", None),
        P("task", None, "batch"),
        P("task", "batch"),
        P(),
        P(),
        P(),
        P(),
        P(),
        P(),
        P(),
        P(),
        P(("task", "batch"), None),
    )
    return jax.shard_map(
        local,
        mesh=mesh,
        in_specs=placed,
        out_specs=(
            P(("task", "batch"), None),
            P(("task", "batch"), None),
            P("task", None, "batch"),
            P("task", "batch", None),
            P("task", None),
            P("task", None, "batch"),
            P("task", "batch"),
        ),
        check_vma=False,
    )
```

```python
import functools

import jax
import jax.numpy as jnp
from jax import lax
from jax.experimental import pallas as pl
from jax.experimental.pallas import tpu as pltpu
from jax.sharding import PartitionSpec as P


BF = jnp.bfloat16
F = jnp.float32
PAD = 16
NEG = -1e30
MESH = pl.DeviceIdType.MESH


def dg(a, b, ca, cb):
    return lax.dot_general(a, b, (((ca,), (cb,)), ((), ())), preferred_element_type=F)


def attn_fwd_kernel(slots, plen, len_ref, q_ref, k_ref, v_ref, pk_ref, pv_ref, o_ref, lse_ref, km):
    rows, pair = q_ref.shape
    blk = rows // slots
    hd = pair // 2
    scale = hd ** -0.5
    single = len_ref[0, 0] > blk
    first = lax.broadcasted_iota(jnp.int32, (1, pair), 1) < hd
    zero = jnp.zeros((), BF)
    k = k_ref[...]
    km[0] = jnp.where(first, k, zero)
    km[1] = jnp.where(first, zero, k)
    vt = v_ref[...].T
    tri = lax.broadcasted_iota(jnp.int32, (blk, blk), 0) <= lax.broadcasted_iota(jnp.int32, (blk, blk), 1)
    live = lax.broadcasted_iota(jnp.int32, (PAD, blk), 0) < plen
    for i in range(slots):
        lo, hi = i * blk, (i + 1) * blk
        q = q_ref[lo:hi, :] * jnp.asarray(scale, BF)
        kp = jnp.where(single, pk_ref[0:PAD, :], pk_ref[i * PAD:(i + 1) * PAD, :])
        vp = jnp.where(single, pv_ref[0:PAD, :], pv_ref[i * PAD:(i + 1) * PAD, :])
        vpt = jnp.concatenate([jnp.where(first, vp, zero), jnp.where(first, zero, vp)], axis=0).T
        sp = dg(jnp.concatenate([jnp.where(first, kp, zero), jnp.where(first, zero, kp)], axis=0), q, 1, 1)
        outs, tops, sums, pps = [], [], [], []
        for h in range(2):
            s_pre = jnp.where(live, sp[h * PAD:(h + 1) * PAD], NEG)
            s_dia = jnp.where(tri, dg(km[h, lo:hi, :], q, 1, 1), NEG)
            top = jnp.maximum(jnp.max(s_dia, axis=0, keepdims=True), jnp.max(s_pre, axis=0, keepdims=True))
            if i:
                s_off = dg(km[h, 0:lo, :], q, 1, 1)
                top = jnp.maximum(top, jnp.where(single, jnp.max(s_off, axis=0, keepdims=True), NEG))
            p_pre = jnp.exp(s_pre - top)
            p_dia = jnp.exp(s_dia - top)
            total = jnp.sum(p_dia, axis=0, keepdims=True) + jnp.sum(p_pre, axis=0, keepdims=True)
            ot = dg(vt[h * hd:(h + 1) * hd, lo:hi], p_dia.astype(BF), 1, 0)
            if i:
                p_off = jnp.exp(s_off - jnp.where(single, top, -NEG))
                total = total + jnp.sum(p_off, axis=0, keepdims=True)
                ot = ot + dg(vt[h * hd:(h + 1) * hd, 0:lo], p_off.astype(BF), 1, 0)
            outs.append(ot)
            tops.append(top)
            sums.append(total)
            pps.append(p_pre.astype(BF))
        pre = dg(vpt, jnp.concatenate(pps, axis=0), 1, 0)
        for h in range(2):
            outs[h] = (outs[h] + pre[h * hd:(h + 1) * hd]) / sums[h]
            lse_ref[0, h:h + 1, lo:hi] = tops[h] + jnp.log(sums[h])
        o_ref[lo:hi, :] = jnp.concatenate(outs, axis=0).T.astype(BF)


def attn_fwd(lengths, qkv, pkv, plen):
    rows = qkv.shape[0]
    width = qkv.shape[1] // 3
    slots = lengths.shape[1]
    pairs = width // 128
    col = lambda off: pl.BlockSpec((rows, 128), lambda h: (0, h + off))
    pcol = lambda off: pl.BlockSpec((slots * PAD, 128), lambda h: (0, h + off))
    return pl.pallas_call(
        functools.partial(attn_fwd_kernel, slots, plen),
        grid=(pairs,),
        in_specs=[pl.BlockSpec(memory_space=pltpu.SMEM), col(0), col(pairs), col(2 * pairs), pcol(0), pcol(pairs)],
        out_specs=[col(0), pl.BlockSpec((1, 2, rows), lambda h: (h, 0, 0))],
        out_shape=[jax.ShapeDtypeStruct((rows, width), BF), jax.ShapeDtypeStruct((pairs, 2, rows), F)],
        scratch_shapes=[pltpu.VMEM((2, rows, 128), BF)],
        compiler_params=pltpu.CompilerParams(vmem_limit_bytes=48 * 2**20),
        name="attend",
    )(lengths, qkv, qkv, qkv, pkv, pkv)


def attn_bwd_kernel(slots, plen, len_ref, q_ref, k_ref, v_ref, pk_ref, pv_ref, o_ref, do_ref, lse_ref,
                    dq_ref, dk_ref, dv_ref, dpk_ref, dpv_ref, km, vm, dka, dva):
    rows, pair = q_ref.shape
    blk = rows // slots
    hd = pair // 2
    scale = hd ** -0.5
    single = len_ref[0, 0] > blk
    first = lax.broadcasted_iota(jnp.int32, (1, pair), 1) < hd
    zero = jnp.zeros((), BF)
    split = lambda a: (jnp.where(first, a, zero), jnp.where(first, zero, a))
    stack = lambda a: jnp.concatenate(split(a), axis=0)
    k = k_ref[...]
    km[0], km[1] = split(k)
    vm[0], vm[1] = split(v_ref[...])
    kt = k.T
    tri = lax.broadcasted_iota(jnp.int32, (blk, blk), 0) <= lax.broadcasted_iota(jnp.int32, (blk, blk), 1)
    live = lax.broadcasted_iota(jnp.int32, (PAD, blk), 0) < plen
    pk_sum = pv_sum = None
    pk_parts, pv_parts = [], []
    for i in range(slots):
        lo, hi = i * blk, (i + 1) * blk
        q = q_ref[lo:hi, :] * jnp.asarray(scale, BF)
        do = do_ref[lo:hi, :]
        kp = stack(jnp.where(single, pk_ref[0:PAD, :], pk_ref[i * PAD:(i + 1) * PAD, :]))
        vp = stack(jnp.where(single, pv_ref[0:PAD, :], pv_ref[i * PAD:(i + 1) * PAD, :]))
        sp = dg(kp, q, 1, 1)
        dpp = dg(vp, do, 1, 1)
        prod = (do.astype(F) * o_ref[lo:hi, :].astype(F)).T
        qs = split(q)
        dos = split(do)
        dqs, dsps = [], []
        dk_new = dv_new = None
        add = lambda a, b: b if a is None else a + b
        pkp = pvp = None
        offk = offv = diak = diav = None
        for h in range(2):
            lse = lse_ref[0, h:h + 1, lo:hi]
            delta = jnp.sum(prod[h * hd:(h + 1) * hd], axis=0, keepdims=True)
            p_pre = jnp.where(live, jnp.exp(sp[h * PAD:(h + 1) * PAD] - lse), 0.0)
            ds_pre = (p_pre * (dpp[h * PAD:(h + 1) * PAD] - delta)).astype(BF)
            p_dia = jnp.where(tri, jnp.exp(dg(km[h, lo:hi, :], q, 1, 1) - lse), 0.0)
            ds_dia = (p_dia * (dg(vm[h, lo:hi, :], do, 1, 1) - delta)).astype(BF)
            diav = add(diav, dg(p_dia.astype(BF), dos[h], 1, 0))
            diak = add(diak, dg(ds_dia, qs[h], 1, 0))
            pvp = add(pvp, dg(p_pre.astype(BF), dos[h], 1, 0))
            pkp = add(pkp, dg(ds_pre, qs[h], 1, 0))
            dqt = dg(kt[h * hd:(h + 1) * hd, lo:hi], ds_dia, 1, 0)
            if i:
                p_off = jnp.exp(dg(km[h, 0:lo, :], q, 1, 1) - jnp.where(single, lse, -NEG))
                ds_off = (p_off * (dg(vm[h, 0:lo, :], do, 1, 1) - delta)).astype(BF)
                offv = add(offv, dg(p_off.astype(BF), dos[h], 1, 0))
                offk = add(offk, dg(ds_off, qs[h], 1, 0))
                dqt = dqt + dg(kt[h * hd:(h + 1) * hd, 0:lo], ds_off, 1, 0)
            dqs.append(dqt)
            dsps.append(ds_pre)
        dqt = jnp.concatenate(dqs, axis=0) + dg(kp.T, jnp.concatenate(dsps, axis=0), 1, 0)
        dq_ref[lo:hi, :] = (dqt.T * scale).astype(BF)
        dka[lo:hi, :] = diak
        dva[lo:hi, :] = diav
        if i:
            dka[0:lo, :] += offk
            dva[0:lo, :] += offv
        pk_parts.append(pkp)
        pv_parts.append(pvp)
    dk_ref[...] = dka[...].astype(BF)
    dv_ref[...] = dva[...].astype(BF)
    for i in range(slots):
        for ref, parts in ((dpk_ref, pk_parts), (dpv_ref, pv_parts)):
            whole = sum(parts) if i == 0 else jnp.zeros_like(parts[0])
            ref[i * PAD:(i + 1) * PAD, :] = jnp.where(single, whole, parts[i])


def attn_bwd(lengths, qkv, pkv, attended, grad_att, lse, plen):
    rows = qkv.shape[0]
    width = qkv.shape[1] // 3
    slots = lengths.shape[1]
    pairs = width // 128
    col = lambda off: pl.BlockSpec((rows, 128), lambda h: (0, h + off))
    pcol = lambda off: pl.BlockSpec((slots * PAD, 128), lambda h: (0, h + off))
    sds = jax.ShapeDtypeStruct
    return pl.pallas_call(
        functools.partial(attn_bwd_kernel, slots, plen),
        grid=(pairs,),
        in_specs=[pl.BlockSpec(memory_space=pltpu.SMEM), col(0), col(pairs), col(2 * pairs), pcol(0), pcol(pairs),
                  col(0), col(0), pl.BlockSpec((1, 2, rows), lambda h: (h, 0, 0))],
        out_specs=[col(0), col(0), col(0), pcol(0), pcol(0)],
        out_shape=[sds((rows, width), BF)] * 3 + [sds((slots * PAD, width), F)] * 2,
        scratch_shapes=[pltpu.VMEM((2, rows, 128), BF)] * 2 + [pltpu.VMEM((rows, 128), F)] * 2,
        compiler_params=pltpu.CompilerParams(vmem_limit_bytes=48 * 2**20),
        name="attend_back",
    )(lengths, qkv, qkv, qkv, pkv, pkv, attended, grad_att, lse)


def peer_id(flat, nb):
    return {"task": flat // nb, "batch": flat % nb}


def layer_norm_rows(x, gain, bias):
    inv = 1.0 / x.shape[1]
    mean = jnp.sum(x, axis=1, keepdims=True) * inv
    cen = x - mean
    var = jnp.sum(cen * cen, axis=1, keepdims=True) * inv
    return cen * lax.rsqrt(var + 1e-5) * gain + bias


def greet_all(nt, nb):
    me = lax.axis_index("task") * nb + lax.axis_index("batch")
    total = nt * nb
    barrier = pltpu.get_barrier_semaphore()

    def greet(d, c):
        pl.semaphore_signal(barrier, inc=1, device_id=peer_id(lax.rem(me + d, total), nb), device_id_type=MESH)
        return c

    lax.fori_loop(1, total, greet, 0)
    return barrier, me, total


def front_kernel(nt, nb, td, plen, chunk, cuts,
                 ids_ref, emb_ref, ib_ref, ob_ref, g_ref, b_ref, tok_hbm, w_hbm, inner_hbm, outer_hbm,
                 qkv_hbm, pkv_ref, hid_ref, low_ref,
                 tok, w, inner, outer, normed, qkv, pre, ibf, tbl, rs_out, rs_in, ag_out, ag_in, aa_out, aa_in,
                 ld_sem, st_sem, rs_ss, rs_rs, ag_ss, ag_rs, aa_ss, aa_rs):
    rows, width = tok.shape
    slots = ids_ref.shape[1]
    rc = td * PAD // nb
    pc = outer.shape[2]
    mt = lax.axis_index("task")
    mb = lax.axis_index("batch")
    loads = [pltpu.make_async_copy(s, d, ld_sem.at[i])
             for i, (s, d) in enumerate(((inner_hbm, inner), (tok_hbm, tok), (w_hbm, w), (outer_hbm, outer)))]
    for c in loads:
        c.start()
    barrier, me, total = greet_all(nt, nb)
    pre[...] = jnp.zeros_like(pre)
    loads[0].wait()
    for t in range(td):
        pre[t * PAD:t * PAD + plen, :] = dg(emb_ref[t], inner[t], 1, 0)
    for c in range(nb):
        rs_out[c, 0:rc, :] = pre[c * rc:(c + 1) * rc, :].astype(BF)
    ib = ib_ref[...].astype(F)
    for t in range(td):
        ibf[t * PAD:(t + 1) * PAD, :] = jnp.broadcast_to(ib[t:t + 1], (PAD, ib.shape[1]))
    pl.semaphore_wait(barrier, total - 1)

    def batch_copy(d, src, dst, ss, rs):
        to = lax.rem(mb + d, nb)
        return pltpu.make_async_remote_copy(src_ref=src(to), dst_ref=dst, send_sem=ss.at[d], recv_sem=rs.at[d],
                                            device_id={"task": mt, "batch": to}, device_id_type=MESH)

    rs_copy = [batch_copy(d, lambda to: rs_out.at[to], rs_in.at[d], rs_ss, rs_rs) for d in range(1, nb)]
    for c in rs_copy:
        c.start()
    loads[1].wait()
    gain = g_ref[...].astype(F)
    bias = b_ref[...].astype(F)

    def norm_step(i, c):
        r = pl.ds(pl.multiple_of(i * 128, 128), 128)
        normed[r, :] = layer_norm_rows(tok[r, :].astype(F), gain, bias).astype(BF)
        return c

    lax.fori_loop(0, rows // 128, norm_step, 0)
    loads[2].wait()

    def store(j):
        cols = pl.ds(pl.multiple_of(j * chunk, chunk), chunk)
        return pltpu.make_async_copy(qkv.at[:, cols], qkv_hbm.at[:, cols], st_sem.at[j])

    def mm_step(j, c):
        cols = pl.ds(pl.multiple_of(j * chunk, chunk), chunk)
        qkv[:, cols] = dg(normed[...], w[:, cols], 1, 0).astype(BF)
        store(j).start()
        return c

    steps = w.shape[1] // chunk
    c1, c2 = cuts
    lax.fori_loop(0, c1, mm_step, 0)
    mine = pl.ds(pl.multiple_of(mb * rc, rc), rc)
    own = pre[mine, :] + ibf[mine, :]
    for c in rs_copy:
        c.wait_recv()
    for d in range(1, nb):
        own = own + rs_in[d, 0:rc, :].astype(F)
    hid = jnp.tanh(own)
    hid_ref[...] = hid
    ag_out[0:rc, :] = hid.astype(BF)
    ag_copy = [batch_copy(d, lambda to: ag_out, ag_in.at[d], ag_ss, ag_rs) for d in range(1, nb)]
    for c in ag_copy:
        c.start()
    lax.fori_loop(c1, c2, mm_step, 0)

    def put_low(frm, block):
        low_ref[pl.ds(pl.multiple_of(frm * rc, rc), rc), :] = block

    put_low(mb, ag_out[0:rc, :])
    for c in ag_copy:
        c.wait_recv()
    for d in range(1, nb):
        put_low(lax.rem(mb + nb - d, nb), ag_in[d, 0:rc, :])
    loads[3].wait()
    ob = ob_ref[...].astype(F)
    for t in range(td):
        tbl[t] = (dg(low_ref[t * PAD:(t + 1) * PAD, :], outer[t], 1, 0) + ob[t:t + 1]).astype(BF)

    def aa_copy(d):
        to = lax.rem(me + d, total)
        return pltpu.make_async_remote_copy(src_ref=aa_out.at[to], dst_ref=aa_in.at[me], send_sem=aa_ss.at[d],
                                            recv_sem=aa_rs.at[me], device_id=peer_id(to, nb), device_id_type=MESH)

    def pick(e):
        idx = jnp.int32(0)
        for s in range(slots):
            tid = ids_ref[e, s]
            idx = jnp.where(tid // td == mt, lax.rem(tid, td), idx)
        return tbl[idx]

    def aa_step(d, c):
        to = lax.rem(me + d, total)
        aa_out[to] = pick(to)
        aa_copy(d).start()
        return c

    lax.fori_loop(1, total, aa_step, 0)
    aa_in[me] = pick(me)
    lax.fori_loop(c2, steps, mm_step, 0)

    def aa_wait(d, c):
        frm = lax.rem(me + d, total)
        pltpu.make_async_remote_copy(src_ref=aa_out.at[frm], dst_ref=aa_in.at[frm], send_sem=aa_ss.at[d],
                                     recv_sem=aa_rs.at[frm], device_id=peer_id(frm, nb), device_id_type=MESH).wait()
        return c

    lax.fori_loop(1, total, aa_wait, 0)
    for s in range(slots):
        owner = ids_ref[me, s] // td
        for b in range(nb):
            pkv_ref[s * PAD:(s + 1) * PAD, b * pc:(b + 1) * pc] = aa_in[owner * nb + b]
    for c in rs_copy + ag_copy:
        c.wait_send()

    def st_wait(j, c):
        store(j).wait()
        return c

    lax.fori_loop(0, steps, st_wait, 0)


def front(nt, nb, task_ids, prefix_embed, inner, inner_bias, outer, outer_bias, gain, bias, tokens, weight):
    td, plen, depth = prefix_embed.shape
    rep = inner.shape[2]
    pc = outer.shape[2]
    rows, width = tokens.shape
    slots = task_ids.shape[1]
    total = nt * nb
    rc = td * PAD // nb
    rb = max(rc, PAD)
    chunk = 256
    steps = weight.shape[1] // chunk
    cuts = (steps // 3, 2 * steps // 3)
    sds = jax.ShapeDtypeStruct
    vm = pl.BlockSpec(memory_space=pltpu.VMEM)
    hb = pl.BlockSpec(memory_space=pl.ANY)
    dma = pltpu.SemaphoreType.DMA
    return pl.pallas_call(
        functools.partial(front_kernel, nt, nb, td, plen, chunk, cuts),
        in_specs=[pl.BlockSpec(memory_space=pltpu.SMEM), vm, vm, vm, vm, vm, hb, hb, hb, hb],
        out_specs=[hb, vm, vm, vm],
        out_shape=[sds((rows, weight.shape[1]), BF), sds((slots * PAD, nb * pc), BF), sds((rc, rep), F),
                   sds((td * PAD, rep), BF)],
        scratch_shapes=[
            pltpu.VMEM((rows, width), BF), pltpu.VMEM(weight.shape, BF), pltpu.VMEM(inner.shape, BF),
            pltpu.VMEM(outer.shape, BF), pltpu.VMEM((rows, width), BF), pltpu.VMEM((rows, weight.shape[1]), BF),
            pltpu.VMEM((td * PAD, rep), F), pltpu.VMEM((td * PAD, rep), F), pltpu.VMEM((td, PAD, pc), BF),
            pltpu.VMEM((nb, rb, rep), BF), pltpu.VMEM((nb, rb, rep), BF),
            pltpu.VMEM((rb, rep), BF), pltpu.VMEM((nb, rb, rep), BF),
            pltpu.VMEM((total, PAD, pc), BF), pltpu.VMEM((total, PAD, pc), BF),
            dma((4,)), dma((steps,)), dma((nb,)), dma((nb,)), dma((nb,)), dma((nb,)), dma((total,)), dma((total,)),
        ],
        compiler_params=pltpu.CompilerParams(vmem_limit_bytes=60 * 2**20, collective_id=0, has_side_effects=True),
        name="front",
    )(task_ids, prefix_embed, inner_bias, outer_bias, gain.reshape(1, width), bias.reshape(1, width),
      tokens, weight, inner, outer)


def back_kernel(nt, nb, td, blk,
                ids_ref, hid_ref, g_ref, dpk_ref, dpv_ref, outer_hbm, w_hbm, dq_hbm, dk_hbm, dv_hbm, tok_hbm, gm_hbm,
                ig_hbm, gpre_ref, gtl_ref,
                outer, w, dq, dk, dv, tok, gm, ig, sel, rs_out, rs_in, ag_out, ag_in, aa_out, aa_in, part,
                ld_sem, st_sem, rs_ss, rs_rs, ag_ss, ag_rs, aa_ss, aa_rs):
    rows, width = tok.shape
    slots = ids_ref.shape[1]
    rc = td * PAD // nb
    pc = outer.shape[2]
    mt = lax.axis_index("task")
    mb = lax.axis_index("batch")
    names = ((w_hbm, w), (dq_hbm, dq), (dk_hbm, dk), (dv_hbm, dv), (tok_hbm, tok), (gm_hbm, gm), (outer_hbm, outer))
    loads = [pltpu.make_async_copy(s, d, ld_sem.at[i]) for i, (s, d) in enumerate(names)]
    for c in loads:
        c.start()
    barrier, me, total = greet_all(nt, nb)
    for o in range(nt):
        at = jnp.int32(0)
        for s in range(slots):
            at = jnp.where(ids_ref[me, s] // td == o, s, at)
        for half, ref in enumerate((dpk_ref, dpv_ref)):
            block = ref[at].astype(BF)
            for b in range(nb // 2):
                aa_out[o * nb + half * (nb // 2) + b] = block[:, b * pc:(b + 1) * pc]
    pl.semaphore_wait(barrier, total - 1)

    def aa_copy(d, to, at):
        return pltpu.make_async_remote_copy(src_ref=aa_out.at[to], dst_ref=aa_in.at[at], send_sem=aa_ss.at[d],
                                            recv_sem=aa_rs.at[at], device_id=peer_id(to, nb), device_id_type=MESH)

    def aa_step(d, c):
        aa_copy(d, lax.rem(me + d, total), me).start()
        return c

    lax.fori_loop(1, total, aa_step, 0)
    aa_in[me] = aa_out[me]
    lane = lax.broadcasted_iota(jnp.int32, (1, total * PAD), 1)
    task_of = jnp.zeros((1, total * PAD), jnp.int32)
    for e in range(total):
        idx = jnp.int32(0)
        for s in range(slots):
            tid = ids_ref[e, s]
            idx = jnp.where(tid // td == mt, lax.rem(tid, td), idx)
        task_of = jnp.where(lane // PAD == e, idx, task_of)
    want = task_of * PAD + lax.rem(lane, PAD)
    row = lax.broadcasted_iota(jnp.int32, (td * PAD, total * PAD), 0)
    sel[...] = jnp.where(row == want, 1.0, 0.0).astype(BF)
    gain = g_ref[...].astype(F)
    for c in loads[:6]:
        c.wait()
    inv = 1.0 / width

    def store(i):
        r = pl.ds(pl.multiple_of(i * blk, blk), blk)
        return pltpu.make_async_copy(ig.at[r, :], ig_hbm.at[r, :], st_sem.at[i])

    def mm_step(i, c):
        r = pl.ds(pl.multiple_of(i * blk, blk), blk)
        gn = (dg(dq[r, :], w[:, 0:width], 1, 1) + dg(dk[r, :], w[:, width:2 * width], 1, 1)
              + dg(dv[r, :], w[:, 2 * width:], 1, 1))
        ug = gn * gain
        x = tok[r, :].astype(F)
        cen = x - jnp.sum(x, axis=1, keepdims=True) * inv
        rstd = lax.rsqrt(jnp.sum(cen * cen, axis=1, keepdims=True) * inv + 1e-5)
        xhat = cen * rstd
        m1 = jnp.sum(ug, axis=1, keepdims=True) * inv
        m2 = jnp.sum(ug * xhat, axis=1, keepdims=True) * inv
        ig[r, :] = (gm[r, :] + rstd * (ug - m1 - xhat * m2)).astype(BF)
        store(i).start()
        return c

    steps = rows // blk
    c1, c2 = steps // 4, 3 * steps // 4
    lax.fori_loop(0, c1, mm_step, 0)

    def aa_wait(d, c):
        frm = lax.rem(me + d, total)
        aa_copy(d, frm, frm).wait()
        return c

    lax.fori_loop(1, total, aa_wait, 0)
    gtl_ref[...] = dg(sel[...], aa_in[...].reshape(total * PAD, pc), 1, 0).astype(BF)
    loads[6].wait()
    for t in range(td):
        part[t * PAD:(t + 1) * PAD, :] = dg(gtl_ref[t * PAD:(t + 1) * PAD, :], outer[t], 1, 1)
    for c in range(nb):
        rs_out[c, 0:rc, :] = part[c * rc:(c + 1) * rc, :].astype(BF)

    def batch_copy(d, src, dst, ss, rs):
        to = lax.rem(mb + d, nb)
        return pltpu.make_async_remote_copy(src_ref=src(to), dst_ref=dst, send_sem=ss.at[d], recv_sem=rs.at[d],
                                            device_id={"task": mt, "batch": to}, device_id_type=MESH)

    rs_copy = [batch_copy(d, lambda to: rs_out.at[to], rs_in.at[d], rs_ss, rs_rs) for d in range(1, nb)]
    for c in rs_copy:
        c.start()
    lax.fori_loop(c1, c2, mm_step, 0)
    own = part[pl.ds(pl.multiple_of(mb * rc, rc), rc), :]
    for c in rs_copy:
        c.wait_recv()
    for d in range(1, nb):
        own = own + rs_in[d, 0:rc, :].astype(F)
    hid = hid_ref[...]
    ag_out[0:rc, :] = (own * (1.0 - hid * hid)).astype(BF)
    ag_copy = [batch_copy(d, lambda to: ag_out, ag_in.at[d], ag_ss, ag_rs) for d in range(1, nb)]
    for c in ag_copy:
        c.start()
    lax.fori_loop(c2, steps, mm_step, 0)

    def put(frm, block):
        gpre_ref[pl.ds(pl.multiple_of(frm * rc, rc), rc), :] = block

    put(mb, ag_out[0:rc, :])
    for c in ag_copy:
        c.wait_recv()
    for d in range(1, nb):
        put(lax.rem(mb + nb - d, nb), ag_in[d, 0:rc, :])
    for c in rs_copy + ag_copy:
        c.wait_send()
    for i in range(steps):
        store(i).wait()


def back(nt, nb, task_ids, hid, gain, dpk, dpv, outer, weight, dq, dk, dv, tokens, grad_mid):
    td, rep, pc = outer.shape
    rows, width = tokens.shape
    slots = task_ids.shape[1]
    total = nt * nb
    rc = td * PAD // nb
    rb = max(rc, PAD)
    blk = 128
    sds = jax.ShapeDtypeStruct
    vm = pl.BlockSpec(memory_space=pltpu.VMEM)
    hb = pl.BlockSpec(memory_space=pl.ANY)
    dma = pltpu.SemaphoreType.DMA
    return pl.pallas_call(
        functools.partial(back_kernel, nt, nb, td, blk),
        in_specs=[pl.BlockSpec(memory_space=pltpu.SMEM), vm, vm, vm, vm] + [hb] * 7,
        out_specs=[hb, vm, vm],
        out_shape=[sds((rows, width), BF), sds((td * PAD, rep), BF), sds((td * PAD, pc), BF)],
        scratch_shapes=[
            pltpu.VMEM(outer.shape, BF), pltpu.VMEM(weight.shape, BF)] + [pltpu.VMEM((rows, width), BF)] * 4 + [
            pltpu.VMEM((rows, width), F), pltpu.VMEM((rows, width), BF),
            pltpu.VMEM((td * PAD, total * PAD), BF),
            pltpu.VMEM((nb, rb, rep), BF), pltpu.VMEM((nb, rb, rep), BF),
            pltpu.VMEM((rb, rep), BF), pltpu.VMEM((nb, rb, rep), BF),
            pltpu.VMEM((total, PAD, pc), BF), pltpu.VMEM((total, PAD, pc), BF),
            pltpu.VMEM((td * PAD, rep), F),
            dma((7,)), dma((rows // blk,)), dma((nb,)), dma((nb,)), dma((nb,)), dma((nb,)), dma((total,)), dma((total,)),
        ],
        compiler_params=pltpu.CompilerParams(vmem_limit_bytes=60 * 2**20, collective_id=1, has_side_effects=True),
        name="back",
    )(task_ids, hid, gain.reshape(1, width), dpk.reshape(slots, PAD, width), dpv.reshape(slots, PAD, width),
      outer, weight, dq, dk, dv, tokens, grad_mid)


def tail_kernel(plen, ig_in, emb_ref, inner_ref, gpre_ref, low_ref, gtl_ref,
                ig_out, ge_ref, gi_ref, gib_ref, go_ref, gob_ref, sem):
    step = pl.program_id(0)
    copy = pltpu.make_async_copy(ig_in, ig_out, sem)

    @pl.when(step == 0)
    def _():
        copy.start()

    per = emb_ref.shape[0]
    for k in range(per):
        r = slice(k * PAD, (k + 1) * PAD)
        gp = gpre_ref[r, :]
        gt = gtl_ref[r, :]
        gi_ref[k] = dg(emb_ref[k], gp[0:plen], 0, 0)
        go_ref[k] = dg(low_ref[r, :], gt, 0, 0)
        ge_ref[k] = dg(gp, inner_ref[k], 1, 1)[0:plen]
        at = pl.ds(step * per + k, 1)
        gib_ref[at, :] = jnp.sum(gp[0:plen].astype(F), axis=0, keepdims=True)
        gob_ref[at, :] = jnp.sum(gt[0:plen].astype(F), axis=0, keepdims=True)

    @pl.when(step == pl.num_programs(0) - 1)
    def _():
        copy.wait()


def tail(ig, emb, inner, gpre, low, gtl):
    td, plen, depth = emb.shape
    rep = inner.shape[2]
    pc = gtl.shape[1]
    per = 2
    sds = jax.ShapeDtypeStruct
    hb = pl.BlockSpec(memory_space=pl.ANY)
    lead = lambda *shape: pl.BlockSpec((per,) + shape, lambda i: (i,) + (0,) * len(shape))
    flat = lambda cols: pl.BlockSpec((per * PAD, cols), lambda i: (i, 0))
    full = lambda cols: pl.BlockSpec((td, cols), lambda i: (0, 0))
    return pl.pallas_call(
        functools.partial(tail_kernel, plen),
        grid=(td // per,),
        in_specs=[hb, lead(plen, depth), lead(depth, rep), flat(rep), flat(rep), flat(pc)],
        out_specs=[hb, lead(plen, depth), lead(depth, rep), full(rep), lead(rep, pc), full(pc)],
        out_shape=[sds(ig.shape, BF), sds((td, plen, depth), F), sds((td, depth, rep), F), sds((td, rep), F),
                   sds((td, rep, pc), F), sds((td, pc), F)],
        scratch_shapes=[pltpu.SemaphoreType.DMA],
        compiler_params=pltpu.CompilerParams(vmem_limit_bytes=48 * 2**20),
        name="tail",
    )(ig, emb, inner, gpre, low, gtl)


def layer_norm(values, norm_gain, norm_bias):
    average = jnp.mean(values, axis=-1, keepdims=True)
    centered = values - average
    variance = jnp.mean(centered * centered, axis=-1, keepdims=True)
    return centered * lax.rsqrt(variance + 1e-05) * norm_gain + norm_bias


def gelu_tanh(values):
    return (
        0.5
        * values
        * (1.0 + jnp.tanh(0.7978845608028654 * (values + 0.044715 * values * values * values)))
    )


def local(
    tokens,
    lengths,
    task_ids,
    prefix_embed,
    reparam_inner,
    reparam_inner_bias,
    reparam_outer,
    reparam_outer_bias,
    first_gain,
    first_bias,
    input_weight,
    output_weight,
    second_gain,
    second_bias,
    expand_weight,
    contract_weight,
    output_cotangent,
):
    prefix_len = prefix_embed.shape[1]
    task_count = lax.axis_size("task")
    batch_count = lax.axis_size("batch")
    projected, prefix_kv, hidden_chunk, hidden_low = front(
        task_count, batch_count, task_ids, prefix_embed, reparam_inner, reparam_inner_bias, reparam_outer,
        reparam_outer_bias, first_gain, first_bias, tokens, input_weight,
    )
    gain_two = second_gain.astype(jnp.float32)
    bias_two = second_bias.astype(jnp.float32)
    residual_in = tokens.astype(jnp.float32)
    attended, log_totals = attn_fwd(lengths, projected, prefix_kv, prefix_len)
    mid = residual_in + jnp.dot(attended, output_weight, preferred_element_type=jnp.float32)
    normed_two = layer_norm(mid, gain_two, bias_two).astype(jnp.bfloat16)
    hidden_pre = jnp.dot(normed_two, expand_weight, preferred_element_type=jnp.float32)
    activated = gelu_tanh(hidden_pre).astype(jnp.bfloat16)
    output = (mid + jnp.dot(activated, contract_weight, preferred_element_type=jnp.float32)).astype(
        jnp.bfloat16
    )
    grad_act = jnp.einsum(
        "rc,fc->rf", output_cotangent, contract_weight, preferred_element_type=jnp.float32
    )
    unused_gelu, gelu_pull = jax.vjp(gelu_tanh, hidden_pre)
    grad_hidden = gelu_pull(grad_act)[0].astype(jnp.bfloat16)
    grad_normed_two = jnp.einsum(
        "rf,cf->rc", grad_hidden, expand_weight, preferred_element_type=jnp.float32
    )
    unused_norm_two, norm_two_pull = jax.vjp(
        lambda values: layer_norm(values, gain_two, bias_two), mid
    )
    grad_mid = output_cotangent.astype(jnp.float32) + norm_two_pull(grad_normed_two)[0]
    grad_mid_low = grad_mid.astype(jnp.bfloat16)
    grad_attended = jnp.einsum(
        "rc,dc->rd", grad_mid_low, output_weight, preferred_element_type=jnp.float32
    ).astype(jnp.bfloat16)
    grad_q, grad_k, grad_v, grad_pk, grad_pv = attn_bwd(
        lengths, projected, prefix_kv, attended, grad_attended, log_totals, prefix_len
    )
    input_grad, grad_pre, grad_table = back(
        task_count, batch_count, task_ids, hidden_chunk, first_gain, grad_pk, grad_pv, reparam_outer, input_weight,
        grad_q, grad_k, grad_v, tokens, grad_mid,
    )
    input_grad, grad_embed, grad_inner, grad_inner_bias, grad_outer, grad_outer_bias = tail(
        input_grad, prefix_embed, reparam_inner, grad_pre, hidden_low, grad_table
    )
    return (
        output,
        input_grad,
        grad_embed,
        grad_inner,
        grad_inner_bias,
        grad_outer,
        grad_outer_bias,
    )


def solution(mesh):
    placed = (
        P(("task", "batch"), None),
        P(("task", "batch"), None),
        P(),
        P("task", None, "batch"),
        P("task", "batch", None),
        P("task", None),
        P("task", None, "batch"),
        P("task", "batch"),
        P(),
        P(),
        P(),
        P(),
        P(),
        P(),
        P(),
        P(),
        P(("task", "batch"), None),
    )
    return jax.shard_map(
        local,
        mesh=mesh,
        in_specs=placed,
        out_specs=(
            P(("task", "batch"), None),
            P(("task", "batch"), None),
            P("task", None, "batch"),
            P("task", "batch", None),
            P("task", None),
            P("task", None, "batch"),
            P("task", "batch"),
        ),
        check_vma=False,
    )
```

```python
import functools

import jax
import jax.numpy as jnp
from jax import lax
from jax.experimental import pallas as pl
from jax.experimental.pallas import tpu as pltpu
from jax.sharding import PartitionSpec as P

BF = jnp.bfloat16
F = jnp.float32
PAD = 16
NEG = -1e30
MESH = pl.DeviceIdType.MESH


def dg(a, b, ca, cb):
    return lax.dot_general(a, b, (((ca,), (cb,)), ((), ())), preferred_element_type=F)


def attn_fwd_kernel(slots, plen, len_ref, q_ref, k_ref, v_ref, pk_ref, pv_ref, o_ref, lse_ref, km):
    rows, pair = q_ref.shape
    blk = rows // slots
    hd = pair // 2
    scale = hd ** -0.5
    single = len_ref[0, 0] > blk
    first = lax.broadcasted_iota(jnp.int32, (1, pair), 1) < hd
    zero = jnp.zeros((), BF)
    k = k_ref[...]
    km[0] = jnp.where(first, k, zero)
    km[1] = jnp.where(first, zero, k)
    vt = v_ref[...].T
    tri = lax.broadcasted_iota(jnp.int32, (blk, blk), 0) <= lax.broadcasted_iota(jnp.int32, (blk, blk), 1)
    live = lax.broadcasted_iota(jnp.int32, (PAD, blk), 0) < plen
    for i in range(slots):
        lo, hi = i * blk, (i + 1) * blk
        q = q_ref[lo:hi, :] * jnp.asarray(scale, BF)
        kp = jnp.where(single, pk_ref[0:PAD, :], pk_ref[i * PAD:(i + 1) * PAD, :])
        vp = jnp.where(single, pv_ref[0:PAD, :], pv_ref[i * PAD:(i + 1) * PAD, :])
        vpt = jnp.concatenate([jnp.where(first, vp, zero), jnp.where(first, zero, vp)], axis=0).T
        sp = dg(jnp.concatenate([jnp.where(first, kp, zero), jnp.where(first, zero, kp)], axis=0), q, 1, 1)
        outs, tops, sums, pps = [], [], [], []
        for h in range(2):
            s_pre = jnp.where(live, sp[h * PAD:(h + 1) * PAD], NEG)
            s_dia = jnp.where(tri, dg(km[h, lo:hi, :], q, 1, 1), NEG)
            top = jnp.maximum(jnp.max(s_dia, axis=0, keepdims=True), jnp.max(s_pre, axis=0, keepdims=True))
            if i:
                s_off = dg(km[h, 0:lo, :], q, 1, 1)
                top = jnp.maximum(top, jnp.where(single, jnp.max(s_off, axis=0, keepdims=True), NEG))
            p_pre = jnp.exp(s_pre - top)
            p_dia = jnp.exp(s_dia - top)
            total = jnp.sum(p_dia, axis=0, keepdims=True) + jnp.sum(p_pre, axis=0, keepdims=True)
            ot = dg(vt[h * hd:(h + 1) * hd, lo:hi], p_dia.astype(BF), 1, 0)
            if i:
                p_off = jnp.exp(s_off - jnp.where(single, top, -NEG))
                total = total + jnp.sum(p_off, axis=0, keepdims=True)
                ot = ot + dg(vt[h * hd:(h + 1) * hd, 0:lo], p_off.astype(BF), 1, 0)
            outs.append(ot)
            tops.append(top)
            sums.append(total)
            pps.append(p_pre.astype(BF))
        pre = dg(vpt, jnp.concatenate(pps, axis=0), 1, 0)
        for h in range(2):
            outs[h] = (outs[h] + pre[h * hd:(h + 1) * hd]) / sums[h]
            lse_ref[0, h:h + 1, lo:hi] = tops[h] + jnp.log(sums[h])
        o_ref[lo:hi, :] = jnp.concatenate(outs, axis=0).T.astype(BF)


def attn_fwd(lengths, qkv, pkv, plen):
    rows = qkv.shape[0]
    width = qkv.shape[1] // 3
    slots = lengths.shape[1]
    pairs = width // 128
    col = lambda off: pl.BlockSpec((rows, 128), lambda h: (0, h + off))
    pcol = lambda off: pl.BlockSpec((slots * PAD, 128), lambda h: (0, h + off))
    return pl.pallas_call(
        functools.partial(attn_fwd_kernel, slots, plen),
        grid=(pairs,),
        in_specs=[pl.BlockSpec(memory_space=pltpu.SMEM), col(0), col(pairs), col(2 * pairs), pcol(0), pcol(pairs)],
        out_specs=[col(0), pl.BlockSpec((1, 2, rows), lambda h: (h, 0, 0))],
        out_shape=[jax.ShapeDtypeStruct((rows, width), BF), jax.ShapeDtypeStruct((pairs, 2, rows), F)],
        scratch_shapes=[pltpu.VMEM((2, rows, 128), BF)],
        compiler_params=pltpu.CompilerParams(vmem_limit_bytes=62 * 2**20),
        name="attend",
    )(lengths, qkv, qkv, qkv, pkv, pkv)


def attn_bwd_kernel(slots, plen, len_ref, q_ref, k_ref, v_ref, pk_ref, pv_ref, o_ref, do_ref, lse_ref,
                    dq_ref, dk_ref, dv_ref, dpk_ref, dpv_ref, km, vm, dka, dva):
    rows, pair = q_ref.shape
    blk = rows // slots
    hd = pair // 2
    scale = hd ** -0.5
    single = len_ref[0, 0] > blk
    first = lax.broadcasted_iota(jnp.int32, (1, pair), 1) < hd
    zero = jnp.zeros((), BF)
    split = lambda a: (jnp.where(first, a, zero), jnp.where(first, zero, a))
    stack = lambda a: jnp.concatenate(split(a), axis=0)
    k = k_ref[...]
    km[0], km[1] = split(k)
    vm[0], vm[1] = split(v_ref[...])
    kt = k.T
    tri = lax.broadcasted_iota(jnp.int32, (blk, blk), 0) <= lax.broadcasted_iota(jnp.int32, (blk, blk), 1)
    live = lax.broadcasted_iota(jnp.int32, (PAD, blk), 0) < plen
    pk_sum = pv_sum = None
    pk_parts, pv_parts = [], []
    for i in range(slots):
        lo, hi = i * blk, (i + 1) * blk
        q = q_ref[lo:hi, :] * jnp.asarray(scale, BF)
        do = do_ref[lo:hi, :]
        kp = stack(jnp.where(single, pk_ref[0:PAD, :], pk_ref[i * PAD:(i + 1) * PAD, :]))
        vp = stack(jnp.where(single, pv_ref[0:PAD, :], pv_ref[i * PAD:(i + 1) * PAD, :]))
        sp = dg(kp, q, 1, 1)
        dpp = dg(vp, do, 1, 1)
        prod = (do.astype(F) * o_ref[lo:hi, :].astype(F)).T
        qs = split(q)
        dos = split(do)
        dqs, dsps = [], []
        dk_new = dv_new = None
        add = lambda a, b: b if a is None else a + b
        pkp = pvp = None
        offk = offv = diak = diav = None
        for h in range(2):
            lse = lse_ref[0, h:h + 1, lo:hi]
            delta = jnp.sum(prod[h * hd:(h + 1) * hd], axis=0, keepdims=True)
            p_pre = jnp.where(live, jnp.exp(sp[h * PAD:(h + 1) * PAD] - lse), 0.0)
            ds_pre = (p_pre * (dpp[h * PAD:(h + 1) * PAD] - delta)).astype(BF)
            p_dia = jnp.where(tri, jnp.exp(dg(km[h, lo:hi, :], q, 1, 1) - lse), 0.0)
            ds_dia = (p_dia * (dg(vm[h, lo:hi, :], do, 1, 1) - delta)).astype(BF)
            diav = add(diav, dg(p_dia.astype(BF), dos[h], 1, 0))
            diak = add(diak, dg(ds_dia, qs[h], 1, 0))
            pvp = add(pvp, dg(p_pre.astype(BF), dos[h], 1, 0))
            pkp = add(pkp, dg(ds_pre, qs[h], 1, 0))
            dqt = dg(kt[h * hd:(h + 1) * hd, lo:hi], ds_dia, 1, 0)
            if i:
                p_off = jnp.exp(dg(km[h, 0:lo, :], q, 1, 1) - jnp.where(single, lse, -NEG))
                ds_off = (p_off * (dg(vm[h, 0:lo, :], do, 1, 1) - delta)).astype(BF)
                offv = add(offv, dg(p_off.astype(BF), dos[h], 1, 0))
                offk = add(offk, dg(ds_off, qs[h], 1, 0))
                dqt = dqt + dg(kt[h * hd:(h + 1) * hd, 0:lo], ds_off, 1, 0)
            dqs.append(dqt)
            dsps.append(ds_pre)
        dqt = jnp.concatenate(dqs, axis=0) + dg(kp.T, jnp.concatenate(dsps, axis=0), 1, 0)
        dq_ref[lo:hi, :] = (dqt.T * scale).astype(BF)
        dka[lo:hi, :] = diak
        dva[lo:hi, :] = diav
        if i:
            dka[0:lo, :] += offk
            dva[0:lo, :] += offv
        pk_parts.append(pkp)
        pv_parts.append(pvp)
    dk_ref[...] = dka[...].astype(BF)
    dv_ref[...] = dva[...].astype(BF)
    for i in range(slots):
        for ref, parts in ((dpk_ref, pk_parts), (dpv_ref, pv_parts)):
            whole = sum(parts) if i == 0 else jnp.zeros_like(parts[0])
            ref[i * PAD:(i + 1) * PAD, :] = jnp.where(single, whole, parts[i])


def attn_bwd(lengths, qkv, pkv, attended, grad_att, lse, plen):
    rows = qkv.shape[0]
    width = qkv.shape[1] // 3
    slots = lengths.shape[1]
    pairs = width // 128
    col = lambda off: pl.BlockSpec((rows, 128), lambda h: (0, h + off))
    pcol = lambda off: pl.BlockSpec((slots * PAD, 128), lambda h: (0, h + off))
    sds = jax.ShapeDtypeStruct
    return pl.pallas_call(
        functools.partial(attn_bwd_kernel, slots, plen),
        grid=(pairs,),
        in_specs=[pl.BlockSpec(memory_space=pltpu.SMEM), col(0), col(pairs), col(2 * pairs), pcol(0), pcol(pairs),
                  col(0), col(0), pl.BlockSpec((1, 2, rows), lambda h: (h, 0, 0))],
        out_specs=[col(0), col(0), col(0), pcol(0), pcol(0)],
        out_shape=[sds((rows, width), BF)] * 3 + [sds((slots * PAD, width), F)] * 2,
        scratch_shapes=[pltpu.VMEM((2, rows, 128), BF)] * 2 + [pltpu.VMEM((rows, 128), F)] * 2,
        compiler_params=pltpu.CompilerParams(vmem_limit_bytes=62 * 2**20),
        name="attend_back",
    )(lengths, qkv, qkv, qkv, pkv, pkv, attended, grad_att, lse)


def peer_id(flat, nb):
    return {"task": flat // nb, "batch": flat % nb}


def layer_norm_rows(x, gain, bias):
    inv = 1.0 / x.shape[1]
    mean = jnp.sum(x, axis=1, keepdims=True) * inv
    cen = x - mean
    var = jnp.sum(cen * cen, axis=1, keepdims=True) * inv
    return cen * lax.rsqrt(var + 1e-5) * gain + bias


def greet_all(nt, nb):
    me = lax.axis_index("task") * nb + lax.axis_index("batch")
    total = nt * nb
    barrier = pltpu.get_barrier_semaphore()

    def greet(d, c):
        pl.semaphore_signal(barrier, inc=1, device_id=peer_id(lax.rem(me + d, total), nb), device_id_type=MESH)
        return c

    lax.fori_loop(1, total, greet, 0)
    return barrier, me, total


def front_kernel(nt, nb, td, plen, chunk, cuts,
                 ids_ref, emb_ref, ib_ref, ob_ref, g_ref, b_ref, tok_hbm, w_hbm, inner_hbm, outer_hbm,
                 qkv_hbm, pkv_ref, hid_ref, low_ref,
                 tok, w, inner, outer, normed, qkv, pre, emf, ibf, tbl, rs_out, rs_in, ag_out, ag_in, aa_out, aa_in,
                 ld_sem, st_sem, rs_ss, rs_rs, ag_ss, ag_rs, aa_ss, aa_rs):
    rows, width = tok.shape
    slots = ids_ref.shape[0]
    rc = td * PAD // nb
    pc = outer.shape[2]
    mt = lax.axis_index("task")
    mb = lax.axis_index("batch")
    loads = [pltpu.make_async_copy(s, d, ld_sem.at[i])
             for i, (s, d) in enumerate(((inner_hbm, inner), (tok_hbm, tok), (w_hbm, w), (outer_hbm, outer)))]
    for c in loads:
        c.start()
    barrier, me, total = greet_all(nt, nb)
    pre[...] = jnp.zeros_like(pre)
    emf[...] = emb_ref[...].astype(F).reshape(emf.shape)
    loads[0].wait()
    for t in range(td):
        pre[t * PAD:t * PAD + plen, :] = dg(emf[pl.ds(t, plen, stride=td), :].astype(BF), inner[t], 1, 0)
    for c in range(nb):
        rs_out[c, 0:rc, :] = pre[c * rc:(c + 1) * rc, :].astype(BF)
    ib = ib_ref[...].astype(F)
    for t in range(td):
        ibf[t * PAD:(t + 1) * PAD, :] = jnp.broadcast_to(ib[t:t + 1], (PAD, ib.shape[1]))
    pl.semaphore_wait(barrier, total - 1)

    def batch_copy(d, src, dst, ss, rs):
        to = lax.rem(mb + d, nb)
        return pltpu.make_async_remote_copy(src_ref=src(to), dst_ref=dst, send_sem=ss.at[d], recv_sem=rs.at[d],
                                            device_id={"task": mt, "batch": to}, device_id_type=MESH)

    rs_copy = [batch_copy(d, lambda to: rs_out.at[to], rs_in.at[d], rs_ss, rs_rs) for d in range(1, nb)]
    for c in rs_copy:
        c.start()
    loads[1].wait()
    gain = g_ref[...].astype(F).reshape(1, -1)
    bias = b_ref[...].astype(F).reshape(1, -1)

    def norm_step(i, c):
        r = pl.ds(pl.multiple_of(i * 128, 128), 128)
        normed[r, :] = layer_norm_rows(tok[r, :].astype(F), gain, bias).astype(BF)
        return c

    lax.fori_loop(0, rows // 128, norm_step, 0)
    loads[2].wait()

    def store(j):
        cols = pl.ds(pl.multiple_of(j * chunk, chunk), chunk)
        return pltpu.make_async_copy(qkv.at[:, cols], qkv_hbm.at[:, cols], st_sem.at[j])

    def mm_step(j, c):
        cols = pl.ds(pl.multiple_of(j * chunk, chunk), chunk)
        qkv[:, cols] = dg(normed[...], w[:, cols], 1, 0).astype(BF)
        store(j).start()
        return c

    steps = w.shape[1] // chunk
    c1, c2 = cuts
    lax.fori_loop(0, c1, mm_step, 0)
    mine = pl.ds(pl.multiple_of(mb * rc, rc), rc)
    own = pre[mine, :] + ibf[mine, :]
    for c in rs_copy:
        c.wait_recv()
    for d in range(1, nb):
        own = own + rs_in[d, 0:rc, :].astype(F)
    hid = jnp.tanh(own)
    hid_ref[...] = hid
    ag_out[0:rc, :] = hid.astype(BF)
    ag_copy = [batch_copy(d, lambda to: ag_out, ag_in.at[d], ag_ss, ag_rs) for d in range(1, nb)]
    for c in ag_copy:
        c.start()
    lax.fori_loop(c1, c2, mm_step, 0)

    def put_low(frm, block):
        low_ref[pl.ds(pl.multiple_of(frm * rc, rc), rc), :] = block

    put_low(mb, ag_out[0:rc, :])
    for c in ag_copy:
        c.wait_recv()
    for d in range(1, nb):
        put_low(lax.rem(mb + nb - d, nb), ag_in[d, 0:rc, :])
    loads[3].wait()
    ob = ob_ref[...].astype(F)
    for t in range(td):
        tbl[t] = (dg(low_ref[t * PAD:(t + 1) * PAD, :], outer[t], 1, 0) + ob[t:t + 1]).astype(BF)

    def aa_copy(d):
        to = lax.rem(me + d, total)
        return pltpu.make_async_remote_copy(src_ref=aa_out.at[to], dst_ref=aa_in.at[me], send_sem=aa_ss.at[d],
                                            recv_sem=aa_rs.at[me], device_id=peer_id(to, nb), device_id_type=MESH)

    def pick(e):
        idx = jnp.int32(0)
        for s in range(slots):
            tid = ids_ref[s, e]
            idx = jnp.where(tid // td == mt, lax.rem(tid, td), idx)
        return tbl[idx]

    def aa_step(d, c):
        to = lax.rem(me + d, total)
        aa_out[to] = pick(to)
        aa_copy(d).start()
        return c

    lax.fori_loop(1, total, aa_step, 0)
    aa_in[me] = pick(me)
    lax.fori_loop(c2, steps, mm_step, 0)

    def aa_wait(d, c):
        frm = lax.rem(me + d, total)
        pltpu.make_async_remote_copy(src_ref=aa_out.at[frm], dst_ref=aa_in.at[frm], send_sem=aa_ss.at[d],
                                     recv_sem=aa_rs.at[frm], device_id=peer_id(frm, nb), device_id_type=MESH).wait()
        return c

    lax.fori_loop(1, total, aa_wait, 0)
    for s in range(slots):
        owner = ids_ref[s, me] // td
        for b in range(nb):
            pkv_ref[s * PAD:(s + 1) * PAD, b * pc:(b + 1) * pc] = aa_in[owner * nb + b]
    for c in rs_copy + ag_copy:
        c.wait_send()

    def st_wait(j, c):
        store(j).wait()
        return c

    lax.fori_loop(0, steps, st_wait, 0)


def front(nt, nb, task_ids, prefix_embed, inner, inner_bias, outer, outer_bias, gain, bias, tokens, weight):
    plen, td, depth = prefix_embed.shape
    rep = inner.shape[2]
    pc = outer.shape[2]
    rows, width = tokens.shape
    slots = task_ids.shape[0]
    total = nt * nb
    rc = td * PAD // nb
    rb = max(rc, PAD)
    chunk = 1024
    steps = weight.shape[1] // chunk
    cuts = (steps // 3, 2 * steps // 3)
    sds = jax.ShapeDtypeStruct
    vm = pl.BlockSpec(memory_space=pltpu.VMEM)
    hb = pl.BlockSpec(memory_space=pl.ANY)
    dma = pltpu.SemaphoreType.DMA
    return pl.pallas_call(
        functools.partial(front_kernel, nt, nb, td, plen, chunk, cuts),
        in_specs=[pl.BlockSpec(memory_space=pltpu.SMEM), vm, vm, vm, vm, vm, hb, hb, hb, hb],
        out_specs=[hb, vm, vm, vm],
        out_shape=[sds((rows, weight.shape[1]), BF), sds((slots * PAD, nb * pc), BF), sds((rc, rep), F),
                   sds((td * PAD, rep), BF)],
        scratch_shapes=[
            pltpu.VMEM((rows, width), BF), pltpu.VMEM(weight.shape, BF), pltpu.VMEM(inner.shape, BF),
            pltpu.VMEM(outer.shape, BF), pltpu.VMEM((rows, width), BF), pltpu.VMEM((rows, weight.shape[1]), BF),
            pltpu.VMEM((td * PAD, rep), F), pltpu.VMEM((plen * td, depth), F), pltpu.VMEM((td * PAD, rep), F), pltpu.VMEM((td, PAD, pc), BF),
            pltpu.VMEM((nb, rb, rep), BF), pltpu.VMEM((nb, rb, rep), BF),
            pltpu.VMEM((rb, rep), BF), pltpu.VMEM((nb, rb, rep), BF),
            pltpu.VMEM((total, PAD, pc), BF), pltpu.VMEM((total, PAD, pc), BF),
            dma((4,)), dma((steps,)), dma((nb,)), dma((nb,)), dma((nb,)), dma((nb,)), dma((total,)), dma((total,)),
        ],
        compiler_params=pltpu.CompilerParams(vmem_limit_bytes=62 * 2**20, collective_id=0, has_side_effects=True),
        name="front",
    )(task_ids, prefix_embed, inner_bias, outer_bias, gain, bias,
      tokens, weight, inner, outer)


def middle_kernel(blk, fch, g_ref, b_ref, tok_hbm, att_hbm, ct_hbm, wo_hbm, we_hbm, wc_hbm,
                  out_hbm, gm_hbm, ga_hbm,
                  tok, att, ct, wo, we, wc, mid, n2, mean_s, rstd_s, ld_sem, st_sem):
    rows, width = tok.shape
    ff = we.shape[1]
    names = ((wo_hbm, wo), (att_hbm, att), (tok_hbm, tok), (we_hbm, we), (ct_hbm, ct), (wc_hbm, wc))
    loads = [pltpu.make_async_copy(s, d, ld_sem.at[i]) for i, (s, d) in enumerate(names)]
    for c in loads:
        c.start()
    gain = g_ref[...].astype(F).reshape(1, -1)
    bias = b_ref[...].astype(F).reshape(1, -1)
    inv = 1.0 / width
    steps = rows // blk
    for c in loads[:3]:
        c.wait()

    def first(i, c):
        r = pl.ds(pl.multiple_of(i * blk, blk), blk)
        x = tok[r, :].astype(F) + dg(att[r, :], wo[...], 1, 0)
        mid[r, :] = x
        mean = jnp.sum(x, axis=1, keepdims=True) * inv
        cen = x - mean
        rstd = lax.rsqrt(jnp.sum(cen * cen, axis=1, keepdims=True) * inv + 1e-5)
        mean_s[r, :] = mean
        rstd_s[r, :] = rstd
        n2[r, :] = (cen * rstd * gain + bias).astype(BF)
        return c

    lax.fori_loop(0, steps, first, 0)
    for c in loads[3:]:
        c.wait()

    def stores(i):
        r = pl.ds(pl.multiple_of(i * blk, blk), blk)
        return [pltpu.make_async_copy(s.at[r, :], d.at[r, :], st_sem.at[k, i])
                for k, (s, d) in enumerate(((tok, out_hbm), (mid, gm_hbm), (att, ga_hbm)))]

    def second(i, c):
        r = pl.ds(pl.multiple_of(i * blk, blk), blk)
        x2 = n2[r, :]
        g = ct[r, :]
        pair = lambda k: (dg(x2, we[:, k:k + fch], 1, 0), dg(g, wc[k:k + fch, :], 1, 1))
        y = gn = None
        nxt = pair(0)
        for k in range(0, ff, fch):
            v, up = nxt
            if k + fch < ff:
                nxt = pair(k + fch)
            vv = v * v
            t = jnp.tanh(v * (0.7978845608028654 + (0.7978845608028654 * 0.044715) * vv))
            half = 0.5 + 0.5 * t
            act = (v * half).astype(BF)
            slope = half + v * (0.5 - 0.5 * t * t) * (0.7978845608028654 + (3 * 0.7978845608028654 * 0.044715) * vv)
            gh = (up * slope).astype(BF)
            yk = dg(act, wc[k:k + fch, :], 1, 0)
            gk = dg(gh, we[:, k:k + fch], 1, 1)
            y = yk if y is None else y + yk
            gn = gk if gn is None else gn + gk
        x = mid[r, :]
        tok[r, :] = (x + y).astype(BF)
        rstd = rstd_s[r, :]
        xhat = (x - mean_s[r, :]) * rstd
        ug = gn * gain
        m1 = jnp.sum(ug, axis=1, keepdims=True) * inv
        m2 = jnp.sum(ug * xhat, axis=1, keepdims=True) * inv
        gmid = g.astype(F) + rstd * (ug - m1 - xhat * m2)
        mid[r, :] = gmid
        att[r, :] = dg(gmid.astype(BF), wo[...], 1, 1).astype(BF)
        for cp in stores(i):
            cp.start()
        return c

    lax.fori_loop(0, steps, second, 0)
    for i in range(steps):
        for cp in stores(i):
            cp.wait()


def middle(gain, bias, tokens, attended, ct, wo, we, wc, blk=256, fch=512):
    rows, width = tokens.shape
    ff = we.shape[1]
    sds = jax.ShapeDtypeStruct
    vm = pl.BlockSpec(memory_space=pltpu.VMEM)
    hb = pl.BlockSpec(memory_space=pl.ANY)
    dma = pltpu.SemaphoreType.DMA
    full = lambda t: pltpu.VMEM((rows, width), t)
    return pl.pallas_call(
        functools.partial(middle_kernel, blk, fch),
        in_specs=[vm, vm] + [hb] * 6,
        out_specs=[hb] * 3,
        out_shape=[sds((rows, width), BF), sds((rows, width), F), sds((rows, width), BF)],
        scratch_shapes=[full(BF), full(BF), full(BF), pltpu.VMEM(wo.shape, BF), pltpu.VMEM(we.shape, BF),
                        pltpu.VMEM(wc.shape, BF), full(F), full(BF), pltpu.VMEM((rows, 1), F), pltpu.VMEM((rows, 1), F),
                        dma((6,)), dma((3, rows // blk))],
        compiler_params=pltpu.CompilerParams(vmem_limit_bytes=62 * 2**20),
        name="middle",
    )(gain, bias, tokens, attended, ct, wo, we, wc)


def back_kernel(nt, nb, td, blk,
                ids_ref, hid_ref, g_ref, dpk_ref, dpv_ref, outer_hbm, w_hbm, dq_hbm, dk_hbm, dv_hbm, tok_hbm, gm_hbm,
                ig_hbm, gpre_ref, gtl_ref,
                outer, w, dq, dk, dv, tok, gm, ig, sel, rs_out, rs_in, ag_out, ag_in, aa_out, aa_in, part,
                ld_sem, st_sem, rs_ss, rs_rs, ag_ss, ag_rs, aa_ss, aa_rs):
    rows, width = tok.shape
    slots = ids_ref.shape[0]
    rc = td * PAD // nb
    pc = outer.shape[2]
    mt = lax.axis_index("task")
    mb = lax.axis_index("batch")
    names = ((w_hbm, w), (dq_hbm, dq), (dk_hbm, dk), (dv_hbm, dv), (tok_hbm, tok), (gm_hbm, gm), (outer_hbm, outer))
    loads = [pltpu.make_async_copy(s, d, ld_sem.at[i]) for i, (s, d) in enumerate(names)]
    for c in loads:
        c.start()
    barrier, me, total = greet_all(nt, nb)
    for o in range(nt):
        at = jnp.int32(0)
        for s in range(slots):
            at = jnp.where(ids_ref[s, me] // td == o, s, at)
        for half, ref in enumerate((dpk_ref, dpv_ref)):
            block = ref[at].astype(BF)
            for b in range(nb // 2):
                aa_out[o * nb + half * (nb // 2) + b] = block[:, b * pc:(b + 1) * pc]
    pl.semaphore_wait(barrier, total - 1)

    def aa_copy(d, to, at):
        return pltpu.make_async_remote_copy(src_ref=aa_out.at[to], dst_ref=aa_in.at[at], send_sem=aa_ss.at[d],
                                            recv_sem=aa_rs.at[at], device_id=peer_id(to, nb), device_id_type=MESH)

    def aa_step(d, c):
        aa_copy(d, lax.rem(me + d, total), me).start()
        return c

    lax.fori_loop(1, total, aa_step, 0)
    aa_in[me] = aa_out[me]
    lane = lax.broadcasted_iota(jnp.int32, (1, total * PAD), 1)
    task_of = jnp.zeros((1, total * PAD), jnp.int32)
    for e in range(total):
        idx = jnp.int32(0)
        for s in range(slots):
            tid = ids_ref[s, e]
            idx = jnp.where(tid // td == mt, lax.rem(tid, td), idx)
        task_of = jnp.where(lane // PAD == e, idx, task_of)
    want = task_of * PAD + lax.rem(lane, PAD)
    row = lax.broadcasted_iota(jnp.int32, (td * PAD, total * PAD), 0)
    sel[...] = jnp.where(row == want, 1.0, 0.0).astype(BF)
    gain = g_ref[...].astype(F).reshape(1, -1)
    for c in loads[:6]:
        c.wait()
    inv = 1.0 / width

    def store(i):
        r = pl.ds(pl.multiple_of(i * blk, blk), blk)
        return pltpu.make_async_copy(ig.at[r, :], ig_hbm.at[r, :], st_sem.at[i])

    def mm_step(i, c):
        r = pl.ds(pl.multiple_of(i * blk, blk), blk)
        gn = (dg(dq[r, :], w[:, 0:width], 1, 1) + dg(dk[r, :], w[:, width:2 * width], 1, 1)
              + dg(dv[r, :], w[:, 2 * width:], 1, 1))
        ug = gn * gain
        x = tok[r, :].astype(F)
        cen = x - jnp.sum(x, axis=1, keepdims=True) * inv
        rstd = lax.rsqrt(jnp.sum(cen * cen, axis=1, keepdims=True) * inv + 1e-5)
        xhat = cen * rstd
        m1 = jnp.sum(ug, axis=1, keepdims=True) * inv
        m2 = jnp.sum(ug * xhat, axis=1, keepdims=True) * inv
        ig[r, :] = (gm[r, :] + rstd * (ug - m1 - xhat * m2)).astype(BF)
        store(i).start()
        return c

    steps = rows // blk
    c1, c2 = steps // 4, 3 * steps // 4
    lax.fori_loop(0, c1, mm_step, 0)

    def aa_wait(d, c):
        frm = lax.rem(me + d, total)
        aa_copy(d, frm, frm).wait()
        return c

    lax.fori_loop(1, total, aa_wait, 0)
    gtl_ref[...] = dg(sel[...], aa_in[...].reshape(total * PAD, pc), 1, 0).astype(BF)
    loads[6].wait()
    for t in range(td):
        part[t * PAD:(t + 1) * PAD, :] = dg(gtl_ref[t * PAD:(t + 1) * PAD, :], outer[t], 1, 1)
    for c in range(nb):
        rs_out[c, 0:rc, :] = part[c * rc:(c + 1) * rc, :].astype(BF)

    def batch_copy(d, src, dst, ss, rs):
        to = lax.rem(mb + d, nb)
        return pltpu.make_async_remote_copy(src_ref=src(to), dst_ref=dst, send_sem=ss.at[d], recv_sem=rs.at[d],
                                            device_id={"task": mt, "batch": to}, device_id_type=MESH)

    rs_copy = [batch_copy(d, lambda to: rs_out.at[to], rs_in.at[d], rs_ss, rs_rs) for d in range(1, nb)]
    for c in rs_copy:
        c.start()
    lax.fori_loop(c1, c2, mm_step, 0)
    own = part[pl.ds(pl.multiple_of(mb * rc, rc), rc), :]
    for c in rs_copy:
        c.wait_recv()
    for d in range(1, nb):
        own = own + rs_in[d, 0:rc, :].astype(F)
    hid = hid_ref[...]
    ag_out[0:rc, :] = (own * (1.0 - hid * hid)).astype(BF)
    ag_copy = [batch_copy(d, lambda to: ag_out, ag_in.at[d], ag_ss, ag_rs) for d in range(1, nb)]
    for c in ag_copy:
        c.start()
    lax.fori_loop(c2, steps, mm_step, 0)

    def put(frm, block):
        gpre_ref[pl.ds(pl.multiple_of(frm * rc, rc), rc), :] = block

    put(mb, ag_out[0:rc, :])
    for c in ag_copy:
        c.wait_recv()
    for d in range(1, nb):
        put(lax.rem(mb + nb - d, nb), ag_in[d, 0:rc, :])
    for c in rs_copy + ag_copy:
        c.wait_send()
    for i in range(steps):
        store(i).wait()


def back(nt, nb, task_ids, hid, gain, dpk, dpv, outer, weight, dq, dk, dv, tokens, grad_mid):
    td, rep, pc = outer.shape
    rows, width = tokens.shape
    slots = task_ids.shape[0]
    total = nt * nb
    rc = td * PAD // nb
    rb = max(rc, PAD)
    blk = 256
    sds = jax.ShapeDtypeStruct
    vm = pl.BlockSpec(memory_space=pltpu.VMEM)
    hb = pl.BlockSpec(memory_space=pl.ANY)
    dma = pltpu.SemaphoreType.DMA
    return pl.pallas_call(
        functools.partial(back_kernel, nt, nb, td, blk),
        in_specs=[pl.BlockSpec(memory_space=pltpu.SMEM), vm, vm, vm, vm] + [hb] * 7,
        out_specs=[hb, vm, vm],
        out_shape=[sds((rows, width), BF), sds((td * PAD, rep), BF), sds((td * PAD, pc), BF)],
        scratch_shapes=[
            pltpu.VMEM(outer.shape, BF), pltpu.VMEM(weight.shape, BF)] + [pltpu.VMEM((rows, width), BF)] * 4 + [
            pltpu.VMEM((rows, width), F), pltpu.VMEM((rows, width), BF),
            pltpu.VMEM((td * PAD, total * PAD), BF),
            pltpu.VMEM((nb, rb, rep), BF), pltpu.VMEM((nb, rb, rep), BF),
            pltpu.VMEM((rb, rep), BF), pltpu.VMEM((nb, rb, rep), BF),
            pltpu.VMEM((total, PAD, pc), BF), pltpu.VMEM((total, PAD, pc), BF),
            pltpu.VMEM((td * PAD, rep), F),
            dma((7,)), dma((rows // blk,)), dma((nb,)), dma((nb,)), dma((nb,)), dma((nb,)), dma((total,)), dma((total,)),
        ],
        compiler_params=pltpu.CompilerParams(vmem_limit_bytes=62 * 2**20, collective_id=1, has_side_effects=True),
        name="back",
    )(task_ids, hid, gain, dpk.reshape(slots, PAD, width), dpv.reshape(slots, PAD, width),
      outer, weight, dq, dk, dv, tokens, grad_mid)


def tail_kernel(plen, ig_in, emb_ref, inner_ref, gpre_ref, low_ref, gtl_ref,
                ig_out, ge_ref, gi_ref, gib_ref, go_ref, gob_ref, emf):
    step = pl.program_id(0)
    ig_out[...] = ig_in[...]

    @pl.when(step == 0)
    def _():
        emf[...] = emb_ref[...].astype(F).reshape(emf.shape)

    per = inner_ref.shape[0]
    td = gib_ref.shape[0]
    for k in range(per):
        r = slice(k * PAD, (k + 1) * PAD)
        gp = gpre_ref[r, :]
        gt = gtl_ref[r, :]
        at = pl.ds(step * per + k, 1)
        spread = pl.ds(step * per + k, plen, stride=td)
        gi_ref[k] = dg(emf[spread, :].astype(BF), gp[0:plen], 0, 0)
        go_ref[k] = dg(low_ref[r, :], gt, 0, 0)
        ge_ref[spread, :] = dg(gp, inner_ref[k], 1, 1)[0:plen]
        gib_ref[at, :] = jnp.sum(gp[0:plen].astype(F), axis=0, keepdims=True)
        gob_ref[at, :] = jnp.sum(gt[0:plen].astype(F), axis=0, keepdims=True)


def tail(ig, emb, inner, gpre, low, gtl):
    plen, td, depth = emb.shape
    rep = inner.shape[2]
    pc = gtl.shape[1]
    per = 2
    sds = jax.ShapeDtypeStruct
    rows = pl.BlockSpec((ig.shape[0] * per // td, ig.shape[1]), lambda i: (i, 0))
    lead = lambda *shape: pl.BlockSpec((per,) + shape, lambda i: (i,) + (0,) * len(shape))
    flat = lambda cols: pl.BlockSpec((per * PAD, cols), lambda i: (i, 0))
    full = lambda cols: pl.BlockSpec((td, cols), lambda i: (0, 0))
    return pl.pallas_call(
        functools.partial(tail_kernel, plen),
        grid=(td // per,),
        in_specs=[rows, pl.BlockSpec((plen, td, depth), lambda i: (0, 0, 0)), lead(depth, rep), flat(rep), flat(rep), flat(pc)],
        out_specs=[rows, pl.BlockSpec((plen * td, depth), lambda i: (0, 0)), lead(depth, rep), full(rep), lead(rep, pc), full(pc)],
        out_shape=[sds(ig.shape, BF), sds((plen * td, depth), F), sds((td, depth, rep), F), sds((td, rep), F),
                   sds((td, rep, pc), F), sds((td, pc), F)],
        scratch_shapes=[pltpu.VMEM((plen * td, depth), F)],
        compiler_params=pltpu.CompilerParams(vmem_limit_bytes=62 * 2**20),
        name="tail",
    )(ig, emb, inner, gpre, low, gtl)


def local(
    tokens,
    lengths,
    task_ids,
    prefix_embed,
    reparam_inner,
    reparam_inner_bias,
    reparam_outer,
    reparam_outer_bias,
    first_gain,
    first_bias,
    input_weight,
    output_weight,
    second_gain,
    second_bias,
    expand_weight,
    contract_weight,
    output_cotangent,
):
    prefix_len = prefix_embed.shape[1]
    task_count = lax.axis_size("task")
    batch_count = lax.axis_size("batch")
    ids = task_ids.T
    embed = prefix_embed.transpose(1, 0, 2)
    projected, prefix_kv, hidden_chunk, hidden_low = front(
        task_count, batch_count, ids, embed, reparam_inner, reparam_inner_bias, reparam_outer,
        reparam_outer_bias, first_gain, first_bias, tokens, input_weight,
    )
    attended, log_totals = attn_fwd(lengths, projected, prefix_kv, prefix_len)
    output, grad_mid, grad_attended = middle(
        second_gain, second_bias, tokens, attended, output_cotangent, output_weight, expand_weight, contract_weight
    )
    grad_q, grad_k, grad_v, grad_pk, grad_pv = attn_bwd(
        lengths, projected, prefix_kv, attended, grad_attended, log_totals, prefix_len
    )
    input_grad, grad_pre, grad_table = back(
        task_count, batch_count, ids, hidden_chunk, first_gain, grad_pk, grad_pv, reparam_outer, input_weight,
        grad_q, grad_k, grad_v, tokens, grad_mid,
    )
    input_grad, grad_embed, grad_inner, grad_inner_bias, grad_outer, grad_outer_bias = tail(
        input_grad, embed, reparam_inner, grad_pre, hidden_low, grad_table
    )
    grad_embed = grad_embed.reshape(embed.shape).transpose(1, 0, 2)
    return (
        output,
        input_grad,
        grad_embed,
        grad_inner,
        grad_inner_bias,
        grad_outer,
        grad_outer_bias,
    )


def solution(mesh):
    placed = (
        P(("task", "batch"), None),
        P(("task", "batch"), None),
        P(),
        P("task", None, "batch"),
        P("task", "batch", None),
        P("task", None),
        P("task", None, "batch"),
        P("task", "batch"),
        P(),
        P(),
        P(),
        P(),
        P(),
        P(),
        P(),
        P(),
        P(("task", "batch"), None),
    )
    return jax.shard_map(
        local,
        mesh=mesh,
        in_specs=placed,
        out_specs=(
            P(("task", "batch"), None),
            P(("task", "batch"), None),
            P("task", None, "batch"),
            P("task", "batch", None),
            P("task", None),
            P("task", None, "batch"),
            P("task", "batch"),
        ),
        check_vma=False,
    )
```

```python
import functools

import jax
import jax.numpy as jnp
from jax import lax
from jax.experimental import pallas as pl
from jax.experimental.pallas import tpu as pltpu
from jax.sharding import PartitionSpec as P

BF = jnp.bfloat16
F = jnp.float32
PAD = 16
NEG = -1e30
MESH = pl.DeviceIdType.MESH


def dg(a, b, ca, cb):
    return lax.dot_general(a, b, (((ca,), (cb,)), ((), ())), preferred_element_type=F)


def attn_bwd_kernel(slots, plen, len_ref, q_ref, k_ref, v_ref, pk_ref, pv_ref, o_ref, do_ref, lse_ref,
                    dq_ref, dk_ref, dv_ref, dpk_ref, dpv_ref, km, vm, dka, dva):
    rows, pair = q_ref.shape
    blk = rows // slots
    hd = pair // 2
    scale = hd ** -0.5
    single = len_ref[0, 0] > blk
    first = lax.broadcasted_iota(jnp.int32, (1, pair), 1) < hd
    zero = jnp.zeros((), BF)
    split = lambda a: (jnp.where(first, a, zero), jnp.where(first, zero, a))
    stack = lambda a: jnp.concatenate(split(a), axis=0)
    k = k_ref[...]
    km[0], km[1] = split(k)
    vm[0], vm[1] = split(v_ref[...])
    kt = k.T
    tri = lax.broadcasted_iota(jnp.int32, (blk, blk), 0) <= lax.broadcasted_iota(jnp.int32, (blk, blk), 1)
    live = lax.broadcasted_iota(jnp.int32, (PAD, blk), 0) < plen
    pk_parts, pv_parts = [], []
    add = lambda a, b: b if a is None else a + b

    def scores(i, h):
        lo, hi = i * blk, (i + 1) * blk
        q = q_ref[lo:hi, :] * jnp.asarray(scale, BF)
        do = do_ref[lo:hi, :]
        return dg(km[h, 0:hi, :], q, 1, 1), dg(vm[h, 0:hi, :], do, 1, 1)

    def start(i):
        lo, hi = i * blk, (i + 1) * blk
        q = q_ref[lo:hi, :] * jnp.asarray(scale, BF)
        do = do_ref[lo:hi, :]
        kp = stack(jnp.where(single, pk_ref[0:PAD, :], pk_ref[i * PAD:(i + 1) * PAD, :]))
        vp = stack(jnp.where(single, pv_ref[0:PAD, :], pv_ref[i * PAD:(i + 1) * PAD, :]))
        prod = (do.astype(F) * o_ref[lo:hi, :].astype(F)).T
        return dict(q=split(q), do=split(do), kp=kp, sp=dg(kp, q, 1, 1), dpp=dg(vp, do, 1, 1), prod=prod,
                    dqs=[], dsps=[], dk=None, dv=None, pk=None, pv=None)

    def elem(i, h, st, s, dp):
        lo, hi = i * blk, (i + 1) * blk
        lse = lse_ref[0, h:h + 1, lo:hi]
        delta = jnp.sum(st["prod"][h * hd:(h + 1) * hd], axis=0, keepdims=True)
        p_pre = jnp.where(live, jnp.exp(st["sp"][h * PAD:(h + 1) * PAD] - lse), 0.0)
        ds_pre = (p_pre * (st["dpp"][h * PAD:(h + 1) * PAD] - delta)).astype(BF)
        p = jnp.where(tri, jnp.exp(s[lo:] - lse), 0.0)
        ds = (p * (dp[lo:] - delta)).astype(BF)
        p = p.astype(BF)
        if i:
            p_off = jnp.exp(s[:lo] - jnp.where(single, lse, -NEG))
            ds_off = (p_off * (dp[:lo] - delta)).astype(BF)
            p = jnp.concatenate([p_off.astype(BF), p], axis=0)
            ds = jnp.concatenate([ds_off, ds], axis=0)
        return p, ds, p_pre.astype(BF), ds_pre

    def grads(i, h, st, p, ds, p_pre, ds_pre):
        lo, hi = i * blk, (i + 1) * blk
        st["dv"] = add(st["dv"], dg(p, st["do"][h], 1, 0))
        st["dk"] = add(st["dk"], dg(ds, st["q"][h], 1, 0))
        st["pv"] = add(st["pv"], dg(p_pre, st["do"][h], 1, 0))
        st["pk"] = add(st["pk"], dg(ds_pre, st["q"][h], 1, 0))
        st["dqs"].append(dg(kt[h * hd:(h + 1) * hd, 0:hi], ds, 1, 0))
        st["dsps"].append(ds_pre)

    def finish(i, st):
        lo, hi = i * blk, (i + 1) * blk
        dqt = jnp.concatenate(st["dqs"], axis=0) + dg(st["kp"].T, jnp.concatenate(st["dsps"], axis=0), 1, 0)
        dq_ref[lo:hi, :] = (dqt.T * scale).astype(BF)
        dka[lo:hi, :] = st["dk"][lo:]
        dva[lo:hi, :] = st["dv"][lo:]
        if i:
            dka[0:lo, :] += st["dk"][:lo]
            dva[0:lo, :] += st["dv"][:lo]
        pk_parts.append(st["pk"])
        pv_parts.append(st["pv"])

    items = [(i, h) for i in range(slots) for h in range(2)]
    sts = {}
    def sc(n):
        i, h = items[n]
        if i not in sts: sts[i] = start(i)
        return scores(i, h)
    nxt = sc(0)
    for n, (i, h) in enumerate(items):
        cur = nxt
        if n + 1 < len(items):
            nxt = sc(n + 1)
        grads(i, h, sts[i], *elem(i, h, sts[i], *cur))
        if h:
            finish(i, sts[i])
    dk_ref[...] = dka[...].astype(BF)
    dv_ref[...] = dva[...].astype(BF)
    for i in range(slots):
        for ref, parts in ((dpk_ref, pk_parts), (dpv_ref, pv_parts)):
            whole = sum(parts) if i == 0 else jnp.zeros_like(parts[0])
            ref[i * PAD:(i + 1) * PAD, :] = jnp.where(single, whole, parts[i])


def attn_bwd(lengths, qkv, pkv, attended, grad_att, lse, plen):
    rows = qkv.shape[0]
    width = qkv.shape[1] // 3
    slots = lengths.shape[1]
    pairs = width // 128
    col = lambda off: pl.BlockSpec((rows, 128), lambda h: (0, h + off))
    pcol = lambda off: pl.BlockSpec((slots * PAD, 128), lambda h: (0, h + off))
    sds = jax.ShapeDtypeStruct
    return pl.pallas_call(
        functools.partial(attn_bwd_kernel, slots, plen),
        grid=(pairs,),
        in_specs=[pl.BlockSpec(memory_space=pltpu.SMEM), col(0), col(pairs), col(2 * pairs), pcol(0), pcol(pairs),
                  col(0), col(0), pl.BlockSpec((1, 2, rows), lambda h: (h, 0, 0))],
        out_specs=[col(0), col(0), col(0), pcol(0), pcol(0)],
        out_shape=[sds((rows, width), BF)] * 3 + [sds((slots * PAD, width), F)] * 2,
        scratch_shapes=[pltpu.VMEM((2, rows, 128), BF)] * 2 + [pltpu.VMEM((rows, 128), F)] * 2,
        compiler_params=pltpu.CompilerParams(vmem_limit_bytes=62 * 2**20),
        name="attend_back",
    )(lengths, qkv, qkv, qkv, pkv, pkv, attended, grad_att, lse)


def peer_id(flat, nb):
    return {"task": flat // nb, "batch": flat % nb}


def layer_norm_rows(x, gain, bias):
    inv = 1.0 / x.shape[1]
    mean = jnp.sum(x, axis=1, keepdims=True) * inv
    cen = x - mean
    var = jnp.sum(cen * cen, axis=1, keepdims=True) * inv
    return cen * lax.rsqrt(var + 1e-5) * gain + bias


def greet_all(nt, nb):
    me = lax.axis_index("task") * nb + lax.axis_index("batch")
    total = nt * nb
    barrier = pltpu.get_barrier_semaphore()

    def greet(d, c):
        pl.semaphore_signal(barrier, inc=1, device_id=peer_id(lax.rem(me + d, total), nb), device_id_type=MESH)
        return c

    lax.fori_loop(1, total, greet, 0)
    return barrier, me, total


def spread_heads(block, heads, hd):
    wide = jnp.concatenate([block] * heads, axis=0)
    row = lax.broadcasted_iota(jnp.int32, wide.shape, 0) // PAD
    lane = lax.broadcasted_iota(jnp.int32, wide.shape, 1) // hd
    return jnp.where(row == lane, wide, jnp.zeros((), wide.dtype))


def prefix_rows(ref, single, i, lo, hi):
    own = ref[pl.ds(pl.multiple_of(i * PAD, PAD), PAD), lo:hi]
    return jnp.where(single, ref[0:PAD, lo:hi], own)


def front_kernel(nt, nb, td, plen, chunk,
                 ids_ref, len_ref, emb_ref, ib_ref, ob_ref, g_ref, b_ref, tok_hbm, w_hbm, inner_hbm, outer_hbm,
                 qkv_hbm, att_hbm, pkv_ref, hid_ref, low_ref, lse_ref,
                 tok, w, inner, outer, normed, qkv, ot_s, km, top_s, sum_s, pre, emf, ibf, tbl, rs_out, rs_in, ag_out, ag_in, aa_out, aa_in,
                 ld_sem, st_sem, at_sem, rs_ss, rs_rs, ag_ss, ag_rs, aa_ss, aa_rs):
    rows, width = tok.shape
    slots = ids_ref.shape[0]
    rc = td * PAD // nb
    pc = outer.shape[2]
    mt = lax.axis_index("task")
    mb = lax.axis_index("batch")
    loads = [pltpu.make_async_copy(s, d, ld_sem.at[i])
             for i, (s, d) in enumerate(((inner_hbm, inner), (tok_hbm, tok), (w_hbm, w), (outer_hbm, outer)))]
    for c in loads:
        c.start()
    barrier, me, total = greet_all(nt, nb)
    pre[...] = jnp.zeros_like(pre)
    emf[...] = emb_ref[...].astype(F).reshape(emf.shape)
    loads[0].wait()
    for t in range(td):
        pre[t * PAD:t * PAD + plen, :] = dg(emf[pl.ds(t, plen, stride=td), :].astype(BF), inner[t], 1, 0)
    for c in range(nb):
        rs_out[c, 0:rc, :] = pre[c * rc:(c + 1) * rc, :].astype(BF)
    ib = ib_ref[...].astype(F)
    for t in range(td):
        ibf[t * PAD:(t + 1) * PAD, :] = jnp.broadcast_to(ib[t:t + 1], (PAD, ib.shape[1]))
    pl.semaphore_wait(barrier, total - 1)

    def batch_copy(d, src, dst, ss, rs):
        to = lax.rem(mb + d, nb)
        return pltpu.make_async_remote_copy(src_ref=src(to), dst_ref=dst, send_sem=ss.at[d], recv_sem=rs.at[d],
                                            device_id={"task": mt, "batch": to}, device_id_type=MESH)

    rs_copy = [batch_copy(d, lambda to: rs_out.at[to], rs_in.at[d], rs_ss, rs_rs) for d in range(1, nb)]
    for c in rs_copy:
        c.start()
    loads[1].wait()
    gain = g_ref[...].astype(F).reshape(1, -1)
    bias = b_ref[...].astype(F).reshape(1, -1)

    def norm_step(i, c):
        r = pl.ds(pl.multiple_of(i * 128, 128), 128)
        normed[r, :] = layer_norm_rows(tok[r, :].astype(F), gain, bias).astype(BF)
        return c

    lax.fori_loop(0, rows // 128, norm_step, 0)
    loads[2].wait()

    def store(j):
        cols = pl.ds(pl.multiple_of(j * chunk, chunk), chunk)
        return pltpu.make_async_copy(qkv.at[:, cols], qkv_hbm.at[:, cols], st_sem.at[j])

    def mm_step(j, c):
        cols = pl.ds(pl.multiple_of(j * chunk, chunk), chunk)
        qkv[:, cols] = dg(normed[...], w[:, cols], 1, 0).astype(BF)
        store(j).start()
        return c

    steps = w.shape[1] // chunk
    lax.fori_loop(0, steps - 1, mm_step, 0)
    mine = pl.ds(pl.multiple_of(mb * rc, rc), rc)
    own = pre[mine, :] + ibf[mine, :]
    for c in rs_copy:
        c.wait_recv()
    for d in range(1, nb):
        own = own + rs_in[d, 0:rc, :].astype(F)
    hid = jnp.tanh(own)
    hid_ref[...] = hid
    ag_out[0:rc, :] = hid.astype(BF)
    ag_copy = [batch_copy(d, lambda to: ag_out, ag_in.at[d], ag_ss, ag_rs) for d in range(1, nb)]
    for c in ag_copy:
        c.start()
    lax.fori_loop(steps - 1, steps, mm_step, 0)

    def put_low(frm, block):
        low_ref[pl.ds(pl.multiple_of(frm * rc, rc), rc), :] = block

    def aa_copy(d, to, at):
        return pltpu.make_async_remote_copy(src_ref=aa_out.at[to], dst_ref=aa_in.at[at], send_sem=aa_ss.at[d],
                                            recv_sem=aa_rs.at[at], device_id=peer_id(to, nb), device_id_type=MESH)

    def pick(e):
        idx = jnp.int32(0)
        for s in range(slots):
            tid = ids_ref[s, e]
            idx = jnp.where(tid // td == mt, lax.rem(tid, td), idx)
        return tbl[idx]

    def send_table():
        put_low(mb, ag_out[0:rc, :])
        for c in ag_copy:
            c.wait_recv()
        for d in range(1, nb):
            put_low(lax.rem(mb + nb - d, nb), ag_in[d, 0:rc, :])
        loads[3].wait()
        ob = ob_ref[...].astype(F)
        for t in range(td):
            tbl[t] = (dg(low_ref[t * PAD:(t + 1) * PAD, :], outer[t], 1, 0) + ob[t:t + 1]).astype(BF)

        def aa_step(d, c):
            to = lax.rem(me + d, total)
            aa_out[to] = pick(to)
            aa_copy(d, to, me).start()
            return c

        lax.fori_loop(1, total, aa_step, 0)
        aa_in[me] = pick(me)

    blk = rows // slots
    hd = 64
    pair = 2 * hd
    pairs = width // pair
    scale = hd ** -0.5
    single = len_ref[0, 0] > blk
    first = lax.broadcasted_iota(jnp.int32, (1, pair), 1) < hd
    zero = jnp.zeros((), BF)
    tri = lax.broadcasted_iota(jnp.int32, (blk, blk), 0) <= lax.broadcasted_iota(jnp.int32, (blk, blk), 1)

    def attend(h, c):
        pl.when(h == 1)(send_table)
        part = lambda third: qkv[:, pl.ds(pl.multiple_of(third * width + h * pair, pair), pair)]
        q_all = part(0) * jnp.asarray(scale, BF)
        k = part(1)
        km[0] = jnp.where(first, k, zero)
        km[1] = jnp.where(first, zero, k)
        vt = part(2).T

        def scores(i):
            q = q_all[i * blk:(i + 1) * blk]
            return [dg(km[j, 0:(i + 1) * blk, :], q, 1, 1) for j in range(2)]

        nxt = scores(0)
        for i in range(slots):
            lo, hi = i * blk, (i + 1) * blk
            cur = nxt
            if i + 1 < slots:
                nxt = scores(i + 1)
            for j, s in enumerate(cur):
                s_dia = jnp.where(tri, s[lo:], NEG)
                top = jnp.max(s_dia, axis=0, keepdims=True)
                if i:
                    top = jnp.maximum(top, jnp.where(single, jnp.max(s[:lo], axis=0, keepdims=True), NEG))
                p = jnp.exp(s_dia - top)
                tot = jnp.sum(p, axis=0, keepdims=True)
                p = p.astype(BF)
                if i:
                    p_off = jnp.exp(s[:lo] - jnp.where(single, top, -NEG))
                    tot = tot + jnp.sum(p_off, axis=0, keepdims=True)
                    p = jnp.concatenate([p_off.astype(BF), p], axis=0)
                ot_s[pl.ds(pl.multiple_of(h * pair + j * hd, hd), hd), lo:hi] = dg(vt[j * hd:(j + 1) * hd, 0:hi], p, 1, 0)
                top_s[h, j:j + 1, lo:hi] = top
                sum_s[h, j:j + 1, lo:hi] = tot
        return c

    lax.fori_loop(0, pairs, attend, 0)

    def aa_wait(d, c):
        frm = lax.rem(me + d, total)
        aa_copy(d, frm, frm).wait()
        return c

    lax.fori_loop(1, total, aa_wait, 0)
    for s in range(slots):
        owner = ids_ref[s, me] // td
        for b in range(nb):
            pkv_ref[s * PAD:(s + 1) * PAD, b * pc:(b + 1) * pc] = aa_in[owner * nb + b]
    heads = 2 * pairs

    def rows_of(i):
        return pl.ds(pl.multiple_of(i * blk, blk), blk)

    def att_store(i):
        return pltpu.make_async_copy(normed.at[rows_of(i), :], att_hbm.at[rows_of(i), :], at_sem.at[i])

    def merge(i, c):
        cols = rows_of(i)
        spread = lambda x: spread_heads(x, heads, hd)
        q = qkv[cols, 0:width] * jnp.asarray(scale, BF)
        sp = dg(spread(prefix_rows(pkv_ref, single, i, 0, width)), q, 1, 1)
        live = lax.broadcasted_iota(jnp.int32, (PAD, blk), 0) < plen
        ps, alphas, invs = [], [], []
        for hh in range(heads):
            s = jnp.where(live, sp[hh * PAD:(hh + 1) * PAD], NEG)
            told = top_s[hh // 2, hh % 2:hh % 2 + 1, cols]
            top = jnp.maximum(told, jnp.max(s, axis=0, keepdims=True))
            p = jnp.exp(s - top)
            alpha = jnp.exp(told - top)
            tot = alpha * sum_s[hh // 2, hh % 2:hh % 2 + 1, cols] + jnp.sum(p, axis=0, keepdims=True)
            lse_ref[hh // 2, hh % 2:hh % 2 + 1, cols] = top + jnp.log(tot)
            inv = 1.0 / tot
            ps.append(p.astype(BF))
            alphas.append(alpha * inv)
            invs.append(inv)
        vt = spread(prefix_rows(pkv_ref, single, i, width, 2 * width)).T
        pre = dg(vt, jnp.concatenate(ps, axis=0), 1, 0)
        outs = [ot_s[hh * hd:(hh + 1) * hd, cols] * alphas[hh] + pre[hh * hd:(hh + 1) * hd] * invs[hh]
                for hh in range(heads)]
        normed[cols, :] = jnp.concatenate(outs, axis=0).T.astype(BF)
        att_store(i).start()
        return c

    lax.fori_loop(0, slots, merge, 0)
    for c in rs_copy + ag_copy:
        c.wait_send()
    for j in range(steps):
        store(j).wait()
    for i in range(slots):
        att_store(i).wait()


def front(nt, nb, task_ids, lengths, prefix_embed, inner, inner_bias, outer, outer_bias, gain, bias, tokens, weight):
    plen, td, depth = prefix_embed.shape
    rep = inner.shape[2]
    pc = outer.shape[2]
    rows, width = tokens.shape
    slots = task_ids.shape[0]
    total = nt * nb
    rc = td * PAD // nb
    rb = max(rc, PAD)
    chunk = 1024
    steps = weight.shape[1] // chunk
    sds = jax.ShapeDtypeStruct
    vm = pl.BlockSpec(memory_space=pltpu.VMEM)
    hb = pl.BlockSpec(memory_space=pl.ANY)
    dma = pltpu.SemaphoreType.DMA
    return pl.pallas_call(
        functools.partial(front_kernel, nt, nb, td, plen, chunk),
        in_specs=[pl.BlockSpec(memory_space=pltpu.SMEM)] * 2 + [vm] * 5 + [hb] * 4,
        out_specs=[hb, hb, vm, vm, vm, vm],
        out_shape=[sds((rows, weight.shape[1]), BF), sds((rows, width), BF), sds((slots * PAD, nb * pc), BF), sds((rc, rep), F),
                   sds((td * PAD, rep), BF), sds((width // 128, 2, rows), F)],
        scratch_shapes=[
            pltpu.VMEM((rows, width), BF), pltpu.VMEM(weight.shape, BF), pltpu.VMEM(inner.shape, BF),
            pltpu.VMEM(outer.shape, BF), pltpu.VMEM((rows, width), BF), pltpu.VMEM((rows, weight.shape[1]), BF),
            pltpu.VMEM((width, rows), F), pltpu.VMEM((2, rows, 128), BF),
            pltpu.VMEM((width // 128, 2, rows), F), pltpu.VMEM((width // 128, 2, rows), F),
            pltpu.VMEM((td * PAD, rep), F), pltpu.VMEM((plen * td, depth), F), pltpu.VMEM((td * PAD, rep), F), pltpu.VMEM((td, PAD, pc), BF),
            pltpu.VMEM((nb, rb, rep), BF), pltpu.VMEM((nb, rb, rep), BF),
            pltpu.VMEM((rb, rep), BF), pltpu.VMEM((nb, rb, rep), BF),
            pltpu.VMEM((total, PAD, pc), BF), pltpu.VMEM((total, PAD, pc), BF),
            dma((4,)), dma((steps,)), dma((slots,)), dma((nb,)), dma((nb,)), dma((nb,)), dma((nb,)), dma((total,)), dma((total,)),
        ],
        compiler_params=pltpu.CompilerParams(vmem_limit_bytes=62 * 2**20, collective_id=0, has_side_effects=True),
        name="front_attend",
    )(task_ids, lengths, prefix_embed, inner_bias, outer_bias, gain, bias,
      tokens, weight, inner, outer)


def middle_kernel(blk, fch, g_ref, b_ref, tok_hbm, att_hbm, ct_hbm, wo_hbm, we_hbm, wc_hbm,
                  out_hbm, gm_hbm, ga_hbm,
                  tok, att, ct, wo, we, wc, mid, n2, mean_s, rstd_s, ld_sem, st_sem):
    rows, width = tok.shape
    ff = we.shape[1]
    names = ((wo_hbm, wo), (att_hbm, att), (tok_hbm, tok), (we_hbm, we), (ct_hbm, ct), (wc_hbm, wc))
    loads = [pltpu.make_async_copy(s, d, ld_sem.at[i]) for i, (s, d) in enumerate(names)]
    for c in loads:
        c.start()
    gain = g_ref[...].astype(F).reshape(1, -1)
    bias = b_ref[...].astype(F).reshape(1, -1)
    inv = 1.0 / width
    steps = rows // blk
    for c in loads[:3]:
        c.wait()

    def first(i, c):
        r = pl.ds(pl.multiple_of(i * blk, blk), blk)
        x = tok[r, :].astype(F) + dg(att[r, :], wo[...], 1, 0)
        mid[r, :] = x
        mean = jnp.sum(x, axis=1, keepdims=True) * inv
        cen = x - mean
        rstd = lax.rsqrt(jnp.sum(cen * cen, axis=1, keepdims=True) * inv + 1e-5)
        mean_s[r, :] = mean
        rstd_s[r, :] = rstd
        n2[r, :] = (cen * rstd * gain + bias).astype(BF)
        return c

    lax.fori_loop(0, steps, first, 0)
    for c in loads[3:]:
        c.wait()

    def stores(i):
        r = pl.ds(pl.multiple_of(i * blk, blk), blk)
        return [pltpu.make_async_copy(s.at[r, :], d.at[r, :], st_sem.at[k, i])
                for k, (s, d) in enumerate(((tok, out_hbm), (mid, gm_hbm), (att, ga_hbm)))]

    def second(i, c):
        r = pl.ds(pl.multiple_of(i * blk, blk), blk)
        x2 = n2[r, :]
        g = ct[r, :]
        pair = lambda k: (dg(x2, we[:, k:k + fch], 1, 0), dg(g, wc[k:k + fch, :], 1, 1))
        y = gn = None
        nxt = pair(0)
        for k in range(0, ff, fch):
            v, up = nxt
            if k + fch < ff:
                nxt = pair(k + fch)
            vv = v * v
            t = jnp.tanh(v * (0.7978845608028654 + (0.7978845608028654 * 0.044715) * vv))
            half = 0.5 + 0.5 * t
            act = (v * half).astype(BF)
            slope = half + v * (0.5 - 0.5 * t * t) * (0.7978845608028654 + (3 * 0.7978845608028654 * 0.044715) * vv)
            gh = (up * slope).astype(BF)
            yk = dg(act, wc[k:k + fch, :], 1, 0)
            gk = dg(gh, we[:, k:k + fch], 1, 1)
            y = yk if y is None else y + yk
            gn = gk if gn is None else gn + gk
        x = mid[r, :]
        tok[r, :] = (x + y).astype(BF)
        rstd = rstd_s[r, :]
        xhat = (x - mean_s[r, :]) * rstd
        ug = gn * gain
        m1 = jnp.sum(ug, axis=1, keepdims=True) * inv
        m2 = jnp.sum(ug * xhat, axis=1, keepdims=True) * inv
        gmid = g.astype(F) + rstd * (ug - m1 - xhat * m2)
        mid[r, :] = gmid
        att[r, :] = dg(gmid.astype(BF), wo[...], 1, 1).astype(BF)
        for cp in stores(i):
            cp.start()
        return c

    lax.fori_loop(0, steps, second, 0)
    for i in range(steps):
        for cp in stores(i):
            cp.wait()


def middle(gain, bias, tokens, attended, ct, wo, we, wc, blk=256, fch=512):
    rows, width = tokens.shape
    ff = we.shape[1]
    sds = jax.ShapeDtypeStruct
    vm = pl.BlockSpec(memory_space=pltpu.VMEM)
    hb = pl.BlockSpec(memory_space=pl.ANY)
    dma = pltpu.SemaphoreType.DMA
    full = lambda t: pltpu.VMEM((rows, width), t)
    return pl.pallas_call(
        functools.partial(middle_kernel, blk, fch),
        in_specs=[vm, vm] + [hb] * 6,
        out_specs=[hb] * 3,
        out_shape=[sds((rows, width), BF), sds((rows, width), F), sds((rows, width), BF)],
        scratch_shapes=[full(BF), full(BF), full(BF), pltpu.VMEM(wo.shape, BF), pltpu.VMEM(we.shape, BF),
                        pltpu.VMEM(wc.shape, BF), full(F), full(BF), pltpu.VMEM((rows, 1), F), pltpu.VMEM((rows, 1), F),
                        dma((6,)), dma((3, rows // blk))],
        compiler_params=pltpu.CompilerParams(vmem_limit_bytes=62 * 2**20),
        name="middle",
    )(gain, bias, tokens, attended, ct, wo, we, wc)


def back_kernel(nt, nb, td, blk,
                ids_ref, hid_ref, g_ref, dpk_ref, dpv_ref, outer_hbm, w_hbm, dq_hbm, dk_hbm, dv_hbm, tok_hbm, gm_hbm,
                ig_hbm, gpre_ref, gtl_ref,
                outer, w, dq, dk, dv, tok, gm, ig, sel, rs_out, rs_in, ag_out, ag_in, aa_out, aa_in, part,
                ld_sem, st_sem, rs_ss, rs_rs, ag_ss, ag_rs, aa_ss, aa_rs):
    rows, width = tok.shape
    slots = ids_ref.shape[0]
    rc = td * PAD // nb
    pc = outer.shape[2]
    mt = lax.axis_index("task")
    mb = lax.axis_index("batch")
    names = ((w_hbm, w), (dq_hbm, dq), (dk_hbm, dk), (dv_hbm, dv), (tok_hbm, tok), (gm_hbm, gm), (outer_hbm, outer))
    loads = [pltpu.make_async_copy(s, d, ld_sem.at[i]) for i, (s, d) in enumerate(names)]
    for c in loads:
        c.start()
    barrier, me, total = greet_all(nt, nb)
    for o in range(nt):
        at = jnp.int32(0)
        for s in range(slots):
            at = jnp.where(ids_ref[s, me] // td == o, s, at)
        for half, ref in enumerate((dpk_ref, dpv_ref)):
            block = ref[at].astype(BF)
            for b in range(nb // 2):
                aa_out[o * nb + half * (nb // 2) + b] = block[:, b * pc:(b + 1) * pc]
    pl.semaphore_wait(barrier, total - 1)

    def aa_copy(d, to, at):
        return pltpu.make_async_remote_copy(src_ref=aa_out.at[to], dst_ref=aa_in.at[at], send_sem=aa_ss.at[d],
                                            recv_sem=aa_rs.at[at], device_id=peer_id(to, nb), device_id_type=MESH)

    def aa_step(d, c):
        aa_copy(d, lax.rem(me + d, total), me).start()
        return c

    lax.fori_loop(1, total, aa_step, 0)
    aa_in[me] = aa_out[me]
    lane = lax.broadcasted_iota(jnp.int32, (1, total * PAD), 1)
    task_of = jnp.zeros((1, total * PAD), jnp.int32)
    for e in range(total):
        idx = jnp.int32(0)
        for s in range(slots):
            tid = ids_ref[s, e]
            idx = jnp.where(tid // td == mt, lax.rem(tid, td), idx)
        task_of = jnp.where(lane // PAD == e, idx, task_of)
    want = task_of * PAD + lax.rem(lane, PAD)
    row = lax.broadcasted_iota(jnp.int32, (td * PAD, total * PAD), 0)
    sel[...] = jnp.where(row == want, 1.0, 0.0).astype(BF)
    gain = g_ref[...].astype(F).reshape(1, -1)
    for c in loads[:6]:
        c.wait()
    inv = 1.0 / width

    def store(i):
        r = pl.ds(pl.multiple_of(i * blk, blk), blk)
        return pltpu.make_async_copy(ig.at[r, :], ig_hbm.at[r, :], st_sem.at[i])

    def mm_step(i, c):
        r = pl.ds(pl.multiple_of(i * blk, blk), blk)
        gn = (dg(dq[r, :], w[:, 0:width], 1, 1) + dg(dk[r, :], w[:, width:2 * width], 1, 1)
              + dg(dv[r, :], w[:, 2 * width:], 1, 1))
        ug = gn * gain
        x = tok[r, :].astype(F)
        cen = x - jnp.sum(x, axis=1, keepdims=True) * inv
        rstd = lax.rsqrt(jnp.sum(cen * cen, axis=1, keepdims=True) * inv + 1e-5)
        xhat = cen * rstd
        m1 = jnp.sum(ug, axis=1, keepdims=True) * inv
        m2 = jnp.sum(ug * xhat, axis=1, keepdims=True) * inv
        ig[r, :] = (gm[r, :] + rstd * (ug - m1 - xhat * m2)).astype(BF)
        store(i).start()
        return c

    steps = rows // blk
    c1, c2 = steps // 4, 3 * steps // 4
    lax.fori_loop(0, c1, mm_step, 0)

    def aa_wait(d, c):
        frm = lax.rem(me + d, total)
        aa_copy(d, frm, frm).wait()
        return c

    lax.fori_loop(1, total, aa_wait, 0)
    gtl_ref[...] = dg(sel[...], aa_in[...].reshape(total * PAD, pc), 1, 0).astype(BF)
    loads[6].wait()
    for t in range(td):
        part[t * PAD:(t + 1) * PAD, :] = dg(gtl_ref[t * PAD:(t + 1) * PAD, :], outer[t], 1, 1)
    for c in range(nb):
        rs_out[c, 0:rc, :] = part[c * rc:(c + 1) * rc, :].astype(BF)

    def batch_copy(d, src, dst, ss, rs):
        to = lax.rem(mb + d, nb)
        return pltpu.make_async_remote_copy(src_ref=src(to), dst_ref=dst, send_sem=ss.at[d], recv_sem=rs.at[d],
                                            device_id={"task": mt, "batch": to}, device_id_type=MESH)

    rs_copy = [batch_copy(d, lambda to: rs_out.at[to], rs_in.at[d], rs_ss, rs_rs) for d in range(1, nb)]
    for c in rs_copy:
        c.start()
    lax.fori_loop(c1, c2, mm_step, 0)
    own = part[pl.ds(pl.multiple_of(mb * rc, rc), rc), :]
    for c in rs_copy:
        c.wait_recv()
    for d in range(1, nb):
        own = own + rs_in[d, 0:rc, :].astype(F)
    hid = hid_ref[...]
    ag_out[0:rc, :] = (own * (1.0 - hid * hid)).astype(BF)
    ag_copy = [batch_copy(d, lambda to: ag_out, ag_in.at[d], ag_ss, ag_rs) for d in range(1, nb)]
    for c in ag_copy:
        c.start()
    lax.fori_loop(c2, steps, mm_step, 0)

    def put(frm, block):
        gpre_ref[pl.ds(pl.multiple_of(frm * rc, rc), rc), :] = block

    put(mb, ag_out[0:rc, :])
    for c in ag_copy:
        c.wait_recv()
    for d in range(1, nb):
        put(lax.rem(mb + nb - d, nb), ag_in[d, 0:rc, :])
    for c in rs_copy + ag_copy:
        c.wait_send()
    for i in range(steps):
        store(i).wait()


def back(nt, nb, task_ids, hid, gain, dpk, dpv, outer, weight, dq, dk, dv, tokens, grad_mid):
    td, rep, pc = outer.shape
    rows, width = tokens.shape
    slots = task_ids.shape[0]
    total = nt * nb
    rc = td * PAD // nb
    rb = max(rc, PAD)
    blk = 256
    sds = jax.ShapeDtypeStruct
    vm = pl.BlockSpec(memory_space=pltpu.VMEM)
    hb = pl.BlockSpec(memory_space=pl.ANY)
    dma = pltpu.SemaphoreType.DMA
    return pl.pallas_call(
        functools.partial(back_kernel, nt, nb, td, blk),
        in_specs=[pl.BlockSpec(memory_space=pltpu.SMEM), vm, vm, vm, vm] + [hb] * 7,
        out_specs=[hb, vm, vm],
        out_shape=[sds((rows, width), BF), sds((td * PAD, rep), BF), sds((td * PAD, pc), BF)],
        scratch_shapes=[
            pltpu.VMEM(outer.shape, BF), pltpu.VMEM(weight.shape, BF)] + [pltpu.VMEM((rows, width), BF)] * 4 + [
            pltpu.VMEM((rows, width), F), pltpu.VMEM((rows, width), BF),
            pltpu.VMEM((td * PAD, total * PAD), BF),
            pltpu.VMEM((nb, rb, rep), BF), pltpu.VMEM((nb, rb, rep), BF),
            pltpu.VMEM((rb, rep), BF), pltpu.VMEM((nb, rb, rep), BF),
            pltpu.VMEM((total, PAD, pc), BF), pltpu.VMEM((total, PAD, pc), BF),
            pltpu.VMEM((td * PAD, rep), F),
            dma((7,)), dma((rows // blk,)), dma((nb,)), dma((nb,)), dma((nb,)), dma((nb,)), dma((total,)), dma((total,)),
        ],
        compiler_params=pltpu.CompilerParams(vmem_limit_bytes=62 * 2**20, collective_id=1, has_side_effects=True),
        name="back",
    )(task_ids, hid, gain, dpk.reshape(slots, PAD, width), dpv.reshape(slots, PAD, width),
      outer, weight, dq, dk, dv, tokens, grad_mid)


def tail_kernel(plen, ig_in, emb_ref, inner_ref, gpre_ref, low_ref, gtl_ref,
                ig_out, ge_ref, gi_ref, gib_ref, go_ref, gob_ref, emf):
    step = pl.program_id(0)
    ig_out[...] = ig_in[...]

    @pl.when(step == 0)
    def _():
        emf[...] = emb_ref[...].astype(F).reshape(emf.shape)

    per = inner_ref.shape[0]
    td = gib_ref.shape[0]
    for k in range(per):
        r = slice(k * PAD, (k + 1) * PAD)
        gp = gpre_ref[r, :]
        gt = gtl_ref[r, :]
        at = pl.ds(step * per + k, 1)
        spread = pl.ds(step * per + k, plen, stride=td)
        gi_ref[k] = dg(emf[spread, :].astype(BF), gp[0:plen], 0, 0)
        go_ref[k] = dg(low_ref[r, :], gt, 0, 0)
        ge_ref[spread, :] = dg(gp, inner_ref[k], 1, 1)[0:plen]
        gib_ref[at, :] = jnp.sum(gp[0:plen].astype(F), axis=0, keepdims=True)
        gob_ref[at, :] = jnp.sum(gt[0:plen].astype(F), axis=0, keepdims=True)


def tail(ig, emb, inner, gpre, low, gtl):
    plen, td, depth = emb.shape
    rep = inner.shape[2]
    pc = gtl.shape[1]
    per = 2
    sds = jax.ShapeDtypeStruct
    rows = pl.BlockSpec((ig.shape[0] * per // td, ig.shape[1]), lambda i: (i, 0))
    lead = lambda *shape: pl.BlockSpec((per,) + shape, lambda i: (i,) + (0,) * len(shape))
    flat = lambda cols: pl.BlockSpec((per * PAD, cols), lambda i: (i, 0))
    full = lambda cols: pl.BlockSpec((td, cols), lambda i: (0, 0))
    return pl.pallas_call(
        functools.partial(tail_kernel, plen),
        grid=(td // per,),
        in_specs=[rows, pl.BlockSpec((plen, td, depth), lambda i: (0, 0, 0)), lead(depth, rep), flat(rep), flat(rep), flat(pc)],
        out_specs=[rows, pl.BlockSpec((plen * td, depth), lambda i: (0, 0)), lead(depth, rep), full(rep), lead(rep, pc), full(pc)],
        out_shape=[sds(ig.shape, BF), sds((plen * td, depth), F), sds((td, depth, rep), F), sds((td, rep), F),
                   sds((td, rep, pc), F), sds((td, pc), F)],
        scratch_shapes=[pltpu.VMEM((plen * td, depth), F)],
        compiler_params=pltpu.CompilerParams(vmem_limit_bytes=62 * 2**20),
        name="tail",
    )(ig, emb, inner, gpre, low, gtl)


def local(
    tokens,
    lengths,
    task_ids,
    prefix_embed,
    reparam_inner,
    reparam_inner_bias,
    reparam_outer,
    reparam_outer_bias,
    first_gain,
    first_bias,
    input_weight,
    output_weight,
    second_gain,
    second_bias,
    expand_weight,
    contract_weight,
    output_cotangent,
):
    prefix_len = prefix_embed.shape[1]
    task_count = lax.axis_size("task")
    batch_count = lax.axis_size("batch")
    ids = task_ids.T
    embed = prefix_embed.transpose(1, 0, 2)
    projected, attended, prefix_kv, hidden_chunk, hidden_low, log_totals = front(
        task_count, batch_count, ids, lengths, embed, reparam_inner, reparam_inner_bias, reparam_outer,
        reparam_outer_bias, first_gain, first_bias, tokens, input_weight,
    )
    output, grad_mid, grad_attended = middle(
        second_gain, second_bias, tokens, attended, output_cotangent, output_weight, expand_weight, contract_weight
    )
    grad_q, grad_k, grad_v, grad_pk, grad_pv = attn_bwd(
        lengths, projected, prefix_kv, attended, grad_attended, log_totals, prefix_len
    )
    input_grad, grad_pre, grad_table = back(
        task_count, batch_count, ids, hidden_chunk, first_gain, grad_pk, grad_pv, reparam_outer, input_weight,
        grad_q, grad_k, grad_v, tokens, grad_mid,
    )
    input_grad, grad_embed, grad_inner, grad_inner_bias, grad_outer, grad_outer_bias = tail(
        input_grad, embed, reparam_inner, grad_pre, hidden_low, grad_table
    )
    grad_embed = grad_embed.reshape(embed.shape).transpose(1, 0, 2)
    return (
        output,
        input_grad,
        grad_embed,
        grad_inner,
        grad_inner_bias,
        grad_outer,
        grad_outer_bias,
    )


def solution(mesh):
    placed = (
        P(("task", "batch"), None),
        P(("task", "batch"), None),
        P(),
        P("task", None, "batch"),
        P("task", "batch", None),
        P("task", None),
        P("task", None, "batch"),
        P("task", "batch"),
        P(),
        P(),
        P(),
        P(),
        P(),
        P(),
        P(),
        P(),
        P(("task", "batch"), None),
    )
    return jax.shard_map(
        local,
        mesh=mesh,
        in_specs=placed,
        out_specs=(
            P(("task", "batch"), None),
            P(("task", "batch"), None),
            P("task", None, "batch"),
            P("task", "batch", None),
            P("task", None),
            P("task", None, "batch"),
            P("task", "batch"),
        ),
        check_vma=False,
    )
```

```python
import functools

import jax
import jax.numpy as jnp
from jax import lax
from jax.experimental import pallas as pl
from jax.experimental.pallas import tpu as pltpu
from jax.sharding import PartitionSpec as P

BF = jnp.bfloat16
F = jnp.float32
PAD = 16
NEG = -1e30
MESH = pl.DeviceIdType.MESH


def dg(a, b, ca, cb):
    return lax.dot_general(a, b, (((ca,), (cb,)), ((), ())), preferred_element_type=F)


def peer_id(flat, nb):
    return {"task": flat // nb, "batch": flat % nb}


def layer_norm_rows(x, gain, bias):
    inv = 1.0 / x.shape[1]
    mean = jnp.sum(x, axis=1, keepdims=True) * inv
    cen = x - mean
    var = jnp.sum(cen * cen, axis=1, keepdims=True) * inv
    return cen * lax.rsqrt(var + 1e-5) * gain + bias


def greet_all(nt, nb):
    me = lax.axis_index("task") * nb + lax.axis_index("batch")
    total = nt * nb
    barrier = pltpu.get_barrier_semaphore()

    def greet(d, c):
        pl.semaphore_signal(barrier, inc=1, device_id=peer_id(lax.rem(me + d, total), nb), device_id_type=MESH)
        return c

    lax.fori_loop(1, total, greet, 0)
    return barrier, me, total


def spread_heads(block, heads, hd):
    wide = jnp.concatenate([block] * heads, axis=0)
    row = lax.broadcasted_iota(jnp.int32, wide.shape, 0) // PAD
    lane = lax.broadcasted_iota(jnp.int32, wide.shape, 1) // hd
    return jnp.where(row == lane, wide, jnp.zeros((), wide.dtype))


def prefix_rows(ref, single, i, lo, hi):
    own = ref[pl.ds(pl.multiple_of(i * PAD, PAD), PAD), lo:hi]
    return jnp.where(single, ref[0:PAD, lo:hi], own)


def front_kernel(nt, nb, td, plen, chunk,
                 ids_ref, len_ref, emb_ref, ib_ref, ob_ref, g_ref, b_ref, tok_hbm, w_hbm, inner_hbm, outer_hbm,
                 qkv_hbm, att_hbm, pkv_ref, hid_ref, low_ref, lse_ref,
                 tok, w, inner, outer, normed, qkv, ot_s, km, top_s, sum_s, pre, emf, ibf, tbl, rs_out, rs_in, ag_out, ag_in, aa_out, aa_in,
                 ld_sem, st_sem, at_sem, rs_ss, rs_rs, ag_ss, ag_rs, aa_ss, aa_rs):
    rows, width = tok.shape
    slots = ids_ref.shape[0]
    rc = td * PAD // nb
    pc = outer.shape[2]
    mt = lax.axis_index("task")
    mb = lax.axis_index("batch")
    loads = [pltpu.make_async_copy(s, d, ld_sem.at[i])
             for i, (s, d) in enumerate(((inner_hbm, inner), (tok_hbm, tok), (w_hbm, w), (outer_hbm, outer)))]
    for c in loads:
        c.start()
    barrier, me, total = greet_all(nt, nb)
    pre[...] = jnp.zeros_like(pre)
    emf[...] = emb_ref[...].astype(F).reshape(emf.shape)
    loads[0].wait()
    for t in range(td):
        pre[t * PAD:t * PAD + plen, :] = dg(emf[pl.ds(t, plen, stride=td), :].astype(BF), inner[t], 1, 0)
    for c in range(nb):
        rs_out[c, 0:rc, :] = pre[c * rc:(c + 1) * rc, :].astype(BF)
    ib = ib_ref[...].astype(F)
    for t in range(td):
        ibf[t * PAD:(t + 1) * PAD, :] = jnp.broadcast_to(ib[t:t + 1], (PAD, ib.shape[1]))
    pl.semaphore_wait(barrier, total - 1)

    def batch_copy(d, src, dst, ss, rs):
        to = lax.rem(mb + d, nb)
        return pltpu.make_async_remote_copy(src_ref=src(to), dst_ref=dst, send_sem=ss.at[d], recv_sem=rs.at[d],
                                            device_id={"task": mt, "batch": to}, device_id_type=MESH)

    rs_copy = [batch_copy(d, lambda to: rs_out.at[to], rs_in.at[d], rs_ss, rs_rs) for d in range(1, nb)]
    for c in rs_copy:
        c.start()
    loads[1].wait()
    gain = g_ref[...].astype(F).reshape(1, -1)
    bias = b_ref[...].astype(F).reshape(1, -1)

    def norm_step(i, c):
        r = pl.ds(pl.multiple_of(i * 128, 128), 128)
        normed[r, :] = layer_norm_rows(tok[r, :].astype(F), gain, bias).astype(BF)
        return c

    lax.fori_loop(0, rows // 128, norm_step, 0)
    loads[2].wait()

    def store(j):
        cols = pl.ds(pl.multiple_of(j * chunk, chunk), chunk)
        return pltpu.make_async_copy(qkv.at[:, cols], qkv_hbm.at[:, cols], st_sem.at[j])

    def mm_step(j, c):
        cols = pl.ds(pl.multiple_of(j * chunk, chunk), chunk)
        qkv[:, cols] = dg(normed[...], w[:, cols], 1, 0).astype(BF)
        store(j).start()
        return c

    steps = w.shape[1] // chunk
    lax.fori_loop(0, steps - 1, mm_step, 0)
    mine = pl.ds(pl.multiple_of(mb * rc, rc), rc)
    own = pre[mine, :] + ibf[mine, :]
    for c in rs_copy:
        c.wait_recv()
    for d in range(1, nb):
        own = own + rs_in[d, 0:rc, :].astype(F)
    hid = jnp.tanh(own)
    hid_ref[...] = hid
    ag_out[0:rc, :] = hid.astype(BF)
    ag_copy = [batch_copy(d, lambda to: ag_out, ag_in.at[d], ag_ss, ag_rs) for d in range(1, nb)]
    for c in ag_copy:
        c.start()
    lax.fori_loop(steps - 1, steps, mm_step, 0)

    def put_low(frm, block):
        low_ref[pl.ds(pl.multiple_of(frm * rc, rc), rc), :] = block

    def aa_copy(d, to, at):
        return pltpu.make_async_remote_copy(src_ref=aa_out.at[to], dst_ref=aa_in.at[at], send_sem=aa_ss.at[d],
                                            recv_sem=aa_rs.at[at], device_id=peer_id(to, nb), device_id_type=MESH)

    def pick(e):
        idx = jnp.int32(0)
        for s in range(slots):
            tid = ids_ref[s, e]
            idx = jnp.where(tid // td == mt, lax.rem(tid, td), idx)
        return tbl[idx]

    def send_table():
        put_low(mb, ag_out[0:rc, :])
        for c in ag_copy:
            c.wait_recv()
        for d in range(1, nb):
            put_low(lax.rem(mb + nb - d, nb), ag_in[d, 0:rc, :])
        loads[3].wait()
        ob = ob_ref[...].astype(F)
        for t in range(td):
            tbl[t] = (dg(low_ref[t * PAD:(t + 1) * PAD, :], outer[t], 1, 0) + ob[t:t + 1]).astype(BF)

        def aa_step(d, c):
            to = lax.rem(me + d, total)
            aa_out[to] = pick(to)
            aa_copy(d, to, me).start()
            return c

        lax.fori_loop(1, total, aa_step, 0)
        aa_in[me] = pick(me)

    blk = rows // slots
    hd = 64
    pair = 2 * hd
    pairs = width // pair
    scale = hd ** -0.5
    single = len_ref[0, 0] > blk
    first = lax.broadcasted_iota(jnp.int32, (1, pair), 1) < hd
    zero = jnp.zeros((), BF)
    tri = lax.broadcasted_iota(jnp.int32, (blk, blk), 0) <= lax.broadcasted_iota(jnp.int32, (blk, blk), 1)

    def attend(h, c):
        pl.when(h == 1)(send_table)
        part = lambda third: qkv[:, pl.ds(pl.multiple_of(third * width + h * pair, pair), pair)]
        q_all = part(0) * jnp.asarray(scale, BF)
        k = part(1)
        km[0] = jnp.where(first, k, zero)
        km[1] = jnp.where(first, zero, k)
        vt = part(2).T

        def scores(i):
            q = q_all[i * blk:(i + 1) * blk]
            return [dg(km[j, 0:(i + 1) * blk, :], q, 1, 1) for j in range(2)]

        nxt = scores(0)
        for i in range(slots):
            lo, hi = i * blk, (i + 1) * blk
            cur = nxt
            if i + 1 < slots:
                nxt = scores(i + 1)
            for j, s in enumerate(cur):
                s_dia = jnp.where(tri, s[lo:], NEG)
                top = jnp.max(s_dia, axis=0, keepdims=True)
                if i:
                    top = jnp.maximum(top, jnp.where(single, jnp.max(s[:lo], axis=0, keepdims=True), NEG))
                p = jnp.exp(s_dia - top)
                tot = jnp.sum(p, axis=0, keepdims=True)
                p = p.astype(BF)
                if i:
                    p_off = jnp.exp(s[:lo] - jnp.where(single, top, -NEG))
                    tot = tot + jnp.sum(p_off, axis=0, keepdims=True)
                    p = jnp.concatenate([p_off.astype(BF), p], axis=0)
                ot_s[pl.ds(pl.multiple_of(h * pair + j * hd, hd), hd), lo:hi] = dg(vt[j * hd:(j + 1) * hd, 0:hi], p, 1, 0)
                top_s[h, j:j + 1, lo:hi] = top
                sum_s[h, j:j + 1, lo:hi] = tot
        return c

    lax.fori_loop(0, pairs, attend, 0)

    def aa_wait(d, c):
        frm = lax.rem(me + d, total)
        aa_copy(d, frm, frm).wait()
        return c

    lax.fori_loop(1, total, aa_wait, 0)
    for s in range(slots):
        owner = ids_ref[s, me] // td
        for b in range(nb):
            pkv_ref[s * PAD:(s + 1) * PAD, b * pc:(b + 1) * pc] = aa_in[owner * nb + b]
    heads = 2 * pairs

    def rows_of(i):
        return pl.ds(pl.multiple_of(i * blk, blk), blk)

    def att_store(i):
        return pltpu.make_async_copy(normed.at[rows_of(i), :], att_hbm.at[rows_of(i), :], at_sem.at[i])

    def merge(i, c):
        cols = rows_of(i)
        spread = lambda x: spread_heads(x, heads, hd)
        q = qkv[cols, 0:width] * jnp.asarray(scale, BF)
        sp = dg(spread(prefix_rows(pkv_ref, single, i, 0, width)), q, 1, 1)
        live = lax.broadcasted_iota(jnp.int32, (PAD, blk), 0) < plen
        ps, alphas, invs = [], [], []
        for hh in range(heads):
            s = jnp.where(live, sp[hh * PAD:(hh + 1) * PAD], NEG)
            told = top_s[hh // 2, hh % 2:hh % 2 + 1, cols]
            top = jnp.maximum(told, jnp.max(s, axis=0, keepdims=True))
            p = jnp.exp(s - top)
            alpha = jnp.exp(told - top)
            tot = alpha * sum_s[hh // 2, hh % 2:hh % 2 + 1, cols] + jnp.sum(p, axis=0, keepdims=True)
            lse_ref[hh // 2, hh % 2:hh % 2 + 1, cols] = top + jnp.log(tot)
            inv = 1.0 / tot
            ps.append(p.astype(BF))
            alphas.append(alpha * inv)
            invs.append(inv)
        vt = spread(prefix_rows(pkv_ref, single, i, width, 2 * width)).T
        pre = dg(vt, jnp.concatenate(ps, axis=0), 1, 0)
        outs = [ot_s[hh * hd:(hh + 1) * hd, cols] * alphas[hh] + pre[hh * hd:(hh + 1) * hd] * invs[hh]
                for hh in range(heads)]
        normed[cols, :] = jnp.concatenate(outs, axis=0).T.astype(BF)
        att_store(i).start()
        return c

    lax.fori_loop(0, slots, merge, 0)
    for c in rs_copy + ag_copy:
        c.wait_send()
    for j in range(steps):
        store(j).wait()
    for i in range(slots):
        att_store(i).wait()


def front(nt, nb, task_ids, lengths, prefix_embed, inner, inner_bias, outer, outer_bias, gain, bias, tokens, weight):
    plen, td, depth = prefix_embed.shape
    rep = inner.shape[2]
    pc = outer.shape[2]
    rows, width = tokens.shape
    slots = task_ids.shape[0]
    total = nt * nb
    rc = td * PAD // nb
    rb = max(rc, PAD)
    chunk = 1024
    steps = weight.shape[1] // chunk
    sds = jax.ShapeDtypeStruct
    vm = pl.BlockSpec(memory_space=pltpu.VMEM)
    hb = pl.BlockSpec(memory_space=pl.ANY)
    dma = pltpu.SemaphoreType.DMA
    return pl.pallas_call(
        functools.partial(front_kernel, nt, nb, td, plen, chunk),
        in_specs=[pl.BlockSpec(memory_space=pltpu.SMEM)] * 2 + [vm] * 5 + [hb] * 4,
        out_specs=[hb, hb, vm, vm, vm, vm],
        out_shape=[sds((rows, weight.shape[1]), BF), sds((rows, width), BF), sds((slots * PAD, nb * pc), BF), sds((rc, rep), F),
                   sds((td * PAD, rep), BF), sds((width // 128, 2, rows), F)],
        scratch_shapes=[
            pltpu.VMEM((rows, width), BF), pltpu.VMEM(weight.shape, BF), pltpu.VMEM(inner.shape, BF),
            pltpu.VMEM(outer.shape, BF), pltpu.VMEM((rows, width), BF), pltpu.VMEM((rows, weight.shape[1]), BF),
            pltpu.VMEM((width, rows), F), pltpu.VMEM((2, rows, 128), BF),
            pltpu.VMEM((width // 128, 2, rows), F), pltpu.VMEM((width // 128, 2, rows), F),
            pltpu.VMEM((td * PAD, rep), F), pltpu.VMEM((plen * td, depth), F), pltpu.VMEM((td * PAD, rep), F), pltpu.VMEM((td, PAD, pc), BF),
            pltpu.VMEM((nb, rb, rep), BF), pltpu.VMEM((nb, rb, rep), BF),
            pltpu.VMEM((rb, rep), BF), pltpu.VMEM((nb, rb, rep), BF),
            pltpu.VMEM((total, PAD, pc), BF), pltpu.VMEM((total, PAD, pc), BF),
            dma((4,)), dma((steps,)), dma((slots,)), dma((nb,)), dma((nb,)), dma((nb,)), dma((nb,)), dma((total,)), dma((total,)),
        ],
        compiler_params=pltpu.CompilerParams(vmem_limit_bytes=62 * 2**20, collective_id=0, has_side_effects=True),
        name="front_attend",
    )(task_ids, lengths, prefix_embed, inner_bias, outer_bias, gain, bias,
      tokens, weight, inner, outer)


def middle_kernel(blk, fch, g_ref, b_ref, tok_hbm, att_hbm, ct_hbm, wo_hbm, we_hbm, wc_hbm,
                  out_hbm, gm_hbm, ga_hbm,
                  tok, att, ct, wo, we, wc, mid, n2, mean_s, rstd_s, ld_sem, st_sem):
    rows, width = tok.shape
    ff = we.shape[1]
    names = ((wo_hbm, wo), (att_hbm, att), (tok_hbm, tok), (we_hbm, we), (ct_hbm, ct), (wc_hbm, wc))
    loads = [pltpu.make_async_copy(s, d, ld_sem.at[i]) for i, (s, d) in enumerate(names)]
    for c in loads:
        c.start()
    gain = g_ref[...].astype(F).reshape(1, -1)
    bias = b_ref[...].astype(F).reshape(1, -1)
    inv = 1.0 / width
    steps = rows // blk
    for c in loads[:3]:
        c.wait()

    def first(i, c):
        r = pl.ds(pl.multiple_of(i * blk, blk), blk)
        x = tok[r, :].astype(F) + dg(att[r, :], wo[...], 1, 0)
        mid[r, :] = x
        mean = jnp.sum(x, axis=1, keepdims=True) * inv
        cen = x - mean
        rstd = lax.rsqrt(jnp.sum(cen * cen, axis=1, keepdims=True) * inv + 1e-5)
        mean_s[r, :] = mean
        rstd_s[r, :] = rstd
        n2[r, :] = (cen * rstd * gain + bias).astype(BF)
        return c

    lax.fori_loop(0, steps, first, 0)
    for c in loads[3:]:
        c.wait()

    def stores(i):
        r = pl.ds(pl.multiple_of(i * blk, blk), blk)
        return [pltpu.make_async_copy(s.at[r, :], d.at[r, :], st_sem.at[k, i])
                for k, (s, d) in enumerate(((tok, out_hbm), (mid, gm_hbm), (att, ga_hbm)))]

    def second(i, c):
        r = pl.ds(pl.multiple_of(i * blk, blk), blk)
        x2 = n2[r, :]
        g = ct[r, :]
        pair = lambda k: (dg(x2, we[:, k:k + fch], 1, 0), dg(g, wc[k:k + fch, :], 1, 1))
        y = gn = None
        nxt = pair(0)
        for k in range(0, ff, fch):
            v, up = nxt
            if k + fch < ff:
                nxt = pair(k + fch)
            vv = v * v
            t = jnp.tanh(v * (0.7978845608028654 + (0.7978845608028654 * 0.044715) * vv))
            half = 0.5 + 0.5 * t
            act = (v * half).astype(BF)
            slope = half + v * (0.5 - 0.5 * t * t) * (0.7978845608028654 + (3 * 0.7978845608028654 * 0.044715) * vv)
            gh = (up * slope).astype(BF)
            yk = dg(act, wc[k:k + fch, :], 1, 0)
            gk = dg(gh, we[:, k:k + fch], 1, 1)
            y = yk if y is None else y + yk
            gn = gk if gn is None else gn + gk
        x = mid[r, :]
        tok[r, :] = (x + y).astype(BF)
        rstd = rstd_s[r, :]
        xhat = (x - mean_s[r, :]) * rstd
        ug = gn * gain
        m1 = jnp.sum(ug, axis=1, keepdims=True) * inv
        m2 = jnp.sum(ug * xhat, axis=1, keepdims=True) * inv
        gmid = g.astype(F) + rstd * (ug - m1 - xhat * m2)
        mid[r, :] = gmid
        att[r, :] = dg(gmid.astype(BF), wo[...], 1, 1).astype(BF)
        for cp in stores(i):
            cp.start()
        return c

    lax.fori_loop(0, steps, second, 0)
    for i in range(steps):
        for cp in stores(i):
            cp.wait()


def middle(gain, bias, tokens, attended, ct, wo, we, wc, blk=256, fch=512):
    rows, width = tokens.shape
    ff = we.shape[1]
    sds = jax.ShapeDtypeStruct
    vm = pl.BlockSpec(memory_space=pltpu.VMEM)
    hb = pl.BlockSpec(memory_space=pl.ANY)
    dma = pltpu.SemaphoreType.DMA
    full = lambda t: pltpu.VMEM((rows, width), t)
    return pl.pallas_call(
        functools.partial(middle_kernel, blk, fch),
        in_specs=[vm, vm] + [hb] * 6,
        out_specs=[hb] * 3,
        out_shape=[sds((rows, width), BF), sds((rows, width), F), sds((rows, width), BF)],
        scratch_shapes=[full(BF), full(BF), full(BF), pltpu.VMEM(wo.shape, BF), pltpu.VMEM(we.shape, BF),
                        pltpu.VMEM(wc.shape, BF), full(F), full(BF), pltpu.VMEM((rows, 1), F), pltpu.VMEM((rows, 1), F),
                        dma((6,)), dma((3, rows // blk))],
        compiler_params=pltpu.CompilerParams(vmem_limit_bytes=62 * 2**20),
        name="middle",
    )(gain, bias, tokens, attended, ct, wo, we, wc)


def back_kernel(nt, nb, td, plen, blk,
                ids_ref, len_ref, hid_ref, g_ref, lse_ref, pkv_ref, outer_hbm, w_hbm, qkv_hbm, att_hbm, do_hbm, tok_hbm,
                gm_hbm,
                ig_hbm, gpre_ref, gtl_ref,
                outer, w, qkv, att, do_s, tok, gm, dqkv, dqp, km, vm, dka, dva, del_s, dpk_s, dpv_s, gbuf,
                sel, rs_out, rs_in, ag_out, ag_in, aa_out, aa_in, part,
                ld_sem, bl_sem, st_sem, rs_ss, rs_rs, ag_ss, ag_rs, aa_ss, aa_rs):
    rows, width = tok.shape
    slots = ids_ref.shape[0]
    rc = td * PAD // nb
    pc = outer.shape[2]
    hd = 64
    pair = 2 * hd
    pairs = width // pair
    heads = 2 * pairs
    scale = hd ** -0.5
    inv = 1.0 / width
    single = len_ref[0, 0] > blk
    mt = lax.axis_index("task")
    mb = lax.axis_index("batch")

    def rows_of(i):
        return pl.ds(pl.multiple_of(i * blk, blk), blk)

    def block_loads(i):
        r = rows_of(i)
        return [pltpu.make_async_copy(s, d, bl_sem.at[k, i]) for k, (s, d) in enumerate((
            (qkv_hbm.at[r, 0:width], qkv.at[r, 0:width]), (do_hbm.at[r, :], do_s.at[r, :]), (att_hbm.at[r, :], att.at[r, :])))]

    rest = slice(width, 3 * width)
    names = ((qkv_hbm.at[:, rest], qkv.at[:, rest]), (outer_hbm, outer), (w_hbm, w), (tok_hbm, tok), (gm_hbm, gm))
    loads = [pltpu.make_async_copy(s, d, ld_sem.at[i]) for i, (s, d) in enumerate(names)]
    for i in range(slots):
        for c in block_loads(i):
            c.start()
    for c in loads:
        c.start()
    barrier, me, total = greet_all(nt, nb)
    live = lax.broadcasted_iota(jnp.int32, (PAD, blk), 0) < plen
    lane_head = lax.broadcasted_iota(jnp.int32, (heads, width), 1) // hd
    picker = jnp.where(lane_head == lax.broadcasted_iota(jnp.int32, (heads, width), 0), 1.0, 0.0).astype(BF)
    own_block = (lax.broadcasted_iota(jnp.int32, (heads * PAD, width), 0) // PAD
                 == lax.broadcasted_iota(jnp.int32, (heads * PAD, width), 1) // hd)

    def prefix_step(i, c):
        cols = rows_of(i)
        for cp in block_loads(i):
            cp.wait()
        q = qkv[cols, 0:width] * jnp.asarray(scale, BF)
        do = do_s[cols, :]
        prod = do.astype(F) * att[cols, :].astype(F)
        high = prod.astype(BF)
        delta = dg(picker, high, 1, 1) + dg(picker, (prod - high.astype(F)).astype(BF), 1, 1)
        kp = spread_heads(prefix_rows(pkv_ref, single, i, 0, width), heads, hd)
        vp = spread_heads(prefix_rows(pkv_ref, single, i, width, 2 * width), heads, hd)
        sp = dg(kp, q, 1, 1)
        dpp = dg(vp, do, 1, 1)
        ps, dss = [], []
        for hh in range(heads):
            one = slice(hh * PAD, (hh + 1) * PAD)
            del_s[hh // 2, hh % 2:hh % 2 + 1, cols] = delta[hh:hh + 1]
            pr = jnp.where(live, jnp.exp(sp[one] - lse_ref[hh // 2, hh % 2:hh % 2 + 1, cols]), 0.0)
            ps.append(pr.astype(BF))
            dss.append((pr * (dpp[one] - delta[hh:hh + 1])).astype(BF))
        ds = jnp.concatenate(dss, axis=0)
        fold = lambda x: jnp.sum(jnp.where(own_block, x, 0.0).reshape(heads, PAD, width), axis=0)
        dpk_s[i] = fold(dg(ds, q, 1, 0))
        dpv_s[i] = fold(dg(jnp.concatenate(ps, axis=0), do, 1, 0))
        dqp[:, cols] = dg(kp.T, ds, 1, 0)
        return c

    lax.fori_loop(0, slots, prefix_step, 0)
    for ref in (dpk_s, dpv_s):
        whole = ref[0]
        for i in range(1, slots):
            whole = whole + ref[i]
        ref[0] = jnp.where(single, whole, ref[0])
        for i in range(1, slots):
            ref[i] = jnp.where(single, 0.0, ref[i])
    for o in range(nt):
        at = jnp.int32(0)
        for s in range(slots):
            at = jnp.where(ids_ref[s, me] // td == o, s, at)
        for half, ref in enumerate((dpk_s, dpv_s)):
            block = ref[at].astype(BF)
            for b in range(nb // 2):
                aa_out[o * nb + half * (nb // 2) + b] = block[:, b * pc:(b + 1) * pc]
    pl.semaphore_wait(barrier, total - 1)

    def aa_copy(d, to, at):
        return pltpu.make_async_remote_copy(src_ref=aa_out.at[to], dst_ref=aa_in.at[at], send_sem=aa_ss.at[d],
                                            recv_sem=aa_rs.at[at], device_id=peer_id(to, nb), device_id_type=MESH)

    def aa_step(d, c):
        aa_copy(d, lax.rem(me + d, total), me).start()
        return c

    lax.fori_loop(1, total, aa_step, 0)
    aa_in[me] = aa_out[me]
    lane = lax.broadcasted_iota(jnp.int32, (1, total * PAD), 1)
    task_of = jnp.zeros((1, total * PAD), jnp.int32)
    for e in range(total):
        idx = jnp.int32(0)
        for s in range(slots):
            tid = ids_ref[s, e]
            idx = jnp.where(tid // td == mt, lax.rem(tid, td), idx)
        task_of = jnp.where(lane // PAD == e, idx, task_of)
    want = task_of * PAD + lax.rem(lane, PAD)
    row = lax.broadcasted_iota(jnp.int32, (td * PAD, total * PAD), 0)
    sel[...] = jnp.where(row == want, 1.0, 0.0).astype(BF)

    def batch_copy(d, src, dst, ss, rs):
        to = lax.rem(mb + d, nb)
        return pltpu.make_async_remote_copy(src_ref=src(to), dst_ref=dst, send_sem=ss.at[d], recv_sem=rs.at[d],
                                            device_id={"task": mt, "batch": to}, device_id_type=MESH)

    rs_copy = [batch_copy(d, lambda to: rs_out.at[to], rs_in.at[d], rs_ss, rs_rs) for d in range(1, nb)]
    ag_copy = [batch_copy(d, lambda to: ag_out, ag_in.at[d], ag_ss, ag_rs) for d in range(1, nb)]

    def sum_table():
        def aa_wait(d, c):
            frm = lax.rem(me + d, total)
            aa_copy(d, frm, frm).wait()
            return c

        lax.fori_loop(1, total, aa_wait, 0)
        gtl_ref[...] = dg(sel[...], aa_in[...].reshape(total * PAD, pc), 1, 0).astype(BF)
        loads[1].wait()
        for t in range(td):
            part[t * PAD:(t + 1) * PAD, :] = dg(gtl_ref[t * PAD:(t + 1) * PAD, :], outer[t], 1, 1)
        for c in range(nb):
            rs_out[c, 0:rc, :] = part[c * rc:(c + 1) * rc, :].astype(BF)
        for c in rs_copy:
            c.start()

    def sum_hidden():
        own = part[pl.ds(pl.multiple_of(mb * rc, rc), rc), :]
        for c in rs_copy:
            c.wait_recv()
        for d in range(1, nb):
            own = own + rs_in[d, 0:rc, :].astype(F)
        hid = hid_ref[...]
        ag_out[0:rc, :] = (own * (1.0 - hid * hid)).astype(BF)
        for c in ag_copy:
            c.start()

    loads[0].wait()
    first = lax.broadcasted_iota(jnp.int32, (1, pair), 1) < hd
    zero = jnp.zeros((), BF)
    split = lambda a: (jnp.where(first, a, zero), jnp.where(first, zero, a))
    tri = lax.broadcasted_iota(jnp.int32, (blk, blk), 0) <= lax.broadcasted_iota(jnp.int32, (blk, blk), 1)
    add = lambda a, b: b if a is None else a + b

    def attend(h, c):
        pl.when(h == 2)(sum_table)
        pl.when(h == 5)(sum_hidden)
        cols_of = lambda third: pl.ds(pl.multiple_of(third * width + h * pair, pair), pair)
        q_all = qkv[:, cols_of(0)] * jnp.asarray(scale, BF)
        do_all = do_s[:, cols_of(0)]
        k = qkv[:, cols_of(1)]
        km[0], km[1] = split(k)
        vm[0], vm[1] = split(qkv[:, cols_of(2)])
        kt = k.T
        qs, dos = split(q_all), split(do_all)

        def scores(i, j):
            lo, hi = i * blk, (i + 1) * blk
            return dg(km[j, 0:hi, :], q_all[lo:hi], 1, 1), dg(vm[j, 0:hi, :], do_all[lo:hi], 1, 1)

        items = [(i, j) for i in range(slots) for j in range(2)]
        nxt = scores(*items[0])
        for n, (i, j) in enumerate(items):
            lo, hi = i * blk, (i + 1) * blk
            s, dp = nxt
            if n + 1 < len(items):
                nxt = scores(*items[n + 1])
            lse = lse_ref[h, j:j + 1, lo:hi]
            delta = del_s[h, j:j + 1, lo:hi]
            p = jnp.where(tri, jnp.exp(s[lo:] - lse), 0.0)
            ds = (p * (dp[lo:] - delta)).astype(BF)
            p = p.astype(BF)
            if i:
                off = jnp.exp(s[:lo] - jnp.where(single, lse, -NEG))
                ds = jnp.concatenate([(off * (dp[:lo] - delta)).astype(BF), ds], axis=0)
                p = jnp.concatenate([off.astype(BF), p], axis=0)
            if j == 0:
                dk = dv = None
                dqs = []
            dv = add(dv, dg(p, dos[j][lo:hi], 1, 0))
            dk = add(dk, dg(ds, qs[j][lo:hi], 1, 0))
            dqs.append(dg(kt[j * hd:(j + 1) * hd, 0:hi], ds, 1, 0))
            if j:
                dqt = jnp.concatenate(dqs, axis=0) + dqp[pl.ds(pl.multiple_of(h * pair, pair), pair), lo:hi]
                dqkv[lo:hi, cols_of(0)] = (dqt.T * scale).astype(BF)
                dka[lo:hi, :] = dk[lo:]
                dva[lo:hi, :] = dv[lo:]
                if i:
                    dka[0:lo, :] += dk[:lo]
                    dva[0:lo, :] += dv[:lo]
        dqkv[:, cols_of(1)] = dka[...].astype(BF)
        dqkv[:, cols_of(2)] = dva[...].astype(BF)
        return c

    lax.fori_loop(0, pairs, attend, 0)
    gain = g_ref[...].astype(F).reshape(1, -1)
    for c in loads[2:]:
        c.wait()

    def store(i):
        return pltpu.make_async_copy(tok.at[rows_of(i), :], ig_hbm.at[rows_of(i), :], st_sem.at[i])

    def product(i):
        return dg(dqkv[rows_of(i), :], w[...], 1, 1)

    def norm_back(i, gn):
        r = rows_of(i)
        ug = gn * gain
        x = tok[r, :].astype(F)
        cen = x - jnp.sum(x, axis=1, keepdims=True) * inv
        rstd = lax.rsqrt(jnp.sum(cen * cen, axis=1, keepdims=True) * inv + 1e-5)
        xhat = cen * rstd
        m1 = jnp.sum(ug, axis=1, keepdims=True) * inv
        m2 = jnp.sum(ug * xhat, axis=1, keepdims=True) * inv
        tok[r, :] = (gm[r, :] + rstd * (ug - m1 - xhat * m2)).astype(BF)
        store(i).start()

    gbuf[0] = product(0)

    def mm_step(i, c):
        gbuf[lax.rem(i, 2)] = product(i)
        norm_back(i - 1, gbuf[lax.rem(i + 1, 2)])
        return c

    lax.fori_loop(1, slots, mm_step, 0)
    norm_back(slots - 1, gbuf[(slots - 1) % 2])

    def put(frm, block):
        gpre_ref[pl.ds(pl.multiple_of(frm * rc, rc), rc), :] = block

    put(mb, ag_out[0:rc, :])
    for c in ag_copy:
        c.wait_recv()
    for d in range(1, nb):
        put(lax.rem(mb + nb - d, nb), ag_in[d, 0:rc, :])
    for c in rs_copy + ag_copy:
        c.wait_send()
    for i in range(slots):
        store(i).wait()


def back(nt, nb, task_ids, lengths, hid, gain, lse, pkv, outer, weight, qkv, attended, grad_att, tokens, grad_mid, plen):
    td, rep, pc = outer.shape
    rows, width = tokens.shape
    slots = task_ids.shape[0]
    total = nt * nb
    rc = td * PAD // nb
    rb = max(rc, PAD)
    blk = rows // slots
    sds = jax.ShapeDtypeStruct
    vm = pl.BlockSpec(memory_space=pltpu.VMEM)
    hb = pl.BlockSpec(memory_space=pl.ANY)
    dma = pltpu.SemaphoreType.DMA
    full = lambda t: pltpu.VMEM((rows, width), t)
    return pl.pallas_call(
        functools.partial(back_kernel, nt, nb, td, plen, blk),
        in_specs=[pl.BlockSpec(memory_space=pltpu.SMEM)] * 2 + [vm] * 4 + [hb] * 7,
        out_specs=[hb, vm, vm],
        out_shape=[sds((rows, width), BF), sds((td * PAD, rep), BF), sds((td * PAD, pc), BF)],
        scratch_shapes=[
            pltpu.VMEM(outer.shape, BF), pltpu.VMEM(weight.shape, BF), pltpu.VMEM(qkv.shape, BF), full(BF), full(BF),
            full(BF), full(F), pltpu.VMEM(qkv.shape, BF), pltpu.VMEM((width, rows), F),
            pltpu.VMEM((2, rows, 128), BF), pltpu.VMEM((2, rows, 128), BF), pltpu.VMEM((rows, 128), F),
            pltpu.VMEM((rows, 128), F), pltpu.VMEM(lse.shape, F), pltpu.VMEM((slots, PAD, width), F),
            pltpu.VMEM((slots, PAD, width), F), pltpu.VMEM((2, blk, width), F),
            pltpu.VMEM((td * PAD, total * PAD), BF),
            pltpu.VMEM((nb, rb, rep), BF), pltpu.VMEM((nb, rb, rep), BF),
            pltpu.VMEM((rb, rep), BF), pltpu.VMEM((nb, rb, rep), BF),
            pltpu.VMEM((total, PAD, pc), BF), pltpu.VMEM((total, PAD, pc), BF),
            pltpu.VMEM((td * PAD, rep), F),
            dma((5,)), dma((3, slots)), dma((slots,)), dma((nb,)), dma((nb,)), dma((nb,)), dma((nb,)), dma((total,)),
            dma((total,)),
        ],
        compiler_params=pltpu.CompilerParams(vmem_limit_bytes=62 * 2**20, collective_id=1, has_side_effects=True),
        name="back_attend",
    )(task_ids, lengths, hid, gain, lse, pkv, outer, weight, qkv, attended, grad_att, tokens, grad_mid)


def tail_kernel(plen, ig_in, emb_ref, inner_ref, gpre_ref, low_ref, gtl_ref,
                ig_out, ge_ref, gi_ref, gib_ref, go_ref, gob_ref, emf):
    step = pl.program_id(0)
    ig_out[...] = ig_in[...]

    @pl.when(step == 0)
    def _():
        emf[...] = emb_ref[...].astype(F).reshape(emf.shape)

    per = inner_ref.shape[0]
    td = gib_ref.shape[0]
    for k in range(per):
        r = slice(k * PAD, (k + 1) * PAD)
        gp = gpre_ref[r, :]
        gt = gtl_ref[r, :]
        at = pl.ds(step * per + k, 1)
        spread = pl.ds(step * per + k, plen, stride=td)
        gi_ref[k] = dg(emf[spread, :].astype(BF), gp[0:plen], 0, 0)
        go_ref[k] = dg(low_ref[r, :], gt, 0, 0)
        ge_ref[spread, :] = dg(gp, inner_ref[k], 1, 1)[0:plen]
        gib_ref[at, :] = jnp.sum(gp[0:plen].astype(F), axis=0, keepdims=True)
        gob_ref[at, :] = jnp.sum(gt[0:plen].astype(F), axis=0, keepdims=True)


def tail(ig, emb, inner, gpre, low, gtl):
    plen, td, depth = emb.shape
    rep = inner.shape[2]
    pc = gtl.shape[1]
    per = 2
    sds = jax.ShapeDtypeStruct
    rows = pl.BlockSpec((ig.shape[0] * per // td, ig.shape[1]), lambda i: (i, 0))
    lead = lambda *shape: pl.BlockSpec((per,) + shape, lambda i: (i,) + (0,) * len(shape))
    flat = lambda cols: pl.BlockSpec((per * PAD, cols), lambda i: (i, 0))
    full = lambda cols: pl.BlockSpec((td, cols), lambda i: (0, 0))
    return pl.pallas_call(
        functools.partial(tail_kernel, plen),
        grid=(td // per,),
        in_specs=[rows, pl.BlockSpec((plen, td, depth), lambda i: (0, 0, 0)), lead(depth, rep), flat(rep), flat(rep), flat(pc)],
        out_specs=[rows, pl.BlockSpec((plen * td, depth), lambda i: (0, 0)), lead(depth, rep), full(rep), lead(rep, pc), full(pc)],
        out_shape=[sds(ig.shape, BF), sds((plen * td, depth), F), sds((td, depth, rep), F), sds((td, rep), F),
                   sds((td, rep, pc), F), sds((td, pc), F)],
        scratch_shapes=[pltpu.VMEM((plen * td, depth), F)],
        compiler_params=pltpu.CompilerParams(vmem_limit_bytes=62 * 2**20),
        name="tail",
    )(ig, emb, inner, gpre, low, gtl)


def local(
    tokens,
    lengths,
    task_ids,
    prefix_embed,
    reparam_inner,
    reparam_inner_bias,
    reparam_outer,
    reparam_outer_bias,
    first_gain,
    first_bias,
    input_weight,
    output_weight,
    second_gain,
    second_bias,
    expand_weight,
    contract_weight,
    output_cotangent,
):
    prefix_len = prefix_embed.shape[1]
    task_count = lax.axis_size("task")
    batch_count = lax.axis_size("batch")
    ids = task_ids.T
    embed = prefix_embed.transpose(1, 0, 2)
    projected, attended, prefix_kv, hidden_chunk, hidden_low, log_totals = front(
        task_count, batch_count, ids, lengths, embed, reparam_inner, reparam_inner_bias, reparam_outer,
        reparam_outer_bias, first_gain, first_bias, tokens, input_weight,
    )
    output, grad_mid, grad_attended = middle(
        second_gain, second_bias, tokens, attended, output_cotangent, output_weight, expand_weight, contract_weight
    )
    input_grad, grad_pre, grad_table = back(
        task_count, batch_count, ids, lengths, hidden_chunk, first_gain, log_totals, prefix_kv, reparam_outer,
        input_weight, projected, attended, grad_attended, tokens, grad_mid, prefix_len,
    )
    input_grad, grad_embed, grad_inner, grad_inner_bias, grad_outer, grad_outer_bias = tail(
        input_grad, embed, reparam_inner, grad_pre, hidden_low, grad_table
    )
    grad_embed = grad_embed.reshape(embed.shape).transpose(1, 0, 2)
    return (
        output,
        input_grad,
        grad_embed,
        grad_inner,
        grad_inner_bias,
        grad_outer,
        grad_outer_bias,
    )


def solution(mesh):
    placed = (
        P(("task", "batch"), None),
        P(("task", "batch"), None),
        P(),
        P("task", None, "batch"),
        P("task", "batch", None),
        P("task", None),
        P("task", None, "batch"),
        P("task", "batch"),
        P(),
        P(),
        P(),
        P(),
        P(),
        P(),
        P(),
        P(),
        P(("task", "batch"), None),
    )
    return jax.shard_map(
        local,
        mesh=mesh,
        in_specs=placed,
        out_specs=(
            P(("task", "batch"), None),
            P(("task", "batch"), None),
            P("task", None, "batch"),
            P("task", "batch", None),
            P("task", None),
            P("task", None, "batch"),
            P("task", "batch"),
        ),
        check_vma=False,
    )
```

```python
import functools

import jax
import jax.numpy as jnp
from jax import lax
from jax.experimental import pallas as pl
from jax.experimental.pallas import tpu as pltpu
from jax.sharding import PartitionSpec as P

BF = jnp.bfloat16
F = jnp.float32
PAD = 16
NEG = -1e30
MESH = pl.DeviceIdType.MESH


def dg(a, b, ca, cb):
    return lax.dot_general(a, b, (((ca,), (cb,)), ((), ())), preferred_element_type=F)


AHEAD = 3


def peer_id(flat, nb):
    return {"task": flat // nb, "batch": flat % nb}


def layer_norm_rows(x, gain, bias):
    inv = 1.0 / x.shape[1]
    mean = jnp.sum(x, axis=1, keepdims=True) * inv
    cen = x - mean
    var = jnp.sum(cen * cen, axis=1, keepdims=True) * inv
    return cen * lax.rsqrt(var + 1e-5) * gain + bias


def greet_all(nt, nb):
    me = lax.axis_index("task") * nb + lax.axis_index("batch")
    total = nt * nb
    barrier = pltpu.get_barrier_semaphore()

    def greet(d, c):
        pl.semaphore_signal(barrier, inc=1, device_id=peer_id(lax.rem(me + d, total), nb), device_id_type=MESH)
        return c

    lax.fori_loop(1, total, greet, 0)
    return barrier, me, total


def spread_heads(block, heads, hd):
    wide = jnp.concatenate([block] * heads, axis=0)
    row = lax.broadcasted_iota(jnp.int32, wide.shape, 0) // PAD
    lane = lax.broadcasted_iota(jnp.int32, wide.shape, 1) // hd
    return jnp.where(row == lane, wide, jnp.zeros((), wide.dtype))


def prefix_rows(ref, single, i, lo, hi):
    own = ref[pl.ds(pl.multiple_of(i * PAD, PAD), PAD), lo:hi]
    return jnp.where(single, ref[0:PAD, lo:hi], own)


def front_kernel(nt, nb, td, plen, chunk,
                 ids_ref, len_ref, emb_ref, ib_ref, ob_ref, g_ref, b_ref, tok_hbm, w_hbm, inner_hbm, outer_hbm,
                 qkv_hbm, att_hbm, pkv_ref, hid_ref, low_ref, lse_ref,
                 tok, w, inner, outer, normed, qkv, ot_s, km, top_s, sum_s, pre, emf, ibf, tbl, rs_out, rs_in, ag_out, ag_in, aa_out, aa_in,
                 ld_sem, st_sem, at_sem, rs_ss, rs_rs, ag_ss, ag_rs, aa_ss, aa_rs):
    rows, width = tok.shape
    slots = ids_ref.shape[0]
    rc = td * PAD // nb
    pc = outer.shape[2]
    mt = lax.axis_index("task")
    mb = lax.axis_index("batch")
    loads = [pltpu.make_async_copy(s, d, ld_sem.at[i])
             for i, (s, d) in enumerate(((inner_hbm, inner), (tok_hbm, tok), (w_hbm, w), (outer_hbm, outer)))]
    for c in loads:
        c.start()
    barrier, me, total = greet_all(nt, nb)
    pre[...] = jnp.zeros_like(pre)
    emf[...] = emb_ref[...].astype(F).reshape(emf.shape)
    loads[0].wait()
    for t in range(td):
        pre[t * PAD:t * PAD + plen, :] = dg(emf[pl.ds(t, plen, stride=td), :].astype(BF), inner[t], 1, 0)
    for c in range(nb):
        rs_out[c, 0:rc, :] = pre[c * rc:(c + 1) * rc, :].astype(BF)
    ib = ib_ref[...].astype(F)
    for t in range(td):
        ibf[t * PAD:(t + 1) * PAD, :] = jnp.broadcast_to(ib[t:t + 1], (PAD, ib.shape[1]))
    pl.semaphore_wait(barrier, total - 1)

    def batch_copy(d, src, dst, ss, rs):
        to = lax.rem(mb + d, nb)
        return pltpu.make_async_remote_copy(src_ref=src(to), dst_ref=dst, send_sem=ss.at[d], recv_sem=rs.at[d],
                                            device_id={"task": mt, "batch": to}, device_id_type=MESH)

    rs_copy = [batch_copy(d, lambda to: rs_out.at[to], rs_in.at[d], rs_ss, rs_rs) for d in range(1, nb)]
    for c in rs_copy:
        c.start()
    loads[1].wait()
    gain = g_ref[...].astype(F).reshape(1, -1)
    bias = b_ref[...].astype(F).reshape(1, -1)

    def norm_step(i, c):
        r = pl.ds(pl.multiple_of(i * 128, 128), 128)
        normed[r, :] = layer_norm_rows(tok[r, :].astype(F), gain, bias).astype(BF)
        return c

    lax.fori_loop(0, rows // 128, norm_step, 0)
    loads[2].wait()

    def store(j):
        cols = pl.ds(pl.multiple_of(j * chunk, chunk), chunk)
        return pltpu.make_async_copy(qkv.at[:, cols], qkv_hbm.at[:, cols], st_sem.at[j])

    def mm_step(j, c):
        cols = pl.ds(pl.multiple_of(j * chunk, chunk), chunk)
        qkv[:, cols] = dg(normed[...], w[:, cols], 1, 0).astype(BF)
        store(j).start()
        return c

    steps = w.shape[1] // chunk
    lax.fori_loop(0, steps - 1, mm_step, 0)
    mine = pl.ds(pl.multiple_of(mb * rc, rc), rc)
    own = pre[mine, :] + ibf[mine, :]
    for c in rs_copy:
        c.wait_recv()
    for d in range(1, nb):
        own = own + rs_in[d, 0:rc, :].astype(F)
    hid = jnp.tanh(own)
    hid_ref[...] = hid
    ag_out[0:rc, :] = hid.astype(BF)
    ag_copy = [batch_copy(d, lambda to: ag_out, ag_in.at[d], ag_ss, ag_rs) for d in range(1, nb)]
    for c in ag_copy:
        c.start()
    lax.fori_loop(steps - 1, steps, mm_step, 0)

    def put_low(frm, block):
        low_ref[pl.ds(pl.multiple_of(frm * rc, rc), rc), :] = block

    def aa_copy(d, to, at):
        return pltpu.make_async_remote_copy(src_ref=aa_out.at[to], dst_ref=aa_in.at[at], send_sem=aa_ss.at[d],
                                            recv_sem=aa_rs.at[at], device_id=peer_id(to, nb), device_id_type=MESH)

    def pick(e):
        idx = jnp.int32(0)
        for s in range(slots):
            tid = ids_ref[s, e]
            idx = jnp.where(tid // td == mt, lax.rem(tid, td), idx)
        return tbl[idx]

    def send_table():
        put_low(mb, ag_out[0:rc, :])
        for c in ag_copy:
            c.wait_recv()
        for d in range(1, nb):
            put_low(lax.rem(mb + nb - d, nb), ag_in[d, 0:rc, :])
        loads[3].wait()
        ob = ob_ref[...].astype(F)
        for t in range(td):
            tbl[t] = (dg(low_ref[t * PAD:(t + 1) * PAD, :], outer[t], 1, 0) + ob[t:t + 1]).astype(BF)

        def aa_step(d, c):
            to = lax.rem(me + d, total)
            aa_out[to] = pick(to)
            aa_copy(d, to, me).start()
            return c

        lax.fori_loop(1, total, aa_step, 0)
        aa_in[me] = pick(me)

    blk = rows // slots
    hd = 64
    pair = 2 * hd
    pairs = width // pair
    scale = hd ** -0.5
    single = len_ref[0, 0] > blk
    first = lax.broadcasted_iota(jnp.int32, (1, pair), 1) < hd
    zero = jnp.zeros((), BF)
    tri = lax.broadcasted_iota(jnp.int32, (blk, blk), 0) <= lax.broadcasted_iota(jnp.int32, (blk, blk), 1)

    def attend(h, c):
        pl.when(h == 2)(send_table)
        part = lambda third: qkv[:, pl.ds(pl.multiple_of(third * width + h * pair, pair), pair)]
        q_all = part(0) * jnp.asarray(scale, BF)
        k = part(1)
        km[0] = jnp.where(first, k, zero)
        km[1] = jnp.where(first, zero, k)
        vt = part(2).T
        ones = jnp.ones((PAD, rows), BF)
        vts = [jnp.concatenate([vt[j * hd:(j + 1) * hd], ones], axis=0) for j in range(2)]
        items = [(i, j) for i in range(slots) for j in range(2)]

        def scores(n):
            i, j = items[n]
            return dg(km[j, 0:(i + 1) * blk, :], q_all[i * blk:(i + 1) * blk], 1, 1)

        def top_of(n, s):
            lo = items[n][0] * blk
            top = jnp.max(jnp.where(tri, s[lo:], NEG), axis=0, keepdims=True)
            if lo:
                top = jnp.maximum(top, jnp.where(single, jnp.max(s[:lo], axis=0, keepdims=True), NEG))
            return top

        ahead = [scores(n) for n in range(AHEAD)]
        nxt_top = top_of(0, ahead[0])
        for n, (i, j) in enumerate(items):
            lo, hi = i * blk, (i + 1) * blk
            s, top = ahead.pop(0), nxt_top
            if n + AHEAD < len(items):
                ahead.append(scores(n + AHEAD))
            if n + 1 < len(items):
                nxt_top = top_of(n + 1, ahead[0])
            p = jnp.exp(jnp.where(tri, s[lo:], NEG) - top).astype(BF)
            if i:
                p = jnp.concatenate([jnp.exp(s[:lo] - jnp.where(single, top, -NEG)).astype(BF), p], axis=0)
            ot = dg(vts[j][:, 0:hi], p, 1, 0)
            ot_s[pl.ds(pl.multiple_of(h * pair + j * hd, hd), hd), lo:hi] = ot[:hd]
            top_s[h, j:j + 1, lo:hi] = top
            sum_s[h, j:j + 1, lo:hi] = ot[hd:hd + 1]
        return c

    lax.fori_loop(0, pairs, attend, 0)

    def aa_wait(d, c):
        frm = lax.rem(me + d, total)
        aa_copy(d, frm, frm).wait()
        return c

    lax.fori_loop(1, total, aa_wait, 0)
    for s in range(slots):
        owner = ids_ref[s, me] // td
        for b in range(nb):
            pkv_ref[s * PAD:(s + 1) * PAD, b * pc:(b + 1) * pc] = aa_in[owner * nb + b]
    heads = 2 * pairs

    def rows_of(i):
        return pl.ds(pl.multiple_of(i * blk, blk), blk)

    def att_store(i):
        return pltpu.make_async_copy(normed.at[rows_of(i), :], att_hbm.at[rows_of(i), :], at_sem.at[i])

    def merge(i, c):
        cols = rows_of(i)
        spread = lambda x: spread_heads(x, heads, hd)
        q = qkv[cols, 0:width] * jnp.asarray(scale, BF)
        sp = dg(spread(prefix_rows(pkv_ref, single, i, 0, width)), q, 1, 1)
        live = lax.broadcasted_iota(jnp.int32, (PAD, blk), 0) < plen
        ps, alphas, invs = [], [], []
        for hh in range(heads):
            s = jnp.where(live, sp[hh * PAD:(hh + 1) * PAD], NEG)
            told = top_s[hh // 2, hh % 2:hh % 2 + 1, cols]
            top = jnp.maximum(told, jnp.max(s, axis=0, keepdims=True))
            p = jnp.exp(s - top)
            alpha = jnp.exp(told - top)
            tot = alpha * sum_s[hh // 2, hh % 2:hh % 2 + 1, cols] + jnp.sum(p, axis=0, keepdims=True)
            lse_ref[hh // 2, hh % 2:hh % 2 + 1, cols] = top + jnp.log(tot)
            inv = 1.0 / tot
            ps.append(p.astype(BF))
            alphas.append(alpha * inv)
            invs.append(inv)
        vt = spread(prefix_rows(pkv_ref, single, i, width, 2 * width)).T
        pre = dg(vt, jnp.concatenate(ps, axis=0), 1, 0)
        outs = [ot_s[hh * hd:(hh + 1) * hd, cols] * alphas[hh] + pre[hh * hd:(hh + 1) * hd] * invs[hh]
                for hh in range(heads)]
        normed[cols, :] = jnp.concatenate(outs, axis=0).T.astype(BF)
        att_store(i).start()
        return c

    lax.fori_loop(0, slots, merge, 0)
    for c in rs_copy + ag_copy:
        c.wait_send()
    for j in range(steps):
        store(j).wait()
    for i in range(slots):
        att_store(i).wait()


def front(nt, nb, task_ids, lengths, prefix_embed, inner, inner_bias, outer, outer_bias, gain, bias, tokens, weight):
    plen, td, depth = prefix_embed.shape
    rep = inner.shape[2]
    pc = outer.shape[2]
    rows, width = tokens.shape
    slots = task_ids.shape[0]
    total = nt * nb
    rc = td * PAD // nb
    rb = max(rc, PAD)
    chunk = 1024
    steps = weight.shape[1] // chunk
    sds = jax.ShapeDtypeStruct
    vm = pl.BlockSpec(memory_space=pltpu.VMEM)
    hb = pl.BlockSpec(memory_space=pl.ANY)
    dma = pltpu.SemaphoreType.DMA
    return pl.pallas_call(
        functools.partial(front_kernel, nt, nb, td, plen, chunk),
        in_specs=[pl.BlockSpec(memory_space=pltpu.SMEM)] * 2 + [vm] * 5 + [hb] * 4,
        out_specs=[hb, hb, vm, vm, vm, vm],
        out_shape=[sds((rows, weight.shape[1]), BF), sds((rows, width), BF), sds((slots * PAD, nb * pc), BF), sds((rc, rep), F),
                   sds((td * PAD, rep), BF), sds((width // 128, 2, rows), F)],
        scratch_shapes=[
            pltpu.VMEM((rows, width), BF), pltpu.VMEM(weight.shape, BF), pltpu.VMEM(inner.shape, BF),
            pltpu.VMEM(outer.shape, BF), pltpu.VMEM((rows, width), BF), pltpu.VMEM((rows, weight.shape[1]), BF),
            pltpu.VMEM((width, rows), F), pltpu.VMEM((2, rows, 128), BF),
            pltpu.VMEM((width // 128, 2, rows), F), pltpu.VMEM((width // 128, 2, rows), F),
            pltpu.VMEM((td * PAD, rep), F), pltpu.VMEM((plen * td, depth), F), pltpu.VMEM((td * PAD, rep), F), pltpu.VMEM((td, PAD, pc), BF),
            pltpu.VMEM((nb, rb, rep), BF), pltpu.VMEM((nb, rb, rep), BF),
            pltpu.VMEM((rb, rep), BF), pltpu.VMEM((nb, rb, rep), BF),
            pltpu.VMEM((total, PAD, pc), BF), pltpu.VMEM((total, PAD, pc), BF),
            dma((4,)), dma((steps,)), dma((slots,)), dma((nb,)), dma((nb,)), dma((nb,)), dma((nb,)), dma((total,)), dma((total,)),
        ],
        compiler_params=pltpu.CompilerParams(vmem_limit_bytes=62 * 2**20, collective_id=0, has_side_effects=True),
        name="front_attend",
    )(task_ids, lengths, prefix_embed, inner_bias, outer_bias, gain, bias,
      tokens, weight, inner, outer)


def middle_kernel(blk, fch, g_ref, b_ref, tok_hbm, att_hbm, ct_hbm, wo_hbm, we_hbm, wc_hbm,
                  out_hbm, gm_hbm, ga_hbm,
                  tok, att, ct, wo, we, wc, mid, n2, mean_s, rstd_s, ld_sem, st_sem):
    rows, width = tok.shape
    ff = we.shape[1]
    names = ((wo_hbm, wo), (att_hbm, att), (tok_hbm, tok), (we_hbm, we), (ct_hbm, ct), (wc_hbm, wc))
    loads = [pltpu.make_async_copy(s, d, ld_sem.at[i]) for i, (s, d) in enumerate(names)]
    for c in loads:
        c.start()
    gain = g_ref[...].astype(F).reshape(1, -1)
    bias = b_ref[...].astype(F).reshape(1, -1)
    inv = 1.0 / width
    steps = rows // blk
    for c in loads[:3]:
        c.wait()

    def first(i, c):
        r = pl.ds(pl.multiple_of(i * blk, blk), blk)
        x = tok[r, :].astype(F) + dg(att[r, :], wo[...], 1, 0)
        mid[r, :] = x
        mean = jnp.sum(x, axis=1, keepdims=True) * inv
        cen = x - mean
        rstd = lax.rsqrt(jnp.sum(cen * cen, axis=1, keepdims=True) * inv + 1e-5)
        mean_s[r, :] = mean
        rstd_s[r, :] = rstd
        n2[r, :] = (cen * rstd * gain + bias).astype(BF)
        return c

    lax.fori_loop(0, steps, first, 0)
    for c in loads[3:]:
        c.wait()

    def stores(i):
        r = pl.ds(pl.multiple_of(i * blk, blk), blk)
        return [pltpu.make_async_copy(s.at[r, :], d.at[r, :], st_sem.at[k, i])
                for k, (s, d) in enumerate(((tok, out_hbm), (mid, gm_hbm), (att, ga_hbm)))]

    def second(i, c):
        r = pl.ds(pl.multiple_of(i * blk, blk), blk)
        x2 = n2[r, :]
        g = ct[r, :]
        pair = lambda k: (dg(x2, we[:, k:k + fch], 1, 0), dg(g, wc[k:k + fch, :], 1, 1))
        y = gn = None
        nxt = pair(0)
        for k in range(0, ff, fch):
            v, up = nxt
            if k + fch < ff:
                nxt = pair(k + fch)
            vv = v * v
            t = jnp.tanh(v * (0.7978845608028654 + (0.7978845608028654 * 0.044715) * vv))
            half = 0.5 + 0.5 * t
            act = (v * half).astype(BF)
            slope = half + v * (0.5 - 0.5 * t * t) * (0.7978845608028654 + (3 * 0.7978845608028654 * 0.044715) * vv)
            gh = (up * slope).astype(BF)
            yk = dg(act, wc[k:k + fch, :], 1, 0)
            gk = dg(gh, we[:, k:k + fch], 1, 1)
            y = yk if y is None else y + yk
            gn = gk if gn is None else gn + gk
        x = mid[r, :]
        tok[r, :] = (x + y).astype(BF)
        rstd = rstd_s[r, :]
        xhat = (x - mean_s[r, :]) * rstd
        ug = gn * gain
        m1 = jnp.sum(ug, axis=1, keepdims=True) * inv
        m2 = jnp.sum(ug * xhat, axis=1, keepdims=True) * inv
        gmid = g.astype(F) + rstd * (ug - m1 - xhat * m2)
        mid[r, :] = gmid
        att[r, :] = dg(gmid.astype(BF), wo[...], 1, 1).astype(BF)
        for cp in stores(i):
            cp.start()
        return c

    lax.fori_loop(0, steps, second, 0)
    for i in range(steps):
        for cp in stores(i):
            cp.wait()


def middle(gain, bias, tokens, attended, ct, wo, we, wc, blk=256, fch=512):
    rows, width = tokens.shape
    ff = we.shape[1]
    sds = jax.ShapeDtypeStruct
    vm = pl.BlockSpec(memory_space=pltpu.VMEM)
    hb = pl.BlockSpec(memory_space=pl.ANY)
    dma = pltpu.SemaphoreType.DMA
    full = lambda t: pltpu.VMEM((rows, width), t)
    return pl.pallas_call(
        functools.partial(middle_kernel, blk, fch),
        in_specs=[vm, vm] + [hb] * 6,
        out_specs=[hb] * 3,
        out_shape=[sds((rows, width), BF), sds((rows, width), F), sds((rows, width), BF)],
        scratch_shapes=[full(BF), full(BF), full(BF), pltpu.VMEM(wo.shape, BF), pltpu.VMEM(we.shape, BF),
                        pltpu.VMEM(wc.shape, BF), full(F), full(BF), pltpu.VMEM((rows, 1), F), pltpu.VMEM((rows, 1), F),
                        dma((6,)), dma((3, rows // blk))],
        compiler_params=pltpu.CompilerParams(vmem_limit_bytes=62 * 2**20),
        name="middle",
    )(gain, bias, tokens, attended, ct, wo, we, wc)


def back_kernel(nt, nb, td, plen, blk,
                ids_ref, len_ref, hid_ref, g_ref, lse_ref, pkv_ref, outer_hbm, w_hbm, qkv_hbm, att_hbm, do_hbm, tok_hbm,
                gm_hbm,
                ig_hbm, gpre_ref, gtl_ref,
                outer, w, qkv, att, do_s, tok, gm, dqkv, dqp, km, vm, dka, dva, del_s, dpk_s, dpv_s, gbuf,
                sel, rs_out, rs_in, ag_out, ag_in, aa_out, aa_in, part,
                ld_sem, bl_sem, st_sem, rs_ss, rs_rs, ag_ss, ag_rs, aa_ss, aa_rs):
    rows, width = tok.shape
    slots = ids_ref.shape[0]
    rc = td * PAD // nb
    pc = outer.shape[2]
    hd = 64
    pair = 2 * hd
    pairs = width // pair
    heads = 2 * pairs
    scale = hd ** -0.5
    inv = 1.0 / width
    single = len_ref[0, 0] > blk
    mt = lax.axis_index("task")
    mb = lax.axis_index("batch")

    def rows_of(i):
        return pl.ds(pl.multiple_of(i * blk, blk), blk)

    def block_loads(i):
        r = rows_of(i)
        return [pltpu.make_async_copy(s, d, bl_sem.at[k, i]) for k, (s, d) in enumerate((
            (qkv_hbm.at[r, 0:width], qkv.at[r, 0:width]), (do_hbm.at[r, :], do_s.at[r, :]), (att_hbm.at[r, :], att.at[r, :])))]

    rest = slice(width, 3 * width)
    names = ((qkv_hbm.at[:, rest], qkv.at[:, rest]), (outer_hbm, outer), (w_hbm, w), (tok_hbm, tok), (gm_hbm, gm))
    loads = [pltpu.make_async_copy(s, d, ld_sem.at[i]) for i, (s, d) in enumerate(names)]
    for i in range(slots):
        for c in block_loads(i):
            c.start()
    for c in loads:
        c.start()
    barrier, me, total = greet_all(nt, nb)
    live = lax.broadcasted_iota(jnp.int32, (PAD, blk), 0) < plen
    lane_head = lax.broadcasted_iota(jnp.int32, (heads, width), 1) // hd
    picker = jnp.where(lane_head == lax.broadcasted_iota(jnp.int32, (heads, width), 0), 1.0, 0.0).astype(BF)
    own_block = (lax.broadcasted_iota(jnp.int32, (heads * PAD, width), 0) // PAD
                 == lax.broadcasted_iota(jnp.int32, (heads * PAD, width), 1) // hd)

    def prefix_step(i, c):
        cols = rows_of(i)
        for cp in block_loads(i):
            cp.wait()
        q = qkv[cols, 0:width] * jnp.asarray(scale, BF)
        do = do_s[cols, :]
        prod = do.astype(F) * att[cols, :].astype(F)
        high = prod.astype(BF)
        delta = dg(picker, high, 1, 1) + dg(picker, (prod - high.astype(F)).astype(BF), 1, 1)
        kp = spread_heads(prefix_rows(pkv_ref, single, i, 0, width), heads, hd)
        vp = spread_heads(prefix_rows(pkv_ref, single, i, width, 2 * width), heads, hd)
        sp = dg(kp, q, 1, 1)
        dpp = dg(vp, do, 1, 1)
        ps, dss = [], []
        for hh in range(heads):
            one = slice(hh * PAD, (hh + 1) * PAD)
            del_s[hh // 2, hh % 2:hh % 2 + 1, cols] = delta[hh:hh + 1]
            pr = jnp.where(live, jnp.exp(sp[one] - lse_ref[hh // 2, hh % 2:hh % 2 + 1, cols]), 0.0)
            ps.append(pr.astype(BF))
            dss.append((pr * (dpp[one] - delta[hh:hh + 1])).astype(BF))
        ds = jnp.concatenate(dss, axis=0)
        fold = lambda x: jnp.sum(jnp.where(own_block, x, 0.0).reshape(heads, PAD, width), axis=0)
        dpk_s[i] = fold(dg(ds, q, 1, 0))
        dpv_s[i] = fold(dg(jnp.concatenate(ps, axis=0), do, 1, 0))
        dqp[:, cols] = dg(kp.T, ds, 1, 0)
        return c

    lax.fori_loop(0, slots, prefix_step, 0)
    for ref in (dpk_s, dpv_s):
        whole = ref[0]
        for i in range(1, slots):
            whole = whole + ref[i]
        ref[0] = jnp.where(single, whole, ref[0])
        for i in range(1, slots):
            ref[i] = jnp.where(single, 0.0, ref[i])
    for o in range(nt):
        at = jnp.int32(0)
        for s in range(slots):
            at = jnp.where(ids_ref[s, me] // td == o, s, at)
        for half, ref in enumerate((dpk_s, dpv_s)):
            block = ref[at].astype(BF)
            for b in range(nb // 2):
                aa_out[o * nb + half * (nb // 2) + b] = block[:, b * pc:(b + 1) * pc]
    pl.semaphore_wait(barrier, total - 1)

    def aa_copy(d, to, at):
        return pltpu.make_async_remote_copy(src_ref=aa_out.at[to], dst_ref=aa_in.at[at], send_sem=aa_ss.at[d],
                                            recv_sem=aa_rs.at[at], device_id=peer_id(to, nb), device_id_type=MESH)

    def aa_step(d, c):
        aa_copy(d, lax.rem(me + d, total), me).start()
        return c

    lax.fori_loop(1, total, aa_step, 0)
    aa_in[me] = aa_out[me]
    lane = lax.broadcasted_iota(jnp.int32, (1, total * PAD), 1)
    task_of = jnp.zeros((1, total * PAD), jnp.int32)
    for e in range(total):
        idx = jnp.int32(0)
        for s in range(slots):
            tid = ids_ref[s, e]
            idx = jnp.where(tid // td == mt, lax.rem(tid, td), idx)
        task_of = jnp.where(lane // PAD == e, idx, task_of)
    want = task_of * PAD + lax.rem(lane, PAD)
    row = lax.broadcasted_iota(jnp.int32, (td * PAD, total * PAD), 0)
    sel[...] = jnp.where(row == want, 1.0, 0.0).astype(BF)

    def batch_copy(d, src, dst, ss, rs):
        to = lax.rem(mb + d, nb)
        return pltpu.make_async_remote_copy(src_ref=src(to), dst_ref=dst, send_sem=ss.at[d], recv_sem=rs.at[d],
                                            device_id={"task": mt, "batch": to}, device_id_type=MESH)

    rs_copy = [batch_copy(d, lambda to: rs_out.at[to], rs_in.at[d], rs_ss, rs_rs) for d in range(1, nb)]
    ag_copy = [batch_copy(d, lambda to: ag_out, ag_in.at[d], ag_ss, ag_rs) for d in range(1, nb)]

    def sum_table():
        def aa_wait(d, c):
            frm = lax.rem(me + d, total)
            aa_copy(d, frm, frm).wait()
            return c

        lax.fori_loop(1, total, aa_wait, 0)
        gtl_ref[...] = dg(sel[...], aa_in[...].reshape(total * PAD, pc), 1, 0).astype(BF)
        loads[1].wait()
        for t in range(td):
            part[t * PAD:(t + 1) * PAD, :] = dg(gtl_ref[t * PAD:(t + 1) * PAD, :], outer[t], 1, 1)
        for c in range(nb):
            rs_out[c, 0:rc, :] = part[c * rc:(c + 1) * rc, :].astype(BF)
        for c in rs_copy:
            c.start()

    def sum_hidden():
        own = part[pl.ds(pl.multiple_of(mb * rc, rc), rc), :]
        for c in rs_copy:
            c.wait_recv()
        for d in range(1, nb):
            own = own + rs_in[d, 0:rc, :].astype(F)
        hid = hid_ref[...]
        ag_out[0:rc, :] = (own * (1.0 - hid * hid)).astype(BF)
        for c in ag_copy:
            c.start()

    loads[0].wait()
    first = lax.broadcasted_iota(jnp.int32, (1, pair), 1) < hd
    zero = jnp.zeros((), BF)
    split = lambda a: (jnp.where(first, a, zero), jnp.where(first, zero, a))
    tri = lax.broadcasted_iota(jnp.int32, (blk, blk), 0) <= lax.broadcasted_iota(jnp.int32, (blk, blk), 1)
    add = lambda a, b: b if a is None else a + b

    def attend(h, c):
        pl.when(h == 2)(sum_table)
        pl.when(h == 5)(sum_hidden)
        cols_of = lambda third: pl.ds(pl.multiple_of(third * width + h * pair, pair), pair)
        q_all = qkv[:, cols_of(0)] * jnp.asarray(scale, BF)
        do_all = do_s[:, cols_of(0)]
        k = qkv[:, cols_of(1)]
        km[0], km[1] = split(k)
        vm[0], vm[1] = split(qkv[:, cols_of(2)])
        kt = k.T
        qs, dos = split(q_all), split(do_all)

        def scores(i, j):
            lo, hi = i * blk, (i + 1) * blk
            return dg(km[j, 0:hi, :], q_all[lo:hi], 1, 1), dg(vm[j, 0:hi, :], do_all[lo:hi], 1, 1)

        items = [(i, j) for i in range(slots) for j in range(2)]
        ahead = [scores(*items[n]) for n in range(2)]
        for n, (i, j) in enumerate(items):
            lo, hi = i * blk, (i + 1) * blk
            s, dp = ahead.pop(0)
            if n + 2 < len(items):
                ahead.append(scores(*items[n + 2]))
            lse = lse_ref[h, j:j + 1, lo:hi]
            delta = del_s[h, j:j + 1, lo:hi]
            p = jnp.where(tri, jnp.exp(s[lo:] - lse), 0.0)
            ds = (p * (dp[lo:] - delta)).astype(BF)
            p = p.astype(BF)
            if i:
                off = jnp.exp(s[:lo] - jnp.where(single, lse, -NEG))
                ds = jnp.concatenate([(off * (dp[:lo] - delta)).astype(BF), ds], axis=0)
                p = jnp.concatenate([off.astype(BF), p], axis=0)
            if j == 0:
                dk = dv = None
                dqs = []
            dv = add(dv, dg(p, dos[j][lo:hi], 1, 0))
            dk = add(dk, dg(ds, qs[j][lo:hi], 1, 0))
            dqs.append(dg(kt[j * hd:(j + 1) * hd, 0:hi], ds, 1, 0))
            if j:
                dqt = jnp.concatenate(dqs, axis=0) + dqp[pl.ds(pl.multiple_of(h * pair, pair), pair), lo:hi]
                dqkv[lo:hi, cols_of(0)] = (dqt.T * scale).astype(BF)
                dka[lo:hi, :] = dk[lo:]
                dva[lo:hi, :] = dv[lo:]
                if i:
                    dka[0:lo, :] += dk[:lo]
                    dva[0:lo, :] += dv[:lo]
        dqkv[:, cols_of(1)] = dka[...].astype(BF)
        dqkv[:, cols_of(2)] = dva[...].astype(BF)
        return c

    lax.fori_loop(0, pairs, attend, 0)
    gain = g_ref[...].astype(F).reshape(1, -1)
    for c in loads[2:]:
        c.wait()

    def store(i):
        return pltpu.make_async_copy(tok.at[rows_of(i), :], ig_hbm.at[rows_of(i), :], st_sem.at[i])

    def product(i):
        return dg(dqkv[rows_of(i), :], w[...], 1, 1)

    def norm_back(i, gn):
        r = rows_of(i)
        ug = gn * gain
        x = tok[r, :].astype(F)
        cen = x - jnp.sum(x, axis=1, keepdims=True) * inv
        rstd = lax.rsqrt(jnp.sum(cen * cen, axis=1, keepdims=True) * inv + 1e-5)
        xhat = cen * rstd
        m1 = jnp.sum(ug, axis=1, keepdims=True) * inv
        m2 = jnp.sum(ug * xhat, axis=1, keepdims=True) * inv
        tok[r, :] = (gm[r, :] + rstd * (ug - m1 - xhat * m2)).astype(BF)
        store(i).start()

    gbuf[0] = product(0)

    def mm_step(i, c):
        gbuf[lax.rem(i, 2)] = product(i)
        norm_back(i - 1, gbuf[lax.rem(i + 1, 2)])
        return c

    lax.fori_loop(1, slots, mm_step, 0)
    norm_back(slots - 1, gbuf[(slots - 1) % 2])

    def put(frm, block):
        gpre_ref[pl.ds(pl.multiple_of(frm * rc, rc), rc), :] = block

    put(mb, ag_out[0:rc, :])
    for c in ag_copy:
        c.wait_recv()
    for d in range(1, nb):
        put(lax.rem(mb + nb - d, nb), ag_in[d, 0:rc, :])
    for c in rs_copy + ag_copy:
        c.wait_send()
    for i in range(slots):
        store(i).wait()


def back(nt, nb, task_ids, lengths, hid, gain, lse, pkv, outer, weight, qkv, attended, grad_att, tokens, grad_mid, plen):
    td, rep, pc = outer.shape
    rows, width = tokens.shape
    slots = task_ids.shape[0]
    total = nt * nb
    rc = td * PAD // nb
    rb = max(rc, PAD)
    blk = rows // slots
    sds = jax.ShapeDtypeStruct
    vm = pl.BlockSpec(memory_space=pltpu.VMEM)
    hb = pl.BlockSpec(memory_space=pl.ANY)
    dma = pltpu.SemaphoreType.DMA
    full = lambda t: pltpu.VMEM((rows, width), t)
    return pl.pallas_call(
        functools.partial(back_kernel, nt, nb, td, plen, blk),
        in_specs=[pl.BlockSpec(memory_space=pltpu.SMEM)] * 2 + [vm] * 4 + [hb] * 7,
        out_specs=[hb, vm, vm],
        out_shape=[sds((rows, width), BF), sds((td * PAD, rep), BF), sds((td * PAD, pc), BF)],
        scratch_shapes=[
            pltpu.VMEM(outer.shape, BF), pltpu.VMEM(weight.shape, BF), pltpu.VMEM(qkv.shape, BF), full(BF), full(BF),
            full(BF), full(F), pltpu.VMEM(qkv.shape, BF), pltpu.VMEM((width, rows), F),
            pltpu.VMEM((2, rows, 128), BF), pltpu.VMEM((2, rows, 128), BF), pltpu.VMEM((rows, 128), F),
            pltpu.VMEM((rows, 128), F), pltpu.VMEM(lse.shape, F), pltpu.VMEM((slots, PAD, width), F),
            pltpu.VMEM((slots, PAD, width), F), pltpu.VMEM((2, blk, width), F),
            pltpu.VMEM((td * PAD, total * PAD), BF),
            pltpu.VMEM((nb, rb, rep), BF), pltpu.VMEM((nb, rb, rep), BF),
            pltpu.VMEM((rb, rep), BF), pltpu.VMEM((nb, rb, rep), BF),
            pltpu.VMEM((total, PAD, pc), BF), pltpu.VMEM((total, PAD, pc), BF),
            pltpu.VMEM((td * PAD, rep), F),
            dma((5,)), dma((3, slots)), dma((slots,)), dma((nb,)), dma((nb,)), dma((nb,)), dma((nb,)), dma((total,)),
            dma((total,)),
        ],
        compiler_params=pltpu.CompilerParams(vmem_limit_bytes=62 * 2**20, collective_id=1, has_side_effects=True),
        name="back_attend",
    )(task_ids, lengths, hid, gain, lse, pkv, outer, weight, qkv, attended, grad_att, tokens, grad_mid)


def tail_kernel(plen, emb_ref, gpre_ref, low_ref, gtl_ref, ig_in, inner_hbm,
                ge_ref, gib_ref, gob_ref, ig_out, gi_hbm, go_hbm,
                ig, inner, gi, go, emf, embp, embt, lowt, ld_sem, ig_sem, gi_sem, go_sem):
    td = gib_ref.shape[0]
    ig_load = pltpu.make_async_copy(ig_in, ig, ld_sem.at[0])
    in_load = pltpu.make_async_copy(inner_hbm, inner, ld_sem.at[1])
    ig_load.start()
    in_load.start()
    emf[...] = emb_ref[...].astype(F).reshape(emf.shape)
    embp[...] = jnp.zeros_like(embp)
    for t in range(td):
        embp[t * PAD:t * PAD + plen, :] = emf[pl.ds(t, plen, stride=td), :]
    embt[...] = embp[...].astype(BF).T
    lowt[...] = low_ref[...].T
    zero = jnp.zeros((), BF)

    def stores(t):
        return [pltpu.make_async_copy(go.at[t], go_hbm.at[t], go_sem.at[t]),
                pltpu.make_async_copy(gi.at[t], gi_hbm.at[t], gi_sem.at[t])]

    def step(t, c):
        only = lambda x: jnp.where(lax.broadcasted_iota(jnp.int32, x.shape, 0) // PAD == t, x, zero)
        go[t] = dg(lowt[...], only(gtl_ref[...]), 1, 0)
        gi[t] = dg(embt[...], only(gpre_ref[...]), 1, 0)
        for cp in stores(t):
            cp.start()
        return c

    lax.fori_loop(0, td // 2, step, 0)
    ig_load.wait()
    ig_store = pltpu.make_async_copy(ig, ig_out, ig_sem)
    ig_store.start()
    lax.fori_loop(td // 2, td, step, 0)
    in_load.wait()
    for t in range(td):
        ge_ref[pl.ds(t, plen, stride=td), :] = dg(gpre_ref[t * PAD:(t + 1) * PAD, :], inner[t], 1, 1)[0:plen]
    shape = (td, td * PAD)
    own = lax.broadcasted_iota(jnp.int32, shape, 0) == lax.broadcasted_iota(jnp.int32, shape, 1) // PAD
    picker = jnp.where(own, 1.0, 0.0).astype(BF)
    gib_ref[...] = dg(picker, gpre_ref[...], 1, 0)
    gob_ref[...] = dg(picker, gtl_ref[...], 1, 0)

    def wait_step(t, c):
        for cp in stores(t):
            cp.wait()
        return c

    lax.fori_loop(0, td, wait_step, 0)
    ig_store.wait()


def tail(ig, emb, inner, gpre, low, gtl):
    plen, td, depth = emb.shape
    rep = inner.shape[2]
    pc = gtl.shape[1]
    sds = jax.ShapeDtypeStruct
    vm = pl.BlockSpec(memory_space=pltpu.VMEM)
    hb = pl.BlockSpec(memory_space=pl.ANY)
    dma = pltpu.SemaphoreType.DMA
    ge, gib, gob, ig, gi, go = pl.pallas_call(
        functools.partial(tail_kernel, plen),
        in_specs=[vm, vm, vm, vm, hb, hb],
        out_specs=[vm, vm, vm, hb, hb, hb],
        out_shape=[sds((plen * td, depth), F), sds((td, rep), F), sds((td, pc), F), sds(ig.shape, BF),
                   sds((td, depth, rep), F), sds((td, rep, pc), F)],
        scratch_shapes=[pltpu.VMEM(ig.shape, BF), pltpu.VMEM(inner.shape, BF), pltpu.VMEM((td, depth, rep), F),
                        pltpu.VMEM((td, rep, pc), F), pltpu.VMEM((plen * td, depth), F), pltpu.VMEM((td * PAD, depth), F),
                        pltpu.VMEM((depth, td * PAD), BF), pltpu.VMEM((rep, td * PAD), BF),
                        dma((2,)), dma, dma((td,)), dma((td,))],
        compiler_params=pltpu.CompilerParams(vmem_limit_bytes=62 * 2**20),
        name="tail",
    )(emb, gpre, low, gtl, ig, inner)
    return ig, ge, gi, gib, go, gob


def local(
    tokens,
    lengths,
    task_ids,
    prefix_embed,
    reparam_inner,
    reparam_inner_bias,
    reparam_outer,
    reparam_outer_bias,
    first_gain,
    first_bias,
    input_weight,
    output_weight,
    second_gain,
    second_bias,
    expand_weight,
    contract_weight,
    output_cotangent,
):
    prefix_len = prefix_embed.shape[1]
    task_count = lax.axis_size("task")
    batch_count = lax.axis_size("batch")
    ids = task_ids.T
    embed = prefix_embed.transpose(1, 0, 2)
    projected, attended, prefix_kv, hidden_chunk, hidden_low, log_totals = front(
        task_count, batch_count, ids, lengths, embed, reparam_inner, reparam_inner_bias, reparam_outer,
        reparam_outer_bias, first_gain, first_bias, tokens, input_weight,
    )
    output, grad_mid, grad_attended = middle(
        second_gain, second_bias, tokens, attended, output_cotangent, output_weight, expand_weight, contract_weight
    )
    input_grad, grad_pre, grad_table = back(
        task_count, batch_count, ids, lengths, hidden_chunk, first_gain, log_totals, prefix_kv, reparam_outer,
        input_weight, projected, attended, grad_attended, tokens, grad_mid, prefix_len,
    )
    input_grad, grad_embed, grad_inner, grad_inner_bias, grad_outer, grad_outer_bias = tail(
        input_grad, embed, reparam_inner, grad_pre, hidden_low, grad_table
    )
    grad_embed = grad_embed.reshape(embed.shape).transpose(1, 0, 2)
    return (
        output,
        input_grad,
        grad_embed,
        grad_inner,
        grad_inner_bias,
        grad_outer,
        grad_outer_bias,
    )


def solution(mesh):
    placed = (
        P(("task", "batch"), None),
        P(("task", "batch"), None),
        P(),
        P("task", None, "batch"),
        P("task", "batch", None),
        P("task", None),
        P("task", None, "batch"),
        P("task", "batch"),
        P(),
        P(),
        P(),
        P(),
        P(),
        P(),
        P(),
        P(),
        P(("task", "batch"), None),
    )
    return jax.shard_map(
        local,
        mesh=mesh,
        in_specs=placed,
        out_specs=(
            P(("task", "batch"), None),
            P(("task", "batch"), None),
            P("task", None, "batch"),
            P("task", "batch", None),
            P("task", None),
            P("task", None, "batch"),
            P("task", "batch"),
        ),
        check_vma=False,
    )
```

```python
import functools

import jax
import jax.numpy as jnp
from jax import lax
from jax.experimental import pallas as pl
from jax.experimental.pallas import tpu as pltpu
from jax.sharding import PartitionSpec as P

BF = jnp.bfloat16
F = jnp.float32
PAD = 16
NEG = -1e30
MESH = pl.DeviceIdType.MESH


def dg(a, b, ca, cb):
    return lax.dot_general(a, b, (((ca,), (cb,)), ((), ())), preferred_element_type=F)


AHEAD = 3
PARTS = 4


def peer_id(flat, nb):
    return {"task": flat // nb, "batch": flat % nb}


def layer_norm_rows(x, gain, bias):
    inv = 1.0 / x.shape[1]
    mean = jnp.sum(x, axis=1, keepdims=True) * inv
    cen = x - mean
    var = jnp.sum(cen * cen, axis=1, keepdims=True) * inv
    return cen * lax.rsqrt(var + 1e-5) * gain + bias


def greet_all(nt, nb):
    me = lax.axis_index("task") * nb + lax.axis_index("batch")
    total = nt * nb
    barrier = pltpu.get_barrier_semaphore()

    def greet(d, c):
        pl.semaphore_signal(barrier, inc=1, device_id=peer_id(lax.rem(me + d, total), nb), device_id_type=MESH)
        return c

    lax.fori_loop(1, total, greet, 0)
    return barrier, me, total


def strip_rows(slots, blk):
    at = [blk * i * (i + 1) for i in range(slots + 1)]
    return at, at[-1]


def strip_parts(total):
    return [slice(n * total // PARTS, (n + 1) * total // PARTS) for n in range(PARTS)]


def spread_heads(block, heads, hd):
    wide = jnp.concatenate([block] * heads, axis=0)
    row = lax.broadcasted_iota(jnp.int32, wide.shape, 0) // PAD
    lane = lax.broadcasted_iota(jnp.int32, wide.shape, 1) // hd
    return jnp.where(row == lane, wide, jnp.zeros((), wide.dtype))


def prefix_rows(ref, single, i, lo, hi):
    own = ref[pl.ds(pl.multiple_of(i * PAD, PAD), PAD), lo:hi]
    return jnp.where(single, ref[0:PAD, lo:hi], own)


def front_kernel(nt, nb, td, plen, chunk,
                 ids_ref, len_ref, emb_ref, ib_ref, ob_ref, g_ref, b_ref, tok_hbm, w_hbm, inner_hbm, outer_hbm,
                 qkv_hbm, att_hbm, p_hbm, pkv_ref, hid_ref, low_ref, lse_ref, fac_ref,
                 tok, w, inner, outer, normed, qkv, ot_s, km, p_s, top_s, sum_s, pre, emf, ibf, tbl, rs_out, rs_in, ag_out, ag_in, aa_out, aa_in,
                 ld_sem, st_sem, at_sem, p_sem, rs_ss, rs_rs, ag_ss, ag_rs, aa_ss, aa_rs):
    rows, width = tok.shape
    slots = ids_ref.shape[0]
    rc = td * PAD // nb
    pc = outer.shape[2]
    mt = lax.axis_index("task")
    mb = lax.axis_index("batch")
    loads = [pltpu.make_async_copy(s, d, ld_sem.at[i])
             for i, (s, d) in enumerate(((inner_hbm, inner), (tok_hbm, tok), (w_hbm, w), (outer_hbm, outer)))]
    for c in loads[:2]:
        c.start()
    barrier, me, total = greet_all(nt, nb)
    pre[...] = jnp.zeros_like(pre)
    emf[...] = emb_ref[...].astype(F).reshape(emf.shape)
    loads[0].wait()
    for c in loads[2:]:
        c.start()
    for t in range(td):
        pre[t * PAD:t * PAD + plen, :] = dg(emf[pl.ds(t, plen, stride=td), :].astype(BF), inner[t], 1, 0)
    for c in range(nb):
        rs_out[c, 0:rc, :] = pre[c * rc:(c + 1) * rc, :].astype(BF)
    ib = ib_ref[...].astype(F)
    for t in range(td):
        ibf[t * PAD:(t + 1) * PAD, :] = jnp.broadcast_to(ib[t:t + 1], (PAD, ib.shape[1]))
    pl.semaphore_wait(barrier, total - 1)

    def batch_copy(d, src, dst, ss, rs):
        to = lax.rem(mb + d, nb)
        return pltpu.make_async_remote_copy(src_ref=src(to), dst_ref=dst, send_sem=ss.at[d], recv_sem=rs.at[d],
                                            device_id={"task": mt, "batch": to}, device_id_type=MESH)

    rs_copy = [batch_copy(d, lambda to: rs_out.at[to], rs_in.at[d], rs_ss, rs_rs) for d in range(1, nb)]
    for c in rs_copy:
        c.start()
    loads[1].wait()
    gain = g_ref[...].astype(F).reshape(1, -1)
    bias = b_ref[...].astype(F).reshape(1, -1)

    def norm_step(i, c):
        r = pl.ds(pl.multiple_of(i * 128, 128), 128)
        normed[r, :] = layer_norm_rows(tok[r, :].astype(F), gain, bias).astype(BF)
        return c

    lax.fori_loop(0, rows // 128, norm_step, 0)
    loads[2].wait()

    def store(j):
        cols = pl.ds(pl.multiple_of(j * chunk, chunk), chunk)
        return pltpu.make_async_copy(qkv.at[:, cols], qkv_hbm.at[:, cols], st_sem.at[j])

    def mm_step(j, c):
        cols = pl.ds(pl.multiple_of(j * chunk, chunk), chunk)
        qkv[:, cols] = dg(normed[...], w[:, cols], 1, 0).astype(BF)
        store(j).start()
        return c

    steps = w.shape[1] // chunk
    lax.fori_loop(0, steps - 1, mm_step, 0)
    mine = pl.ds(pl.multiple_of(mb * rc, rc), rc)
    own = pre[mine, :] + ibf[mine, :]
    for c in rs_copy:
        c.wait_recv()
    for d in range(1, nb):
        own = own + rs_in[d, 0:rc, :].astype(F)
    hid = jnp.tanh(own)
    hid_ref[...] = hid
    ag_out[0:rc, :] = hid.astype(BF)
    ag_copy = [batch_copy(d, lambda to: ag_out, ag_in.at[d], ag_ss, ag_rs) for d in range(1, nb)]
    for c in ag_copy:
        c.start()
    lax.fori_loop(steps - 1, steps, mm_step, 0)

    def put_low(frm, block):
        low_ref[pl.ds(pl.multiple_of(frm * rc, rc), rc), :] = block

    def aa_copy(d, to, at):
        return pltpu.make_async_remote_copy(src_ref=aa_out.at[to], dst_ref=aa_in.at[at], send_sem=aa_ss.at[d],
                                            recv_sem=aa_rs.at[at], device_id=peer_id(to, nb), device_id_type=MESH)

    def pick(e):
        idx = jnp.int32(0)
        for s in range(slots):
            tid = ids_ref[s, e]
            idx = jnp.where(tid // td == mt, lax.rem(tid, td), idx)
        return tbl[idx]

    def send_table():
        put_low(mb, ag_out[0:rc, :])
        for c in ag_copy:
            c.wait_recv()
        for d in range(1, nb):
            put_low(lax.rem(mb + nb - d, nb), ag_in[d, 0:rc, :])
        loads[3].wait()
        ob = ob_ref[...].astype(F)
        for t in range(td):
            tbl[t] = (dg(low_ref[t * PAD:(t + 1) * PAD, :], outer[t], 1, 0) + ob[t:t + 1]).astype(BF)

        def aa_step(d, c):
            to = lax.rem(me + d, total)
            aa_out[to] = pick(to)
            aa_copy(d, to, me).start()
            return c

        lax.fori_loop(1, total, aa_step, 0)
        aa_in[me] = pick(me)

    blk = rows // slots
    hd = 64
    pair = 2 * hd
    pairs = width // pair
    scale = hd ** -0.5
    single = len_ref[0, 0] > blk
    first = lax.broadcasted_iota(jnp.int32, (1, pair), 1) < hd
    zero = jnp.zeros((), BF)
    tri = lax.broadcasted_iota(jnp.int32, (blk, blk), 0) <= lax.broadcasted_iota(jnp.int32, (blk, blk), 1)

    at_row, p_rows = strip_rows(slots, blk)

    def p_copies(h):
        buf = lax.rem(h, 2)
        return [pltpu.make_async_copy(p_s.at[buf, r], p_hbm.at[h, r], p_sem.at[buf, n])
                for n, r in enumerate(strip_parts(p_rows))]

    def p_wait(h):
        for cp in p_copies(h):
            cp.wait()

    def attend(h, c):
        pl.when(h == 2)(send_table)
        pl.when(h >= 2)(lambda: p_wait(h - 2))
        buf = lax.rem(h, 2)
        part = lambda third: qkv[:, pl.ds(pl.multiple_of(third * width + h * pair, pair), pair)]
        q_all = part(0) * jnp.asarray(scale, BF)
        k = part(1)
        km[0] = jnp.where(first, k, zero)
        km[1] = jnp.where(first, zero, k)
        vt = part(2).T
        ones = jnp.ones((PAD, rows), BF)
        vts = [jnp.concatenate([vt[j * hd:(j + 1) * hd], ones], axis=0) for j in range(2)]
        items = [(i, j) for i in range(slots) for j in range(2)]

        def scores(n):
            i, j = items[n]
            return dg(km[j, 0:(i + 1) * blk, :], q_all[i * blk:(i + 1) * blk], 1, 1)

        def top_of(n, s):
            lo = items[n][0] * blk
            top = jnp.max(jnp.where(tri, s[lo:], NEG), axis=0, keepdims=True)
            if lo:
                top = jnp.maximum(top, jnp.where(single, jnp.max(s[:lo], axis=0, keepdims=True), NEG))
            return top

        ahead = [scores(n) for n in range(AHEAD)]
        nxt_top = top_of(0, ahead[0])
        for n, (i, j) in enumerate(items):
            lo, hi = i * blk, (i + 1) * blk
            s, top = ahead.pop(0), nxt_top
            if n + AHEAD < len(items):
                ahead.append(scores(n + AHEAD))
            if n + 1 < len(items):
                nxt_top = top_of(n + 1, ahead[0])
            p = jnp.exp(jnp.where(tri, s[lo:], NEG) - top).astype(BF)
            if i:
                p = jnp.concatenate([jnp.exp(s[:lo] - jnp.where(single, top, -NEG)).astype(BF), p], axis=0)
            p_s[buf, at_row[i] + j * hi:at_row[i] + (j + 1) * hi, :] = p
            ot = dg(vts[j][:, 0:hi], p, 1, 0)
            ot_s[pl.ds(pl.multiple_of(h * pair + j * hd, hd), hd), lo:hi] = ot[:hd]
            top_s[h, j:j + 1, lo:hi] = top
            sum_s[h, j:j + 1, lo:hi] = ot[hd:hd + 1]
        for cp in p_copies(h):
            cp.start()
        return c

    lax.fori_loop(0, pairs, attend, 0)

    def aa_wait(d, c):
        frm = lax.rem(me + d, total)
        aa_copy(d, frm, frm).wait()
        return c

    lax.fori_loop(1, total, aa_wait, 0)
    for s in range(slots):
        owner = ids_ref[s, me] // td
        for b in range(nb):
            pkv_ref[s * PAD:(s + 1) * PAD, b * pc:(b + 1) * pc] = aa_in[owner * nb + b]
    heads = 2 * pairs

    def rows_of(i):
        return pl.ds(pl.multiple_of(i * blk, blk), blk)

    def att_store(i):
        return pltpu.make_async_copy(normed.at[rows_of(i), :], att_hbm.at[rows_of(i), :], at_sem.at[i])

    def merge(i, c):
        cols = rows_of(i)
        spread = lambda x: spread_heads(x, heads, hd)
        q = qkv[cols, 0:width] * jnp.asarray(scale, BF)
        sp = dg(spread(prefix_rows(pkv_ref, single, i, 0, width)), q, 1, 1)
        live = lax.broadcasted_iota(jnp.int32, (PAD, blk), 0) < plen
        ps, alphas, invs = [], [], []
        for hh in range(heads):
            s = jnp.where(live, sp[hh * PAD:(hh + 1) * PAD], NEG)
            told = top_s[hh // 2, hh % 2:hh % 2 + 1, cols]
            top = jnp.maximum(told, jnp.max(s, axis=0, keepdims=True))
            p = jnp.exp(s - top)
            alpha = jnp.exp(told - top)
            tot = alpha * sum_s[hh // 2, hh % 2:hh % 2 + 1, cols] + jnp.sum(p, axis=0, keepdims=True)
            lse_ref[hh // 2, hh % 2:hh % 2 + 1, cols] = top + jnp.log(tot)
            inv = 1.0 / tot
            ps.append(p.astype(BF))
            alphas.append(alpha * inv)
            fac_ref[hh // 2, hh % 2:hh % 2 + 1, cols] = alpha * inv
            invs.append(inv)
        vt = spread(prefix_rows(pkv_ref, single, i, width, 2 * width)).T
        pre = dg(vt, jnp.concatenate(ps, axis=0), 1, 0)
        outs = [ot_s[hh * hd:(hh + 1) * hd, cols] * alphas[hh] + pre[hh * hd:(hh + 1) * hd] * invs[hh]
                for hh in range(heads)]
        normed[cols, :] = jnp.concatenate(outs, axis=0).T.astype(BF)
        att_store(i).start()
        return c

    lax.fori_loop(0, slots, merge, 0)
    for c in rs_copy + ag_copy:
        c.wait_send()
    for j in range(steps):
        store(j).wait()
    p_wait(pairs - 2)
    p_wait(pairs - 1)
    for i in range(slots):
        att_store(i).wait()


def front(nt, nb, task_ids, lengths, prefix_embed, inner, inner_bias, outer, outer_bias, gain, bias, tokens, weight):
    plen, td, depth = prefix_embed.shape
    rep = inner.shape[2]
    pc = outer.shape[2]
    rows, width = tokens.shape
    slots = task_ids.shape[0]
    total = nt * nb
    rc = td * PAD // nb
    rb = max(rc, PAD)
    chunk = 1024
    steps = weight.shape[1] // chunk
    p_rows = strip_rows(slots, rows // slots)[1]
    sds = jax.ShapeDtypeStruct
    vm = pl.BlockSpec(memory_space=pltpu.VMEM)
    hb = pl.BlockSpec(memory_space=pl.ANY)
    dma = pltpu.SemaphoreType.DMA
    return pl.pallas_call(
        functools.partial(front_kernel, nt, nb, td, plen, chunk),
        in_specs=[pl.BlockSpec(memory_space=pltpu.SMEM)] * 2 + [vm] * 5 + [hb] * 4,
        out_specs=[hb, hb, hb, vm, vm, vm, vm, vm],
        out_shape=[sds((rows, weight.shape[1]), BF), sds((rows, width), BF), sds((width // 128, p_rows, rows // slots), BF), sds((slots * PAD, nb * pc), BF), sds((rc, rep), F),
                   sds((td * PAD, rep), BF), sds((width // 128, 2, rows), F), sds((width // 128, 2, rows), F)],
        scratch_shapes=[
            pltpu.VMEM((rows, width), BF), pltpu.VMEM(weight.shape, BF), pltpu.VMEM(inner.shape, BF),
            pltpu.VMEM(outer.shape, BF), pltpu.VMEM((rows, width), BF), pltpu.VMEM((rows, weight.shape[1]), BF),
            pltpu.VMEM((width, rows), F), pltpu.VMEM((2, rows, 128), BF), pltpu.VMEM((2, p_rows, rows // slots), BF),
            pltpu.VMEM((width // 128, 2, rows), F), pltpu.VMEM((width // 128, 2, rows), F),
            pltpu.VMEM((td * PAD, rep), F), pltpu.VMEM((plen * td, depth), F), pltpu.VMEM((td * PAD, rep), F), pltpu.VMEM((td, PAD, pc), BF),
            pltpu.VMEM((nb, rb, rep), BF), pltpu.VMEM((nb, rb, rep), BF),
            pltpu.VMEM((rb, rep), BF), pltpu.VMEM((nb, rb, rep), BF),
            pltpu.VMEM((total, PAD, pc), BF), pltpu.VMEM((total, PAD, pc), BF),
            dma((4,)), dma((steps,)), dma((slots,)), dma((2, PARTS)), dma((nb,)), dma((nb,)), dma((nb,)), dma((nb,)), dma((total,)), dma((total,)),
        ],
        compiler_params=pltpu.CompilerParams(vmem_limit_bytes=62 * 2**20, collective_id=0, has_side_effects=True),
        name="front_attend",
    )(task_ids, lengths, prefix_embed, inner_bias, outer_bias, gain, bias,
      tokens, weight, inner, outer)


def middle_kernel(blk, fch, g_ref, b_ref, tok_hbm, att_hbm, ct_hbm, wo_hbm, we_hbm, wc_hbm,
                  out_hbm, gm_hbm, ga_hbm,
                  tok, att, ct, wo, we, wc, mid, n2, mean_s, rstd_s, ld_sem, st_sem):
    rows, width = tok.shape
    ff = we.shape[1]
    names = ((wo_hbm, wo), (att_hbm, att), (tok_hbm, tok), (we_hbm, we), (ct_hbm, ct), (wc_hbm, wc))
    loads = [pltpu.make_async_copy(s, d, ld_sem.at[i]) for i, (s, d) in enumerate(names)]
    for c in loads:
        c.start()
    gain = g_ref[...].astype(F).reshape(1, -1)
    bias = b_ref[...].astype(F).reshape(1, -1)
    inv = 1.0 / width
    steps = rows // blk
    for c in loads[:3]:
        c.wait()

    def first(i, c):
        r = pl.ds(pl.multiple_of(i * blk, blk), blk)
        x = tok[r, :].astype(F) + dg(att[r, :], wo[...], 1, 0)
        mid[r, :] = x
        mean = jnp.sum(x, axis=1, keepdims=True) * inv
        cen = x - mean
        rstd = lax.rsqrt(jnp.sum(cen * cen, axis=1, keepdims=True) * inv + 1e-5)
        mean_s[r, :] = mean
        rstd_s[r, :] = rstd
        n2[r, :] = (cen * rstd * gain + bias).astype(BF)
        return c

    lax.fori_loop(0, steps, first, 0)
    for c in loads[3:]:
        c.wait()

    def stores(i):
        r = pl.ds(pl.multiple_of(i * blk, blk), blk)
        return [pltpu.make_async_copy(s.at[r, :], d.at[r, :], st_sem.at[k, i])
                for k, (s, d) in enumerate(((tok, out_hbm), (mid, gm_hbm), (att, ga_hbm)))]

    def second(i, c):
        r = pl.ds(pl.multiple_of(i * blk, blk), blk)
        x2 = n2[r, :]
        g = ct[r, :]
        pair = lambda k: (dg(x2, we[:, k:k + fch], 1, 0), dg(g, wc[k:k + fch, :], 1, 1))
        y = gn = None
        nxt = pair(0)
        for k in range(0, ff, fch):
            v, up = nxt
            if k + fch < ff:
                nxt = pair(k + fch)
            vv = v * v
            t = jnp.tanh(v * (0.7978845608028654 + (0.7978845608028654 * 0.044715) * vv))
            half = 0.5 + 0.5 * t
            act = (v * half).astype(BF)
            slope = half + v * (0.5 - 0.5 * t * t) * (0.7978845608028654 + (3 * 0.7978845608028654 * 0.044715) * vv)
            gh = (up * slope).astype(BF)
            yk = dg(act, wc[k:k + fch, :], 1, 0)
            gk = dg(gh, we[:, k:k + fch], 1, 1)
            y = yk if y is None else y + yk
            gn = gk if gn is None else gn + gk
        x = mid[r, :]
        tok[r, :] = (x + y).astype(BF)
        rstd = rstd_s[r, :]
        xhat = (x - mean_s[r, :]) * rstd
        ug = gn * gain
        m1 = jnp.sum(ug, axis=1, keepdims=True) * inv
        m2 = jnp.sum(ug * xhat, axis=1, keepdims=True) * inv
        gmid = g.astype(F) + rstd * (ug - m1 - xhat * m2)
        mid[r, :] = gmid
        att[r, :] = dg(gmid.astype(BF), wo[...], 1, 1).astype(BF)
        for cp in stores(i):
            cp.start()
        return c

    lax.fori_loop(0, steps, second, 0)
    for i in range(steps):
        for cp in stores(i):
            cp.wait()


def middle(gain, bias, tokens, attended, ct, wo, we, wc, blk=256, fch=512):
    rows, width = tokens.shape
    ff = we.shape[1]
    sds = jax.ShapeDtypeStruct
    vm = pl.BlockSpec(memory_space=pltpu.VMEM)
    hb = pl.BlockSpec(memory_space=pl.ANY)
    dma = pltpu.SemaphoreType.DMA
    full = lambda t: pltpu.VMEM((rows, width), t)
    return pl.pallas_call(
        functools.partial(middle_kernel, blk, fch),
        in_specs=[vm, vm] + [hb] * 6,
        out_specs=[hb] * 3,
        out_shape=[sds((rows, width), BF), sds((rows, width), F), sds((rows, width), BF)],
        scratch_shapes=[full(BF), full(BF), full(BF), pltpu.VMEM(wo.shape, BF), pltpu.VMEM(we.shape, BF),
                        pltpu.VMEM(wc.shape, BF), full(F), full(BF), pltpu.VMEM((rows, 1), F), pltpu.VMEM((rows, 1), F),
                        dma((6,)), dma((3, rows // blk))],
        compiler_params=pltpu.CompilerParams(vmem_limit_bytes=62 * 2**20),
        name="middle",
    )(gain, bias, tokens, attended, ct, wo, we, wc)


def back_kernel(nt, nb, td, plen, blk,
                ids_ref, len_ref, hid_ref, g_ref, lse_ref, fac_ref, pkv_ref, outer_hbm, w_hbm, qkv_hbm, att_hbm, do_hbm, tok_hbm,
                gm_hbm, p_hbm,
                ig_hbm, gpre_ref, gtl_ref,
                outer, w, qkv, att, do_s, tok, gm, dqkv, dqp, p_s, vm, dka, dva, del_s, dpk_s, dpv_s, gbuf,
                sel, rs_out, rs_in, ag_out, ag_in, aa_out, aa_in, part,
                ld_sem, bl_sem, p_sem, st_sem, rs_ss, rs_rs, ag_ss, ag_rs, aa_ss, aa_rs):
    rows, width = tok.shape
    slots = ids_ref.shape[0]
    rc = td * PAD // nb
    pc = outer.shape[2]
    hd = 64
    pair = 2 * hd
    pairs = width // pair
    heads = 2 * pairs
    scale = hd ** -0.5
    inv = 1.0 / width
    single = len_ref[0, 0] > blk
    mt = lax.axis_index("task")
    mb = lax.axis_index("batch")

    def rows_of(i):
        return pl.ds(pl.multiple_of(i * blk, blk), blk)

    def block_loads(i):
        r = rows_of(i)
        return [pltpu.make_async_copy(s, d, bl_sem.at[k, i]) for k, (s, d) in enumerate((
            (qkv_hbm.at[r, 0:width], qkv.at[r, 0:width]), (do_hbm.at[r, :], do_s.at[r, :]), (att_hbm.at[r, :], att.at[r, :])))]

    rest = slice(width, 3 * width)
    names = ((qkv_hbm.at[:, rest], qkv.at[:, rest]), (outer_hbm, outer), (w_hbm, w), (tok_hbm, tok), (gm_hbm, gm))
    loads = [pltpu.make_async_copy(s, d, ld_sem.at[i]) for i, (s, d) in enumerate(names)]
    for i in range(slots):
        for c in block_loads(i):
            c.start()
    at_row, p_rows = strip_rows(slots, blk)

    def p_copies(h):
        buf = lax.rem(h, 2)
        return [pltpu.make_async_copy(p_hbm.at[h, r], p_s.at[buf, r], p_sem.at[buf, n])
                for n, r in enumerate(strip_parts(p_rows))]

    barrier, me, total = greet_all(nt, nb)
    live = lax.broadcasted_iota(jnp.int32, (PAD, blk), 0) < plen
    lane_head = lax.broadcasted_iota(jnp.int32, (heads, width), 1) // hd
    picker = jnp.where(lane_head == lax.broadcasted_iota(jnp.int32, (heads, width), 0), 1.0, 0.0).astype(BF)
    own_block = (lax.broadcasted_iota(jnp.int32, (heads * PAD, width), 0) // PAD
                 == lax.broadcasted_iota(jnp.int32, (heads * PAD, width), 1) // hd)

    def prefix_step(i, c):
        cols = rows_of(i)
        for cp in block_loads(i):
            cp.wait()

        @pl.when(i == 1)
        def _():
            for cp in loads[:1] + p_copies(0) + p_copies(1):
                cp.start()

        q = qkv[cols, 0:width] * jnp.asarray(scale, BF)
        do = do_s[cols, :]
        prod = do.astype(F) * att[cols, :].astype(F)
        high = prod.astype(BF)
        delta = dg(picker, high, 1, 1) + dg(picker, (prod - high.astype(F)).astype(BF), 1, 1)
        kp = spread_heads(prefix_rows(pkv_ref, single, i, 0, width), heads, hd)
        vp = spread_heads(prefix_rows(pkv_ref, single, i, width, 2 * width), heads, hd)
        sp = dg(kp, q, 1, 1)
        dpp = dg(vp, do, 1, 1)
        ps, dss = [], []
        for hh in range(heads):
            one = slice(hh * PAD, (hh + 1) * PAD)
            del_s[hh // 2, hh % 2:hh % 2 + 1, cols] = delta[hh:hh + 1] * fac_ref[hh // 2, hh % 2:hh % 2 + 1, cols]
            pr = jnp.where(live, jnp.exp(sp[one] - lse_ref[hh // 2, hh % 2:hh % 2 + 1, cols]), 0.0)
            ps.append(pr.astype(BF))
            dss.append((pr * (dpp[one] - delta[hh:hh + 1])).astype(BF))
        ds = jnp.concatenate(dss, axis=0)
        fold = lambda x: jnp.sum(jnp.where(own_block, x, 0.0).reshape(heads, PAD, width), axis=0)
        dpk_s[i] = fold(dg(ds, q, 1, 0))
        dpv_s[i] = fold(dg(jnp.concatenate(ps, axis=0), do, 1, 0))
        dqp[:, cols] = dg(kp.T, ds, 1, 0)
        return c

    lax.fori_loop(0, slots, prefix_step, 0)
    for c in loads[1:]:
        c.start()
    for ref in (dpk_s, dpv_s):
        whole = ref[0]
        for i in range(1, slots):
            whole = whole + ref[i]
        ref[0] = jnp.where(single, whole, ref[0])
        for i in range(1, slots):
            ref[i] = jnp.where(single, 0.0, ref[i])
    for o in range(nt):
        at = jnp.int32(0)
        for s in range(slots):
            at = jnp.where(ids_ref[s, me] // td == o, s, at)
        for half, ref in enumerate((dpk_s, dpv_s)):
            block = ref[at].astype(BF)
            for b in range(nb // 2):
                aa_out[o * nb + half * (nb // 2) + b] = block[:, b * pc:(b + 1) * pc]
    pl.semaphore_wait(barrier, total - 1)

    def aa_copy(d, to, at):
        return pltpu.make_async_remote_copy(src_ref=aa_out.at[to], dst_ref=aa_in.at[at], send_sem=aa_ss.at[d],
                                            recv_sem=aa_rs.at[at], device_id=peer_id(to, nb), device_id_type=MESH)

    def aa_step(d, c):
        aa_copy(d, lax.rem(me + d, total), me).start()
        return c

    lax.fori_loop(1, total, aa_step, 0)
    aa_in[me] = aa_out[me]
    lane = lax.broadcasted_iota(jnp.int32, (1, total * PAD), 1)
    task_of = jnp.zeros((1, total * PAD), jnp.int32)
    for e in range(total):
        idx = jnp.int32(0)
        for s in range(slots):
            tid = ids_ref[s, e]
            idx = jnp.where(tid // td == mt, lax.rem(tid, td), idx)
        task_of = jnp.where(lane // PAD == e, idx, task_of)
    want = task_of * PAD + lax.rem(lane, PAD)
    row = lax.broadcasted_iota(jnp.int32, (td * PAD, total * PAD), 0)
    sel[...] = jnp.where(row == want, 1.0, 0.0).astype(BF)

    def batch_copy(d, src, dst, ss, rs):
        to = lax.rem(mb + d, nb)
        return pltpu.make_async_remote_copy(src_ref=src(to), dst_ref=dst, send_sem=ss.at[d], recv_sem=rs.at[d],
                                            device_id={"task": mt, "batch": to}, device_id_type=MESH)

    rs_copy = [batch_copy(d, lambda to: rs_out.at[to], rs_in.at[d], rs_ss, rs_rs) for d in range(1, nb)]
    ag_copy = [batch_copy(d, lambda to: ag_out, ag_in.at[d], ag_ss, ag_rs) for d in range(1, nb)]

    def sum_table():
        def aa_wait(d, c):
            frm = lax.rem(me + d, total)
            aa_copy(d, frm, frm).wait()
            return c

        lax.fori_loop(1, total, aa_wait, 0)
        gtl_ref[...] = dg(sel[...], aa_in[...].reshape(total * PAD, pc), 1, 0).astype(BF)
        loads[1].wait()
        for t in range(td):
            part[t * PAD:(t + 1) * PAD, :] = dg(gtl_ref[t * PAD:(t + 1) * PAD, :], outer[t], 1, 1)
        for c in range(nb):
            rs_out[c, 0:rc, :] = part[c * rc:(c + 1) * rc, :].astype(BF)
        for c in rs_copy:
            c.start()

    def sum_hidden():
        own = part[pl.ds(pl.multiple_of(mb * rc, rc), rc), :]
        for c in rs_copy:
            c.wait_recv()
        for d in range(1, nb):
            own = own + rs_in[d, 0:rc, :].astype(F)
        hid = hid_ref[...]
        ag_out[0:rc, :] = (own * (1.0 - hid * hid)).astype(BF)
        for c in ag_copy:
            c.start()

    loads[0].wait()
    first = lax.broadcasted_iota(jnp.int32, (1, pair), 1) < hd
    zero = jnp.zeros((), BF)
    split = lambda a: (jnp.where(first, a, zero), jnp.where(first, zero, a))
    add = lambda a, b: b if a is None else a + b

    def attend(h, c):
        pl.when(h == 3)(sum_table)
        pl.when(h == 6)(sum_hidden)
        cols_of = lambda third: pl.ds(pl.multiple_of(third * width + h * pair, pair), pair)
        for cp in p_copies(h):
            cp.wait()
        buf = lax.rem(h, 2)
        q_all = qkv[:, cols_of(0)] * jnp.asarray(scale, BF)
        vm[0], vm[1] = split(qkv[:, cols_of(2)])
        kt = qkv[:, cols_of(1)].T
        fac = jnp.concatenate([jnp.broadcast_to(fac_ref[h, j:j + 1, :], (hd, rows)) for j in range(2)], axis=0).T
        do_all = (do_s[:, cols_of(0)].astype(F) * fac).astype(BF)
        qs, dos = split(q_all), split(do_all)

        def scores(i, j):
            lo, hi = i * blk, (i + 1) * blk
            return dg(vm[j, 0:hi, :], do_all[lo:hi], 1, 1)

        items = [(i, j) for i in range(slots) for j in range(2)]
        ahead = [scores(*items[n]) for n in range(2)]
        for n, (i, j) in enumerate(items):
            lo, hi = i * blk, (i + 1) * blk
            dp = ahead.pop(0)
            if n + 2 < len(items):
                ahead.append(scores(*items[n + 2]))
            p = p_s[buf, at_row[i] + j * hi:at_row[i] + (j + 1) * hi, :]
            ds = (p.astype(F) * (dp - del_s[h, j:j + 1, lo:hi])).astype(BF)
            if j == 0:
                dk = dv = None
                dqs = []
            dv = add(dv, dg(p, dos[j][lo:hi], 1, 0))
            dk = add(dk, dg(ds, qs[j][lo:hi], 1, 0))
            dqs.append(dg(kt[j * hd:(j + 1) * hd, 0:hi], ds, 1, 0))
            if j:
                dqt = jnp.concatenate(dqs, axis=0) + dqp[pl.ds(pl.multiple_of(h * pair, pair), pair), lo:hi]
                dqkv[lo:hi, cols_of(0)] = (dqt.T * scale).astype(BF)
                dka[lo:hi, :] = dk[lo:]
                dva[lo:hi, :] = dv[lo:]
                if i:
                    dka[0:lo, :] += dk[:lo]
                    dva[0:lo, :] += dv[:lo]
        dqkv[:, cols_of(1)] = dka[...].astype(BF)
        dqkv[:, cols_of(2)] = dva[...].astype(BF)

        @pl.when(h + 2 < pairs)
        def _():
            for cp in p_copies(h + 2):
                cp.start()

        return c

    lax.fori_loop(0, pairs, attend, 0)
    gain = g_ref[...].astype(F).reshape(1, -1)
    for c in loads[2:]:
        c.wait()

    def store(i):
        return pltpu.make_async_copy(tok.at[rows_of(i), :], ig_hbm.at[rows_of(i), :], st_sem.at[i])

    def product(i):
        return dg(dqkv[rows_of(i), :], w[...], 1, 1)

    def norm_back(i, gn):
        r = rows_of(i)
        ug = gn * gain
        x = tok[r, :].astype(F)
        cen = x - jnp.sum(x, axis=1, keepdims=True) * inv
        rstd = lax.rsqrt(jnp.sum(cen * cen, axis=1, keepdims=True) * inv + 1e-5)
        xhat = cen * rstd
        m1 = jnp.sum(ug, axis=1, keepdims=True) * inv
        m2 = jnp.sum(ug * xhat, axis=1, keepdims=True) * inv
        tok[r, :] = (gm[r, :] + rstd * (ug - m1 - xhat * m2)).astype(BF)
        store(i).start()

    gbuf[0] = product(0)

    def mm_step(i, c):
        gbuf[lax.rem(i, 2)] = product(i)
        norm_back(i - 1, gbuf[lax.rem(i + 1, 2)])
        return c

    lax.fori_loop(1, slots, mm_step, 0)
    norm_back(slots - 1, gbuf[(slots - 1) % 2])

    def put(frm, block):
        gpre_ref[pl.ds(pl.multiple_of(frm * rc, rc), rc), :] = block

    put(mb, ag_out[0:rc, :])
    for c in ag_copy:
        c.wait_recv()
    for d in range(1, nb):
        put(lax.rem(mb + nb - d, nb), ag_in[d, 0:rc, :])
    for c in rs_copy + ag_copy:
        c.wait_send()
    for i in range(slots):
        store(i).wait()


def back(nt, nb, task_ids, lengths, hid, gain, lse, fac, pkv, outer, weight, qkv, attended, grad_att, tokens, grad_mid,
         lifted, plen):
    td, rep, pc = outer.shape
    rows, width = tokens.shape
    slots = task_ids.shape[0]
    total = nt * nb
    rc = td * PAD // nb
    rb = max(rc, PAD)
    blk = rows // slots
    sds = jax.ShapeDtypeStruct
    vm = pl.BlockSpec(memory_space=pltpu.VMEM)
    hb = pl.BlockSpec(memory_space=pl.ANY)
    dma = pltpu.SemaphoreType.DMA
    full = lambda t: pltpu.VMEM((rows, width), t)
    return pl.pallas_call(
        functools.partial(back_kernel, nt, nb, td, plen, blk),
        in_specs=[pl.BlockSpec(memory_space=pltpu.SMEM)] * 2 + [vm] * 5 + [hb] * 8,
        out_specs=[hb, vm, vm],
        out_shape=[sds((rows, width), BF), sds((td * PAD, rep), BF), sds((td * PAD, pc), BF)],
        scratch_shapes=[
            pltpu.VMEM(outer.shape, BF), pltpu.VMEM(weight.shape, BF), pltpu.VMEM(qkv.shape, BF), full(BF), full(BF),
            full(BF), full(F), pltpu.VMEM(qkv.shape, BF), pltpu.VMEM((width, rows), F),
            pltpu.VMEM((2,) + lifted.shape[1:], BF), pltpu.VMEM((2, rows, 128), BF), pltpu.VMEM((rows, 128), F),
            pltpu.VMEM((rows, 128), F), pltpu.VMEM(lse.shape, F), pltpu.VMEM((slots, PAD, width), F),
            pltpu.VMEM((slots, PAD, width), F), pltpu.VMEM((2, blk, width), F),
            pltpu.VMEM((td * PAD, total * PAD), BF),
            pltpu.VMEM((nb, rb, rep), BF), pltpu.VMEM((nb, rb, rep), BF),
            pltpu.VMEM((rb, rep), BF), pltpu.VMEM((nb, rb, rep), BF),
            pltpu.VMEM((total, PAD, pc), BF), pltpu.VMEM((total, PAD, pc), BF),
            pltpu.VMEM((td * PAD, rep), F),
            dma((5,)), dma((3, slots)), dma((2, PARTS)), dma((slots,)), dma((nb,)), dma((nb,)), dma((nb,)), dma((nb,)), dma((total,)),
            dma((total,)),
        ],
        compiler_params=pltpu.CompilerParams(vmem_limit_bytes=62 * 2**20, collective_id=1, has_side_effects=True),
        name="back_attend",
    )(task_ids, lengths, hid, gain, lse, fac, pkv, outer, weight, qkv, attended, grad_att, tokens, grad_mid, lifted)


def tail_kernel(plen, emb_ref, gpre_ref, low_ref, gtl_ref, ig_in, inner_hbm,
                ge_ref, gib_ref, gob_ref, ig_out, gi_hbm, go_hbm,
                ig, inner, gi, go, emf, embp, embt, lowt, ld_sem, ig_sem, gi_sem, go_sem):
    td = gib_ref.shape[0]
    ig_load = pltpu.make_async_copy(ig_in, ig, ld_sem.at[0])
    in_load = pltpu.make_async_copy(inner_hbm, inner, ld_sem.at[1])
    ig_load.start()
    in_load.start()
    emf[...] = emb_ref[...].astype(F).reshape(emf.shape)
    embp[...] = jnp.zeros_like(embp)
    for t in range(td):
        embp[t * PAD:t * PAD + plen, :] = emf[pl.ds(t, plen, stride=td), :]
    embt[...] = embp[...].astype(BF).T
    lowt[...] = low_ref[...].T
    zero = jnp.zeros((), BF)

    def stores(t):
        return [pltpu.make_async_copy(go.at[t], go_hbm.at[t], go_sem.at[t]),
                pltpu.make_async_copy(gi.at[t], gi_hbm.at[t], gi_sem.at[t])]

    def step(t, c):
        only = lambda x: jnp.where(lax.broadcasted_iota(jnp.int32, x.shape, 0) // PAD == t, x, zero)
        go[t] = dg(lowt[...], only(gtl_ref[...]), 1, 0)
        gi[t] = dg(embt[...], only(gpre_ref[...]), 1, 0)
        for cp in stores(t):
            cp.start()
        return c

    lax.fori_loop(0, td // 2, step, 0)
    ig_load.wait()
    ig_store = pltpu.make_async_copy(ig, ig_out, ig_sem)
    ig_store.start()
    lax.fori_loop(td // 2, td, step, 0)
    in_load.wait()
    for t in range(td):
        ge_ref[pl.ds(t, plen, stride=td), :] = dg(gpre_ref[t * PAD:(t + 1) * PAD, :], inner[t], 1, 1)[0:plen]
    shape = (td, td * PAD)
    own = lax.broadcasted_iota(jnp.int32, shape, 0) == lax.broadcasted_iota(jnp.int32, shape, 1) // PAD
    picker = jnp.where(own, 1.0, 0.0).astype(BF)
    gib_ref[...] = dg(picker, gpre_ref[...], 1, 0)
    gob_ref[...] = dg(picker, gtl_ref[...], 1, 0)

    def wait_step(t, c):
        for cp in stores(t):
            cp.wait()
        return c

    lax.fori_loop(0, td, wait_step, 0)
    ig_store.wait()


def tail(ig, emb, inner, gpre, low, gtl):
    plen, td, depth = emb.shape
    rep = inner.shape[2]
    pc = gtl.shape[1]
    sds = jax.ShapeDtypeStruct
    vm = pl.BlockSpec(memory_space=pltpu.VMEM)
    hb = pl.BlockSpec(memory_space=pl.ANY)
    dma = pltpu.SemaphoreType.DMA
    ge, gib, gob, ig, gi, go = pl.pallas_call(
        functools.partial(tail_kernel, plen),
        in_specs=[vm, vm, vm, vm, hb, hb],
        out_specs=[vm, vm, vm, hb, hb, hb],
        out_shape=[sds((plen * td, depth), F), sds((td, rep), F), sds((td, pc), F), sds(ig.shape, BF),
                   sds((td, depth, rep), F), sds((td, rep, pc), F)],
        scratch_shapes=[pltpu.VMEM(ig.shape, BF), pltpu.VMEM(inner.shape, BF), pltpu.VMEM((td, depth, rep), F),
                        pltpu.VMEM((td, rep, pc), F), pltpu.VMEM((plen * td, depth), F), pltpu.VMEM((td * PAD, depth), F),
                        pltpu.VMEM((depth, td * PAD), BF), pltpu.VMEM((rep, td * PAD), BF),
                        dma((2,)), dma, dma((td,)), dma((td,))],
        compiler_params=pltpu.CompilerParams(vmem_limit_bytes=62 * 2**20),
        name="tail",
    )(emb, gpre, low, gtl, ig, inner)
    return ig, ge, gi, gib, go, gob


def local(
    tokens,
    lengths,
    task_ids,
    prefix_embed,
    reparam_inner,
    reparam_inner_bias,
    reparam_outer,
    reparam_outer_bias,
    first_gain,
    first_bias,
    input_weight,
    output_weight,
    second_gain,
    second_bias,
    expand_weight,
    contract_weight,
    output_cotangent,
):
    prefix_len = prefix_embed.shape[1]
    task_count = lax.axis_size("task")
    batch_count = lax.axis_size("batch")
    ids = task_ids.T
    embed = prefix_embed.transpose(1, 0, 2)
    projected, attended, lifted, prefix_kv, hidden_chunk, hidden_low, log_totals, factors = front(
        task_count, batch_count, ids, lengths, embed, reparam_inner, reparam_inner_bias, reparam_outer,
        reparam_outer_bias, first_gain, first_bias, tokens, input_weight,
    )
    output, grad_mid, grad_attended = middle(
        second_gain, second_bias, tokens, attended, output_cotangent, output_weight, expand_weight, contract_weight
    )
    input_grad, grad_pre, grad_table = back(
        task_count, batch_count, ids, lengths, hidden_chunk, first_gain, log_totals, factors, prefix_kv, reparam_outer,
        input_weight, projected, attended, grad_attended, tokens, grad_mid, lifted, prefix_len,
    )
    input_grad, grad_embed, grad_inner, grad_inner_bias, grad_outer, grad_outer_bias = tail(
        input_grad, embed, reparam_inner, grad_pre, hidden_low, grad_table
    )
    grad_embed = grad_embed.reshape(embed.shape).transpose(1, 0, 2)
    return (
        output,
        input_grad,
        grad_embed,
        grad_inner,
        grad_inner_bias,
        grad_outer,
        grad_outer_bias,
    )


def solution(mesh):
    placed = (
        P(("task", "batch"), None),
        P(("task", "batch"), None),
        P(),
        P("task", None, "batch"),
        P("task", "batch", None),
        P("task", None),
        P("task", None, "batch"),
        P("task", "batch"),
        P(),
        P(),
        P(),
        P(),
        P(),
        P(),
        P(),
        P(),
        P(("task", "batch"), None),
    )
    return jax.shard_map(
        local,
        mesh=mesh,
        in_specs=placed,
        out_specs=(
            P(("task", "batch"), None),
            P(("task", "batch"), None),
            P("task", None, "batch"),
            P("task", "batch", None),
            P("task", None),
            P("task", None, "batch"),
            P("task", "batch"),
        ),
        check_vma=False,
    )
```

```python
import functools

import jax
import jax.numpy as jnp
from jax import lax
from jax.experimental import pallas as pl
from jax.experimental.pallas import tpu as pltpu
from jax.sharding import PartitionSpec as P

BF = jnp.bfloat16
F = jnp.float32
PAD = 16
NEG = -1e30
MESH = pl.DeviceIdType.MESH


def dg(a, b, ca, cb):
    return lax.dot_general(a, b, (((ca,), (cb,)), ((), ())), preferred_element_type=F)


AHEAD = 3
PARTS = 4
GROUP = 4


def peer_id(flat, nb):
    return {"task": flat // nb, "batch": flat % nb}


def layer_norm_rows(x, gain, bias):
    inv = 1.0 / x.shape[1]
    mean = jnp.sum(x, axis=1, keepdims=True) * inv
    cen = x - mean
    var = jnp.sum(cen * cen, axis=1, keepdims=True) * inv
    return cen * lax.rsqrt(var + 1e-5) * gain + bias


def greet_all(nt, nb):
    me = lax.axis_index("task") * nb + lax.axis_index("batch")
    total = nt * nb
    barrier = pltpu.get_barrier_semaphore()

    def greet(d, c):
        pl.semaphore_signal(barrier, inc=1, device_id=peer_id(lax.rem(me + d, total), nb), device_id_type=MESH)
        return c

    lax.fori_loop(1, total, greet, 0)
    return barrier, me, total


def strip_rows(slots, blk):
    at = [blk * i * (i + 1) for i in range(slots + 1)]
    return at, at[-1]


def strip_parts(total):
    return [slice(n * total // PARTS, (n + 1) * total // PARTS) for n in range(PARTS)]


def spread_heads(block, heads, hd):
    wide = jnp.concatenate([block] * heads, axis=0)
    row = lax.broadcasted_iota(jnp.int32, wide.shape, 0) // PAD
    lane = lax.broadcasted_iota(jnp.int32, wide.shape, 1) // hd
    return jnp.where(row == lane, wide, jnp.zeros((), wide.dtype))


def prefix_rows(ref, single, i, lo, hi):
    own = ref[pl.ds(pl.multiple_of(i * PAD, PAD), PAD), lo:hi]
    return jnp.where(single, ref[0:PAD, lo:hi], own)


def front_kernel(nt, nb, td, plen, chunk,
                 ids_ref, len_ref, emb_ref, ib_ref, ob_ref, g_ref, b_ref, tok_hbm, w_hbm, inner_hbm, outer_hbm,
                 qkv_hbm, att_hbm, p_hbm, pkv_ref, hid_ref, low_ref, lse_ref, fac_ref,
                 tok, w, inner, outer, normed, qkv, ot_s, km, p_s, top_s, sum_s, pre, emf, ibf, tbl, rs_out, rs_in, ag_out, ag_in, aa_out, aa_in,
                 ld_sem, st_sem, at_sem, p_sem, rs_ss, rs_rs, ag_ss, ag_rs, aa_ss, aa_rs):
    rows, width = tok.shape
    slots = ids_ref.shape[0]
    rc = td * PAD // nb
    pc = outer.shape[2]
    mt = lax.axis_index("task")
    mb = lax.axis_index("batch")
    loads = [pltpu.make_async_copy(s, d, ld_sem.at[i])
             for i, (s, d) in enumerate(((inner_hbm, inner), (tok_hbm, tok), (w_hbm, w), (outer_hbm, outer)))]
    for c in loads[:2]:
        c.start()
    barrier, me, total = greet_all(nt, nb)
    pre[...] = jnp.zeros_like(pre)
    emf[...] = emb_ref[...].astype(F).reshape(emf.shape)
    loads[0].wait()
    for c in loads[2:]:
        c.start()
    for t in range(td):
        pre[t * PAD:t * PAD + plen, :] = dg(emf[pl.ds(t, plen, stride=td), :].astype(BF), inner[t], 1, 0)
    for c in range(nb):
        rs_out[c, 0:rc, :] = pre[c * rc:(c + 1) * rc, :].astype(BF)
    ib = ib_ref[...].astype(F)
    for t in range(td):
        ibf[t * PAD:(t + 1) * PAD, :] = jnp.broadcast_to(ib[t:t + 1], (PAD, ib.shape[1]))
    pl.semaphore_wait(barrier, total - 1)

    def batch_copy(d, src, dst, ss, rs):
        to = lax.rem(mb + d, nb)
        return pltpu.make_async_remote_copy(src_ref=src(to), dst_ref=dst, send_sem=ss.at[d], recv_sem=rs.at[d],
                                            device_id={"task": mt, "batch": to}, device_id_type=MESH)

    rs_copy = [batch_copy(d, lambda to: rs_out.at[to], rs_in.at[d], rs_ss, rs_rs) for d in range(1, nb)]
    for c in rs_copy:
        c.start()
    loads[1].wait()
    gain = g_ref[...].astype(F).reshape(1, -1)
    bias = b_ref[...].astype(F).reshape(1, -1)

    def norm_step(i, c):
        r = pl.ds(pl.multiple_of(i * 128, 128), 128)
        normed[r, :] = layer_norm_rows(tok[r, :].astype(F), gain, bias).astype(BF)
        return c

    lax.fori_loop(0, rows // 128, norm_step, 0)
    loads[2].wait()

    def store(j):
        cols = pl.ds(pl.multiple_of(j * chunk, chunk), chunk)
        return pltpu.make_async_copy(qkv.at[:, cols], qkv_hbm.at[:, cols], st_sem.at[j])

    def mm_step(j, c):
        cols = pl.ds(pl.multiple_of(j * chunk, chunk), chunk)
        qkv[:, cols] = dg(normed[...], w[:, cols], 1, 0).astype(BF)
        store(j).start()
        return c

    steps = w.shape[1] // chunk
    lax.fori_loop(0, steps - 1, mm_step, 0)
    mine = pl.ds(pl.multiple_of(mb * rc, rc), rc)
    own = pre[mine, :] + ibf[mine, :]
    for c in rs_copy:
        c.wait_recv()
    for d in range(1, nb):
        own = own + rs_in[d, 0:rc, :].astype(F)
    hid = jnp.tanh(own)
    hid_ref[...] = hid
    ag_out[0:rc, :] = hid.astype(BF)
    ag_copy = [batch_copy(d, lambda to: ag_out, ag_in.at[d], ag_ss, ag_rs) for d in range(1, nb)]
    for c in ag_copy:
        c.start()
    lax.fori_loop(steps - 1, steps, mm_step, 0)

    def put_low(frm, block):
        low_ref[pl.ds(pl.multiple_of(frm * rc, rc), rc), :] = block

    def aa_copy(d, to, at):
        return pltpu.make_async_remote_copy(src_ref=aa_out.at[to], dst_ref=aa_in.at[at], send_sem=aa_ss.at[d],
                                            recv_sem=aa_rs.at[at], device_id=peer_id(to, nb), device_id_type=MESH)

    def pick(e):
        idx = jnp.int32(0)
        for s in range(slots):
            tid = ids_ref[s, e]
            idx = jnp.where(tid // td == mt, lax.rem(tid, td), idx)
        return tbl[idx]

    def send_table():
        put_low(mb, ag_out[0:rc, :])
        for c in ag_copy:
            c.wait_recv()
        for d in range(1, nb):
            put_low(lax.rem(mb + nb - d, nb), ag_in[d, 0:rc, :])
        loads[3].wait()
        ob = ob_ref[...].astype(F)
        for t in range(td):
            tbl[t] = (dg(low_ref[t * PAD:(t + 1) * PAD, :], outer[t], 1, 0) + ob[t:t + 1]).astype(BF)

        def aa_step(d, c):
            to = lax.rem(me + d, total)
            aa_out[to] = pick(to)
            aa_copy(d, to, me).start()
            return c

        lax.fori_loop(1, total, aa_step, 0)
        aa_in[me] = pick(me)

    blk = rows // slots
    hd = 64
    pair = 2 * hd
    pairs = width // pair
    scale = hd ** -0.5
    single = len_ref[0, 0] > blk
    first = lax.broadcasted_iota(jnp.int32, (1, pair), 1) < hd
    zero = jnp.zeros((), BF)
    tri = lax.broadcasted_iota(jnp.int32, (blk, blk), 0) <= lax.broadcasted_iota(jnp.int32, (blk, blk), 1)

    at_row, p_rows = strip_rows(slots, blk)

    def p_copies(h):
        buf = lax.rem(h, 2)
        return [pltpu.make_async_copy(p_s.at[buf, r], p_hbm.at[h, r], p_sem.at[buf, n])
                for n, r in enumerate(strip_parts(p_rows))]

    def p_wait(h):
        for cp in p_copies(h):
            cp.wait()

    def attend(h, c):
        pl.when(h == 2)(send_table)
        pl.when(h >= 2)(lambda: p_wait(h - 2))
        buf = lax.rem(h, 2)
        part = lambda third: qkv[:, pl.ds(pl.multiple_of(third * width + h * pair, pair), pair)]
        q_all = part(0) * jnp.asarray(scale, BF)
        k = part(1)
        km[0] = jnp.where(first, k, zero)
        km[1] = jnp.where(first, zero, k)
        vt = part(2).T
        ones = jnp.ones((PAD, rows), BF)
        vts = [jnp.concatenate([vt[j * hd:(j + 1) * hd], ones], axis=0) for j in range(2)]
        items = [(i, j) for i in range(slots) for j in range(2)]

        def scores(n):
            i, j = items[n]
            return dg(km[j, 0:(i + 1) * blk, :], q_all[i * blk:(i + 1) * blk], 1, 1)

        def top_of(n, s):
            lo = items[n][0] * blk
            top = jnp.max(jnp.where(tri, s[lo:], NEG), axis=0, keepdims=True)
            if lo:
                top = jnp.maximum(top, jnp.where(single, jnp.max(s[:lo], axis=0, keepdims=True), NEG))
            return top

        ahead = [scores(n) for n in range(AHEAD)]
        nxt_top = top_of(0, ahead[0])
        for n, (i, j) in enumerate(items):
            lo, hi = i * blk, (i + 1) * blk
            s, top = ahead.pop(0), nxt_top
            if n + AHEAD < len(items):
                ahead.append(scores(n + AHEAD))
            if n + 1 < len(items):
                nxt_top = top_of(n + 1, ahead[0])
            p = jnp.exp(jnp.where(tri, s[lo:], NEG) - top).astype(BF)
            if i:
                p = jnp.concatenate([jnp.exp(s[:lo] - jnp.where(single, top, -NEG)).astype(BF), p], axis=0)
            p_s[buf, at_row[i] + j * hi:at_row[i] + (j + 1) * hi, :] = p
            ot = dg(vts[j][:, 0:hi], p, 1, 0)
            ot_s[pl.ds(pl.multiple_of(h * pair + j * hd, hd), hd), lo:hi] = ot[:hd]
            top_s[h, j:j + 1, lo:hi] = top
            sum_s[h, j:j + 1, lo:hi] = ot[hd:hd + 1]
        for cp in p_copies(h):
            cp.start()
        return c

    lax.fori_loop(0, pairs, attend, 0)

    def aa_wait(d, c):
        frm = lax.rem(me + d, total)
        aa_copy(d, frm, frm).wait()
        return c

    lax.fori_loop(1, total, aa_wait, 0)
    for s in range(slots):
        owner = ids_ref[s, me] // td
        for b in range(nb):
            pkv_ref[s * PAD:(s + 1) * PAD, b * pc:(b + 1) * pc] = aa_in[owner * nb + b]
    heads = 2 * pairs

    def rows_of(i):
        return pl.ds(pl.multiple_of(i * blk, blk), blk)

    def att_store(i):
        return pltpu.make_async_copy(normed.at[rows_of(i), :], att_hbm.at[rows_of(i), :], at_sem.at[i])

    live = lax.broadcasted_iota(jnp.int32, (PAD, blk), 0) < plen
    spread = lambda x: spread_heads(x, heads, hd)

    def merge(g, c):
        blocks = [g * GROUP + n for n in range(GROUP)]
        sps = [dg(spread(prefix_rows(pkv_ref, single, i, 0, width)), qkv[rows_of(i), 0:width] * jnp.asarray(scale, BF), 1, 1)
               for i in blocks]
        vts = [spread(prefix_rows(pkv_ref, single, i, width, 2 * width)).T for i in blocks]
        pres, alphas, invs = [], [], []
        for i, sp, vt in zip(blocks, sps, vts):
            cols = rows_of(i)
            ps = []
            for hh in range(heads):
                at = (hh // 2, slice(hh % 2, hh % 2 + 1), cols)
                s = jnp.where(live, sp[hh * PAD:(hh + 1) * PAD], NEG)
                told = top_s[at]
                top = jnp.maximum(told, jnp.max(s, axis=0, keepdims=True))
                p = jnp.exp(s - top)
                alpha = jnp.exp(told - top)
                tot = alpha * sum_s[at] + jnp.sum(p, axis=0, keepdims=True)
                lse_ref[at] = top + jnp.log(tot)
                inv = 1.0 / tot
                ps.append(p.astype(BF))
                alphas.append(alpha * inv)
                fac_ref[at] = alpha * inv
                invs.append(inv)
            pres.append(dg(vt, jnp.concatenate(ps, axis=0), 1, 0))
        for n, i in enumerate(blocks):
            cols = rows_of(i)
            outs = [ot_s[hh * hd:(hh + 1) * hd, cols] * alphas[n * heads + hh]
                    + pres[n][hh * hd:(hh + 1) * hd] * invs[n * heads + hh] for hh in range(heads)]
            normed[cols, :] = jnp.concatenate(outs, axis=0).T.astype(BF)
            att_store(i).start()
        return c

    lax.fori_loop(0, slots // GROUP, merge, 0)
    for c in rs_copy + ag_copy:
        c.wait_send()
    for j in range(steps):
        store(j).wait()
    p_wait(pairs - 2)
    p_wait(pairs - 1)
    for i in range(slots):
        att_store(i).wait()


def front(nt, nb, task_ids, lengths, prefix_embed, inner, inner_bias, outer, outer_bias, gain, bias, tokens, weight):
    plen, td, depth = prefix_embed.shape
    rep = inner.shape[2]
    pc = outer.shape[2]
    rows, width = tokens.shape
    slots = task_ids.shape[0]
    total = nt * nb
    rc = td * PAD // nb
    rb = max(rc, PAD)
    chunk = 1024
    steps = weight.shape[1] // chunk
    p_rows = strip_rows(slots, rows // slots)[1]
    sds = jax.ShapeDtypeStruct
    vm = pl.BlockSpec(memory_space=pltpu.VMEM)
    hb = pl.BlockSpec(memory_space=pl.ANY)
    dma = pltpu.SemaphoreType.DMA
    return pl.pallas_call(
        functools.partial(front_kernel, nt, nb, td, plen, chunk),
        in_specs=[pl.BlockSpec(memory_space=pltpu.SMEM)] * 2 + [vm] * 5 + [hb] * 4,
        out_specs=[hb, hb, hb, vm, vm, vm, vm, vm],
        out_shape=[sds((rows, weight.shape[1]), BF), sds((rows, width), BF), sds((width // 128, p_rows, rows // slots), BF), sds((slots * PAD, nb * pc), BF), sds((rc, rep), F),
                   sds((td * PAD, rep), BF), sds((width // 128, 2, rows), F), sds((width // 128, 2, rows), F)],
        scratch_shapes=[
            pltpu.VMEM((rows, width), BF), pltpu.VMEM(weight.shape, BF), pltpu.VMEM(inner.shape, BF),
            pltpu.VMEM(outer.shape, BF), pltpu.VMEM((rows, width), BF), pltpu.VMEM((rows, weight.shape[1]), BF),
            pltpu.VMEM((width, rows), F), pltpu.VMEM((2, rows, 128), BF), pltpu.VMEM((2, p_rows, rows // slots), BF),
            pltpu.VMEM((width // 128, 2, rows), F), pltpu.VMEM((width // 128, 2, rows), F),
            pltpu.VMEM((td * PAD, rep), F), pltpu.VMEM((plen * td, depth), F), pltpu.VMEM((td * PAD, rep), F), pltpu.VMEM((td, PAD, pc), BF),
            pltpu.VMEM((nb, rb, rep), BF), pltpu.VMEM((nb, rb, rep), BF),
            pltpu.VMEM((rb, rep), BF), pltpu.VMEM((nb, rb, rep), BF),
            pltpu.VMEM((total, PAD, pc), BF), pltpu.VMEM((total, PAD, pc), BF),
            dma((4,)), dma((steps,)), dma((slots,)), dma((2, PARTS)), dma((nb,)), dma((nb,)), dma((nb,)), dma((nb,)), dma((total,)), dma((total,)),
        ],
        compiler_params=pltpu.CompilerParams(vmem_limit_bytes=62 * 2**20, collective_id=0, has_side_effects=True),
        name="front_attend",
    )(task_ids, lengths, prefix_embed, inner_bias, outer_bias, gain, bias,
      tokens, weight, inner, outer)


def middle_kernel(blk, fch, g_ref, b_ref, tok_hbm, att_hbm, ct_hbm, wo_hbm, we_hbm, wc_hbm,
                  out_hbm, gm_hbm, ga_hbm,
                  tok, att, ct, wo, we, wc, mid, n2, mean_s, rstd_s, ld_sem, st_sem):
    rows, width = tok.shape
    ff = we.shape[1]
    names = ((wo_hbm, wo), (att_hbm, att), (tok_hbm, tok), (we_hbm, we), (ct_hbm, ct), (wc_hbm, wc))
    loads = [pltpu.make_async_copy(s, d, ld_sem.at[i]) for i, (s, d) in enumerate(names)]
    for c in loads:
        c.start()
    gain = g_ref[...].astype(F).reshape(1, -1)
    bias = b_ref[...].astype(F).reshape(1, -1)
    inv = 1.0 / width
    steps = rows // blk
    for c in loads[:3]:
        c.wait()

    def first(i, c):
        r = pl.ds(pl.multiple_of(i * blk, blk), blk)
        x = tok[r, :].astype(F) + dg(att[r, :], wo[...], 1, 0)
        mid[r, :] = x
        mean = jnp.sum(x, axis=1, keepdims=True) * inv
        cen = x - mean
        rstd = lax.rsqrt(jnp.sum(cen * cen, axis=1, keepdims=True) * inv + 1e-5)
        mean_s[r, :] = mean
        rstd_s[r, :] = rstd
        n2[r, :] = (cen * rstd * gain + bias).astype(BF)
        return c

    lax.fori_loop(0, steps, first, 0)
    for c in loads[3:]:
        c.wait()

    def stores(i):
        r = pl.ds(pl.multiple_of(i * blk, blk), blk)
        return [pltpu.make_async_copy(s.at[r, :], d.at[r, :], st_sem.at[k, i])
                for k, (s, d) in enumerate(((tok, out_hbm), (mid, gm_hbm), (att, ga_hbm)))]

    def second(i, c):
        r = pl.ds(pl.multiple_of(i * blk, blk), blk)
        x2 = n2[r, :]
        g = ct[r, :]
        pair = lambda k: (dg(x2, we[:, k:k + fch], 1, 0), dg(g, wc[k:k + fch, :], 1, 1))
        y = gn = None
        nxt = pair(0)
        for k in range(0, ff, fch):
            v, up = nxt
            if k + fch < ff:
                nxt = pair(k + fch)
            vv = v * v
            t = jnp.tanh(v * (0.7978845608028654 + (0.7978845608028654 * 0.044715) * vv))
            half = 0.5 + 0.5 * t
            act = (v * half).astype(BF)
            slope = half + v * (0.5 - 0.5 * t * t) * (0.7978845608028654 + (3 * 0.7978845608028654 * 0.044715) * vv)
            gh = (up * slope).astype(BF)
            yk = dg(act, wc[k:k + fch, :], 1, 0)
            gk = dg(gh, we[:, k:k + fch], 1, 1)
            y = yk if y is None else y + yk
            gn = gk if gn is None else gn + gk
        x = mid[r, :]
        tok[r, :] = (x + y).astype(BF)
        rstd = rstd_s[r, :]
        xhat = (x - mean_s[r, :]) * rstd
        ug = gn * gain
        m1 = jnp.sum(ug, axis=1, keepdims=True) * inv
        m2 = jnp.sum(ug * xhat, axis=1, keepdims=True) * inv
        gmid = g.astype(F) + rstd * (ug - m1 - xhat * m2)
        mid[r, :] = gmid
        att[r, :] = dg(gmid.astype(BF), wo[...], 1, 1).astype(BF)
        for cp in stores(i):
            cp.start()
        return c

    lax.fori_loop(0, steps, second, 0)
    for i in range(steps):
        for cp in stores(i):
            cp.wait()


def middle(gain, bias, tokens, attended, ct, wo, we, wc, blk=256, fch=512):
    rows, width = tokens.shape
    ff = we.shape[1]
    sds = jax.ShapeDtypeStruct
    vm = pl.BlockSpec(memory_space=pltpu.VMEM)
    hb = pl.BlockSpec(memory_space=pl.ANY)
    dma = pltpu.SemaphoreType.DMA
    full = lambda t: pltpu.VMEM((rows, width), t)
    return pl.pallas_call(
        functools.partial(middle_kernel, blk, fch),
        in_specs=[vm, vm] + [hb] * 6,
        out_specs=[hb] * 3,
        out_shape=[sds((rows, width), BF), sds((rows, width), F), sds((rows, width), BF)],
        scratch_shapes=[full(BF), full(BF), full(BF), pltpu.VMEM(wo.shape, BF), pltpu.VMEM(we.shape, BF),
                        pltpu.VMEM(wc.shape, BF), full(F), full(BF), pltpu.VMEM((rows, 1), F), pltpu.VMEM((rows, 1), F),
                        dma((6,)), dma((3, rows // blk))],
        compiler_params=pltpu.CompilerParams(vmem_limit_bytes=62 * 2**20),
        name="middle",
    )(gain, bias, tokens, attended, ct, wo, we, wc)


def back_kernel(nt, nb, td, plen, blk,
                ids_ref, len_ref, hid_ref, g_ref, lse_ref, fac_ref, pkv_ref, outer_hbm, w_hbm, qkv_hbm, att_hbm, do_hbm, tok_hbm,
                gm_hbm, p_hbm,
                ig_hbm, gpre_ref, gtl_ref,
                outer, w, qkv, att, do_s, tok, gm, dqkv, dqp, p_s, vm, dka, dva, del_s, dpk_s, dpv_s, gbuf,
                sel, rs_out, rs_in, ag_out, ag_in, aa_out, aa_in, part,
                ld_sem, bl_sem, p_sem, st_sem, rs_ss, rs_rs, ag_ss, ag_rs, aa_ss, aa_rs):
    rows, width = tok.shape
    slots = ids_ref.shape[0]
    rc = td * PAD // nb
    pc = outer.shape[2]
    hd = 64
    pair = 2 * hd
    pairs = width // pair
    heads = 2 * pairs
    scale = hd ** -0.5
    inv = 1.0 / width
    single = len_ref[0, 0] > blk
    mt = lax.axis_index("task")
    mb = lax.axis_index("batch")

    def rows_of(i):
        return pl.ds(pl.multiple_of(i * blk, blk), blk)

    def block_loads(i):
        r = rows_of(i)
        return [pltpu.make_async_copy(s, d, bl_sem.at[k, i]) for k, (s, d) in enumerate((
            (qkv_hbm.at[r, 0:width], qkv.at[r, 0:width]), (do_hbm.at[r, :], do_s.at[r, :]), (att_hbm.at[r, :], att.at[r, :])))]

    rest = slice(width, 3 * width)
    names = ((qkv_hbm.at[:, rest], qkv.at[:, rest]), (outer_hbm, outer), (w_hbm, w), (tok_hbm, tok), (gm_hbm, gm))
    loads = [pltpu.make_async_copy(s, d, ld_sem.at[i]) for i, (s, d) in enumerate(names)]
    for i in range(slots):
        for c in block_loads(i):
            c.start()
    at_row, p_rows = strip_rows(slots, blk)

    def p_copies(h):
        buf = lax.rem(h, 2)
        return [pltpu.make_async_copy(p_hbm.at[h, r], p_s.at[buf, r], p_sem.at[buf, n])
                for n, r in enumerate(strip_parts(p_rows))]

    barrier, me, total = greet_all(nt, nb)
    live = lax.broadcasted_iota(jnp.int32, (PAD, blk), 0) < plen
    lane_head = lax.broadcasted_iota(jnp.int32, (heads, width), 1) // hd
    picker = jnp.where(lane_head == lax.broadcasted_iota(jnp.int32, (heads, width), 0), 1.0, 0.0).astype(BF)
    own_block = (lax.broadcasted_iota(jnp.int32, (heads * PAD, width), 0) // PAD
                 == lax.broadcasted_iota(jnp.int32, (heads * PAD, width), 1) // hd)

    def prefix_step(g, c):
        blocks = [g * GROUP + n for n in range(GROUP)]
        for i in blocks:
            for cp in block_loads(i):
                cp.wait()

        @pl.when(g == 0)
        def _():
            for cp in loads[:1] + p_copies(0) + p_copies(1):
                cp.start()

        qs = [qkv[rows_of(i), 0:width] * jnp.asarray(scale, BF) for i in blocks]
        dos = [do_s[rows_of(i), :] for i in blocks]
        kps = [spread_heads(prefix_rows(pkv_ref, single, i, 0, width), heads, hd) for i in blocks]
        sps = [dg(kp, q, 1, 1) for kp, q in zip(kps, qs)]
        dpps = [dg(spread_heads(prefix_rows(pkv_ref, single, i, width, 2 * width), heads, hd), do, 1, 1)
                for i, do in zip(blocks, dos)]
        deltas = []
        for i, do in zip(blocks, dos):
            prod = do.astype(F) * att[rows_of(i), :].astype(F)
            high = prod.astype(BF)
            deltas.append(dg(picker, high, 1, 1) + dg(picker, (prod - high.astype(F)).astype(BF), 1, 1))
        fold = lambda x: jnp.sum(jnp.where(own_block, x, 0.0).reshape(heads, PAD, width), axis=0)
        for i, q, do, kp, sp, dpp, delta in zip(blocks, qs, dos, kps, sps, dpps, deltas):
            cols = rows_of(i)
            ps, dss = [], []
            for hh in range(heads):
                one = slice(hh * PAD, (hh + 1) * PAD)
                at = (hh // 2, slice(hh % 2, hh % 2 + 1), cols)
                del_s[at] = delta[hh:hh + 1] * fac_ref[at]
                pr = jnp.where(live, jnp.exp(sp[one] - lse_ref[at]), 0.0)
                ps.append(pr.astype(BF))
                dss.append((pr * (dpp[one] - delta[hh:hh + 1])).astype(BF))
            ds = jnp.concatenate(dss, axis=0)
            dpk_s[i] = fold(dg(ds, q, 1, 0))
            dpv_s[i] = fold(dg(jnp.concatenate(ps, axis=0), do, 1, 0))
            dqp[:, cols] = dg(kp.T, ds, 1, 0)
        return c

    lax.fori_loop(0, slots // GROUP, prefix_step, 0)
    for c in loads[1:]:
        c.start()
    for ref in (dpk_s, dpv_s):
        whole = ref[0]
        for i in range(1, slots):
            whole = whole + ref[i]
        ref[0] = jnp.where(single, whole, ref[0])
        for i in range(1, slots):
            ref[i] = jnp.where(single, 0.0, ref[i])
    for o in range(nt):
        at = jnp.int32(0)
        for s in range(slots):
            at = jnp.where(ids_ref[s, me] // td == o, s, at)
        for half, ref in enumerate((dpk_s, dpv_s)):
            block = ref[at].astype(BF)
            for b in range(nb // 2):
                aa_out[o * nb + half * (nb // 2) + b] = block[:, b * pc:(b + 1) * pc]
    pl.semaphore_wait(barrier, total - 1)

    def aa_copy(d, to, at):
        return pltpu.make_async_remote_copy(src_ref=aa_out.at[to], dst_ref=aa_in.at[at], send_sem=aa_ss.at[d],
                                            recv_sem=aa_rs.at[at], device_id=peer_id(to, nb), device_id_type=MESH)

    def aa_step(d, c):
        aa_copy(d, lax.rem(me + d, total), me).start()
        return c

    lax.fori_loop(1, total, aa_step, 0)
    aa_in[me] = aa_out[me]
    lane = lax.broadcasted_iota(jnp.int32, (1, total * PAD), 1)
    task_of = jnp.zeros((1, total * PAD), jnp.int32)
    for e in range(total):
        idx = jnp.int32(0)
        for s in range(slots):
            tid = ids_ref[s, e]
            idx = jnp.where(tid // td == mt, lax.rem(tid, td), idx)
        task_of = jnp.where(lane // PAD == e, idx, task_of)
    want = task_of * PAD + lax.rem(lane, PAD)
    row = lax.broadcasted_iota(jnp.int32, (td * PAD, total * PAD), 0)
    sel[...] = jnp.where(row == want, 1.0, 0.0).astype(BF)

    def batch_copy(d, src, dst, ss, rs):
        to = lax.rem(mb + d, nb)
        return pltpu.make_async_remote_copy(src_ref=src(to), dst_ref=dst, send_sem=ss.at[d], recv_sem=rs.at[d],
                                            device_id={"task": mt, "batch": to}, device_id_type=MESH)

    rs_copy = [batch_copy(d, lambda to: rs_out.at[to], rs_in.at[d], rs_ss, rs_rs) for d in range(1, nb)]
    ag_copy = [batch_copy(d, lambda to: ag_out, ag_in.at[d], ag_ss, ag_rs) for d in range(1, nb)]

    def sum_table():
        def aa_wait(d, c):
            frm = lax.rem(me + d, total)
            aa_copy(d, frm, frm).wait()
            return c

        lax.fori_loop(1, total, aa_wait, 0)
        gtl_ref[...] = dg(sel[...], aa_in[...].reshape(total * PAD, pc), 1, 0).astype(BF)
        loads[1].wait()
        for t in range(td):
            part[t * PAD:(t + 1) * PAD, :] = dg(gtl_ref[t * PAD:(t + 1) * PAD, :], outer[t], 1, 1)
        for c in range(nb):
            rs_out[c, 0:rc, :] = part[c * rc:(c + 1) * rc, :].astype(BF)
        for c in rs_copy:
            c.start()

    def sum_hidden():
        own = part[pl.ds(pl.multiple_of(mb * rc, rc), rc), :]
        for c in rs_copy:
            c.wait_recv()
        for d in range(1, nb):
            own = own + rs_in[d, 0:rc, :].astype(F)
        hid = hid_ref[...]
        ag_out[0:rc, :] = (own * (1.0 - hid * hid)).astype(BF)
        for c in ag_copy:
            c.start()

    loads[0].wait()
    first = lax.broadcasted_iota(jnp.int32, (1, pair), 1) < hd
    zero = jnp.zeros((), BF)
    split = lambda a: (jnp.where(first, a, zero), jnp.where(first, zero, a))
    add = lambda a, b: b if a is None else a + b

    def attend(h, c):
        pl.when(h == 3)(sum_table)
        pl.when(h == 6)(sum_hidden)
        cols_of = lambda third: pl.ds(pl.multiple_of(third * width + h * pair, pair), pair)
        for cp in p_copies(h):
            cp.wait()
        buf = lax.rem(h, 2)
        q_all = qkv[:, cols_of(0)] * jnp.asarray(scale, BF)
        vm[0], vm[1] = split(qkv[:, cols_of(2)])
        kt = qkv[:, cols_of(1)].T
        fac = jnp.concatenate([jnp.broadcast_to(fac_ref[h, j:j + 1, :], (hd, rows)) for j in range(2)], axis=0).T
        do_all = (do_s[:, cols_of(0)].astype(F) * fac).astype(BF)
        qs, dos = split(q_all), split(do_all)

        def scores(i, j):
            lo, hi = i * blk, (i + 1) * blk
            return dg(vm[j, 0:hi, :], do_all[lo:hi], 1, 1)

        items = [(i, j) for i in reversed(range(slots)) for j in range(2)]
        ahead = [scores(*items[n]) for n in range(2)]
        for n, (i, j) in enumerate(items):
            lo, hi = i * blk, (i + 1) * blk
            dp = ahead.pop(0)
            if n + 2 < len(items):
                ahead.append(scores(*items[n + 2]))
            p = p_s[buf, at_row[i] + j * hi:at_row[i] + (j + 1) * hi, :]
            ds = (p.astype(F) * (dp - del_s[h, j:j + 1, lo:hi])).astype(BF)
            if j == 0:
                dk = dv = None
                dqs = []
            dv = add(dv, dg(p, dos[j][lo:hi], 1, 0))
            dk = add(dk, dg(ds, qs[j][lo:hi], 1, 0))
            dqs.append(dg(kt[j * hd:(j + 1) * hd, 0:hi], ds, 1, 0))
            if j:
                dqt = jnp.concatenate(dqs, axis=0) + dqp[pl.ds(pl.multiple_of(h * pair, pair), pair), lo:hi]
                dqkv[lo:hi, cols_of(0)] = (dqt.T * scale).astype(BF)
                if i == slots - 1:
                    dka[...] = dk
                    dva[...] = dv
                else:
                    dka[0:hi, :] += dk
                    dva[0:hi, :] += dv
        dqkv[:, cols_of(1)] = dka[...].astype(BF)
        dqkv[:, cols_of(2)] = dva[...].astype(BF)

        @pl.when(h + 2 < pairs)
        def _():
            for cp in p_copies(h + 2):
                cp.start()

        return c

    lax.fori_loop(0, pairs, attend, 0)
    gain = g_ref[...].astype(F).reshape(1, -1)
    for c in loads[2:]:
        c.wait()

    def store(i):
        return pltpu.make_async_copy(tok.at[rows_of(i), :], ig_hbm.at[rows_of(i), :], st_sem.at[i])

    def product(i):
        return dg(dqkv[rows_of(i), :], w[...], 1, 1)

    def norm_back(i, gn):
        r = rows_of(i)
        ug = gn * gain
        x = tok[r, :].astype(F)
        cen = x - jnp.sum(x, axis=1, keepdims=True) * inv
        rstd = lax.rsqrt(jnp.sum(cen * cen, axis=1, keepdims=True) * inv + 1e-5)
        xhat = cen * rstd
        m1 = jnp.sum(ug, axis=1, keepdims=True) * inv
        m2 = jnp.sum(ug * xhat, axis=1, keepdims=True) * inv
        tok[r, :] = (gm[r, :] + rstd * (ug - m1 - xhat * m2)).astype(BF)
        store(i).start()

    gbuf[0] = product(0)

    def mm_step(i, c):
        gbuf[lax.rem(i, 2)] = product(i)
        norm_back(i - 1, gbuf[lax.rem(i + 1, 2)])
        return c

    lax.fori_loop(1, slots, mm_step, 0)
    norm_back(slots - 1, gbuf[(slots - 1) % 2])

    def put(frm, block):
        gpre_ref[pl.ds(pl.multiple_of(frm * rc, rc), rc), :] = block

    put(mb, ag_out[0:rc, :])
    for c in ag_copy:
        c.wait_recv()
    for d in range(1, nb):
        put(lax.rem(mb + nb - d, nb), ag_in[d, 0:rc, :])
    for c in rs_copy + ag_copy:
        c.wait_send()
    for i in range(slots):
        store(i).wait()


def back(nt, nb, task_ids, lengths, hid, gain, lse, fac, pkv, outer, weight, qkv, attended, grad_att, tokens, grad_mid,
         lifted, plen):
    td, rep, pc = outer.shape
    rows, width = tokens.shape
    slots = task_ids.shape[0]
    total = nt * nb
    rc = td * PAD // nb
    rb = max(rc, PAD)
    blk = rows // slots
    sds = jax.ShapeDtypeStruct
    vm = pl.BlockSpec(memory_space=pltpu.VMEM)
    hb = pl.BlockSpec(memory_space=pl.ANY)
    dma = pltpu.SemaphoreType.DMA
    full = lambda t: pltpu.VMEM((rows, width), t)
    return pl.pallas_call(
        functools.partial(back_kernel, nt, nb, td, plen, blk),
        in_specs=[pl.BlockSpec(memory_space=pltpu.SMEM)] * 2 + [vm] * 5 + [hb] * 8,
        out_specs=[hb, vm, vm],
        out_shape=[sds((rows, width), BF), sds((td * PAD, rep), BF), sds((td * PAD, pc), BF)],
        scratch_shapes=[
            pltpu.VMEM(outer.shape, BF), pltpu.VMEM(weight.shape, BF), pltpu.VMEM(qkv.shape, BF), full(BF), full(BF),
            full(BF), full(F), pltpu.VMEM(qkv.shape, BF), pltpu.VMEM((width, rows), F),
            pltpu.VMEM((2,) + lifted.shape[1:], BF), pltpu.VMEM((2, rows, 128), BF), pltpu.VMEM((rows, 128), F),
            pltpu.VMEM((rows, 128), F), pltpu.VMEM(lse.shape, F), pltpu.VMEM((slots, PAD, width), F),
            pltpu.VMEM((slots, PAD, width), F), pltpu.VMEM((2, blk, width), F),
            pltpu.VMEM((td * PAD, total * PAD), BF),
            pltpu.VMEM((nb, rb, rep), BF), pltpu.VMEM((nb, rb, rep), BF),
            pltpu.VMEM((rb, rep), BF), pltpu.VMEM((nb, rb, rep), BF),
            pltpu.VMEM((total, PAD, pc), BF), pltpu.VMEM((total, PAD, pc), BF),
            pltpu.VMEM((td * PAD, rep), F),
            dma((5,)), dma((3, slots)), dma((2, PARTS)), dma((slots,)), dma((nb,)), dma((nb,)), dma((nb,)), dma((nb,)), dma((total,)),
            dma((total,)),
        ],
        compiler_params=pltpu.CompilerParams(vmem_limit_bytes=62 * 2**20, collective_id=1, has_side_effects=True),
        name="back_attend",
    )(task_ids, lengths, hid, gain, lse, fac, pkv, outer, weight, qkv, attended, grad_att, tokens, grad_mid, lifted)


def tail_kernel(plen, emb_ref, gpre_ref, low_ref, gtl_ref, ig_in, inner_hbm,
                ge_ref, gib_ref, gob_ref, ig_out, gi_hbm, go_hbm,
                ig, inner, gi, go, emf, embp, embt, lowt, ld_sem, ig_sem, gi_sem, go_sem):
    td = gib_ref.shape[0]
    ig_load = pltpu.make_async_copy(ig_in, ig, ld_sem.at[0])
    in_load = pltpu.make_async_copy(inner_hbm, inner, ld_sem.at[1])
    ig_load.start()
    in_load.start()
    emf[...] = emb_ref[...].astype(F).reshape(emf.shape)
    embp[...] = jnp.zeros_like(embp)
    for t in range(td):
        embp[t * PAD:t * PAD + plen, :] = emf[pl.ds(t, plen, stride=td), :]
    embt[...] = embp[...].astype(BF).T
    lowt[...] = low_ref[...].T
    zero = jnp.zeros((), BF)

    def stores(t):
        return [pltpu.make_async_copy(go.at[t], go_hbm.at[t], go_sem.at[t]),
                pltpu.make_async_copy(gi.at[t], gi_hbm.at[t], gi_sem.at[t])]

    def step(t, c):
        only = lambda x: jnp.where(lax.broadcasted_iota(jnp.int32, x.shape, 0) // PAD == t, x, zero)
        go[t] = dg(lowt[...], only(gtl_ref[...]), 1, 0)
        gi[t] = dg(embt[...], only(gpre_ref[...]), 1, 0)
        for cp in stores(t):
            cp.start()
        return c

    lax.fori_loop(0, td // 2, step, 0)
    ig_load.wait()
    ig_store = pltpu.make_async_copy(ig, ig_out, ig_sem)
    ig_store.start()
    lax.fori_loop(td // 2, td, step, 0)
    in_load.wait()
    for t in range(td):
        ge_ref[pl.ds(t, plen, stride=td), :] = dg(gpre_ref[t * PAD:(t + 1) * PAD, :], inner[t], 1, 1)[0:plen]
    shape = (td, td * PAD)
    own = lax.broadcasted_iota(jnp.int32, shape, 0) == lax.broadcasted_iota(jnp.int32, shape, 1) // PAD
    picker = jnp.where(own, 1.0, 0.0).astype(BF)
    gib_ref[...] = dg(picker, gpre_ref[...], 1, 0)
    gob_ref[...] = dg(picker, gtl_ref[...], 1, 0)

    def wait_step(t, c):
        for cp in stores(t):
            cp.wait()
        return c

    lax.fori_loop(0, td, wait_step, 0)
    ig_store.wait()


def tail(ig, emb, inner, gpre, low, gtl):
    plen, td, depth = emb.shape
    rep = inner.shape[2]
    pc = gtl.shape[1]
    sds = jax.ShapeDtypeStruct
    vm = pl.BlockSpec(memory_space=pltpu.VMEM)
    hb = pl.BlockSpec(memory_space=pl.ANY)
    dma = pltpu.SemaphoreType.DMA
    ge, gib, gob, ig, gi, go = pl.pallas_call(
        functools.partial(tail_kernel, plen),
        in_specs=[vm, vm, vm, vm, hb, hb],
        out_specs=[vm, vm, vm, hb, hb, hb],
        out_shape=[sds((plen * td, depth), F), sds((td, rep), F), sds((td, pc), F), sds(ig.shape, BF),
                   sds((td, depth, rep), F), sds((td, rep, pc), F)],
        scratch_shapes=[pltpu.VMEM(ig.shape, BF), pltpu.VMEM(inner.shape, BF), pltpu.VMEM((td, depth, rep), F),
                        pltpu.VMEM((td, rep, pc), F), pltpu.VMEM((plen * td, depth), F), pltpu.VMEM((td * PAD, depth), F),
                        pltpu.VMEM((depth, td * PAD), BF), pltpu.VMEM((rep, td * PAD), BF),
                        dma((2,)), dma, dma((td,)), dma((td,))],
        compiler_params=pltpu.CompilerParams(vmem_limit_bytes=62 * 2**20),
        name="tail",
    )(emb, gpre, low, gtl, ig, inner)
    return ig, ge, gi, gib, go, gob


def local(
    tokens,
    lengths,
    task_ids,
    prefix_embed,
    reparam_inner,
    reparam_inner_bias,
    reparam_outer,
    reparam_outer_bias,
    first_gain,
    first_bias,
    input_weight,
    output_weight,
    second_gain,
    second_bias,
    expand_weight,
    contract_weight,
    output_cotangent,
):
    prefix_len = prefix_embed.shape[1]
    task_count = lax.axis_size("task")
    batch_count = lax.axis_size("batch")
    ids = task_ids.T
    embed = prefix_embed.transpose(1, 0, 2)
    projected, attended, lifted, prefix_kv, hidden_chunk, hidden_low, log_totals, factors = front(
        task_count, batch_count, ids, lengths, embed, reparam_inner, reparam_inner_bias, reparam_outer,
        reparam_outer_bias, first_gain, first_bias, tokens, input_weight,
    )
    output, grad_mid, grad_attended = middle(
        second_gain, second_bias, tokens, attended, output_cotangent, output_weight, expand_weight, contract_weight
    )
    input_grad, grad_pre, grad_table = back(
        task_count, batch_count, ids, lengths, hidden_chunk, first_gain, log_totals, factors, prefix_kv, reparam_outer,
        input_weight, projected, attended, grad_attended, tokens, grad_mid, lifted, prefix_len,
    )
    input_grad, grad_embed, grad_inner, grad_inner_bias, grad_outer, grad_outer_bias = tail(
        input_grad, embed, reparam_inner, grad_pre, hidden_low, grad_table
    )
    grad_embed = grad_embed.reshape(embed.shape).transpose(1, 0, 2)
    return (
        output,
        input_grad,
        grad_embed,
        grad_inner,
        grad_inner_bias,
        grad_outer,
        grad_outer_bias,
    )


def solution(mesh):
    placed = (
        P(("task", "batch"), None),
        P(("task", "batch"), None),
        P(),
        P("task", None, "batch"),
        P("task", "batch", None),
        P("task", None),
        P("task", None, "batch"),
        P("task", "batch"),
        P(),
        P(),
        P(),
        P(),
        P(),
        P(),
        P(),
        P(),
        P(("task", "batch"), None),
    )
    return jax.shard_map(
        local,
        mesh=mesh,
        in_specs=placed,
        out_specs=(
            P(("task", "batch"), None),
            P(("task", "batch"), None),
            P("task", None, "batch"),
            P("task", "batch", None),
            P("task", None),
            P("task", None, "batch"),
            P("task", "batch"),
        ),
        check_vma=False,
    )
```

```python
import functools

import jax
import jax.numpy as jnp
from jax import lax
from jax.experimental import pallas as pl
from jax.experimental.pallas import tpu as pltpu
from jax.sharding import PartitionSpec as P

BF = jnp.bfloat16
F = jnp.float32
PAD = 16
NEG = -1e30
MESH = pl.DeviceIdType.MESH


def dg(a, b, ca, cb):
    return lax.dot_general(a, b, (((ca,), (cb,)), ((), ())), preferred_element_type=F)


AHEAD = 3
PARTS = 4
GROUP = 4


def peer_id(flat, nb):
    return {"task": flat // nb, "batch": flat % nb}


def layer_norm_rows(x, gain, bias):
    inv = 1.0 / x.shape[1]
    mean = jnp.sum(x, axis=1, keepdims=True) * inv
    cen = x - mean
    var = jnp.sum(cen * cen, axis=1, keepdims=True) * inv
    return cen * lax.rsqrt(var + 1e-5) * gain + bias


def greet_all(nt, nb):
    me = lax.axis_index("task") * nb + lax.axis_index("batch")
    total = nt * nb
    barrier = pltpu.get_barrier_semaphore()

    def greet(d, c):
        pl.semaphore_signal(barrier, inc=1, device_id=peer_id(lax.rem(me + d, total), nb), device_id_type=MESH)
        return c

    lax.fori_loop(1, total, greet, 0)
    return barrier, me, total


def strip_rows(slots, blk):
    at = [blk * i * (i + 1) for i in range(slots + 1)]
    return at, at[-1]


def strip_parts(total):
    return [slice(n * total // PARTS, (n + 1) * total // PARTS) for n in range(PARTS)]


def spread_heads(block, heads, hd):
    wide = jnp.concatenate([block] * heads, axis=0)
    row = lax.broadcasted_iota(jnp.int32, wide.shape, 0) // PAD
    lane = lax.broadcasted_iota(jnp.int32, wide.shape, 1) // hd
    return jnp.where(row == lane, wide, jnp.zeros((), wide.dtype))


def prefix_rows(ref, single, i, lo, hi):
    own = ref[pl.ds(pl.multiple_of(i * PAD, PAD), PAD), lo:hi]
    return jnp.where(single, ref[0:PAD, lo:hi], own)


def front_kernel(nt, nb, td, plen, chunk,
                 ids_ref, len_ref, emb_ref, ib_ref, ob_ref, g_ref, b_ref, tok_hbm, w_hbm, inner_hbm, outer_hbm,
                 qkv_hbm, att_hbm, p_hbm, pkv_ref, hid_ref, low_ref, lse_ref, fac_ref,
                 tok, w, inner, outer, normed, qkv, ot_s, km, p_s, top_s, sum_s, pre, emf, ibf, tbl, rs_out, rs_in, ag_out, ag_in, aa_out, aa_in,
                 ld_sem, st_sem, at_sem, p_sem, rs_ss, rs_rs, ag_ss, ag_rs, aa_ss, aa_rs):
    rows, width = tok.shape
    slots = ids_ref.shape[0]
    rc = td * PAD // nb
    pc = outer.shape[2]
    mt = lax.axis_index("task")
    mb = lax.axis_index("batch")
    loads = [pltpu.make_async_copy(s, d, ld_sem.at[i])
             for i, (s, d) in enumerate(((inner_hbm, inner), (tok_hbm, tok), (w_hbm, w), (outer_hbm, outer)))]
    for c in loads[:2]:
        c.start()
    barrier, me, total = greet_all(nt, nb)
    pre[...] = jnp.zeros_like(pre)
    emf[...] = emb_ref[...].astype(F).reshape(emf.shape)
    loads[0].wait()
    for c in loads[2:]:
        c.start()
    for t in range(td):
        pre[t * PAD:t * PAD + plen, :] = dg(emf[pl.ds(t, plen, stride=td), :].astype(BF), inner[t], 1, 0)
    for c in range(nb):
        rs_out[c, 0:rc, :] = pre[c * rc:(c + 1) * rc, :].astype(BF)
    ib = ib_ref[...].astype(F)
    for t in range(td):
        ibf[t * PAD:(t + 1) * PAD, :] = jnp.broadcast_to(ib[t:t + 1], (PAD, ib.shape[1]))
    pl.semaphore_wait(barrier, total - 1)

    def batch_copy(d, src, dst, ss, rs):
        to = lax.rem(mb + d, nb)
        return pltpu.make_async_remote_copy(src_ref=src(to), dst_ref=dst, send_sem=ss.at[d], recv_sem=rs.at[d],
                                            device_id={"task": mt, "batch": to}, device_id_type=MESH)

    rs_copy = [batch_copy(d, lambda to: rs_out.at[to], rs_in.at[d], rs_ss, rs_rs) for d in range(1, nb)]
    for c in rs_copy:
        c.start()
    loads[1].wait()
    gain = g_ref[...].astype(F).reshape(1, -1)
    bias = b_ref[...].astype(F).reshape(1, -1)

    def norm_step(i, c):
        r = pl.ds(pl.multiple_of(i * 256, 256), 256)
        normed[r, :] = layer_norm_rows(tok[r, :].astype(F), gain, bias).astype(BF)
        return c

    lax.fori_loop(0, rows // 256, norm_step, 0)
    loads[2].wait()

    def store(j):
        cols = pl.ds(pl.multiple_of(j * chunk, chunk), chunk)
        return pltpu.make_async_copy(qkv.at[:, cols], qkv_hbm.at[:, cols], st_sem.at[j])

    def mm_step(j, c):
        cols = pl.ds(pl.multiple_of(j * chunk, chunk), chunk)
        qkv[:, cols] = dg(normed[...], w[:, cols], 1, 0).astype(BF)
        store(j).start()
        return c

    steps = w.shape[1] // chunk
    lax.fori_loop(0, steps - 1, mm_step, 0)
    mine = pl.ds(pl.multiple_of(mb * rc, rc), rc)
    own = pre[mine, :] + ibf[mine, :]
    for c in rs_copy:
        c.wait_recv()
    for d in range(1, nb):
        own = own + rs_in[d, 0:rc, :].astype(F)
    hid = jnp.tanh(own)
    hid_ref[...] = hid
    ag_out[0:rc, :] = hid.astype(BF)
    ag_copy = [batch_copy(d, lambda to: ag_out, ag_in.at[d], ag_ss, ag_rs) for d in range(1, nb)]
    for c in ag_copy:
        c.start()
    lax.fori_loop(steps - 1, steps, mm_step, 0)

    def put_low(frm, block):
        low_ref[pl.ds(pl.multiple_of(frm * rc, rc), rc), :] = block

    def aa_copy(d, to, at):
        return pltpu.make_async_remote_copy(src_ref=aa_out.at[to], dst_ref=aa_in.at[at], send_sem=aa_ss.at[d],
                                            recv_sem=aa_rs.at[at], device_id=peer_id(to, nb), device_id_type=MESH)

    def pick(e):
        idx = jnp.int32(0)
        for s in range(slots):
            tid = ids_ref[s, e]
            idx = jnp.where(tid // td == mt, lax.rem(tid, td), idx)
        return tbl[idx]

    def send_table():
        put_low(mb, ag_out[0:rc, :])
        for c in ag_copy:
            c.wait_recv()
        for d in range(1, nb):
            put_low(lax.rem(mb + nb - d, nb), ag_in[d, 0:rc, :])
        loads[3].wait()
        ob = ob_ref[...].astype(F)
        for t in range(td):
            tbl[t] = (dg(low_ref[t * PAD:(t + 1) * PAD, :], outer[t], 1, 0) + ob[t:t + 1]).astype(BF)

        def aa_step(d, c):
            to = lax.rem(me + d, total)
            aa_out[to] = pick(to)
            aa_copy(d, to, me).start()
            return c

        lax.fori_loop(1, total, aa_step, 0)
        aa_in[me] = pick(me)

    blk = rows // slots
    hd = 64
    pair = 2 * hd
    pairs = width // pair
    scale = hd ** -0.5
    single = len_ref[0, 0] > blk
    first = lax.broadcasted_iota(jnp.int32, (1, pair), 1) < hd
    zero = jnp.zeros((), BF)
    tri = lax.broadcasted_iota(jnp.int32, (blk, blk), 0) <= lax.broadcasted_iota(jnp.int32, (blk, blk), 1)

    at_row, p_rows = strip_rows(slots, blk)

    def p_copies(h):
        buf = lax.rem(h, 2)
        return [pltpu.make_async_copy(p_s.at[buf, r], p_hbm.at[h, r], p_sem.at[buf, n])
                for n, r in enumerate(strip_parts(p_rows))]

    def p_wait(h):
        for cp in p_copies(h):
            cp.wait()

    def attend(h, c):
        pl.when(h == 3)(send_table)
        pl.when(h >= 2)(lambda: p_wait(h - 2))
        buf = lax.rem(h, 2)
        part = lambda third: qkv[:, pl.ds(pl.multiple_of(third * width + h * pair, pair), pair)]
        q_all = part(0) * jnp.asarray(scale, BF)
        k = part(1)
        km[0] = jnp.where(first, k, zero)
        km[1] = jnp.where(first, zero, k)
        vt = part(2).T
        ones = jnp.ones((PAD, rows), BF)
        vts = [jnp.concatenate([vt[j * hd:(j + 1) * hd], ones], axis=0) for j in range(2)]
        items = [(i, j) for i in range(slots) for j in range(2)]

        def scores(n):
            i, j = items[n]
            return dg(km[j, 0:(i + 1) * blk, :], q_all[i * blk:(i + 1) * blk], 1, 1)

        def top_of(n, s):
            lo = items[n][0] * blk
            top = jnp.max(jnp.where(tri, s[lo:], NEG), axis=0, keepdims=True)
            if lo:
                top = jnp.maximum(top, jnp.where(single, jnp.max(s[:lo], axis=0, keepdims=True), NEG))
            return top

        ahead = [scores(n) for n in range(AHEAD)]
        nxt_top = top_of(0, ahead[0])
        for n, (i, j) in enumerate(items):
            lo, hi = i * blk, (i + 1) * blk
            s, top = ahead.pop(0), nxt_top
            if n + AHEAD < len(items):
                ahead.append(scores(n + AHEAD))
            if n + 1 < len(items):
                nxt_top = top_of(n + 1, ahead[0])
            p = jnp.exp(jnp.where(tri, s[lo:], NEG) - top).astype(BF)
            if i:
                p = jnp.concatenate([jnp.exp(s[:lo] - jnp.where(single, top, -NEG)).astype(BF), p], axis=0)
            p_s[buf, at_row[i] + j * hi:at_row[i] + (j + 1) * hi, :] = p
            ot = dg(vts[j][:, 0:hi], p, 1, 0)
            ot_s[pl.ds(pl.multiple_of(h * pair + j * hd, hd), hd), lo:hi] = ot[:hd]
            top_s[h, j:j + 1, lo:hi] = top
            sum_s[h, j:j + 1, lo:hi] = ot[hd:hd + 1]
        for cp in p_copies(h):
            cp.start()
        return c

    lax.fori_loop(0, pairs, attend, 0)

    def aa_wait(d, c):
        frm = lax.rem(me + d, total)
        aa_copy(d, frm, frm).wait()
        return c

    lax.fori_loop(1, total, aa_wait, 0)
    for s in range(slots):
        owner = ids_ref[s, me] // td
        for b in range(nb):
            pkv_ref[s * PAD:(s + 1) * PAD, b * pc:(b + 1) * pc] = aa_in[owner * nb + b]
    heads = 2 * pairs

    def rows_of(i):
        return pl.ds(pl.multiple_of(i * blk, blk), blk)

    def att_store(i):
        return pltpu.make_async_copy(normed.at[rows_of(i), :], att_hbm.at[rows_of(i), :], at_sem.at[i])

    live = lax.broadcasted_iota(jnp.int32, (PAD, blk), 0) < plen
    spread = lambda x: spread_heads(x, heads, hd)

    def merge(g, c):
        blocks = [g * GROUP + n for n in range(GROUP)]
        sps = [dg(spread(prefix_rows(pkv_ref, single, i, 0, width)), qkv[rows_of(i), 0:width] * jnp.asarray(scale, BF), 1, 1)
               for i in blocks]
        vts = [spread(prefix_rows(pkv_ref, single, i, width, 2 * width)).T for i in blocks]
        pres, alphas, invs = [], [], []
        for i, sp, vt in zip(blocks, sps, vts):
            cols = rows_of(i)
            ps = []
            for hh in range(heads):
                at = (hh // 2, slice(hh % 2, hh % 2 + 1), cols)
                s = jnp.where(live, sp[hh * PAD:(hh + 1) * PAD], NEG)
                told = top_s[at]
                top = jnp.maximum(told, jnp.max(s, axis=0, keepdims=True))
                p = jnp.exp(s - top)
                alpha = jnp.exp(told - top)
                tot = alpha * sum_s[at] + jnp.sum(p, axis=0, keepdims=True)
                lse_ref[at] = top + jnp.log(tot)
                inv = 1.0 / tot
                ps.append(p.astype(BF))
                alphas.append(alpha * inv)
                fac_ref[at] = alpha * inv
                invs.append(inv)
            pres.append(dg(vt, jnp.concatenate(ps, axis=0), 1, 0))
        for n, i in enumerate(blocks):
            cols = rows_of(i)
            outs = [ot_s[hh * hd:(hh + 1) * hd, cols] * alphas[n * heads + hh]
                    + pres[n][hh * hd:(hh + 1) * hd] * invs[n * heads + hh] for hh in range(heads)]
            normed[cols, :] = jnp.concatenate(outs, axis=0).T.astype(BF)
            att_store(i).start()
        return c

    lax.fori_loop(0, slots // GROUP, merge, 0)
    for c in rs_copy + ag_copy:
        c.wait_send()
    for j in range(steps):
        store(j).wait()
    p_wait(pairs - 2)
    p_wait(pairs - 1)
    for i in range(slots):
        att_store(i).wait()


def front(nt, nb, task_ids, lengths, prefix_embed, inner, inner_bias, outer, outer_bias, gain, bias, tokens, weight):
    plen, td, depth = prefix_embed.shape
    rep = inner.shape[2]
    pc = outer.shape[2]
    rows, width = tokens.shape
    slots = task_ids.shape[0]
    total = nt * nb
    rc = td * PAD // nb
    rb = max(rc, PAD)
    chunk = 1024
    steps = weight.shape[1] // chunk
    p_rows = strip_rows(slots, rows // slots)[1]
    sds = jax.ShapeDtypeStruct
    vm = pl.BlockSpec(memory_space=pltpu.VMEM)
    hb = pl.BlockSpec(memory_space=pl.ANY)
    dma = pltpu.SemaphoreType.DMA
    return pl.pallas_call(
        functools.partial(front_kernel, nt, nb, td, plen, chunk),
        in_specs=[pl.BlockSpec(memory_space=pltpu.SMEM)] * 2 + [vm] * 5 + [hb] * 4,
        out_specs=[hb, hb, hb, vm, vm, vm, vm, vm],
        out_shape=[sds((rows, weight.shape[1]), BF), sds((rows, width), BF), sds((width // 128, p_rows, rows // slots), BF), sds((slots * PAD, nb * pc), BF), sds((rc, rep), F),
                   sds((td * PAD, rep), BF), sds((width // 128, 2, rows), F), sds((width // 128, 2, rows), F)],
        scratch_shapes=[
            pltpu.VMEM((rows, width), BF), pltpu.VMEM(weight.shape, BF), pltpu.VMEM(inner.shape, BF),
            pltpu.VMEM(outer.shape, BF), pltpu.VMEM((rows, width), BF), pltpu.VMEM((rows, weight.shape[1]), BF),
            pltpu.VMEM((width, rows), F), pltpu.VMEM((2, rows, 128), BF), pltpu.VMEM((2, p_rows, rows // slots), BF),
            pltpu.VMEM((width // 128, 2, rows), F), pltpu.VMEM((width // 128, 2, rows), F),
            pltpu.VMEM((td * PAD, rep), F), pltpu.VMEM((plen * td, depth), F), pltpu.VMEM((td * PAD, rep), F), pltpu.VMEM((td, PAD, pc), BF),
            pltpu.VMEM((nb, rb, rep), BF), pltpu.VMEM((nb, rb, rep), BF),
            pltpu.VMEM((rb, rep), BF), pltpu.VMEM((nb, rb, rep), BF),
            pltpu.VMEM((total, PAD, pc), BF), pltpu.VMEM((total, PAD, pc), BF),
            dma((4,)), dma((steps,)), dma((slots,)), dma((2, PARTS)), dma((nb,)), dma((nb,)), dma((nb,)), dma((nb,)), dma((total,)), dma((total,)),
        ],
        compiler_params=pltpu.CompilerParams(vmem_limit_bytes=62 * 2**20, collective_id=0, has_side_effects=True),
        name="front_attend",
    )(task_ids, lengths, prefix_embed, inner_bias, outer_bias, gain, bias,
      tokens, weight, inner, outer)


def middle_kernel(blk, fch, g_ref, b_ref, tok_hbm, att_hbm, ct_hbm, wo_hbm, we_hbm, wc_hbm,
                  out_hbm, gm_hbm, ga_hbm,
                  tok, att, ct, wo, we, wc, mid, n2, mean_s, rstd_s, ld_sem, st_sem):
    rows, width = tok.shape
    ff = we.shape[1]
    names = ((wo_hbm, wo), (att_hbm, att), (tok_hbm, tok), (we_hbm, we), (ct_hbm, ct), (wc_hbm, wc))
    loads = [pltpu.make_async_copy(s, d, ld_sem.at[i]) for i, (s, d) in enumerate(names)]
    for c in loads:
        c.start()
    gain = g_ref[...].astype(F).reshape(1, -1)
    bias = b_ref[...].astype(F).reshape(1, -1)
    inv = 1.0 / width
    steps = rows // blk
    for c in loads[:3]:
        c.wait()

    def first(i, c):
        r = pl.ds(pl.multiple_of(i * blk, blk), blk)
        x = tok[r, :].astype(F) + dg(att[r, :], wo[...], 1, 0)
        mid[r, :] = x
        mean = jnp.sum(x, axis=1, keepdims=True) * inv
        cen = x - mean
        rstd = lax.rsqrt(jnp.sum(cen * cen, axis=1, keepdims=True) * inv + 1e-5)
        mean_s[r, :] = mean
        rstd_s[r, :] = rstd
        n2[r, :] = (cen * rstd * gain + bias).astype(BF)
        return c

    lax.fori_loop(0, steps, first, 0)
    for c in loads[3:]:
        c.wait()

    def stores(i):
        r = pl.ds(pl.multiple_of(i * blk, blk), blk)
        return [pltpu.make_async_copy(s.at[r, :], d.at[r, :], st_sem.at[k, i])
                for k, (s, d) in enumerate(((tok, out_hbm), (mid, gm_hbm), (att, ga_hbm)))]

    def second(i, c):
        r = pl.ds(pl.multiple_of(i * blk, blk), blk)
        x2 = n2[r, :]
        g = ct[r, :]
        pair = lambda k: (dg(x2, we[:, k:k + fch], 1, 0), dg(g, wc[k:k + fch, :], 1, 1))
        y = gn = None
        nxt = pair(0)
        for k in range(0, ff, fch):
            v, up = nxt
            if k + fch < ff:
                nxt = pair(k + fch)
            vv = v * v
            t = jnp.tanh(v * (0.7978845608028654 + (0.7978845608028654 * 0.044715) * vv))
            half = 0.5 + 0.5 * t
            act = (v * half).astype(BF)
            slope = half + v * (0.5 - 0.5 * t * t) * (0.7978845608028654 + (3 * 0.7978845608028654 * 0.044715) * vv)
            gh = (up * slope).astype(BF)
            yk = dg(act, wc[k:k + fch, :], 1, 0)
            gk = dg(gh, we[:, k:k + fch], 1, 1)
            y = yk if y is None else y + yk
            gn = gk if gn is None else gn + gk
        x = mid[r, :]
        tok[r, :] = (x + y).astype(BF)
        rstd = rstd_s[r, :]
        xhat = (x - mean_s[r, :]) * rstd
        ug = gn * gain
        m1 = jnp.sum(ug, axis=1, keepdims=True) * inv
        m2 = jnp.sum(ug * xhat, axis=1, keepdims=True) * inv
        gmid = g.astype(F) + rstd * (ug - m1 - xhat * m2)
        mid[r, :] = gmid
        att[r, :] = dg(gmid.astype(BF), wo[...], 1, 1).astype(BF)
        for cp in stores(i):
            cp.start()
        return c

    lax.fori_loop(0, steps, second, 0)
    for i in range(steps):
        for cp in stores(i):
            cp.wait()


def middle(gain, bias, tokens, attended, ct, wo, we, wc, blk=256, fch=512):
    rows, width = tokens.shape
    ff = we.shape[1]
    sds = jax.ShapeDtypeStruct
    vm = pl.BlockSpec(memory_space=pltpu.VMEM)
    hb = pl.BlockSpec(memory_space=pl.ANY)
    dma = pltpu.SemaphoreType.DMA
    full = lambda t: pltpu.VMEM((rows, width), t)
    return pl.pallas_call(
        functools.partial(middle_kernel, blk, fch),
        in_specs=[vm, vm] + [hb] * 6,
        out_specs=[hb] * 3,
        out_shape=[sds((rows, width), BF), sds((rows, width), F), sds((rows, width), BF)],
        scratch_shapes=[full(BF), full(BF), full(BF), pltpu.VMEM(wo.shape, BF), pltpu.VMEM(we.shape, BF),
                        pltpu.VMEM(wc.shape, BF), full(F), full(BF), pltpu.VMEM((rows, 1), F), pltpu.VMEM((rows, 1), F),
                        dma((6,)), dma((3, rows // blk))],
        compiler_params=pltpu.CompilerParams(vmem_limit_bytes=62 * 2**20),
        name="middle",
    )(gain, bias, tokens, attended, ct, wo, we, wc)


def back_kernel(nt, nb, td, plen, blk,
                ids_ref, len_ref, hid_ref, g_ref, lse_ref, fac_ref, pkv_ref, outer_hbm, w_hbm, qkv_hbm, att_hbm, do_hbm, tok_hbm,
                gm_hbm, p_hbm,
                ig_hbm, gpre_ref, gtl_ref,
                outer, w, qkv, att, do_s, tok, gm, dqkv, dqp, p_s, vm, dka, dva, del_s, dpk_s, dpv_s, gbuf,
                sel, rs_out, rs_in, ag_out, ag_in, aa_out, aa_in, part,
                ld_sem, bl_sem, p_sem, st_sem, rs_ss, rs_rs, ag_ss, ag_rs, aa_ss, aa_rs):
    rows, width = tok.shape
    slots = ids_ref.shape[0]
    rc = td * PAD // nb
    pc = outer.shape[2]
    hd = 64
    pair = 2 * hd
    pairs = width // pair
    heads = 2 * pairs
    scale = hd ** -0.5
    inv = 1.0 / width
    single = len_ref[0, 0] > blk
    mt = lax.axis_index("task")
    mb = lax.axis_index("batch")

    def rows_of(i):
        return pl.ds(pl.multiple_of(i * blk, blk), blk)

    def block_loads(i):
        r = rows_of(i)
        return [pltpu.make_async_copy(s, d, bl_sem.at[k, i]) for k, (s, d) in enumerate((
            (qkv_hbm.at[r, 0:width], qkv.at[r, 0:width]), (do_hbm.at[r, :], do_s.at[r, :]), (att_hbm.at[r, :], att.at[r, :])))]

    rest = slice(width, 3 * width)
    names = ((qkv_hbm.at[:, rest], qkv.at[:, rest]), (outer_hbm, outer), (w_hbm, w), (tok_hbm, tok), (gm_hbm, gm))
    loads = [pltpu.make_async_copy(s, d, ld_sem.at[i]) for i, (s, d) in enumerate(names)]
    for i in range(slots):
        for c in block_loads(i):
            c.start()
    at_row, p_rows = strip_rows(slots, blk)

    def p_copies(h):
        buf = lax.rem(h, 2)
        return [pltpu.make_async_copy(p_hbm.at[h, r], p_s.at[buf, r], p_sem.at[buf, n])
                for n, r in enumerate(strip_parts(p_rows))]

    barrier, me, total = greet_all(nt, nb)
    live = lax.broadcasted_iota(jnp.int32, (PAD, blk), 0) < plen
    lane_head = lax.broadcasted_iota(jnp.int32, (heads, width), 1) // hd
    picker = jnp.where(lane_head == lax.broadcasted_iota(jnp.int32, (heads, width), 0), 1.0, 0.0).astype(BF)
    own_block = (lax.broadcasted_iota(jnp.int32, (heads * PAD, width), 0) // PAD
                 == lax.broadcasted_iota(jnp.int32, (heads * PAD, width), 1) // hd)

    def prefix_step(g, c):
        blocks = [g * GROUP + n for n in range(GROUP)]
        for i in blocks:
            for cp in block_loads(i):
                cp.wait()

        @pl.when(g == 0)
        def _():
            for cp in loads[:1] + p_copies(0) + p_copies(1):
                cp.start()

        qs = [qkv[rows_of(i), 0:width] * jnp.asarray(scale, BF) for i in blocks]
        dos = [do_s[rows_of(i), :] for i in blocks]
        kps = [spread_heads(prefix_rows(pkv_ref, single, i, 0, width), heads, hd) for i in blocks]
        sps = [dg(kp, q, 1, 1) for kp, q in zip(kps, qs)]
        dpps = [dg(spread_heads(prefix_rows(pkv_ref, single, i, width, 2 * width), heads, hd), do, 1, 1)
                for i, do in zip(blocks, dos)]
        deltas = []
        for i, do in zip(blocks, dos):
            prod = do.astype(F) * att[rows_of(i), :].astype(F)
            high = prod.astype(BF)
            deltas.append(dg(picker, high, 1, 1) + dg(picker, (prod - high.astype(F)).astype(BF), 1, 1))
        fold = lambda x: jnp.sum(jnp.where(own_block, x, 0.0).reshape(heads, PAD, width), axis=0)
        for i, q, do, kp, sp, dpp, delta in zip(blocks, qs, dos, kps, sps, dpps, deltas):
            cols = rows_of(i)
            ps, dss = [], []
            for hh in range(heads):
                one = slice(hh * PAD, (hh + 1) * PAD)
                at = (hh // 2, slice(hh % 2, hh % 2 + 1), cols)
                del_s[at] = delta[hh:hh + 1] * fac_ref[at]
                pr = jnp.where(live, jnp.exp(sp[one] - lse_ref[at]), 0.0)
                ps.append(pr.astype(BF))
                dss.append((pr * (dpp[one] - delta[hh:hh + 1])).astype(BF))
            ds = jnp.concatenate(dss, axis=0)
            dpk_s[i] = fold(dg(ds, q, 1, 0))
            dpv_s[i] = fold(dg(jnp.concatenate(ps, axis=0), do, 1, 0))
            dqp[:, cols] = dg(kp.T, ds, 1, 0)
        return c

    lax.fori_loop(0, slots // GROUP, prefix_step, 0)
    for c in loads[1:]:
        c.start()
    for ref in (dpk_s, dpv_s):
        whole = ref[0]
        for i in range(1, slots):
            whole = whole + ref[i]
        ref[0] = jnp.where(single, whole, ref[0])
        for i in range(1, slots):
            ref[i] = jnp.where(single, 0.0, ref[i])
    for o in range(nt):
        at = jnp.int32(0)
        for s in range(slots):
            at = jnp.where(ids_ref[s, me] // td == o, s, at)
        for half, ref in enumerate((dpk_s, dpv_s)):
            block = ref[at].astype(BF)
            for b in range(nb // 2):
                aa_out[o * nb + half * (nb // 2) + b] = block[:, b * pc:(b + 1) * pc]
    pl.semaphore_wait(barrier, total - 1)

    def aa_copy(d, to, at):
        return pltpu.make_async_remote_copy(src_ref=aa_out.at[to], dst_ref=aa_in.at[at], send_sem=aa_ss.at[d],
                                            recv_sem=aa_rs.at[at], device_id=peer_id(to, nb), device_id_type=MESH)

    def aa_step(d, c):
        aa_copy(d, lax.rem(me + d, total), me).start()
        return c

    lax.fori_loop(1, total, aa_step, 0)
    aa_in[me] = aa_out[me]
    lane = lax.broadcasted_iota(jnp.int32, (1, total * PAD), 1)
    task_of = jnp.zeros((1, total * PAD), jnp.int32)
    for e in range(total):
        idx = jnp.int32(0)
        for s in range(slots):
            tid = ids_ref[s, e]
            idx = jnp.where(tid // td == mt, lax.rem(tid, td), idx)
        task_of = jnp.where(lane // PAD == e, idx, task_of)
    want = task_of * PAD + lax.rem(lane, PAD)
    row = lax.broadcasted_iota(jnp.int32, (td * PAD, total * PAD), 0)
    sel[...] = jnp.where(row == want, 1.0, 0.0).astype(BF)

    def batch_copy(d, src, dst, ss, rs):
        to = lax.rem(mb + d, nb)
        return pltpu.make_async_remote_copy(src_ref=src(to), dst_ref=dst, send_sem=ss.at[d], recv_sem=rs.at[d],
                                            device_id={"task": mt, "batch": to}, device_id_type=MESH)

    rs_copy = [batch_copy(d, lambda to: rs_out.at[to], rs_in.at[d], rs_ss, rs_rs) for d in range(1, nb)]
    ag_copy = [batch_copy(d, lambda to: ag_out, ag_in.at[d], ag_ss, ag_rs) for d in range(1, nb)]

    def sum_table():
        def aa_wait(d, c):
            frm = lax.rem(me + d, total)
            aa_copy(d, frm, frm).wait()
            return c

        lax.fori_loop(1, total, aa_wait, 0)
        gtl_ref[...] = dg(sel[...], aa_in[...].reshape(total * PAD, pc), 1, 0).astype(BF)
        loads[1].wait()
        for t in range(td):
            part[t * PAD:(t + 1) * PAD, :] = dg(gtl_ref[t * PAD:(t + 1) * PAD, :], outer[t], 1, 1)
        for c in range(nb):
            rs_out[c, 0:rc, :] = part[c * rc:(c + 1) * rc, :].astype(BF)
        for c in rs_copy:
            c.start()

    def sum_hidden():
        own = part[pl.ds(pl.multiple_of(mb * rc, rc), rc), :]
        for c in rs_copy:
            c.wait_recv()
        for d in range(1, nb):
            own = own + rs_in[d, 0:rc, :].astype(F)
        hid = hid_ref[...]
        ag_out[0:rc, :] = (own * (1.0 - hid * hid)).astype(BF)
        for c in ag_copy:
            c.start()

    loads[0].wait()
    first = lax.broadcasted_iota(jnp.int32, (1, pair), 1) < hd
    zero = jnp.zeros((), BF)
    split = lambda a: (jnp.where(first, a, zero), jnp.where(first, zero, a))
    add = lambda a, b: b if a is None else a + b

    def attend(h, c):
        pl.when(h == 3)(sum_table)
        pl.when(h == 6)(sum_hidden)
        cols_of = lambda third: pl.ds(pl.multiple_of(third * width + h * pair, pair), pair)
        for cp in p_copies(h):
            cp.wait()
        buf = lax.rem(h, 2)
        q_all = qkv[:, cols_of(0)] * jnp.asarray(scale, BF)
        vm[0], vm[1] = split(qkv[:, cols_of(2)])
        kt = qkv[:, cols_of(1)].T
        fac = jnp.concatenate([jnp.broadcast_to(fac_ref[h, j:j + 1, :], (hd, rows)) for j in range(2)], axis=0).T
        do_all = (do_s[:, cols_of(0)].astype(F) * fac).astype(BF)
        qs, dos = split(q_all), split(do_all)

        def scores(i, j):
            lo, hi = i * blk, (i + 1) * blk
            return dg(vm[j, 0:hi, :], do_all[lo:hi], 1, 1)

        items = [(i, j) for i in reversed(range(slots)) for j in range(2)]
        ahead = [scores(*items[n]) for n in range(2)]
        for n, (i, j) in enumerate(items):
            lo, hi = i * blk, (i + 1) * blk
            dp = ahead.pop(0)
            if n + 2 < len(items):
                ahead.append(scores(*items[n + 2]))
            p = p_s[buf, at_row[i] + j * hi:at_row[i] + (j + 1) * hi, :]
            ds = (p.astype(F) * (dp - del_s[h, j:j + 1, lo:hi])).astype(BF)
            if j == 0:
                dk = dv = None
                dqs = []
            dv = add(dv, dg(p, dos[j][lo:hi], 1, 0))
            dk = add(dk, dg(ds, qs[j][lo:hi], 1, 0))
            dqs.append(dg(kt[j * hd:(j + 1) * hd, 0:hi], ds, 1, 0))
            if j:
                dqt = jnp.concatenate(dqs, axis=0) + dqp[pl.ds(pl.multiple_of(h * pair, pair), pair), lo:hi]
                dqkv[lo:hi, cols_of(0)] = (dqt.T * scale).astype(BF)
                if i == slots - 1:
                    dka[...] = dk
                    dva[...] = dv
                else:
                    dka[0:hi, :] += dk
                    dva[0:hi, :] += dv
        dqkv[:, cols_of(1)] = dka[...].astype(BF)
        dqkv[:, cols_of(2)] = dva[...].astype(BF)

        @pl.when(h + 2 < pairs)
        def _():
            for cp in p_copies(h + 2):
                cp.start()

        return c

    lax.fori_loop(0, pairs, attend, 0)
    gain = g_ref[...].astype(F).reshape(1, -1)
    for c in loads[2:]:
        c.wait()

    def store(i):
        return pltpu.make_async_copy(tok.at[rows_of(i), :], ig_hbm.at[rows_of(i), :], st_sem.at[i])

    def product(i):
        return dg(dqkv[rows_of(i), :], w[...], 1, 1)

    def norm_back(i, gn):
        r = rows_of(i)
        ug = gn * gain
        x = tok[r, :].astype(F)
        cen = x - jnp.sum(x, axis=1, keepdims=True) * inv
        rstd = lax.rsqrt(jnp.sum(cen * cen, axis=1, keepdims=True) * inv + 1e-5)
        xhat = cen * rstd
        m1 = jnp.sum(ug, axis=1, keepdims=True) * inv
        m2 = jnp.sum(ug * xhat, axis=1, keepdims=True) * inv
        tok[r, :] = (gm[r, :] + rstd * (ug - m1 - xhat * m2)).astype(BF)
        store(i).start()

    gbuf[0] = product(0)

    def mm_step(i, c):
        gbuf[lax.rem(i, 2)] = product(i)
        norm_back(i - 1, gbuf[lax.rem(i + 1, 2)])
        return c

    lax.fori_loop(1, slots, mm_step, 0)
    norm_back(slots - 1, gbuf[(slots - 1) % 2])

    def put(frm, block):
        gpre_ref[pl.ds(pl.multiple_of(frm * rc, rc), rc), :] = block

    put(mb, ag_out[0:rc, :])
    for c in ag_copy:
        c.wait_recv()
    for d in range(1, nb):
        put(lax.rem(mb + nb - d, nb), ag_in[d, 0:rc, :])
    for c in rs_copy + ag_copy:
        c.wait_send()
    for i in range(slots):
        store(i).wait()


def back(nt, nb, task_ids, lengths, hid, gain, lse, fac, pkv, outer, weight, qkv, attended, grad_att, tokens, grad_mid,
         lifted, plen):
    td, rep, pc = outer.shape
    rows, width = tokens.shape
    slots = task_ids.shape[0]
    total = nt * nb
    rc = td * PAD // nb
    rb = max(rc, PAD)
    blk = rows // slots
    sds = jax.ShapeDtypeStruct
    vm = pl.BlockSpec(memory_space=pltpu.VMEM)
    hb = pl.BlockSpec(memory_space=pl.ANY)
    dma = pltpu.SemaphoreType.DMA
    full = lambda t: pltpu.VMEM((rows, width), t)
    return pl.pallas_call(
        functools.partial(back_kernel, nt, nb, td, plen, blk),
        in_specs=[pl.BlockSpec(memory_space=pltpu.SMEM)] * 2 + [vm] * 5 + [hb] * 8,
        out_specs=[hb, vm, vm],
        out_shape=[sds((rows, width), BF), sds((td * PAD, rep), BF), sds((td * PAD, pc), BF)],
        scratch_shapes=[
            pltpu.VMEM(outer.shape, BF), pltpu.VMEM(weight.shape, BF), pltpu.VMEM(qkv.shape, BF), full(BF), full(BF),
            full(BF), full(F), pltpu.VMEM(qkv.shape, BF), pltpu.VMEM((width, rows), F),
            pltpu.VMEM((2,) + lifted.shape[1:], BF), pltpu.VMEM((2, rows, 128), BF), pltpu.VMEM((rows, 128), F),
            pltpu.VMEM((rows, 128), F), pltpu.VMEM(lse.shape, F), pltpu.VMEM((slots, PAD, width), F),
            pltpu.VMEM((slots, PAD, width), F), pltpu.VMEM((2, blk, width), F),
            pltpu.VMEM((td * PAD, total * PAD), BF),
            pltpu.VMEM((nb, rb, rep), BF), pltpu.VMEM((nb, rb, rep), BF),
            pltpu.VMEM((rb, rep), BF), pltpu.VMEM((nb, rb, rep), BF),
            pltpu.VMEM((total, PAD, pc), BF), pltpu.VMEM((total, PAD, pc), BF),
            pltpu.VMEM((td * PAD, rep), F),
            dma((5,)), dma((3, slots)), dma((2, PARTS)), dma((slots,)), dma((nb,)), dma((nb,)), dma((nb,)), dma((nb,)), dma((total,)),
            dma((total,)),
        ],
        compiler_params=pltpu.CompilerParams(vmem_limit_bytes=62 * 2**20, collective_id=1, has_side_effects=True),
        name="back_attend",
    )(task_ids, lengths, hid, gain, lse, fac, pkv, outer, weight, qkv, attended, grad_att, tokens, grad_mid, lifted)


def tail_kernel(plen, emb_ref, gpre_ref, low_ref, gtl_ref, ig_in, inner_hbm,
                ge_ref, gib_ref, gob_ref, ig_out, gi_hbm, go_hbm,
                ig, inner, gi, go, emf, embp, embt, lowt, ld_sem, ig_sem, gi_sem, go_sem):
    td = gib_ref.shape[0]
    ig_load = pltpu.make_async_copy(ig_in, ig, ld_sem.at[0])
    in_load = pltpu.make_async_copy(inner_hbm, inner, ld_sem.at[1])
    ig_load.start()
    in_load.start()
    emf[...] = emb_ref[...].astype(F).reshape(emf.shape)
    embp[...] = jnp.zeros_like(embp)
    for t in range(td):
        embp[t * PAD:t * PAD + plen, :] = emf[pl.ds(t, plen, stride=td), :]
    embt[...] = embp[...].astype(BF).T
    lowt[...] = low_ref[...].T
    zero = jnp.zeros((), BF)

    def stores(t):
        return [pltpu.make_async_copy(go.at[t], go_hbm.at[t], go_sem.at[t]),
                pltpu.make_async_copy(gi.at[t], gi_hbm.at[t], gi_sem.at[t])]

    def step(t, c):
        only = lambda x: jnp.where(lax.broadcasted_iota(jnp.int32, x.shape, 0) // PAD == t, x, zero)
        go[t] = dg(lowt[...], only(gtl_ref[...]), 1, 0)
        gi[t] = dg(embt[...], only(gpre_ref[...]), 1, 0)
        for cp in stores(t):
            cp.start()
        return c

    lax.fori_loop(0, td // 2, step, 0)
    ig_load.wait()
    ig_store = pltpu.make_async_copy(ig, ig_out, ig_sem)
    ig_store.start()
    lax.fori_loop(td // 2, td, step, 0)
    in_load.wait()
    for t in range(td):
        ge_ref[pl.ds(t, plen, stride=td), :] = dg(gpre_ref[t * PAD:(t + 1) * PAD, :], inner[t], 1, 1)[0:plen]
    shape = (td, td * PAD)
    own = lax.broadcasted_iota(jnp.int32, shape, 0) == lax.broadcasted_iota(jnp.int32, shape, 1) // PAD
    picker = jnp.where(own, 1.0, 0.0).astype(BF)
    gib_ref[...] = dg(picker, gpre_ref[...], 1, 0)
    gob_ref[...] = dg(picker, gtl_ref[...], 1, 0)

    def wait_step(t, c):
        for cp in stores(t):
            cp.wait()
        return c

    lax.fori_loop(0, td, wait_step, 0)
    ig_store.wait()


def tail(ig, emb, inner, gpre, low, gtl):
    plen, td, depth = emb.shape
    rep = inner.shape[2]
    pc = gtl.shape[1]
    sds = jax.ShapeDtypeStruct
    vm = pl.BlockSpec(memory_space=pltpu.VMEM)
    hb = pl.BlockSpec(memory_space=pl.ANY)
    dma = pltpu.SemaphoreType.DMA
    ge, gib, gob, ig, gi, go = pl.pallas_call(
        functools.partial(tail_kernel, plen),
        in_specs=[vm, vm, vm, vm, hb, hb],
        out_specs=[vm, vm, vm, hb, hb, hb],
        out_shape=[sds((plen * td, depth), F), sds((td, rep), F), sds((td, pc), F), sds(ig.shape, BF),
                   sds((td, depth, rep), F), sds((td, rep, pc), F)],
        scratch_shapes=[pltpu.VMEM(ig.shape, BF), pltpu.VMEM(inner.shape, BF), pltpu.VMEM((td, depth, rep), F),
                        pltpu.VMEM((td, rep, pc), F), pltpu.VMEM((plen * td, depth), F), pltpu.VMEM((td * PAD, depth), F),
                        pltpu.VMEM((depth, td * PAD), BF), pltpu.VMEM((rep, td * PAD), BF),
                        dma((2,)), dma, dma((td,)), dma((td,))],
        compiler_params=pltpu.CompilerParams(vmem_limit_bytes=62 * 2**20),
        name="tail",
    )(emb, gpre, low, gtl, ig, inner)
    return ig, ge, gi, gib, go, gob


def local(
    tokens,
    lengths,
    task_ids,
    prefix_embed,
    reparam_inner,
    reparam_inner_bias,
    reparam_outer,
    reparam_outer_bias,
    first_gain,
    first_bias,
    input_weight,
    output_weight,
    second_gain,
    second_bias,
    expand_weight,
    contract_weight,
    output_cotangent,
):
    prefix_len = prefix_embed.shape[1]
    task_count = lax.axis_size("task")
    batch_count = lax.axis_size("batch")
    ids = task_ids.T
    embed = prefix_embed.transpose(1, 0, 2)
    projected, attended, lifted, prefix_kv, hidden_chunk, hidden_low, log_totals, factors = front(
        task_count, batch_count, ids, lengths, embed, reparam_inner, reparam_inner_bias, reparam_outer,
        reparam_outer_bias, first_gain, first_bias, tokens, input_weight,
    )
    output, grad_mid, grad_attended = middle(
        second_gain, second_bias, tokens, attended, output_cotangent, output_weight, expand_weight, contract_weight
    )
    input_grad, grad_pre, grad_table = back(
        task_count, batch_count, ids, lengths, hidden_chunk, first_gain, log_totals, factors, prefix_kv, reparam_outer,
        input_weight, projected, attended, grad_attended, tokens, grad_mid, lifted, prefix_len,
    )
    input_grad, grad_embed, grad_inner, grad_inner_bias, grad_outer, grad_outer_bias = tail(
        input_grad, embed, reparam_inner, grad_pre, hidden_low, grad_table
    )
    grad_embed = grad_embed.reshape(embed.shape).transpose(1, 0, 2)
    return (
        output,
        input_grad,
        grad_embed,
        grad_inner,
        grad_inner_bias,
        grad_outer,
        grad_outer_bias,
    )


def solution(mesh):
    placed = (
        P(("task", "batch"), None),
        P(("task", "batch"), None),
        P(),
        P("task", None, "batch"),
        P("task", "batch", None),
        P("task", None),
        P("task", None, "batch"),
        P("task", "batch"),
        P(),
        P(),
        P(),
        P(),
        P(),
        P(),
        P(),
        P(),
        P(("task", "batch"), None),
    )
    return jax.shard_map(
        local,
        mesh=mesh,
        in_specs=placed,
        out_specs=(
            P(("task", "batch"), None),
            P(("task", "batch"), None),
            P("task", None, "batch"),
            P("task", "batch", None),
            P("task", None),
            P("task", None, "batch"),
            P("task", "batch"),
        ),
        check_vma=False,
    )
```

```python
import functools

import jax
import jax.numpy as jnp
from jax import lax
from jax.experimental import pallas as pl
from jax.experimental.pallas import tpu as pltpu
from jax.sharding import PartitionSpec as P

BF = jnp.bfloat16
F = jnp.float32
PAD = 16
NEG = -1e30
MESH = pl.DeviceIdType.MESH


def dg(a, b, ca, cb):
    return lax.dot_general(a, b, (((ca,), (cb,)), ((), ())), preferred_element_type=F)


AHEAD = 3
PARTS = 2
GROUP = 4


def peer_id(flat, nb):
    return {"task": flat // nb, "batch": flat % nb}


def layer_norm_rows(x, gain, bias):
    inv = 1.0 / x.shape[1]
    mean = jnp.sum(x, axis=1, keepdims=True) * inv
    cen = x - mean
    var = jnp.sum(cen * cen, axis=1, keepdims=True) * inv
    return cen * lax.rsqrt(var + 1e-5) * gain + bias


def greet_all(nt, nb):
    me = lax.axis_index("task") * nb + lax.axis_index("batch")
    total = nt * nb
    barrier = pltpu.get_barrier_semaphore()

    def greet(d, c):
        pl.semaphore_signal(barrier, inc=1, device_id=peer_id(lax.rem(me + d, total), nb), device_id_type=MESH)
        return c

    lax.fori_loop(1, total, greet, 0)
    return barrier, me, total


def strip_rows(slots, blk):
    at = [blk * i * (i + 1) for i in range(slots + 1)]
    return at, at[-1]


def strip_parts(total):
    return [slice(n * total // PARTS, (n + 1) * total // PARTS) for n in range(PARTS)]


def spread_heads(block, heads, hd):
    wide = jnp.concatenate([block] * heads, axis=0)
    row = lax.broadcasted_iota(jnp.int32, wide.shape, 0) // PAD
    lane = lax.broadcasted_iota(jnp.int32, wide.shape, 1) // hd
    return jnp.where(row == lane, wide, jnp.zeros((), wide.dtype))


def prefix_rows(ref, single, i, lo, hi):
    own = ref[pl.ds(pl.multiple_of(i * PAD, PAD), PAD), lo:hi]
    return jnp.where(single, ref[0:PAD, lo:hi], own)


def front_kernel(nt, nb, td, plen, chunk,
                 ids_ref, len_ref, emb_ref, ib_ref, ob_ref, g_ref, b_ref, tok_hbm, w_hbm, inner_hbm, outer_hbm,
                 qkv_hbm, att_hbm, p_hbm, pkv_ref, hid_ref, low_ref, lse_ref, fac_ref,
                 tok, w, inner, outer, normed, qkv, ot_s, km, p_s, top_s, sum_s, pre, emf, ibf, tbl, rs_out, rs_in, ag_out, ag_in, aa_out, aa_in,
                 ld_sem, st_sem, at_sem, p_sem, rs_ss, rs_rs, ag_ss, ag_rs, aa_ss, aa_rs):
    rows, width = tok.shape
    slots = ids_ref.shape[0]
    rc = td * PAD // nb
    pc = outer.shape[2]
    mt = lax.axis_index("task")
    mb = lax.axis_index("batch")
    loads = [pltpu.make_async_copy(s, d, ld_sem.at[i])
             for i, (s, d) in enumerate(((inner_hbm, inner), (tok_hbm, tok), (w_hbm, w), (outer_hbm, outer)))]
    for c in loads[:2]:
        c.start()
    barrier, me, total = greet_all(nt, nb)
    pre[...] = jnp.zeros_like(pre)
    emf[...] = emb_ref[...].astype(F).reshape(emf.shape)
    loads[0].wait()
    for c in loads[2:]:
        c.start()
    for t in range(td):
        pre[t * PAD:t * PAD + plen, :] = dg(emf[pl.ds(t, plen, stride=td), :].astype(BF), inner[t], 1, 0)
    for c in range(nb):
        rs_out[c, 0:rc, :] = pre[c * rc:(c + 1) * rc, :].astype(BF)
    ib = ib_ref[...].astype(F)
    for t in range(td):
        ibf[t * PAD:(t + 1) * PAD, :] = jnp.broadcast_to(ib[t:t + 1], (PAD, ib.shape[1]))
    pl.semaphore_wait(barrier, total - 1)

    def batch_copy(d, src, dst, ss, rs):
        to = lax.rem(mb + d, nb)
        return pltpu.make_async_remote_copy(src_ref=src(to), dst_ref=dst, send_sem=ss.at[d], recv_sem=rs.at[d],
                                            device_id={"task": mt, "batch": to}, device_id_type=MESH)

    rs_copy = [batch_copy(d, lambda to: rs_out.at[to], rs_in.at[d], rs_ss, rs_rs) for d in range(1, nb)]
    for c in rs_copy:
        c.start()
    loads[1].wait()
    gain = g_ref[...].astype(F).reshape(1, -1)
    bias = b_ref[...].astype(F).reshape(1, -1)

    def norm_step(i, c):
        r = pl.ds(pl.multiple_of(i * 256, 256), 256)
        normed[r, :] = layer_norm_rows(tok[r, :].astype(F), gain, bias).astype(BF)
        return c

    lax.fori_loop(0, rows // 256, norm_step, 0)
    loads[2].wait()

    def store(j):
        cols = pl.ds(pl.multiple_of(j * chunk, chunk), chunk)
        return pltpu.make_async_copy(qkv.at[:, cols], qkv_hbm.at[:, cols], st_sem.at[j])

    def mm_step(j, c):
        cols = pl.ds(pl.multiple_of(j * chunk, chunk), chunk)
        qkv[:, cols] = dg(normed[...], w[:, cols], 1, 0).astype(BF)
        store(j).start()
        return c

    steps = w.shape[1] // chunk
    lax.fori_loop(0, steps - 1, mm_step, 0)
    mine = pl.ds(pl.multiple_of(mb * rc, rc), rc)
    own = pre[mine, :] + ibf[mine, :]
    for c in rs_copy:
        c.wait_recv()
    for d in range(1, nb):
        own = own + rs_in[d, 0:rc, :].astype(F)
    hid = jnp.tanh(own)
    hid_ref[...] = hid
    ag_out[0:rc, :] = hid.astype(BF)
    ag_copy = [batch_copy(d, lambda to: ag_out, ag_in.at[d], ag_ss, ag_rs) for d in range(1, nb)]
    for c in ag_copy:
        c.start()
    lax.fori_loop(steps - 1, steps, mm_step, 0)

    def put_low(frm, block):
        low_ref[pl.ds(pl.multiple_of(frm * rc, rc), rc), :] = block

    def aa_copy(d, to, at):
        return pltpu.make_async_remote_copy(src_ref=aa_out.at[to], dst_ref=aa_in.at[at], send_sem=aa_ss.at[d],
                                            recv_sem=aa_rs.at[at], device_id=peer_id(to, nb), device_id_type=MESH)

    def pick(e):
        idx = jnp.int32(0)
        for s in range(slots):
            tid = ids_ref[s, e]
            idx = jnp.where(tid // td == mt, lax.rem(tid, td), idx)
        return tbl[idx]

    def send_table():
        put_low(mb, ag_out[0:rc, :])
        for c in ag_copy:
            c.wait_recv()
        for d in range(1, nb):
            put_low(lax.rem(mb + nb - d, nb), ag_in[d, 0:rc, :])
        loads[3].wait()
        ob = ob_ref[...].astype(F)
        for t in range(td):
            tbl[t] = (dg(low_ref[t * PAD:(t + 1) * PAD, :], outer[t], 1, 0) + ob[t:t + 1]).astype(BF)

        def aa_step(d, c):
            to = lax.rem(me + d, total)
            aa_out[to] = pick(to)
            aa_copy(d, to, me).start()
            return c

        lax.fori_loop(1, total, aa_step, 0)
        aa_in[me] = pick(me)

    blk = rows // slots
    hd = 64
    pair = 2 * hd
    pairs = width // pair
    scale = hd ** -0.5
    single = len_ref[0, 0] > blk
    first = lax.broadcasted_iota(jnp.int32, (1, pair), 1) < hd
    zero = jnp.zeros((), BF)
    tri = lax.broadcasted_iota(jnp.int32, (blk, blk), 0) <= lax.broadcasted_iota(jnp.int32, (blk, blk), 1)

    at_row, p_rows = strip_rows(slots, blk)

    def p_copies(h):
        buf = lax.rem(h, 2)
        return [pltpu.make_async_copy(p_s.at[buf, r], p_hbm.at[h, r], p_sem.at[buf, n])
                for n, r in enumerate(strip_parts(p_rows))]

    def p_wait(h):
        for cp in p_copies(h):
            cp.wait()

    def attend(h, c):
        pl.when(h == 3)(send_table)
        pl.when(h >= 2)(lambda: p_wait(h - 2))
        buf = lax.rem(h, 2)
        part = lambda third: qkv[:, pl.ds(pl.multiple_of(third * width + h * pair, pair), pair)]
        q_all = part(0) * jnp.asarray(scale, BF)
        k = part(1)
        km[0] = jnp.where(first, k, zero)
        km[1] = jnp.where(first, zero, k)
        vt = part(2).T
        ones = jnp.ones((PAD, rows), BF)
        vts = [jnp.concatenate([vt[j * hd:(j + 1) * hd], ones], axis=0) for j in range(2)]
        items = [(i, j) for i in range(slots) for j in range(2)]

        def scores(n):
            i, j = items[n]
            return dg(km[j, 0:(i + 1) * blk, :], q_all[i * blk:(i + 1) * blk], 1, 1)

        def top_of(n, s):
            lo = items[n][0] * blk
            top = jnp.max(jnp.where(tri, s[lo:], NEG), axis=0, keepdims=True)
            if lo:
                top = jnp.maximum(top, jnp.where(single, jnp.max(s[:lo], axis=0, keepdims=True), NEG))
            return top

        ahead = [scores(n) for n in range(AHEAD)]
        nxt_top = top_of(0, ahead[0])
        for n, (i, j) in enumerate(items):
            lo, hi = i * blk, (i + 1) * blk
            s, top = ahead.pop(0), nxt_top
            if n + AHEAD < len(items):
                ahead.append(scores(n + AHEAD))
            if n + 1 < len(items):
                nxt_top = top_of(n + 1, ahead[0])
            p = jnp.exp(jnp.where(tri, s[lo:], NEG) - top).astype(BF)
            if i:
                p = jnp.concatenate([jnp.exp(s[:lo] - jnp.where(single, top, -NEG)).astype(BF), p], axis=0)
            p_s[buf, at_row[i] + j * hi:at_row[i] + (j + 1) * hi, :] = p
            ot = dg(vts[j][:, 0:hi], p, 1, 0)
            ot_s[pl.ds(pl.multiple_of(h * pair + j * hd, hd), hd), lo:hi] = ot[:hd]
            top_s[h, j:j + 1, lo:hi] = top
            sum_s[h, j:j + 1, lo:hi] = ot[hd:hd + 1]
        for cp in p_copies(h):
            cp.start()
        return c

    lax.fori_loop(0, pairs, attend, 0)

    def aa_wait(d, c):
        frm = lax.rem(me + d, total)
        aa_copy(d, frm, frm).wait()
        return c

    lax.fori_loop(1, total, aa_wait, 0)
    for s in range(slots):
        owner = ids_ref[s, me] // td
        for b in range(nb):
            pkv_ref[s * PAD:(s + 1) * PAD, b * pc:(b + 1) * pc] = aa_in[owner * nb + b]
    heads = 2 * pairs

    def rows_of(i):
        return pl.ds(pl.multiple_of(i * blk, blk), blk)

    def att_store(i):
        return pltpu.make_async_copy(normed.at[rows_of(i), :], att_hbm.at[rows_of(i), :], at_sem.at[i])

    live = lax.broadcasted_iota(jnp.int32, (PAD, blk), 0) < plen
    spread = lambda x: spread_heads(x, heads, hd)

    def merge(g, c):
        blocks = [g * GROUP + n for n in range(GROUP)]
        sps = [dg(spread(prefix_rows(pkv_ref, single, i, 0, width)), qkv[rows_of(i), 0:width] * jnp.asarray(scale, BF), 1, 1)
               for i in blocks]
        vts = [spread(prefix_rows(pkv_ref, single, i, width, 2 * width)).T for i in blocks]
        pres, alphas, invs = [], [], []
        for i, sp, vt in zip(blocks, sps, vts):
            cols = rows_of(i)
            ps = []
            for hh in range(heads):
                at = (hh // 2, slice(hh % 2, hh % 2 + 1), cols)
                s = jnp.where(live, sp[hh * PAD:(hh + 1) * PAD], NEG)
                told = top_s[at]
                top = jnp.maximum(told, jnp.max(s, axis=0, keepdims=True))
                p = jnp.exp(s - top)
                alpha = jnp.exp(told - top)
                tot = alpha * sum_s[at] + jnp.sum(p, axis=0, keepdims=True)
                lse_ref[at] = top + jnp.log(tot)
                inv = 1.0 / tot
                ps.append(p.astype(BF))
                alphas.append(alpha * inv)
                fac_ref[at] = alpha * inv
                invs.append(inv)
            pres.append(dg(vt, jnp.concatenate(ps, axis=0), 1, 0))
        for n, i in enumerate(blocks):
            cols = rows_of(i)
            outs = [ot_s[hh * hd:(hh + 1) * hd, cols] * alphas[n * heads + hh]
                    + pres[n][hh * hd:(hh + 1) * hd] * invs[n * heads + hh] for hh in range(heads)]
            normed[cols, :] = jnp.concatenate(outs, axis=0).T.astype(BF)
            att_store(i).start()
        return c

    lax.fori_loop(0, slots // GROUP, merge, 0)
    for c in rs_copy + ag_copy:
        c.wait_send()
    for j in range(steps):
        store(j).wait()
    p_wait(pairs - 2)
    p_wait(pairs - 1)
    for i in range(slots):
        att_store(i).wait()


def front(nt, nb, task_ids, lengths, prefix_embed, inner, inner_bias, outer, outer_bias, gain, bias, tokens, weight):
    plen, td, depth = prefix_embed.shape
    rep = inner.shape[2]
    pc = outer.shape[2]
    rows, width = tokens.shape
    slots = task_ids.shape[0]
    total = nt * nb
    rc = td * PAD // nb
    rb = max(rc, PAD)
    chunk = 1024
    steps = weight.shape[1] // chunk
    p_rows = strip_rows(slots, rows // slots)[1]
    sds = jax.ShapeDtypeStruct
    vm = pl.BlockSpec(memory_space=pltpu.VMEM)
    hb = pl.BlockSpec(memory_space=pl.ANY)
    dma = pltpu.SemaphoreType.DMA
    return pl.pallas_call(
        functools.partial(front_kernel, nt, nb, td, plen, chunk),
        in_specs=[pl.BlockSpec(memory_space=pltpu.SMEM)] * 2 + [vm] * 5 + [hb] * 4,
        out_specs=[hb, hb, hb, vm, vm, vm, vm, vm],
        out_shape=[sds((rows, weight.shape[1]), BF), sds((rows, width), BF), sds((width // 128, p_rows, rows // slots), BF), sds((slots * PAD, nb * pc), BF), sds((rc, rep), F),
                   sds((td * PAD, rep), BF), sds((width // 128, 2, rows), F), sds((width // 128, 2, rows), F)],
        scratch_shapes=[
            pltpu.VMEM((rows, width), BF), pltpu.VMEM(weight.shape, BF), pltpu.VMEM(inner.shape, BF),
            pltpu.VMEM(outer.shape, BF), pltpu.VMEM((rows, width), BF), pltpu.VMEM((rows, weight.shape[1]), BF),
            pltpu.VMEM((width, rows), F), pltpu.VMEM((2, rows, 128), BF), pltpu.VMEM((2, p_rows, rows // slots), BF),
            pltpu.VMEM((width // 128, 2, rows), F), pltpu.VMEM((width // 128, 2, rows), F),
            pltpu.VMEM((td * PAD, rep), F), pltpu.VMEM((plen * td, depth), F), pltpu.VMEM((td * PAD, rep), F), pltpu.VMEM((td, PAD, pc), BF),
            pltpu.VMEM((nb, rb, rep), BF), pltpu.VMEM((nb, rb, rep), BF),
            pltpu.VMEM((rb, rep), BF), pltpu.VMEM((nb, rb, rep), BF),
            pltpu.VMEM((total, PAD, pc), BF), pltpu.VMEM((total, PAD, pc), BF),
            dma((4,)), dma((steps,)), dma((slots,)), dma((2, PARTS)), dma((nb,)), dma((nb,)), dma((nb,)), dma((nb,)), dma((total,)), dma((total,)),
        ],
        compiler_params=pltpu.CompilerParams(vmem_limit_bytes=62 * 2**20, collective_id=0, has_side_effects=True),
        name="front_attend",
    )(task_ids, lengths, prefix_embed, inner_bias, outer_bias, gain, bias,
      tokens, weight, inner, outer)


def middle_kernel(blk, fch, g_ref, b_ref, tok_hbm, att_hbm, ct_hbm, wo_hbm, we_hbm, wc_hbm,
                  out_hbm, gm_hbm, ga_hbm,
                  tok, att, ct, wo, we, wc, mid, n2, mean_s, rstd_s, ld_sem, st_sem):
    rows, width = tok.shape
    ff = we.shape[1]
    names = ((wo_hbm, wo), (att_hbm, att), (tok_hbm, tok), (we_hbm, we), (ct_hbm, ct), (wc_hbm, wc))
    loads = [pltpu.make_async_copy(s, d, ld_sem.at[i]) for i, (s, d) in enumerate(names)]
    for c in loads:
        c.start()
    gain = g_ref[...].astype(F).reshape(1, -1)
    bias = b_ref[...].astype(F).reshape(1, -1)
    inv = 1.0 / width
    steps = rows // blk
    for c in loads[:3]:
        c.wait()

    def first(i, c):
        r = pl.ds(pl.multiple_of(i * blk, blk), blk)
        x = tok[r, :].astype(F) + dg(att[r, :], wo[...], 1, 0)
        mid[r, :] = x
        mean = jnp.sum(x, axis=1, keepdims=True) * inv
        cen = x - mean
        rstd = lax.rsqrt(jnp.sum(cen * cen, axis=1, keepdims=True) * inv + 1e-5)
        mean_s[r, :] = mean
        rstd_s[r, :] = rstd
        n2[r, :] = (cen * rstd * gain + bias).astype(BF)
        return c

    lax.fori_loop(0, steps, first, 0)
    for c in loads[3:]:
        c.wait()

    def stores(i):
        r = pl.ds(pl.multiple_of(i * blk, blk), blk)
        return [pltpu.make_async_copy(s.at[r, :], d.at[r, :], st_sem.at[k, i])
                for k, (s, d) in enumerate(((tok, out_hbm), (mid, gm_hbm), (att, ga_hbm)))]

    def second(i, c):
        r = pl.ds(pl.multiple_of(i * blk, blk), blk)
        x2 = n2[r, :]
        g = ct[r, :]
        pair = lambda k: (dg(x2, we[:, k:k + fch], 1, 0), dg(g, wc[k:k + fch, :], 1, 1))
        y = gn = None
        nxt = pair(0)
        for k in range(0, ff, fch):
            v, up = nxt
            if k + fch < ff:
                nxt = pair(k + fch)
            vv = v * v
            t = jnp.tanh(v * (0.7978845608028654 + (0.7978845608028654 * 0.044715) * vv))
            half = 0.5 + 0.5 * t
            act = (v * half).astype(BF)
            slope = half + v * (0.5 - 0.5 * t * t) * (0.7978845608028654 + (3 * 0.7978845608028654 * 0.044715) * vv)
            gh = (up * slope).astype(BF)
            yk = dg(act, wc[k:k + fch, :], 1, 0)
            gk = dg(gh, we[:, k:k + fch], 1, 1)
            y = yk if y is None else y + yk
            gn = gk if gn is None else gn + gk
        x = mid[r, :]
        tok[r, :] = (x + y).astype(BF)
        rstd = rstd_s[r, :]
        xhat = (x - mean_s[r, :]) * rstd
        ug = gn * gain
        m1 = jnp.sum(ug, axis=1, keepdims=True) * inv
        m2 = jnp.sum(ug * xhat, axis=1, keepdims=True) * inv
        gmid = g.astype(F) + rstd * (ug - m1 - xhat * m2)
        mid[r, :] = gmid
        att[r, :] = dg(gmid.astype(BF), wo[...], 1, 1).astype(BF)
        for cp in stores(i):
            cp.start()
        return c

    lax.fori_loop(0, steps, second, 0)
    for i in range(steps):
        for cp in stores(i):
            cp.wait()


def middle(gain, bias, tokens, attended, ct, wo, we, wc, blk=256, fch=512):
    rows, width = tokens.shape
    ff = we.shape[1]
    sds = jax.ShapeDtypeStruct
    vm = pl.BlockSpec(memory_space=pltpu.VMEM)
    hb = pl.BlockSpec(memory_space=pl.ANY)
    dma = pltpu.SemaphoreType.DMA
    full = lambda t: pltpu.VMEM((rows, width), t)
    return pl.pallas_call(
        functools.partial(middle_kernel, blk, fch),
        in_specs=[vm, vm] + [hb] * 6,
        out_specs=[hb] * 3,
        out_shape=[sds((rows, width), BF), sds((rows, width), F), sds((rows, width), BF)],
        scratch_shapes=[full(BF), full(BF), full(BF), pltpu.VMEM(wo.shape, BF), pltpu.VMEM(we.shape, BF),
                        pltpu.VMEM(wc.shape, BF), full(F), full(BF), pltpu.VMEM((rows, 1), F), pltpu.VMEM((rows, 1), F),
                        dma((6,)), dma((3, rows // blk))],
        compiler_params=pltpu.CompilerParams(vmem_limit_bytes=62 * 2**20),
        name="middle",
    )(gain, bias, tokens, attended, ct, wo, we, wc)


def back_kernel(nt, nb, td, plen, blk,
                ids_ref, len_ref, hid_ref, g_ref, lse_ref, fac_ref, pkv_ref, outer_hbm, w_hbm, qkv_hbm, att_hbm, do_hbm, tok_hbm,
                gm_hbm, p_hbm,
                ig_hbm, gpre_ref, gtl_ref,
                outer, w, qkv, att, do_s, tok, gm, dqkv, dqp, p_s, vm, dka, dva, del_s, dpk_s, dpv_s, gbuf,
                sel, rs_out, rs_in, ag_out, ag_in, aa_out, aa_in, part,
                ld_sem, bl_sem, p_sem, st_sem, rs_ss, rs_rs, ag_ss, ag_rs, aa_ss, aa_rs):
    rows, width = tok.shape
    slots = ids_ref.shape[0]
    rc = td * PAD // nb
    pc = outer.shape[2]
    hd = 64
    pair = 2 * hd
    pairs = width // pair
    heads = 2 * pairs
    scale = hd ** -0.5
    inv = 1.0 / width
    single = len_ref[0, 0] > blk
    mt = lax.axis_index("task")
    mb = lax.axis_index("batch")

    def rows_of(i):
        return pl.ds(pl.multiple_of(i * blk, blk), blk)

    def block_loads(i):
        r = rows_of(i)
        return [pltpu.make_async_copy(s, d, bl_sem.at[k, i]) for k, (s, d) in enumerate((
            (qkv_hbm.at[r, 0:width], qkv.at[r, 0:width]), (do_hbm.at[r, :], do_s.at[r, :]), (att_hbm.at[r, :], att.at[r, :])))]

    rest = slice(width, 3 * width)
    names = ((qkv_hbm.at[:, rest], qkv.at[:, rest]), (outer_hbm, outer), (w_hbm, w), (tok_hbm, tok), (gm_hbm, gm))
    loads = [pltpu.make_async_copy(s, d, ld_sem.at[i]) for i, (s, d) in enumerate(names)]
    for i in range(slots):
        for c in block_loads(i):
            c.start()
    at_row, p_rows = strip_rows(slots, blk)

    def p_copies(h):
        buf = lax.rem(h, 2)
        return [pltpu.make_async_copy(p_hbm.at[h, r], p_s.at[buf, r], p_sem.at[buf, n])
                for n, r in enumerate(strip_parts(p_rows))]

    barrier, me, total = greet_all(nt, nb)
    live = lax.broadcasted_iota(jnp.int32, (PAD, blk), 0) < plen
    lane_head = lax.broadcasted_iota(jnp.int32, (heads, width), 1) // hd
    picker = jnp.where(lane_head == lax.broadcasted_iota(jnp.int32, (heads, width), 0), 1.0, 0.0).astype(BF)
    own_block = (lax.broadcasted_iota(jnp.int32, (heads * PAD, width), 0) // PAD
                 == lax.broadcasted_iota(jnp.int32, (heads * PAD, width), 1) // hd)

    def prefix_step(g, c):
        blocks = [g * GROUP + n for n in range(GROUP)]
        for i in blocks:
            for cp in block_loads(i):
                cp.wait()

        @pl.when(g == 0)
        def _():
            for cp in loads[:1] + p_copies(0) + p_copies(1):
                cp.start()

        qs = [qkv[rows_of(i), 0:width] * jnp.asarray(scale, BF) for i in blocks]
        dos = [do_s[rows_of(i), :] for i in blocks]
        kps = [spread_heads(prefix_rows(pkv_ref, single, i, 0, width), heads, hd) for i in blocks]
        sps = [dg(kp, q, 1, 1) for kp, q in zip(kps, qs)]
        dpps = [dg(spread_heads(prefix_rows(pkv_ref, single, i, width, 2 * width), heads, hd), do, 1, 1)
                for i, do in zip(blocks, dos)]
        deltas = []
        for i, do in zip(blocks, dos):
            prod = do.astype(F) * att[rows_of(i), :].astype(F)
            high = prod.astype(BF)
            deltas.append(dg(picker, high, 1, 1) + dg(picker, (prod - high.astype(F)).astype(BF), 1, 1))
        fold = lambda x: jnp.sum(jnp.where(own_block, x, 0.0).reshape(heads, PAD, width), axis=0)
        for i, q, do, kp, sp, dpp, delta in zip(blocks, qs, dos, kps, sps, dpps, deltas):
            cols = rows_of(i)
            ps, dss = [], []
            for hh in range(heads):
                one = slice(hh * PAD, (hh + 1) * PAD)
                at = (hh // 2, slice(hh % 2, hh % 2 + 1), cols)
                del_s[at] = delta[hh:hh + 1] * fac_ref[at]
                pr = jnp.where(live, jnp.exp(sp[one] - lse_ref[at]), 0.0)
                ps.append(pr.astype(BF))
                dss.append((pr * (dpp[one] - delta[hh:hh + 1])).astype(BF))
            ds = jnp.concatenate(dss, axis=0)
            dpk_s[i] = fold(dg(ds, q, 1, 0))
            dpv_s[i] = fold(dg(jnp.concatenate(ps, axis=0), do, 1, 0))
            dqp[:, cols] = dg(kp.T, ds, 1, 0)
        return c

    lax.fori_loop(0, slots // GROUP, prefix_step, 0)
    for c in loads[1:]:
        c.start()
    for ref in (dpk_s, dpv_s):
        whole = ref[0]
        for i in range(1, slots):
            whole = whole + ref[i]
        ref[0] = jnp.where(single, whole, ref[0])
        for i in range(1, slots):
            ref[i] = jnp.where(single, 0.0, ref[i])
    for o in range(nt):
        at = jnp.int32(0)
        for s in range(slots):
            at = jnp.where(ids_ref[s, me] // td == o, s, at)
        for half, ref in enumerate((dpk_s, dpv_s)):
            block = ref[at].astype(BF)
            for b in range(nb // 2):
                aa_out[o * nb + half * (nb // 2) + b] = block[:, b * pc:(b + 1) * pc]
    pl.semaphore_wait(barrier, total - 1)

    def aa_copy(d, to, at):
        return pltpu.make_async_remote_copy(src_ref=aa_out.at[to], dst_ref=aa_in.at[at], send_sem=aa_ss.at[d],
                                            recv_sem=aa_rs.at[at], device_id=peer_id(to, nb), device_id_type=MESH)

    def aa_step(d, c):
        aa_copy(d, lax.rem(me + d, total), me).start()
        return c

    lax.fori_loop(1, total, aa_step, 0)
    aa_in[me] = aa_out[me]
    lane = lax.broadcasted_iota(jnp.int32, (1, total * PAD), 1)
    task_of = jnp.zeros((1, total * PAD), jnp.int32)
    for e in range(total):
        idx = jnp.int32(0)
        for s in range(slots):
            tid = ids_ref[s, e]
            idx = jnp.where(tid // td == mt, lax.rem(tid, td), idx)
        task_of = jnp.where(lane // PAD == e, idx, task_of)
    want = task_of * PAD + lax.rem(lane, PAD)
    row = lax.broadcasted_iota(jnp.int32, (td * PAD, total * PAD), 0)
    sel[...] = jnp.where(row == want, 1.0, 0.0).astype(BF)

    def batch_copy(d, src, dst, ss, rs):
        to = lax.rem(mb + d, nb)
        return pltpu.make_async_remote_copy(src_ref=src(to), dst_ref=dst, send_sem=ss.at[d], recv_sem=rs.at[d],
                                            device_id={"task": mt, "batch": to}, device_id_type=MESH)

    rs_copy = [batch_copy(d, lambda to: rs_out.at[to], rs_in.at[d], rs_ss, rs_rs) for d in range(1, nb)]
    ag_copy = [batch_copy(d, lambda to: ag_out, ag_in.at[d], ag_ss, ag_rs) for d in range(1, nb)]

    def sum_table():
        def aa_wait(d, c):
            frm = lax.rem(me + d, total)
            aa_copy(d, frm, frm).wait()
            return c

        lax.fori_loop(1, total, aa_wait, 0)
        gtl_ref[...] = dg(sel[...], aa_in[...].reshape(total * PAD, pc), 1, 0).astype(BF)
        loads[1].wait()
        for t in range(td):
            part[t * PAD:(t + 1) * PAD, :] = dg(gtl_ref[t * PAD:(t + 1) * PAD, :], outer[t], 1, 1)
        for c in range(nb):
            rs_out[c, 0:rc, :] = part[c * rc:(c + 1) * rc, :].astype(BF)
        for c in rs_copy:
            c.start()

    def sum_hidden():
        own = part[pl.ds(pl.multiple_of(mb * rc, rc), rc), :]
        for c in rs_copy:
            c.wait_recv()
        for d in range(1, nb):
            own = own + rs_in[d, 0:rc, :].astype(F)
        hid = hid_ref[...]
        ag_out[0:rc, :] = (own * (1.0 - hid * hid)).astype(BF)
        for c in ag_copy:
            c.start()

    loads[0].wait()
    first = lax.broadcasted_iota(jnp.int32, (1, pair), 1) < hd
    zero = jnp.zeros((), BF)
    split = lambda a: (jnp.where(first, a, zero), jnp.where(first, zero, a))
    add = lambda a, b: b if a is None else a + b

    def attend(h, c):
        pl.when(h == 3)(sum_table)
        pl.when(h == 6)(sum_hidden)
        cols_of = lambda third: pl.ds(pl.multiple_of(third * width + h * pair, pair), pair)
        for cp in p_copies(h):
            cp.wait()
        buf = lax.rem(h, 2)
        q_all = qkv[:, cols_of(0)] * jnp.asarray(scale, BF)
        vm[0], vm[1] = split(qkv[:, cols_of(2)])
        kt = qkv[:, cols_of(1)].T
        fac = jnp.concatenate([jnp.broadcast_to(fac_ref[h, j:j + 1, :], (hd, rows)) for j in range(2)], axis=0).T
        do_all = (do_s[:, cols_of(0)].astype(F) * fac).astype(BF)
        qs, dos = split(q_all), split(do_all)

        def scores(i, j):
            lo, hi = i * blk, (i + 1) * blk
            return dg(vm[j, 0:hi, :], do_all[lo:hi], 1, 1)

        items = [(i, j) for i in reversed(range(slots)) for j in range(2)]
        ahead = [scores(*items[n]) for n in range(2)]
        for n, (i, j) in enumerate(items):
            lo, hi = i * blk, (i + 1) * blk
            dp = ahead.pop(0)
            if n + 2 < len(items):
                ahead.append(scores(*items[n + 2]))
            p = p_s[buf, at_row[i] + j * hi:at_row[i] + (j + 1) * hi, :]
            ds = (p.astype(F) * (dp - del_s[h, j:j + 1, lo:hi])).astype(BF)
            if j == 0:
                dk = dv = None
                dqs = []
            dv = add(dv, dg(p, dos[j][lo:hi], 1, 0))
            dk = add(dk, dg(ds, qs[j][lo:hi], 1, 0))
            dqs.append(dg(kt[j * hd:(j + 1) * hd, 0:hi], ds, 1, 0))
            if j:
                dqt = jnp.concatenate(dqs, axis=0) + dqp[pl.ds(pl.multiple_of(h * pair, pair), pair), lo:hi]
                dqkv[lo:hi, cols_of(0)] = (dqt.T * scale).astype(BF)
                if i == slots - 1:
                    dka[...] = dk
                    dva[...] = dv
                else:
                    dka[0:hi, :] += dk
                    dva[0:hi, :] += dv
        dqkv[:, cols_of(1)] = dka[...].astype(BF)
        dqkv[:, cols_of(2)] = dva[...].astype(BF)

        @pl.when(h + 2 < pairs)
        def _():
            for cp in p_copies(h + 2):
                cp.start()

        return c

    lax.fori_loop(0, pairs, attend, 0)
    gain = g_ref[...].astype(F).reshape(1, -1)
    for c in loads[2:]:
        c.wait()

    def store(i):
        return pltpu.make_async_copy(tok.at[rows_of(i), :], ig_hbm.at[rows_of(i), :], st_sem.at[i])

    def product(i):
        return dg(dqkv[rows_of(i), :], w[...], 1, 1)

    def norm_back(i, gn):
        r = rows_of(i)
        ug = gn * gain
        x = tok[r, :].astype(F)
        cen = x - jnp.sum(x, axis=1, keepdims=True) * inv
        rstd = lax.rsqrt(jnp.sum(cen * cen, axis=1, keepdims=True) * inv + 1e-5)
        xhat = cen * rstd
        m1 = jnp.sum(ug, axis=1, keepdims=True) * inv
        m2 = jnp.sum(ug * xhat, axis=1, keepdims=True) * inv
        tok[r, :] = (gm[r, :] + rstd * (ug - m1 - xhat * m2)).astype(BF)
        store(i).start()

    gbuf[0] = product(0)

    def mm_step(i, c):
        gbuf[lax.rem(i, 2)] = product(i)
        norm_back(i - 1, gbuf[lax.rem(i + 1, 2)])
        return c

    lax.fori_loop(1, slots, mm_step, 0)
    norm_back(slots - 1, gbuf[(slots - 1) % 2])

    def put(frm, block):
        gpre_ref[pl.ds(pl.multiple_of(frm * rc, rc), rc), :] = block

    put(mb, ag_out[0:rc, :])
    for c in ag_copy:
        c.wait_recv()
    for d in range(1, nb):
        put(lax.rem(mb + nb - d, nb), ag_in[d, 0:rc, :])
    for c in rs_copy + ag_copy:
        c.wait_send()
    for i in range(slots):
        store(i).wait()


def back(nt, nb, task_ids, lengths, hid, gain, lse, fac, pkv, outer, weight, qkv, attended, grad_att, tokens, grad_mid,
         lifted, plen):
    td, rep, pc = outer.shape
    rows, width = tokens.shape
    slots = task_ids.shape[0]
    total = nt * nb
    rc = td * PAD // nb
    rb = max(rc, PAD)
    blk = rows // slots
    sds = jax.ShapeDtypeStruct
    vm = pl.BlockSpec(memory_space=pltpu.VMEM)
    hb = pl.BlockSpec(memory_space=pl.ANY)
    dma = pltpu.SemaphoreType.DMA
    full = lambda t: pltpu.VMEM((rows, width), t)
    return pl.pallas_call(
        functools.partial(back_kernel, nt, nb, td, plen, blk),
        in_specs=[pl.BlockSpec(memory_space=pltpu.SMEM)] * 2 + [vm] * 5 + [hb] * 8,
        out_specs=[hb, vm, vm],
        out_shape=[sds((rows, width), BF), sds((td * PAD, rep), BF), sds((td * PAD, pc), BF)],
        scratch_shapes=[
            pltpu.VMEM(outer.shape, BF), pltpu.VMEM(weight.shape, BF), pltpu.VMEM(qkv.shape, BF), full(BF), full(BF),
            full(BF), full(F), pltpu.VMEM(qkv.shape, BF), pltpu.VMEM((width, rows), F),
            pltpu.VMEM((2,) + lifted.shape[1:], BF), pltpu.VMEM((2, rows, 128), BF), pltpu.VMEM((rows, 128), F),
            pltpu.VMEM((rows, 128), F), pltpu.VMEM(lse.shape, F), pltpu.VMEM((slots, PAD, width), F),
            pltpu.VMEM((slots, PAD, width), F), pltpu.VMEM((2, blk, width), F),
            pltpu.VMEM((td * PAD, total * PAD), BF),
            pltpu.VMEM((nb, rb, rep), BF), pltpu.VMEM((nb, rb, rep), BF),
            pltpu.VMEM((rb, rep), BF), pltpu.VMEM((nb, rb, rep), BF),
            pltpu.VMEM((total, PAD, pc), BF), pltpu.VMEM((total, PAD, pc), BF),
            pltpu.VMEM((td * PAD, rep), F),
            dma((5,)), dma((3, slots)), dma((2, PARTS)), dma((slots,)), dma((nb,)), dma((nb,)), dma((nb,)), dma((nb,)), dma((total,)),
            dma((total,)),
        ],
        compiler_params=pltpu.CompilerParams(vmem_limit_bytes=62 * 2**20, collective_id=1, has_side_effects=True),
        name="back_attend",
    )(task_ids, lengths, hid, gain, lse, fac, pkv, outer, weight, qkv, attended, grad_att, tokens, grad_mid, lifted)


def tail_kernel(plen, emb_ref, gpre_ref, low_ref, gtl_ref, ig_in, inner_hbm,
                ge_ref, gib_ref, gob_ref, ig_out, gi_hbm, go_hbm,
                ig, inner, gi, go, emf, embp, embt, lowt, ld_sem, ig_sem, gi_sem, go_sem):
    td = gib_ref.shape[0]
    ig_load = pltpu.make_async_copy(ig_in, ig, ld_sem.at[0])
    in_load = pltpu.make_async_copy(inner_hbm, inner, ld_sem.at[1])
    ig_load.start()
    in_load.start()
    emf[...] = emb_ref[...].astype(F).reshape(emf.shape)
    embp[...] = jnp.zeros_like(embp)
    for t in range(td):
        embp[t * PAD:t * PAD + plen, :] = emf[pl.ds(t, plen, stride=td), :]
    embt[...] = embp[...].astype(BF).T
    lowt[...] = low_ref[...].T
    zero = jnp.zeros((), BF)

    def stores(t):
        return [pltpu.make_async_copy(go.at[t], go_hbm.at[t], go_sem.at[t]),
                pltpu.make_async_copy(gi.at[t], gi_hbm.at[t], gi_sem.at[t])]

    def step(t, c):
        only = lambda x: jnp.where(lax.broadcasted_iota(jnp.int32, x.shape, 0) // PAD == t, x, zero)
        go[t] = dg(lowt[...], only(gtl_ref[...]), 1, 0)
        gi[t] = dg(embt[...], only(gpre_ref[...]), 1, 0)
        for cp in stores(t):
            cp.start()
        return c

    lax.fori_loop(0, td // 2, step, 0)
    ig_load.wait()
    ig_store = pltpu.make_async_copy(ig, ig_out, ig_sem)
    ig_store.start()
    lax.fori_loop(td // 2, td, step, 0)
    in_load.wait()
    for t in range(td):
        ge_ref[pl.ds(t, plen, stride=td), :] = dg(gpre_ref[t * PAD:(t + 1) * PAD, :], inner[t], 1, 1)[0:plen]
    shape = (td, td * PAD)
    own = lax.broadcasted_iota(jnp.int32, shape, 0) == lax.broadcasted_iota(jnp.int32, shape, 1) // PAD
    picker = jnp.where(own, 1.0, 0.0).astype(BF)
    gib_ref[...] = dg(picker, gpre_ref[...], 1, 0)
    gob_ref[...] = dg(picker, gtl_ref[...], 1, 0)

    def wait_step(t, c):
        for cp in stores(t):
            cp.wait()
        return c

    lax.fori_loop(0, td, wait_step, 0)
    ig_store.wait()


def tail(ig, emb, inner, gpre, low, gtl):
    plen, td, depth = emb.shape
    rep = inner.shape[2]
    pc = gtl.shape[1]
    sds = jax.ShapeDtypeStruct
    vm = pl.BlockSpec(memory_space=pltpu.VMEM)
    hb = pl.BlockSpec(memory_space=pl.ANY)
    dma = pltpu.SemaphoreType.DMA
    ge, gib, gob, ig, gi, go = pl.pallas_call(
        functools.partial(tail_kernel, plen),
        in_specs=[vm, vm, vm, vm, hb, hb],
        out_specs=[vm, vm, vm, hb, hb, hb],
        out_shape=[sds((plen * td, depth), F), sds((td, rep), F), sds((td, pc), F), sds(ig.shape, BF),
                   sds((td, depth, rep), F), sds((td, rep, pc), F)],
        scratch_shapes=[pltpu.VMEM(ig.shape, BF), pltpu.VMEM(inner.shape, BF), pltpu.VMEM((td, depth, rep), F),
                        pltpu.VMEM((td, rep, pc), F), pltpu.VMEM((plen * td, depth), F), pltpu.VMEM((td * PAD, depth), F),
                        pltpu.VMEM((depth, td * PAD), BF), pltpu.VMEM((rep, td * PAD), BF),
                        dma((2,)), dma, dma((td,)), dma((td,))],
        compiler_params=pltpu.CompilerParams(vmem_limit_bytes=62 * 2**20),
        name="tail",
    )(emb, gpre, low, gtl, ig, inner)
    return ig, ge, gi, gib, go, gob


def local(
    tokens,
    lengths,
    task_ids,
    prefix_embed,
    reparam_inner,
    reparam_inner_bias,
    reparam_outer,
    reparam_outer_bias,
    first_gain,
    first_bias,
    input_weight,
    output_weight,
    second_gain,
    second_bias,
    expand_weight,
    contract_weight,
    output_cotangent,
):
    prefix_len = prefix_embed.shape[1]
    task_count = lax.axis_size("task")
    batch_count = lax.axis_size("batch")
    ids = task_ids.T
    embed = prefix_embed.transpose(1, 0, 2)
    projected, attended, lifted, prefix_kv, hidden_chunk, hidden_low, log_totals, factors = front(
        task_count, batch_count, ids, lengths, embed, reparam_inner, reparam_inner_bias, reparam_outer,
        reparam_outer_bias, first_gain, first_bias, tokens, input_weight,
    )
    output, grad_mid, grad_attended = middle(
        second_gain, second_bias, tokens, attended, output_cotangent, output_weight, expand_weight, contract_weight
    )
    input_grad, grad_pre, grad_table = back(
        task_count, batch_count, ids, lengths, hidden_chunk, first_gain, log_totals, factors, prefix_kv, reparam_outer,
        input_weight, projected, attended, grad_attended, tokens, grad_mid, lifted, prefix_len,
    )
    input_grad, grad_embed, grad_inner, grad_inner_bias, grad_outer, grad_outer_bias = tail(
        input_grad, embed, reparam_inner, grad_pre, hidden_low, grad_table
    )
    grad_embed = grad_embed.reshape(embed.shape).transpose(1, 0, 2)
    return (
        output,
        input_grad,
        grad_embed,
        grad_inner,
        grad_inner_bias,
        grad_outer,
        grad_outer_bias,
    )


def solution(mesh):
    placed = (
        P(("task", "batch"), None),
        P(("task", "batch"), None),
        P(),
        P("task", None, "batch"),
        P("task", "batch", None),
        P("task", None),
        P("task", None, "batch"),
        P("task", "batch"),
        P(),
        P(),
        P(),
        P(),
        P(),
        P(),
        P(),
        P(),
        P(("task", "batch"), None),
    )
    return jax.shard_map(
        local,
        mesh=mesh,
        in_specs=placed,
        out_specs=(
            P(("task", "batch"), None),
            P(("task", "batch"), None),
            P("task", None, "batch"),
            P("task", "batch", None),
            P("task", None),
            P("task", None, "batch"),
            P("task", "batch"),
        ),
        check_vma=False,
    )
```
